32 devices in a mesh: seq: 4 (over y, x), shard: 8 (over z, core).
Axes of the slice: x: 2, y: 2, z: 4, core: 2. Of those that a mesh axis runs over, the one named last changes fastest.
Arguments:
- tokens: bfloat16 [8192, 2048], P(('shard', 'seq')), may hold values from -6 to 6
- cotangent: bfloat16 [8192, 2048], P(('shard', 'seq')), may hold values from -6 to 6
- gain_attn: float32 [2048], replicated, may hold values from 0.5 to 1.5
- gain_ffn: float32 [2048], replicated, may hold values from 0.5 to 1.5
- mixer_in: bfloat16 [12288, 2048], P('shard'), may hold values from -0.088388348 to 0.088388348, as said below
- mixer_out: bfloat16 [2048, 4096], P('shard'), may hold values from -0.0625 to 0.0625, as said below
- ffn_in: bfloat16 [8192, 2048], P('shard'), may hold values from -0.088388348 to 0.088388348, as said below
- ffn_out: bfloat16 [2048, 4096], P('shard'), may hold values from -0.0625 to 0.0625, as said below
- segment_order: int32 [8], replicated, may hold values from 0 to 7, each once
- decay_index: int32 [8], replicated, may hold values from 0 to 11
Outputs:
- output: bfloat16 [8192, 2048], P(('shard', 'seq'))
- input_grad: bfloat16 [8192, 2048], P(('shard', 'seq'))
- gain_attn_grad: float32 [2048], replicated
- gain_ffn_grad: float32 [2048], replicated
- mixer_in_grad: float32 [12288, 2048], P('shard')
- mixer_out_grad: float32 [2048, 4096], P('shard')
- ffn_in_grad: float32 [8192, 2048], P('shard')
- ffn_out_grad: float32 [2048, 4096], P('shard')
The draws below stay inside these ranges and needn't reach their ends.
Inputs may be any that keep to these rules, and one draw needn't show every extreme that they name: `segment_order`: a permutation: each place 0 to 7 once. `mixer_in`: independent entries of mean 0 and deviation 2048^-0.5. `mixer_out`: independent entries of mean 0 and deviation 4096^-0.5. `ffn_in`: independent entries of mean 0 and deviation 2048^-0.5. `ffn_out`: independent entries of mean 0 and deviation 4096^-0.5.
All inputs are finite; a program needn't handle non-finite values.
Results may differ from the reference program's by a relative error of at most 0.022.
Values may be sent and summed in bfloat16 or wider, within the bound.
No kernel may reach another device: no remote copies, remote signals or barrier semaphores. Data moves between devices by JAX's collectives and lax.ppermute only.
A program may use at most 512 MiB of HBM per device.

```python
import jax
import jax.numpy as jnp
from jax import lax

D = 2048
HEADS = 8
DK = 256
DV = 512
FF = 4096
DECAY_LEVELS = 12
QK = 2048
V = 4096
SEG = 1024
SEGMENTS = 8
SEQLEN = 8192
BLK = 512


def weight_entries(key, rows, cols, fan_in):
    scale = fan_in ** (-0.5)
    values = jnp.clip(jax.random.normal(key, (rows, cols), jnp.float32), -4.0, 4.0)
    return values * scale


def draw_mixer_in(key, part):
    key = jax.random.fold_in(key, 11)
    return weight_entries(key, 2 * QK + 2 * V, D, D).astype(jnp.bfloat16)


def draw_mixer_out(key, part):
    key = jax.random.fold_in(key, 12)
    return weight_entries(key, D, V, V).astype(jnp.bfloat16)


def draw_ffn_in(key, part):
    key = jax.random.fold_in(key, 13)
    return weight_entries(key, 2 * FF, D, D).astype(jnp.bfloat16)


def draw_ffn_out(key, part):
    key = jax.random.fold_in(key, 14)
    return weight_entries(key, D, FF, FF).astype(jnp.bfloat16)


def set_ends(values, key, least, high):
    longest = values.shape.index(max(values.shape))
    spots = []
    for shift in (0, 1):
        where = [jax.random.randint(jax.random.fold_in(key, axis), (), 0, length) for axis, length in enumerate(values.shape)]
        where[longest] = (where[longest] + shift) % values.shape[longest]
        spots.append(tuple(where))
    return values.at[spots[0]].set(least).at[spots[1]].set(high)


def block_scale(key, dims, pieces, least, high):
    level = 1.0
    for dim, parts in pieces:
        draws = jax.random.uniform(jax.random.fold_in(jax.random.fold_in(key, 6), dim), (parts,), jnp.float32, least / len(pieces), high / len(pieces))
        level = level * jnp.repeat(jnp.exp(draws), dims[dim] // parts).reshape((-1,) + (1,) * (len(dims) - 1 - dim))
    return level


def bell_draw(key, dims, deviation, bound, split=(), kind=jnp.bfloat16):
    loudness = block_scale(key, dims, split, -0.22, 0.18) if split else 1.0
    drawn = jax.random.normal(key, dims, jnp.float32) * deviation * loudness
    return jnp.minimum(jnp.maximum(drawn, -bound), bound).astype(kind)


def setup_inputs(seed: int = 0) -> dict:
    splits = jax.random.split(jax.random.key(seed), 11)
    tokens = bell_draw(splits[0], (SEQLEN, D), 1.0, 6.0, ((0, 32),))
    cotangent = bell_draw(splits[1], (SEQLEN, D), 1.0, 6.0, ((0, 32),))
    gain_attn = jnp.clip(1.0 + 0.1 * jax.random.normal(splits[2], (D,), jnp.float32), 0.5, 1.5)
    gain_ffn = jnp.clip(1.0 + 0.1 * jax.random.normal(splits[3], (D,), jnp.float32), 0.5, 1.5)
    mixer_in = draw_mixer_in(jax.random.fold_in(splits[10], 71), 0)
    mixer_out = draw_mixer_out(jax.random.fold_in(splits[10], 71), 0)
    ffn_in = draw_ffn_in(jax.random.fold_in(splits[10], 71), 0)
    ffn_out = draw_ffn_out(jax.random.fold_in(splits[10], 71), 0)
    segment_order = jax.random.permutation(splits[8], SEGMENTS).astype(jnp.int32)
    decay_index = set_ends(jax.random.randint(splits[9], (HEADS,), 0, DECAY_LEVELS), jax.random.fold_in(splits[9], 1), 0, DECAY_LEVELS - 1).astype(jnp.int32)
    return {"tokens": tokens, "cotangent": cotangent, "gain_attn": gain_attn, "gain_ffn": gain_ffn, "mixer_in": mixer_in, "mixer_out": mixer_out, "ffn_in": ffn_in, "ffn_out": ffn_out, "segment_order": segment_order, "decay_index": decay_index}


@jax.custom_vjp
def reduced_precision(v):
    return lax.optimization_barrier(v.astype(jnp.bfloat16)).astype(jnp.float32)

@jax.custom_vjp
def reduced_backward_cast(v):
    return v

def low_keep(v):
    return (reduced_precision(v), None)

def low_pass(kept, grad):
    return (grad,)

def back_keep(v):
    return (v, None)

def back_low(kept, grad):
    return (reduced_precision(grad),)
reduced_precision.defvjp(low_keep, low_pass)
reduced_backward_cast.defvjp(back_keep, back_low)
EPS_NORM = 1e-06
EPS_GROUP = 1e-05
HIGHEST_ACCURACY = lax.Precision.HIGHEST

def matmul_nt(left, right):
    return lax.dot_general(left, right, (((1,), (1,)), ((), ())), precision=HIGHEST_ACCURACY, preferred_element_type=jnp.float32)

def rms_scale(v, gain):
    return v * lax.rsqrt(lax.optimization_barrier(jnp.mean(v * v, axis=-1, keepdims=True)) + EPS_NORM) * gain

def group_norm(v):
    centred = v - lax.optimization_barrier(jnp.mean(v, axis=-1, keepdims=True))
    return centred * lax.rsqrt(lax.optimization_barrier(jnp.mean(centred * centred, axis=-1, keepdims=True)) + EPS_GROUP)

def rotate(v, angles):
    half = v.shape[-1] // 2
    first = v[..., :half]
    second = v[..., half:]
    cosine = jnp.cos(angles)[:, None, :]
    sine = jnp.sin(angles)[:, None, :]
    return jnp.concatenate([first * cosine - second * sine, second * cosine + first * sine], axis=-1)

def retention_block(retention_state, block, logs):
    queries, keys, value_rows = block
    size = queries.shape[1]
    steps = jnp.arange(size).astype(jnp.float32)
    gap = steps[:, None] - steps[None, :]
    mask = jnp.where(gap[None] >= 0.0, jnp.exp(jnp.maximum(gap, 0.0)[None] * logs[:, None, None]), 0.0)
    scores = reduced_backward_cast(jnp.einsum('hnk,hmk->hnm', queries, keys, precision=HIGHEST_ACCURACY))
    weights = reduced_backward_cast(reduced_precision(scores * mask))
    inner = jnp.einsum('hnm,hmv->hnv', weights, value_rows, precision=HIGHEST_ACCURACY)
    q_decay = jnp.exp((steps + 1.0)[None, :] * logs[:, None])
    k_decay = jnp.exp((size - 1.0 - steps)[None, :] * logs[:, None])
    query_decayed = reduced_backward_cast(reduced_precision(queries * q_decay[..., None]))
    cross_block_term = jnp.einsum('xyq,xqb->xyb', query_decayed, reduced_precision(retention_state), precision=HIGHEST_ACCURACY)
    key_decayed = reduced_backward_cast(reduced_precision(keys * k_decay[..., None]))
    state_increment = reduced_backward_cast(jnp.einsum('qdp,qdg->qpg', key_decayed, value_rows, precision=HIGHEST_ACCURACY))
    new_state = jnp.exp(size * logs)[:, None, None] * retention_state + state_increment
    return (new_state, reduced_backward_cast(inner + cross_block_term))

def reference(tokens, cotangent, gain_attn, gain_ffn, mixer_in, mixer_out, ffn_in, ffn_out, segment_order, decay_index):
    logs = jnp.log1p(-jnp.exp2(-(5.0 + decay_index.astype(jnp.float32))))
    inverse = jnp.argsort(segment_order).astype(jnp.int32)
    offsets = jnp.arange(SEG, dtype=jnp.int32)
    time_rows = (inverse[:, None] * SEG + offsets[None, :]).reshape(-1)
    positions = (segment_order.astype(jnp.int32)[:, None] * SEG + offsets[None, :]).reshape(-1)
    half = DK // 2
    inv_freq = jnp.exp(-jnp.log(10000.0) * jnp.arange(half).astype(jnp.float32) / half)
    angles = positions.astype(jnp.float32)[:, None] * inv_freq[None, :]

    def to_blocks(v):
        return v.reshape(SEQLEN // BLK, BLK, HEADS, v.shape[-1]).transpose(0, 2, 1, 3)

    def step(retention_state, block):
        return retention_block(retention_state, block, logs)

    def forward(x, g_attn, g_ffn, w_in, w_out, f_in, f_out):
        normed = reduced_precision(rms_scale(x, g_attn))
        proj = reduced_backward_cast(matmul_nt(normed, w_in))
        queries = proj[:, :QK].reshape(SEQLEN, HEADS, DK)
        keys = proj[:, QK:2 * QK].reshape(SEQLEN, HEADS, DK)
        value_rows = proj[:, 2 * QK:2 * QK + V].reshape(SEQLEN, HEADS, DV)
        gate = proj[:, 2 * QK + V:]
        queries = reduced_backward_cast(reduced_precision(rotate(queries, angles)))
        keys = reduced_backward_cast(reduced_precision(rotate(keys, angles)))
        value_rows = reduced_backward_cast(reduced_precision(value_rows))
        start = jnp.zeros((HEADS, DK, DV), jnp.float32)
        blocks = (to_blocks(queries[time_rows]), to_blocks(keys[time_rows]), to_blocks(value_rows[time_rows]))
        ignored, outs = lax.scan(jax.checkpoint(step), start, blocks)
        retained = outs.transpose(0, 2, 1, 3).reshape(SEQLEN, HEADS, DV)
        normal_heads = reduced_backward_cast(reduced_precision(group_norm(retained)))
        mixed = normal_heads[positions].reshape(SEQLEN, V)
        hidden = reduced_precision(jax.nn.silu(gate) * mixed)
        attn = reduced_backward_cast(matmul_nt(hidden, w_out))
        resid = x + attn
        normed2 = reduced_precision(rms_scale(resid, g_ffn))
        proj2 = reduced_backward_cast(matmul_nt(normed2, f_in))
        inner2 = reduced_precision(jax.nn.gelu(proj2[:, :FF]) * proj2[:, FF:])
        return resid + reduced_backward_cast(matmul_nt(inner2, f_out))
    inputs = (tokens.astype(jnp.float32), gain_attn.astype(jnp.float32), gain_ffn.astype(jnp.float32), mixer_in.astype(jnp.float32), mixer_out.astype(jnp.float32), ffn_in.astype(jnp.float32), ffn_out.astype(jnp.float32))
    result, pullback = jax.vjp(forward, *inputs)
    grads = pullback(cotangent.astype(jnp.float32))
    return (result.astype(jnp.bfloat16), grads[0].astype(jnp.bfloat16), grads[1], grads[2], grads[3], grads[4], grads[5], grads[6])
```

```python
import jax
import jax.numpy as jnp
import numpy as np
from jax import lax
from jax.sharding import PartitionSpec as P

DK = 256
DV = 512
FF = 4096
QK = 2048
V = 4096


EPS_NORM = 1e-06
EPS_GROUP = 1e-05

F32 = jnp.float32
BF16 = jnp.bfloat16


def dot_nt(left, right, kind=F32):
    return lax.dot_general(
        left, right, (((1,), (1,)), ((), ())), preferred_element_type=F32
    ).astype(kind)


def dot_nn(left, right, kind=F32):
    return lax.dot_general(
        left, right, (((1,), (0,)), ((), ())), preferred_element_type=F32
    ).astype(kind)


def dot_tn(left, right, kind=F32):
    return lax.dot_general(
        left, right, (((0,), (0,)), ((), ())), preferred_element_type=F32
    ).astype(kind)


def rms_scale(v, gain):
    return v * lax.rsqrt(jnp.mean(v * v, axis=-1, keepdims=True) + EPS_NORM) * gain


def group_norm(v):
    centred = v - jnp.mean(v, axis=-1, keepdims=True)
    return centred * lax.rsqrt(jnp.mean(centred * centred, axis=-1, keepdims=True) + EPS_GROUP)


def gated_gelu(first, second):
    return jax.nn.gelu(first) * second


def gated_silu(first, second):
    return jax.nn.silu(first) * second


def unit_tables(group, segments):
    count = 6 * group
    per_shard = count // segments

    def owner(u):
        if u < 2 * group:
            return u % group, u // group
        rest = u - 2 * group
        return (rest % (2 * group)) // 2, 2 + 2 * (rest // (2 * group)) + rest % 2

    keep = np.full((segments, group), -1, np.int32)
    give = np.zeros((segments, group), np.int32)
    place = np.zeros((group, 6), np.int32)
    held = np.zeros((segments, group), np.int32)
    slot_of = np.zeros((count,), np.int32)
    for chip in range(segments // 2):
        for s in range(group):
            mine = [
                u
                for u in range(2 * per_shard * chip, 2 * per_shard * (chip + 1))
                if owner(u)[0] == s
            ]
            assert len(mine) <= 2
            for n, u in enumerate(mine):
                home = u // per_shard
                slot = home if len(mine) == 1 else 2 * chip + n
                if slot == home:
                    keep[slot, s] = u % per_shard
                else:
                    give[home, s] = u % per_shard
                comp = owner(u)[1]
                place[s, comp] = slot
                held[slot, s] = comp
                slot_of[u] = slot
    back = np.zeros((segments, per_shard), np.int32)
    lend = np.zeros((segments,), np.int32)
    for u in range(count):
        home, s = u // per_shard, owner(u)[0]
        if slot_of[u] == home:
            back[home, u % per_shard] = s
        else:
            assert slot_of[u] == home ^ 1
            back[home, u % per_shard] = group
            lend[home ^ 1] = s
    return keep, give, place, held, back, lend


def local(
    tokens,
    cotangent,
    gain_attn,
    gain_ffn,
    mixer_in,
    mixer_out,
    ffn_in,
    ffn_out,
    segment_order,
    decay_index,
):
    rows, width = tokens.shape
    group = lax.axis_size("seq")
    segments = lax.axis_size("shard")
    heads = decay_index.shape[0]
    local_heads = heads // group
    seg_len = rows * group
    blk = min(512, seg_len)
    blocks = seg_len // blk
    unit = local_heads * DK
    vcols = local_heads * DV
    s = lax.axis_index("seq")
    j = lax.axis_index("shard")

    def swap(v, d):
        return lax.ppermute(v, "seq", [(i, i ^ d) for i in range(group)])

    def partner(v):
        return lax.ppermute(v, "shard", [(i, i ^ 1) for i in range(segments)])

    def spread(v):
        if group == 4:
            h = v.shape[0] // 2
            r1 = swap(v, 1)
            r2 = swap(v, 2)
            return [v, r1, r2, jnp.concatenate([swap(r1[:h], 2), swap(r2[h:], 1)], axis=0)]
        return [v] + [swap(v, d) for d in range(1, group)]

    def ordered(parts):
        r = parts[0].shape[0]
        out = jnp.zeros((group * r,) + parts[0].shape[1:], parts[0].dtype)
        for d, part in enumerate(parts):
            out = lax.dynamic_update_slice_in_dim(out, part, (s ^ d) * r, 0)
        return out

    def gather_near(v):
        return jnp.concatenate(spread(v), axis=0)

    def gather_seq(v):
        return ordered(spread(v))

    def scatter_sum(blk_of):
        if group == 4:
            b0, b1, b2, b3 = (blk_of(d) for d in range(4))
            h = b0.shape[0] // 2
            b0 = b0.astype(F32)
            ra = swap(jnp.concatenate([b1[:h], b3[:h]], axis=0), 1).astype(F32)
            rb = swap(jnp.concatenate([b2[h:], b3[h:]], axis=0), 2).astype(F32)
            qa = swap((b2[:h].astype(F32) + ra[h:]).astype(BF16), 2).astype(F32)
            qb = swap((b1[h:].astype(F32) + rb[h:]).astype(BF16), 1).astype(F32)
            return jnp.concatenate([b0[:h] + ra[:h] + qa, b0[h:] + rb[:h] + qb], axis=0)
        total = blk_of(0).astype(F32)
        for d in range(1, group):
            total = total + swap(blk_of(d), d).astype(F32)
        return total

    def scatter_near(v):
        return scatter_sum(lambda d: v[d * rows : (d + 1) * rows])

    def scatter_seq(v):
        return scatter_sum(lambda d: lax.dynamic_slice_in_dim(v, (s ^ d) * rows, rows, 0))

    def gather_shard(v):
        return lax.all_gather(v, "shard", axis=0, tiled=True)

    def reduce_shard(v):
        return lax.psum_scatter(v, "shard", scatter_dimension=0, tiled=True)

    keep, give, place, held, back, lend = (jnp.asarray(t) for t in unit_tables(group, segments))
    units = mixer_in.reshape(-1, unit, width)
    keep_here = keep[j, s]
    given = partner(lax.dynamic_index_in_dim(units, give[j, s], 0, keepdims=False))
    own = lax.dynamic_index_in_dim(units, jnp.maximum(keep_here, 0), 0, keepdims=False)
    slots = gather_shard(jnp.where(keep_here >= 0, own, given)).reshape(segments, unit, width)
    place_here = place[s]
    w_in = jnp.concatenate(
        [lax.dynamic_index_in_dim(slots, place_here[c], 0, keepdims=False) for c in range(6)],
        axis=0,
    )
    w_out = gather_shard(lax.dynamic_slice_in_dim(mixer_out, s * vcols, vcols, 1))
    sub = ffn_in.shape[0] // group
    w_ffn_in = gather_shard(lax.dynamic_slice_in_dim(ffn_in, s * sub, sub, 0))
    ffn_out_cut = ffn_out.reshape(ffn_out.shape[0], segments // 2, group, sub)
    w_ffn_out = gather_shard(
        lax.dynamic_index_in_dim(ffn_out_cut, s, 2, keepdims=False).reshape(ffn_out.shape[0], -1)
    )
    inner_cols = w_ffn_out.shape[1]

    my_rank = jnp.sum(jnp.where(jnp.arange(segments) == j, segment_order, 0))
    all_logs = jnp.log1p(-jnp.exp2(-(5.0 + decay_index.astype(F32))))
    logs = lax.dynamic_slice_in_dim(all_logs, s * local_heads, local_heads)
    half = DK // 2
    inv_freq = jnp.exp(-jnp.log(10000.0) * jnp.arange(half).astype(F32) / half)
    positions = my_rank * seg_len + jnp.arange(seg_len, dtype=jnp.int32)
    angles = positions.astype(F32)[:, None] * inv_freq[None, :]
    cosine = jnp.cos(angles)[:, None, :]
    sine = jnp.sin(angles)[:, None, :]

    def rotate(v, sign):
        first = v[..., :half]
        second = v[..., half:]
        sn = sign * sine
        return jnp.concatenate(
            [first * cosine - second * sn, second * cosine + first * sn], axis=-1
        )

    steps = jnp.arange(blk).astype(F32)
    gap = steps[:, None] - steps[None, :]
    mask = jnp.where(
        gap[None] >= 0.0, jnp.exp(jnp.maximum(gap, 0.0)[None] * logs[:, None, None]), 0.0
    )
    q_decay = jnp.exp((steps + 1.0)[None, :] * logs[:, None])
    k_decay = jnp.exp((blk - 1.0 - steps)[None, :] * logs[:, None])
    block_decay = jnp.exp(blk * logs)[:, None, None]

    xf = tokens.astype(F32)
    normed = gather_seq(rms_scale(xf, gain_attn).astype(BF16))
    proj = dot_nt(normed, w_in)
    queries = rotate(proj[:, :unit].reshape(seg_len, local_heads, DK), 1.0)
    keys = rotate(proj[:, unit : 2 * unit].reshape(seg_len, local_heads, DK), 1.0)
    value_rows = proj[:, 2 * unit : 2 * unit + vcols].reshape(seg_len, local_heads, DV)
    gate = proj[:, 2 * unit + vcols :]
    q_heads, k_heads, v_heads = (
        jnp.transpose(t, (1, 0, 2)).astype(BF16) for t in (queries, keys, value_rows)
    )

    q_blocks = q_heads.reshape(local_heads, blocks, blk, DK)
    k_blocks = k_heads.reshape(local_heads, blocks, blk, DK)
    v_blocks = v_heads.reshape(local_heads, blocks, blk, DV)
    key_decayed = (k_blocks.astype(F32) * k_decay[:, None, :, None]).astype(BF16)
    query_decayed = (q_blocks.astype(F32) * q_decay[:, None, :, None]).astype(BF16)
    updates = jnp.einsum("hcmk,hcmv->chkv", key_decayed, v_blocks, preferred_element_type=F32)
    zero_state = jnp.zeros((local_heads, DK, DV), F32)

    def run_states(start, terms, reverse):
        found = [None] * blocks
        state = start
        for b in reversed(range(blocks)) if reverse else range(blocks):
            found[b] = state
            state = block_decay * state + terms[b]
        return jnp.stack(found), state

    ranks = segment_order
    piece = local_heads * DK // segments
    head_of_row = (j * piece + jnp.arange(piece)) // DK
    piece_logs = jnp.sum(
        jnp.where(head_of_row[:, None] == jnp.arange(local_heads)[None, :], logs[None, :], 0.0),
        axis=1,
    )

    def exchange_states(total, reverse):
        cut = total.astype(BF16).reshape(segments, piece, DV)
        got = lax.all_to_all(cut, "shard", split_axis=0, concat_axis=0, tiled=True).astype(F32)
        apart = ranks[:, None] - ranks[None, :] - 1
        if reverse:
            apart = -apart - 2
        distance = apart.astype(F32)
        coef = jnp.where(
            distance[..., None] >= 0.0,
            jnp.exp(jnp.maximum(distance, 0.0)[..., None] * seg_len * piece_logs),
            0.0,
        )
        joined = jnp.sum(coef[..., None] * got[None], axis=1).astype(BF16)
        back_cut = lax.all_to_all(joined, "shard", split_axis=0, concat_axis=0, tiled=True)
        return back_cut.reshape(local_heads, DK, DV).astype(F32)

    ignored, local_total = run_states(zero_state, updates, False)
    state_in = exchange_states(local_total, False)
    states, ignored1 = run_states(state_in, updates, False)
    scores = jnp.einsum("hcnk,hcmk->hcnm", q_blocks, k_blocks, preferred_element_type=F32)
    weights = (scores * mask[:, None]).astype(BF16)
    inner = jnp.einsum("hcnm,hcmv->hcnv", weights, v_blocks, preferred_element_type=F32)
    states_low = states.astype(BF16)
    cross_block_term = jnp.einsum(
        "hcnk,chkv->hcnv", query_decayed, states_low, preferred_element_type=F32
    )
    retained = (inner + cross_block_term).reshape(local_heads, seg_len, DV)
    normal_heads = group_norm(retained).astype(BF16)
    mixed = jnp.transpose(normal_heads, (1, 0, 2)).reshape(seg_len, vcols)
    hidden = gated_silu(gate, mixed.astype(F32)).astype(BF16)

    resid = xf + scatter_seq(dot_nt(hidden, w_out, BF16))
    normed2 = gather_near(rms_scale(resid, gain_ffn).astype(BF16))
    proj2 = dot_nt(normed2, w_ffn_in)
    first, second = proj2[:, :inner_cols], proj2[:, inner_cols:]
    inner2 = gated_gelu(first, second).astype(BF16)
    output = (resid + scatter_near(dot_nt(inner2, w_ffn_out, BF16))).astype(BF16)

    d_ffn = gather_near(cotangent)
    d_inner2 = dot_nn(d_ffn, w_ffn_out)
    ignored2, gelu_back = jax.vjp(gated_gelu, first, second)
    d_first, d_second = gelu_back(d_inner2)
    dproj2 = jnp.concatenate([d_first, d_second], axis=1).astype(BF16)
    d_normed2 = scatter_near(dot_nn(dproj2, w_ffn_in, BF16))
    g_ffn_out = reduce_shard(dot_tn(d_ffn, inner2, BF16))
    g_ffn_in = reduce_shard(dot_tn(dproj2, normed2, BF16))
    ignored3, norm2_back = jax.vjp(rms_scale, resid, gain_ffn)
    d_resid_part, d_gain_ffn = norm2_back(d_normed2)
    d_resid = cotangent.astype(F32) + d_resid_part
    d_attn = gather_seq(d_resid.astype(BF16))
    d_hidden = dot_nn(d_attn, w_out)
    g_mixer_out = reduce_shard(dot_tn(d_attn, hidden, BF16))
    ignored4, silu_back = jax.vjp(gated_silu, gate, mixed.astype(F32))
    d_gate, d_mixed = silu_back(d_hidden)

    d_heads = jnp.transpose(
        d_mixed.reshape(seg_len, local_heads, DV), (1, 0, 2)
    ).astype(BF16)
    ignored5, group_back = jax.vjp(group_norm, retained)
    (d_retained,) = group_back(d_heads.astype(F32))
    d_out = d_retained.astype(BF16).reshape(local_heads, blocks, blk, DV)
    cross_grads = jnp.einsum("hcnk,hcnv->chkv", query_decayed, d_out, preferred_element_type=F32)
    ignored6, local_grad = run_states(zero_state, cross_grads, True)
    grad_out = exchange_states(local_grad, True)
    d_weights = jnp.einsum(
        "hcnv,hcmv->hcnm", d_out, v_blocks, preferred_element_type=F32
    ).astype(BF16)
    d_scores = (d_weights.astype(F32) * mask[:, None]).astype(BF16)
    d_q = jnp.einsum("hcnm,hcmk->hcnk", d_scores, k_blocks, preferred_element_type=F32)
    d_k = jnp.einsum("hcnm,hcnk->hcmk", d_scores, q_blocks, preferred_element_type=F32)
    d_v = jnp.einsum("hcnm,hcnv->hcmv", weights, d_out, preferred_element_type=F32)
    d_q_scaled = jnp.einsum(
        "hcnv,chkv->hcnk", d_out, states_low, preferred_element_type=F32
    ).astype(BF16)
    d_q = d_q + d_q_scaled.astype(F32) * q_decay[:, None, :, None]
    next_grads, ignored7 = run_states(grad_out, cross_grads, True)
    next_low = next_grads.astype(BF16)
    d_k_scaled = jnp.einsum(
        "hcmv,chkv->hcmk", v_blocks, next_low, preferred_element_type=F32
    ).astype(BF16)
    d_k = d_k + d_k_scaled.astype(F32) * k_decay[:, None, :, None]
    d_v = d_v + jnp.einsum("hcmk,chkv->hcmv", key_decayed, next_low, preferred_element_type=F32)

    def to_rows(v):
        return jnp.transpose(v.reshape(local_heads, seg_len, -1).astype(BF16), (1, 0, 2))

    dq_raw = rotate(to_rows(d_q).astype(F32), -1.0).reshape(seg_len, unit)
    dk_raw = rotate(to_rows(d_k).astype(F32), -1.0).reshape(seg_len, unit)
    dv_raw = to_rows(d_v).reshape(seg_len, vcols)
    dproj = jnp.concatenate(
        [dq_raw.astype(BF16), dk_raw.astype(BF16), dv_raw, d_gate.astype(BF16)], axis=1
    )
    d_normed = scatter_seq(dot_nn(dproj, w_in, BF16))

    held_here = held[:, s]
    by_slot = jnp.concatenate(
        [
            lax.dynamic_slice_in_dim(dproj, held_here[c] * unit, unit, 1)
            for c in range(segments)
        ],
        axis=1,
    )
    g_slot = reduce_shard(dot_tn(by_slot, normed, BF16))

    g_slots = gather_seq(g_slot).reshape(group, unit, width)
    lent = partner(lax.dynamic_index_in_dim(g_slots, lend[j], 0, keepdims=False))
    choices = jnp.concatenate([g_slots, lent[None]], axis=0)
    g_mixer_in = jnp.concatenate(
        [
            lax.dynamic_index_in_dim(choices, back[j, c], 0, keepdims=False)
            for c in range(mixer_in.shape[0] // unit)
        ],
        axis=0,
    ).astype(F32)
    g_mixer_out = jnp.transpose(
        gather_seq(g_mixer_out).reshape(group, -1, vcols), (1, 0, 2)
    ).reshape(mixer_out.shape).astype(F32)
    g_ffn_in = gather_seq(g_ffn_in).astype(F32)
    g_ffn_out = jnp.transpose(
        gather_seq(g_ffn_out).reshape(group, ffn_out.shape[0], segments // 2, sub), (1, 2, 0, 3)
    ).reshape(ffn_out.shape).astype(F32)

    ignored8, norm1_back = jax.vjp(rms_scale, xf, gain_attn)
    d_x_part, d_gain_attn = norm1_back(d_normed)
    input_grad = (d_resid + d_x_part).astype(BF16)
    gain_attn_grad, gain_ffn_grad = lax.psum((d_gain_attn, d_gain_ffn), ("seq", "shard"))
    return (
        output,
        input_grad,
        gain_attn_grad,
        gain_ffn_grad,
        g_mixer_in,
        g_mixer_out,
        g_ffn_in,
        g_ffn_out,
    )


def solution(mesh):
    return jax.shard_map(
        local,
        mesh=mesh,
        in_specs=(
            P(("shard", "seq"), None),
            P(("shard", "seq"), None),
            P(),
            P(),
            P("shard", None),
            P("shard", None),
            P("shard", None),
            P("shard", None),
            P(),
            P(),
        ),
        out_specs=(
            P(("shard", "seq"), None),
            P(("shard", "seq"), None),
            P(),
            P(),
            P("shard", None),
            P("shard", None),
            P("shard", None),
            P("shard", None),
        ),
        check_vma=False,
    )
```

```python
import jax
import jax.numpy as jnp
import numpy as np
from jax import lax
from jax.sharding import PartitionSpec as P

DK = 256
DV = 512
FF = 4096
QK = 2048
V = 4096


EPS_NORM = 1e-06
EPS_GROUP = 1e-05

F32 = jnp.float32
BF16 = jnp.bfloat16


def dot_nt(left, right, kind=F32):
    return lax.dot_general(
        left, right, (((1,), (1,)), ((), ())), preferred_element_type=F32
    ).astype(kind)


def dot_nn(left, right, kind=F32):
    return lax.dot_general(
        left, right, (((1,), (0,)), ((), ())), preferred_element_type=F32
    ).astype(kind)


def dot_tn(left, right, kind=F32):
    return lax.dot_general(
        left, right, (((0,), (0,)), ((), ())), preferred_element_type=F32
    ).astype(kind)


def rms_scale(v, gain):
    return v * lax.rsqrt(jnp.mean(v * v, axis=-1, keepdims=True) + EPS_NORM) * gain


def group_norm(v):
    centred = v - jnp.mean(v, axis=-1, keepdims=True)
    return centred * lax.rsqrt(jnp.mean(centred * centred, axis=-1, keepdims=True) + EPS_GROUP)


def gated_gelu(first, second):
    return jax.nn.gelu(first) * second


def gated_silu(first, second):
    return jax.nn.silu(first) * second


def unit_tables(group, local_heads, segments):
    heads = group * local_heads
    owners = [(n, 0) for n in range(heads)] + [(n, 1) for n in range(heads)]
    for base in (2, 4):
        owners += [(n, base + half) for n in range(heads) for half in range(2)]
    per_shard = len(owners) // segments
    keep = np.full((local_heads, segments, group), -1, np.int32)
    give = np.zeros((local_heads, segments, group), np.int32)
    place = np.zeros((local_heads, group, 6), np.int32)
    held = np.full((local_heads, segments, group), -1, np.int32)
    slot_of = {}
    for chip in range(segments // 2):
        for head in range(heads):
            s, h = divmod(head, local_heads)
            span = range(2 * per_shard * chip, 2 * per_shard * (chip + 1))
            mine = [u for u in span if owners[u][0] == head]
            assert len(mine) <= 2
            for n, u in enumerate(mine):
                home = u // per_shard
                slot = home if len(mine) == 1 else 2 * chip + n
                if slot == home:
                    keep[h, slot, s] = u % per_shard
                else:
                    give[h, home, s] = u % per_shard
                place[h, s, owners[u][1]] = slot
                held[h, slot, s] = owners[u][1]
                slot_of[u] = slot
    lends = [[[] for _ in range(segments)] for _ in range(local_heads)]
    back = np.zeros((segments, per_shard, 3), np.int32)
    for u, (head, _) in enumerate(owners):
        home = u // per_shard
        s, h = divmod(head, local_heads)
        back[home, u % per_shard] = (h, s, -1)
        if slot_of[u] != home:
            assert slot_of[u] == home ^ 1
            back[home, u % per_shard, 2] = len(lends[h][home ^ 1])
            lends[h][home ^ 1].append(s)
    most = max(1, max(len(t) for row in lends for t in row))
    lend = np.asarray(
        [[(t + [0] * most)[:most] for t in row] for row in lends], np.int32
    )
    return keep, give, place, held, back, lend


def tie(*values):
    return lax.optimization_barrier(values)


def local(
    tokens,
    cotangent,
    gain_attn,
    gain_ffn,
    mixer_in,
    mixer_out,
    ffn_in,
    ffn_out,
    segment_order,
    decay_index,
):
    rows, width = tokens.shape
    group = lax.axis_size("seq")
    segments = lax.axis_size("shard")
    heads = decay_index.shape[0]
    local_heads = heads // group
    seg_len = rows * group
    blk = min(512, seg_len)
    blocks = seg_len // blk
    vcols = local_heads * DV
    s = lax.axis_index("seq")
    j = lax.axis_index("shard")

    def swap(v, d):
        return lax.ppermute(v, "seq", [(i, i ^ d) for i in range(group)])

    def cross(v, d):
        return lax.ppermute(v, "shard", [(i, i ^ d) for i in range(segments)])

    def pick(v, i):
        return lax.dynamic_index_in_dim(v, i, 0, keepdims=False)

    def spread(v):
        if group == 4:
            h = v.shape[0] // 2
            r1 = swap(v, 1)
            r2 = swap(v, 2)
            return [v, r1, r2, jnp.concatenate([swap(r1[:h], 2), swap(r2[h:], 1)], axis=0)]
        return [v] + [swap(v, d) for d in range(1, group)]

    def ordered(parts):
        r = parts[0].shape[0]
        out = jnp.zeros((group * r,) + parts[0].shape[1:], parts[0].dtype)
        for d, part in enumerate(parts):
            out = lax.dynamic_update_slice_in_dim(out, part, (s ^ d) * r, 0)
        return out

    def gather_near(v):
        return jnp.concatenate(spread(v), axis=0)

    def gather_seq(v):
        return ordered(spread(v))

    def scatter_sum(blk_of, beside1=(), beside2=()):
        if group == 4:
            b0, b1, b2, b3 = (blk_of(d) for d in range(4))
            h = b0.shape[0] // 2
            b0 = b0.astype(F32)
            ra = swap(jnp.concatenate([b1[:h], b3[:h]], axis=0), 1)
            rb = swap(jnp.concatenate([b2[h:], b3[h:]], axis=0), 2)
            ra, rb, *beside1 = tie(ra, rb, *beside1)
            ra, rb = ra.astype(F32), rb.astype(F32)
            qa = swap((b2[:h].astype(F32) + ra[h:]).astype(BF16), 2)
            qb = swap((b1[h:].astype(F32) + rb[h:]).astype(BF16), 1)
            qa, qb, *beside2 = tie(qa, qb, *beside2)
            total = jnp.concatenate(
                [b0[:h] + ra[:h] + qa.astype(F32), b0[h:] + rb[:h] + qb.astype(F32)], axis=0
            )
            return (total, *beside1, *beside2)
        total = blk_of(0).astype(F32)
        for d in range(1, group):
            total = total + swap(blk_of(d), d).astype(F32)
        return (total, *beside1, *beside2)

    def scatter_near(v, beside1=(), beside2=()):
        return scatter_sum(lambda d: v[d * rows : (d + 1) * rows], beside1, beside2)

    def scatter_seq(v):
        return scatter_sum(lambda d: lax.dynamic_slice_in_dim(v, (s ^ d) * rows, rows, 0))[0]

    def gather_shard(v):
        return lax.all_gather(v, "shard", axis=0, tiled=True)

    def reduce_shard(v):
        return lax.psum_scatter(v, "shard", scatter_dimension=0, tiled=True)

    def sum_all(v):
        step = 1
        while step < group:
            v = v + swap(v, step)
            step *= 2
        step = 1
        while step < segments:
            v = v + cross(v, step)
            step *= 2
        return v

    keep, give, place, held, back, lend = (
        jnp.asarray(t) for t in unit_tables(group, local_heads, segments)
    )
    units = mixer_in.reshape(-1, DK, width)

    def offered(h):
        kept = keep[h, j, s]
        given = cross(pick(units, give[h, j, s]), 1)
        return jnp.where(kept >= 0, pick(units, jnp.maximum(kept, 0)), given)

    sub = ffn_in.shape[0] // group
    ffn_out_cut = ffn_out.reshape(ffn_out.shape[0], segments // 2, group, sub)

    my_rank = jnp.sum(jnp.where(jnp.arange(segments) == j, segment_order, 0))
    all_logs = jnp.log1p(-jnp.exp2(-(5.0 + decay_index.astype(F32))))
    logs = lax.dynamic_slice_in_dim(all_logs, s * local_heads, local_heads)
    half = DK // 2
    inv_freq = jnp.exp(-jnp.log(10000.0) * jnp.arange(half).astype(F32) / half)
    positions = my_rank * seg_len + jnp.arange(seg_len, dtype=jnp.int32)
    angles = positions.astype(F32)[:, None] * inv_freq[None, :]
    cosine = jnp.cos(angles)
    sine = jnp.sin(angles)
    steps = jnp.arange(blk).astype(F32)
    gap = steps[:, None] - steps[None, :]
    masks = jnp.where(
        gap[None] >= 0.0, jnp.exp(jnp.maximum(gap, 0.0)[None] * logs[:, None, None]), 0.0
    )
    q_decays = jnp.exp((steps + 1.0)[None, :] * logs[:, None])[..., None]
    k_decays = jnp.exp((blk - 1.0 - steps)[None, :] * logs[:, None])[..., None]
    block_decays = jnp.exp(blk * logs)

    xf = tokens.astype(F32)
    normed = gather_seq(rms_scale(xf, gain_attn).astype(BF16))
    d_ffn = gather_near(cotangent)
    slots = [gather_shard(offered(0))]
    slots[0], normed, d_ffn, cosine, sine, masks, q_decays, k_decays = tie(
        slots[0], normed, d_ffn, cosine, sine, masks, q_decays, k_decays
    )
    for h in range(1, local_heads):
        slots.append(gather_shard(offered(h)))
    mixer_out_cut = lax.dynamic_slice_in_dim(mixer_out, s * vcols, vcols, 1)
    mixer_out_cut, slots[0] = tie(mixer_out_cut, slots[0])
    w_out = gather_shard(mixer_out_cut)
    ffn_in_cut = lax.dynamic_slice_in_dim(ffn_in, s * sub, sub, 0)
    ffn_in_cut, slots[-1] = tie(ffn_in_cut, slots[-1])
    w_ffn_in = gather_shard(ffn_in_cut)
    ffn_out_here = lax.dynamic_index_in_dim(ffn_out_cut, s, 2, keepdims=False)
    ffn_out_here, slots[-1] = tie(ffn_out_here.reshape(ffn_out.shape[0], -1), slots[-1])
    w_ffn_out = gather_shard(ffn_out_here)
    inner_cols = w_ffn_out.shape[1]

    def rotate(v, sign):
        first = v[..., :half]
        second = v[..., half:]
        sn = sign * sine
        return jnp.concatenate(
            [first * cosine - second * sn, second * cosine + first * sn], axis=-1
        )

    def dots(pattern, left, right):
        return jnp.einsum(pattern, left, right, preferred_element_type=F32)

    def run_states(h, start, terms, reverse):
        found = [None] * blocks
        state = start
        for b in reversed(range(blocks)) if reverse else range(blocks):
            found[b] = state
            state = block_decays[h] * state + terms[b]
        return jnp.stack(found), state

    ranks = segment_order
    piece = DK // segments

    def exchange_states(h, total, reverse):
        cut = total.astype(BF16).reshape(segments, piece, DV)
        got = lax.all_to_all(cut, "shard", split_axis=0, concat_axis=0, tiled=True).astype(F32)
        apart = ranks[:, None] - ranks[None, :] - 1
        if reverse:
            apart = -apart - 2
        distance = apart.astype(F32)
        coef = jnp.where(
            distance >= 0.0, jnp.exp(jnp.maximum(distance, 0.0) * seg_len * logs[h]), 0.0
        )
        joined = jnp.sum(coef[..., None, None] * got[None], axis=1).astype(BF16)
        back_cut = lax.all_to_all(joined, "shard", split_axis=0, concat_axis=0, tiled=True)
        return back_cut.reshape(DK, DV).astype(F32)

    kept = []
    zero_state = jnp.zeros((DK, DV), F32)
    for h in range(local_heads):
        proj = dot_nt(normed, slots[h])
        place_here = place[h, s]
        q_raw, k_raw, v_a, v_b, g_a, g_b = (
            lax.dynamic_slice_in_dim(proj, place_here[c] * DK, DK, 1) for c in range(6)
        )
        q = rotate(q_raw, 1.0).astype(BF16).reshape(blocks, blk, DK)
        k = rotate(k_raw, 1.0).astype(BF16).reshape(blocks, blk, DK)
        v = jnp.concatenate([v_a, v_b], axis=1).astype(BF16).reshape(blocks, blk, DV)
        gate = jnp.concatenate([g_a, g_b], axis=1)
        kd = (k.astype(F32) * k_decays[h]).astype(BF16)
        qd = (q.astype(F32) * q_decays[h]).astype(BF16)
        updates = dots("cmk,cmv->ckv", kd, v)
        ignored, total = run_states(h, zero_state, updates, False)
        state_in = exchange_states(h, total, False)
        states, ignored1 = run_states(h, state_in, updates, False)
        states = states.astype(BF16)
        weights = (dots("cnk,cmk->cnm", q, k) * masks[h]).astype(BF16)
        retained = dots("cnm,cmv->cnv", weights, v) + dots("cnk,ckv->cnv", qd, states)
        retained = retained.reshape(seg_len, DV)
        mixed = group_norm(retained).astype(BF16)
        hidden = gated_silu(gate, mixed.astype(F32)).astype(BF16)
        kept.append((q, k, v, qd, kd, gate, weights, states, retained, mixed, hidden))
    hidden = jnp.concatenate([t[-1] for t in kept], axis=1)

    resid = xf + scatter_seq(dot_nt(hidden, w_out, BF16))
    normed2 = gather_near(rms_scale(resid, gain_ffn).astype(BF16))
    proj2 = dot_nt(normed2, w_ffn_in)
    first, second = proj2[:, :inner_cols], proj2[:, inner_cols:]
    inner2 = gated_gelu(first, second).astype(BF16)

    d_inner2 = dot_nn(d_ffn, w_ffn_out)
    ignored2, gelu_back = jax.vjp(gated_gelu, first, second)
    d_first, d_second = gelu_back(d_inner2)
    dproj2 = jnp.concatenate([d_first, d_second], axis=1).astype(BF16)
    d_normed2, g_ffn_out, g_ffn_in = scatter_near(
        dot_nn(dproj2, w_ffn_in, BF16),
        (dot_tn(d_ffn, inner2, BF16),),
        (dot_tn(dproj2, normed2, BF16),),
    )
    g_ffn_out = reduce_shard(g_ffn_out)
    g_ffn_in = reduce_shard(g_ffn_in)
    ignored3, norm2_back = jax.vjp(rms_scale, resid, gain_ffn)
    d_resid_part, d_gain_ffn = norm2_back(d_normed2)
    d_resid = cotangent.astype(F32) + d_resid_part
    d_attn = gather_seq(d_resid.astype(BF16))
    inner2, d_attn = tie(inner2, d_attn)
    output = (resid + scatter_near(dot_nt(inner2, w_ffn_out, BF16))[0]).astype(BF16)
    d_hidden = dot_nn(d_attn, w_out)
    g_mixer_out = reduce_shard(dot_tn(d_attn, hidden, BF16))

    g_slots = []
    d_normed = None
    for h in range(local_heads):
        q, k, v, qd, kd, gate, weights, states, retained, mixed, ignored = kept[h]
        ignored4, silu_back = jax.vjp(gated_silu, gate, mixed.astype(F32))
        d_gate, d_mixed = silu_back(d_hidden[:, h * DV : (h + 1) * DV])
        ignored5, group_back = jax.vjp(group_norm, retained)
        (d_retained,) = group_back(d_mixed.astype(BF16).astype(F32))
        d_out = d_retained.astype(BF16).reshape(blocks, blk, DV)
        cross_grads = dots("cnk,cnv->ckv", qd, d_out)
        ignored6, total = run_states(h, zero_state, cross_grads, True)
        grad_out = exchange_states(h, total, True)
        d_weights = dots("cnv,cmv->cnm", d_out, v).astype(BF16)
        d_scores = (d_weights.astype(F32) * masks[h]).astype(BF16)
        d_q = dots("cnm,cmk->cnk", d_scores, k)
        d_k = dots("cnm,cnk->cmk", d_scores, q)
        d_v = dots("cnm,cnv->cmv", weights, d_out)
        d_q_scaled = dots("cnv,ckv->cnk", d_out, states).astype(BF16)
        d_q = d_q + d_q_scaled.astype(F32) * q_decays[h]
        next_grads, ignored7 = run_states(h, grad_out, cross_grads, True)
        next_low = next_grads.astype(BF16)
        d_k_scaled = dots("cmv,ckv->cmk", v, next_low).astype(BF16)
        d_k = d_k + d_k_scaled.astype(F32) * k_decays[h]
        d_v = d_v + dots("cmk,ckv->cmv", kd, next_low)
        dq_raw = rotate(d_q.reshape(seg_len, DK).astype(BF16).astype(F32), -1.0)
        dk_raw = rotate(d_k.reshape(seg_len, DK).astype(BF16).astype(F32), -1.0)
        dproj = jnp.concatenate(
            [
                dq_raw.astype(BF16),
                dk_raw.astype(BF16),
                d_v.reshape(seg_len, DV).astype(BF16),
                d_gate.astype(BF16),
            ],
            axis=1,
        )
        held_here = held[h, :, s]
        by_slot = jnp.concatenate(
            [
                jnp.where(
                    held_here[c] >= 0,
                    lax.dynamic_slice_in_dim(dproj, jnp.maximum(held_here[c], 0) * DK, DK, 1),
                    jnp.zeros((), BF16),
                )
                for c in range(segments)
            ],
            axis=1,
        )
        g_slots.append(reduce_shard(dot_tn(by_slot, normed, BF16)))
        part = dot_nn(by_slot, slots[h])
        d_normed = part if d_normed is None else d_normed + part
    d_normed = scatter_seq(d_normed.astype(BF16))

    choices = []
    for h in range(local_heads):
        parts = spread(g_slots[h])
        stack = jnp.stack(parts)
        lent = cross(
            jnp.stack([pick(stack, s ^ lend[h, j, n]) for n in range(lend.shape[-1])]), 1
        )
        choices += [stack, lent]
    choices = jnp.concatenate(choices, axis=0)
    each = group + lend.shape[-1]
    found = back[j]
    index = found[:, 0] * each + jnp.where(
        found[:, 2] < 0, s ^ found[:, 1], group + found[:, 2]
    )
    g_mixer_in = jnp.concatenate(
        [pick(choices, index[c]) for c in range(mixer_in.shape[0] // DK)], axis=0
    ).astype(F32)
    g_mixer_out = jnp.transpose(
        gather_seq(g_mixer_out).reshape(group, -1, vcols), (1, 0, 2)
    ).reshape(mixer_out.shape).astype(F32)
    g_ffn_in = gather_seq(g_ffn_in).astype(F32)
    g_ffn_out = jnp.transpose(
        gather_seq(g_ffn_out).reshape(group, ffn_out.shape[0], segments // 2, sub), (1, 2, 0, 3)
    ).reshape(ffn_out.shape).astype(F32)

    ignored8, norm1_back = jax.vjp(rms_scale, xf, gain_attn)
    d_x_part, d_gain_attn = norm1_back(d_normed)
    input_grad = (d_resid + d_x_part).astype(BF16)
    gain_ffn_grad = sum_all(d_gain_ffn)
    gain_attn_grad = sum_all(d_gain_attn)
    return (
        output,
        input_grad,
        gain_attn_grad,
        gain_ffn_grad,
        g_mixer_in,
        g_mixer_out,
        g_ffn_in,
        g_ffn_out,
    )


def solution(mesh):
    return jax.shard_map(
        local,
        mesh=mesh,
        in_specs=(
            P(("shard", "seq"), None),
            P(("shard", "seq"), None),
            P(),
            P(),
            P("shard", None),
            P("shard", None),
            P("shard", None),
            P("shard", None),
            P(),
            P(),
        ),
        out_specs=(
            P(("shard", "seq"), None),
            P(("shard", "seq"), None),
            P(),
            P(),
            P("shard", None),
            P("shard", None),
            P("shard", None),
            P("shard", None),
        ),
        check_vma=False,
    )
```

```python
import functools

import jax
import jax.numpy as jnp
import numpy as np
from jax import lax
from jax.experimental import pallas as pl
from jax.experimental.pallas import tpu as pltpu
from jax.sharding import PartitionSpec as P

DK = 256
DV = 512
FF = 4096
QK = 2048
V = 4096


EPS_NORM = 1e-06
EPS_GROUP = 1e-05

F32 = jnp.float32
BF16 = jnp.bfloat16


def dot_nt(left, right, kind=F32):
    return lax.dot_general(
        left, right, (((1,), (1,)), ((), ())), preferred_element_type=F32
    ).astype(kind)


def dot_nn(left, right, kind=F32):
    return lax.dot_general(
        left, right, (((1,), (0,)), ((), ())), preferred_element_type=F32
    ).astype(kind)


def dot_tn(left, right, kind=F32):
    return lax.dot_general(
        left, right, (((0,), (0,)), ((), ())), preferred_element_type=F32
    ).astype(kind)


def rms_scale(v, gain):
    return v * lax.rsqrt(jnp.mean(v * v, axis=-1, keepdims=True) + EPS_NORM) * gain


def group_norm(v):
    centred = v - jnp.mean(v, axis=-1, keepdims=True)
    return centred * lax.rsqrt(jnp.mean(centred * centred, axis=-1, keepdims=True) + EPS_GROUP)


def gated_gelu(first, second):
    return jax.nn.gelu(first) * second


def gated_silu(first, second):
    return jax.nn.silu(first) * second


def unit_tables(group, local_heads, segments):
    heads = group * local_heads
    owners = [(n, 0) for n in range(heads)] + [(n, 1) for n in range(heads)]
    for base in (2, 4):
        owners += [(n, base + half) for n in range(heads) for half in range(2)]
    per_shard = len(owners) // segments
    keep = np.full((local_heads, segments, group), -1, np.int32)
    give = np.zeros((local_heads, segments, group), np.int32)
    place = np.zeros((local_heads, group, 6), np.int32)
    held = np.full((local_heads, segments, group), -1, np.int32)
    slot_of = {}
    for chip in range(segments // 2):
        for head in range(heads):
            s, h = divmod(head, local_heads)
            span = range(2 * per_shard * chip, 2 * per_shard * (chip + 1))
            mine = [u for u in span if owners[u][0] == head]
            assert len(mine) <= 2
            for n, u in enumerate(mine):
                home = u // per_shard
                slot = home if len(mine) == 1 else 2 * chip + n
                if slot == home:
                    keep[h, slot, s] = u % per_shard
                else:
                    give[h, home, s] = u % per_shard
                place[h, s, owners[u][1]] = slot
                held[h, slot, s] = owners[u][1]
                slot_of[u] = slot
    lends = [[[] for _ in range(segments)] for _ in range(local_heads)]
    back = np.zeros((segments, per_shard, 3), np.int32)
    for u, (head, _) in enumerate(owners):
        home = u // per_shard
        s, h = divmod(head, local_heads)
        back[home, u % per_shard] = (h, s, -1)
        if slot_of[u] != home:
            assert slot_of[u] == home ^ 1
            back[home, u % per_shard, 2] = len(lends[h][home ^ 1])
            lends[h][home ^ 1].append(s)
    most = max(1, max(len(t) for row in lends for t in row))
    lend = np.asarray(
        [[(t + [0] * most)[:most] for t in row] for row in lends], np.int32
    )
    fills = [[np.flatnonzero(back[t, :, 0] == h) for t in range(segments)] for h in range(local_heads)]
    longest = max(1, max(len(t) for row in fills for t in row))
    fill = np.zeros((local_heads, segments, longest), np.int32)
    for h in range(local_heads):
        for t in range(segments):
            assert len(fills[h][t]) > 0
            fill[h, t] = np.pad(fills[h][t], (0, longest - len(fills[h][t])), mode="edge")
    return keep, give, place, held, back, lend, fill


def tie(*values):
    return lax.optimization_barrier(values)


def place_kernel(sizes, aliased, target, source, *refs):
    out = refs[-1]
    code = source[pl.program_id(1)]
    at = 1 if aliased else 0
    for i, size in enumerate(sizes):
        pieces = refs[at : at + size]
        at += size

        @pl.when(code == i)
        def _(pieces=pieces):
            row = 0
            for piece in pieces:
                out[row : row + piece.shape[0], :] = piece[...].astype(F32)
                row += piece.shape[0]


def place_blocks(parts, target, source, shape, block, where, outer=1, into=None):
    flat = [t for part in parts for t in part]
    aliased = into is not None
    specs = [
        pl.BlockSpec((t.shape[0], t.shape[1] // outer), lambda o, n, target, source: (0, o))
        for t in flat
    ]
    if aliased:
        specs = [pl.BlockSpec(memory_space=pl.ANY)] + specs
        flat = [into] + flat
    return pl.pallas_call(
        functools.partial(place_kernel, [len(part) for part in parts], aliased),
        grid_spec=pltpu.PrefetchScalarGridSpec(
            num_scalar_prefetch=2,
            grid=(outer, target.shape[0]),
            in_specs=specs,
            out_specs=pl.BlockSpec(block, lambda o, n, target, source: where(o, target[n])),
        ),
        out_shape=jax.ShapeDtypeStruct(shape, F32),
        input_output_aliases={2: 0} if aliased else {},
        compiler_params=pltpu.CompilerParams(vmem_limit_bytes=40 * 2**20),
    )(target.astype(jnp.int32), source.astype(jnp.int32), *flat)


def local(
    tokens,
    cotangent,
    gain_attn,
    gain_ffn,
    mixer_in,
    mixer_out,
    ffn_in,
    ffn_out,
    segment_order,
    decay_index,
):
    rows, width = tokens.shape
    group = lax.axis_size("seq")
    segments = lax.axis_size("shard")
    heads = decay_index.shape[0]
    local_heads = heads // group
    seg_len = rows * group
    blk = min(512, seg_len)
    blocks = seg_len // blk
    vcols = local_heads * DV
    s = lax.axis_index("seq")
    j = lax.axis_index("shard")

    def swap(v, d):
        return lax.ppermute(v, "seq", [(i, i ^ d) for i in range(group)])

    def cross(v, d):
        return lax.ppermute(v, "shard", [(i, i ^ d) for i in range(segments)])

    def pick(v, i):
        return lax.dynamic_index_in_dim(v, i, 0, keepdims=False)

    def spread(v):
        if group == 4:
            h = v.shape[0] // 2
            r1 = swap(v, 1)
            r2 = swap(v, 2)
            return [(v,), (r1,), (r2,), (swap(r1[:h], 2), swap(r2[h:], 1))]
        return [(v,)] + [(swap(v, d),) for d in range(1, group)]

    def ordered(parts):
        r = parts[0][0].shape[0]
        out = jnp.zeros((group * r,) + parts[0][0].shape[1:], parts[0][0].dtype)
        for d, part in enumerate(parts):
            row = (s ^ d) * r
            for piece in part:
                out = lax.dynamic_update_slice_in_dim(out, piece, row, 0)
                row = row + piece.shape[0]
        return out

    def gather_near(v):
        return jnp.concatenate([piece for part in spread(v) for piece in part], axis=0)

    def gather_seq(v):
        return ordered(spread(v))

    def scatter_sum(blk_of, beside1=(), beside2=()):
        if group == 4:
            b0, b1, b2, b3 = (blk_of(d) for d in range(4))
            h = b0.shape[0] // 2
            b0 = b0.astype(F32)
            ra = swap(jnp.concatenate([b1[:h], b3[:h]], axis=0), 1)
            rb = swap(jnp.concatenate([b2[h:], b3[h:]], axis=0), 2)
            ra, rb, *beside1 = tie(ra, rb, *beside1)
            ra, rb = ra.astype(F32), rb.astype(F32)
            qa = swap((b2[:h].astype(F32) + ra[h:]).astype(BF16), 2)
            qb = swap((b1[h:].astype(F32) + rb[h:]).astype(BF16), 1)
            qa, qb, *beside2 = tie(qa, qb, *beside2)
            total = jnp.concatenate(
                [b0[:h] + ra[:h] + qa.astype(F32), b0[h:] + rb[:h] + qb.astype(F32)], axis=0
            )
            return (total, *beside1, *beside2)
        total = blk_of(0).astype(F32)
        for d in range(1, group):
            total = total + swap(blk_of(d), d).astype(F32)
        return (total, *beside1, *beside2)

    def scatter_near(v, beside1=(), beside2=()):
        return scatter_sum(lambda d: v[d * rows : (d + 1) * rows], beside1, beside2)

    def scatter_seq(v):
        return scatter_sum(lambda d: lax.dynamic_slice_in_dim(v, (s ^ d) * rows, rows, 0))[0]

    def gather_shard(v):
        return lax.all_gather(v, "shard", axis=0, tiled=True)

    def reduce_shard(v):
        return lax.psum_scatter(v, "shard", scatter_dimension=0, tiled=True)

    def sum_all(v):
        step = 1
        while step < group:
            v = v + swap(v, step)
            step *= 2
        step = 1
        while step < segments:
            v = v + cross(v, step)
            step *= 2
        return v

    keep, give, place, held, back, lend, fill = (
        jnp.asarray(t) for t in unit_tables(group, local_heads, segments)
    )
    units = mixer_in.reshape(-1, DK, width)

    def offered(h):
        kept = keep[h, j, s]
        given = cross(pick(units, give[h, j, s]), 1)
        return jnp.where(kept >= 0, pick(units, jnp.maximum(kept, 0)), given)

    sub = ffn_in.shape[0] // group
    ffn_out_cut = ffn_out.reshape(ffn_out.shape[0], segments // 2, group, sub)

    my_rank = jnp.sum(jnp.where(jnp.arange(segments) == j, segment_order, 0))
    all_logs = jnp.log1p(-jnp.exp2(-(5.0 + decay_index.astype(F32))))
    logs = lax.dynamic_slice_in_dim(all_logs, s * local_heads, local_heads)
    half = DK // 2
    inv_freq = jnp.exp(-jnp.log(10000.0) * jnp.arange(half).astype(F32) / half)
    positions = my_rank * seg_len + jnp.arange(seg_len, dtype=jnp.int32)
    angles = positions.astype(F32)[:, None] * inv_freq[None, :]
    cosine = jnp.cos(angles)
    sine = jnp.sin(angles)
    steps = jnp.arange(blk).astype(F32)
    gap = steps[:, None] - steps[None, :]
    masks = jnp.where(
        gap[None] >= 0.0, jnp.exp(jnp.maximum(gap, 0.0)[None] * logs[:, None, None]), 0.0
    )
    q_decays = jnp.exp((steps + 1.0)[None, :] * logs[:, None])[..., None]
    k_decays = jnp.exp((blk - 1.0 - steps)[None, :] * logs[:, None])[..., None]
    block_decays = jnp.exp(blk * logs)

    xf = tokens.astype(F32)
    normed = gather_seq(rms_scale(xf, gain_attn).astype(BF16))
    d_ffn = gather_near(cotangent)
    slots = [gather_shard(offered(0))]
    slots[0], normed, d_ffn, cosine, sine, masks, q_decays, k_decays = tie(
        slots[0], normed, d_ffn, cosine, sine, masks, q_decays, k_decays
    )
    for h in range(1, local_heads):
        slots.append(gather_shard(offered(h)))
    mixer_out_cut = lax.dynamic_slice_in_dim(mixer_out, s * vcols, vcols, 1)
    mixer_out_cut, slots[0] = tie(mixer_out_cut, slots[0])
    w_out = gather_shard(mixer_out_cut)
    ffn_in_cut = lax.dynamic_slice_in_dim(ffn_in, s * sub, sub, 0)
    ffn_in_cut, slots[-1] = tie(ffn_in_cut, slots[-1])
    w_ffn_in = gather_shard(ffn_in_cut)
    ffn_out_here = lax.dynamic_index_in_dim(ffn_out_cut, s, 2, keepdims=False)
    ffn_out_here, slots[-1] = tie(ffn_out_here.reshape(ffn_out.shape[0], -1), slots[-1])
    w_ffn_out = gather_shard(ffn_out_here)
    inner_cols = w_ffn_out.shape[1]

    def rotate(v, sign):
        first = v[..., :half]
        second = v[..., half:]
        sn = sign * sine
        return jnp.concatenate(
            [first * cosine - second * sn, second * cosine + first * sn], axis=-1
        )

    def dots(pattern, left, right):
        return jnp.einsum(pattern, left, right, preferred_element_type=F32)

    def run_states(h, start, terms, reverse):
        found = [None] * blocks
        state = start
        for b in reversed(range(blocks)) if reverse else range(blocks):
            found[b] = state
            state = block_decays[h] * state + terms[b]
        return jnp.stack(found), state

    ranks = segment_order
    piece = DK // segments

    def exchange_states(h, total, reverse):
        cut = total.astype(BF16).reshape(segments, piece, DV)
        got = lax.all_to_all(cut, "shard", split_axis=0, concat_axis=0, tiled=True)
        if not reverse and h + 1 < local_heads:
            slots[h + 1], got = tie(slots[h + 1], got)
        got = got.astype(F32)
        apart = ranks[:, None] - ranks[None, :] - 1
        if reverse:
            apart = -apart - 2
        distance = apart.astype(F32)
        coef = jnp.where(
            distance >= 0.0, jnp.exp(jnp.maximum(distance, 0.0) * seg_len * logs[h]), 0.0
        )
        joined = jnp.sum(coef[..., None, None] * got[None], axis=1).astype(BF16)
        back_cut = lax.all_to_all(joined, "shard", split_axis=0, concat_axis=0, tiled=True)
        return back_cut.reshape(DK, DV).astype(F32)

    kept = []
    zero_state = jnp.zeros((DK, DV), F32)
    for h in range(local_heads):
        proj = dot_nt(normed, slots[h])
        place_here = place[h, s]
        q_raw, k_raw, v_a, v_b, g_a, g_b = (
            lax.dynamic_slice_in_dim(proj, place_here[c] * DK, DK, 1) for c in range(6)
        )
        q = rotate(q_raw, 1.0).astype(BF16).reshape(blocks, blk, DK)
        k = rotate(k_raw, 1.0).astype(BF16).reshape(blocks, blk, DK)
        v = jnp.concatenate([v_a, v_b], axis=1).astype(BF16).reshape(blocks, blk, DV)
        gate = jnp.concatenate([g_a, g_b], axis=1)
        kd = (k.astype(F32) * k_decays[h]).astype(BF16)
        qd = (q.astype(F32) * q_decays[h]).astype(BF16)
        updates = dots("cmk,cmv->ckv", kd, v)
        ignored, total = run_states(h, zero_state, updates, False)
        state_in = exchange_states(h, total, False)
        states, ignored1 = run_states(h, state_in, updates, False)
        states = states.astype(BF16)
        weights = (dots("cnk,cmk->cnm", q, k) * masks[h]).astype(BF16)
        retained = dots("cnm,cmv->cnv", weights, v) + dots("cnk,ckv->cnv", qd, states)
        retained = retained.reshape(seg_len, DV)
        mixed = group_norm(retained).astype(BF16)
        hidden = gated_silu(gate, mixed.astype(F32)).astype(BF16)
        kept.append((q, k, v, qd, kd, gate, weights, states, retained, mixed, hidden))
    hidden = jnp.concatenate([t[-1] for t in kept], axis=1)

    resid = xf + scatter_seq(dot_nt(hidden, w_out, BF16))
    normed2 = gather_near(rms_scale(resid, gain_ffn).astype(BF16))
    proj2 = dot_nt(normed2, w_ffn_in)
    first, second = proj2[:, :inner_cols], proj2[:, inner_cols:]
    inner2 = gated_gelu(first, second).astype(BF16)

    d_inner2 = dot_nn(d_ffn, w_ffn_out)
    ignored2, gelu_back = jax.vjp(gated_gelu, first, second)
    d_first, d_second = gelu_back(d_inner2)
    dproj2 = jnp.concatenate([d_first, d_second], axis=1).astype(BF16)
    d_normed2, g_ffn_out, g_ffn_in = scatter_near(
        dot_nn(dproj2, w_ffn_in, BF16),
        (dot_tn(d_ffn, inner2, BF16),),
        (dot_tn(dproj2, normed2, BF16),),
    )
    g_ffn_out = reduce_shard(g_ffn_out)
    g_ffn_in = reduce_shard(g_ffn_in)
    ignored3, norm2_back = jax.vjp(rms_scale, resid, gain_ffn)
    d_resid_part, d_gain_ffn = norm2_back(d_normed2)
    d_resid = cotangent.astype(F32) + d_resid_part
    d_attn = gather_seq(d_resid.astype(BF16))
    inner2, d_attn = tie(inner2, d_attn)
    output = (resid + scatter_near(dot_nt(inner2, w_ffn_out, BF16))[0]).astype(BF16)
    d_hidden = dot_nn(d_attn, w_out)
    hidden, g_ffn_in = tie(hidden, g_ffn_in)
    g_mixer_out = reduce_shard(dot_tn(d_attn, hidden, BF16))

    g_slots = []
    d_normed = None
    for h in range(local_heads):
        q, k, v, qd, kd, gate, weights, states, retained, mixed, ignored = kept[h]
        ignored4, silu_back = jax.vjp(gated_silu, gate, mixed.astype(F32))
        d_gate, d_mixed = silu_back(d_hidden[:, h * DV : (h + 1) * DV])
        ignored5, group_back = jax.vjp(group_norm, retained)
        (d_retained,) = group_back(d_mixed.astype(BF16).astype(F32))
        d_out = d_retained.astype(BF16).reshape(blocks, blk, DV)
        cross_grads = dots("cnk,cnv->ckv", qd, d_out)
        ignored6, total = run_states(h, zero_state, cross_grads, True)
        grad_out = exchange_states(h, total, True)
        d_weights = dots("cnv,cmv->cnm", d_out, v).astype(BF16)
        d_scores = (d_weights.astype(F32) * masks[h]).astype(BF16)
        d_q = dots("cnm,cmk->cnk", d_scores, k)
        d_k = dots("cnm,cnk->cmk", d_scores, q)
        d_v = dots("cnm,cnv->cmv", weights, d_out)
        d_q_scaled = dots("cnv,ckv->cnk", d_out, states).astype(BF16)
        d_q = d_q + d_q_scaled.astype(F32) * q_decays[h]
        next_grads, ignored7 = run_states(h, grad_out, cross_grads, True)
        next_low = next_grads.astype(BF16)
        d_k_scaled = dots("cmv,ckv->cmk", v, next_low).astype(BF16)
        d_k = d_k + d_k_scaled.astype(F32) * k_decays[h]
        d_v = d_v + dots("cmk,ckv->cmv", kd, next_low)
        dq_raw = rotate(d_q.reshape(seg_len, DK).astype(BF16).astype(F32), -1.0)
        dk_raw = rotate(d_k.reshape(seg_len, DK).astype(BF16).astype(F32), -1.0)
        dproj = jnp.concatenate(
            [
                dq_raw.astype(BF16),
                dk_raw.astype(BF16),
                d_v.reshape(seg_len, DV).astype(BF16),
                d_gate.astype(BF16),
            ],
            axis=1,
        )
        held_here = held[h, :, s]
        by_slot = jnp.concatenate(
            [
                jnp.where(
                    held_here[c] >= 0,
                    lax.dynamic_slice_in_dim(dproj, jnp.maximum(held_here[c], 0) * DK, DK, 1),
                    jnp.zeros((), BF16),
                )
                for c in range(segments)
            ],
            axis=1,
        )
        g_slots.append(reduce_shard(dot_tn(by_slot, normed, BF16)))
        part = dot_nn(by_slot, slots[h])
        d_normed = part if d_normed is None else d_normed + part
    d_normed = scatter_seq(d_normed.astype(BF16))

    ignored8, norm1_back = jax.vjp(rms_scale, xf, gain_attn)
    d_x_part, d_gain_attn = norm1_back(d_normed)
    input_grad = (d_resid + d_x_part).astype(BF16)
    gain_ffn_grad = sum_all(d_gain_ffn)
    gain_attn_grad = sum_all(d_gain_attn)
    near = jnp.arange(group)
    g_ffn_in = place_blocks(
        spread(g_ffn_in), s ^ near, near, ffn_in.shape, (sub, width), lambda o, n: (n, 0)
    )
    g_mixer_out = place_blocks(
        spread(g_mixer_out),
        s ^ near,
        near,
        mixer_out.shape,
        (mixer_out.shape[0], vcols),
        lambda o, n: (0, n),
    )
    if sub % 128 == 0:
        g_ffn_out = place_blocks(
            spread(g_ffn_out),
            s ^ near,
            near,
            ffn_out.shape,
            (ffn_out.shape[0], sub),
            lambda o, n: (0, o * group + n),
            outer=segments // 2,
        )
    else:
        g_ffn_out = jnp.transpose(
            gather_seq(g_ffn_out).reshape(group, ffn_out.shape[0], segments // 2, sub),
            (1, 2, 0, 3),
        ).reshape(ffn_out.shape).astype(F32)

    g_mixer_in = None
    for h in range(local_heads):
        if h == local_heads - 1:
            g_slots[h], output, input_grad, gain_attn_grad, gain_ffn_grad = tie(
                g_slots[h], output, input_grad, gain_attn_grad, gain_ffn_grad
            )
            g_slots[h], g_ffn_in, g_mixer_out, g_ffn_out = tie(
                g_slots[h], g_ffn_in, g_mixer_out, g_ffn_out
            )
        parts = spread(g_slots[h])
        stack = jnp.stack([jnp.concatenate(part, axis=0) for part in parts])
        lent = cross(
            jnp.stack([pick(stack, s ^ lend[h, j, n]) for n in range(lend.shape[-1])]), 1
        )
        parts += [(lent[n],) for n in range(lend.shape[-1])]
        target = fill[h, j]
        found = back[j][target]
        source = jnp.where(found[:, 2] < 0, s ^ found[:, 1], group + found[:, 2])
        g_mixer_in = place_blocks(
            parts, target, source, mixer_in.shape, (DK, width), lambda o, n: (n, 0), into=g_mixer_in
        )
    return (
        output,
        input_grad,
        gain_attn_grad,
        gain_ffn_grad,
        g_mixer_in,
        g_mixer_out,
        g_ffn_in,
        g_ffn_out,
    )


def solution(mesh):
    return jax.shard_map(
        local,
        mesh=mesh,
        in_specs=(
            P(("shard", "seq"), None),
            P(("shard", "seq"), None),
            P(),
            P(),
            P("shard", None),
            P("shard", None),
            P("shard", None),
            P("shard", None),
            P(),
            P(),
        ),
        out_specs=(
            P(("shard", "seq"), None),
            P(("shard", "seq"), None),
            P(),
            P(),
            P("shard", None),
            P("shard", None),
            P("shard", None),
            P("shard", None),
        ),
        check_vma=False,
    )
```

```python
import functools

import jax
import jax.numpy as jnp
import numpy as np
from jax import lax
from jax.experimental import pallas as pl
from jax.experimental.pallas import tpu as pltpu
from jax.sharding import PartitionSpec as P

DK = 256
DV = 512
FF = 4096
QK = 2048
V = 4096


EPS_NORM = 1e-06
EPS_GROUP = 1e-05

F32 = jnp.float32
BF16 = jnp.bfloat16


def dot_nt(left, right, kind=F32):
    return lax.dot_general(
        left, right, (((1,), (1,)), ((), ())), preferred_element_type=F32
    ).astype(kind)


def dot_nn(left, right, kind=F32):
    return lax.dot_general(
        left, right, (((1,), (0,)), ((), ())), preferred_element_type=F32
    ).astype(kind)


def dot_tn(left, right, kind=F32):
    return lax.dot_general(
        left, right, (((0,), (0,)), ((), ())), preferred_element_type=F32
    ).astype(kind)


def rms_scale(v, gain):
    return v * lax.rsqrt(jnp.mean(v * v, axis=-1, keepdims=True) + EPS_NORM) * gain


def group_norm(v):
    centred = v - jnp.mean(v, axis=-1, keepdims=True)
    return centred * lax.rsqrt(jnp.mean(centred * centred, axis=-1, keepdims=True) + EPS_GROUP)


def gated_gelu(first, second):
    return jax.nn.gelu(first) * second


def gated_silu(first, second):
    return jax.nn.silu(first) * second


def unit_tables(group, local_heads, segments):
    heads = group * local_heads
    owners = [(n, 0) for n in range(heads)] + [(n, 1) for n in range(heads)]
    for base in (2, 4):
        owners += [(n, base + half) for n in range(heads) for half in range(2)]
    per_shard = len(owners) // segments
    keep = np.full((local_heads, segments, group), -1, np.int32)
    give = np.zeros((local_heads, segments, group), np.int32)
    place = np.zeros((local_heads, group, 6), np.int32)
    held = np.full((local_heads, segments, group), -1, np.int32)
    slot_of = {}
    for chip in range(segments // 2):
        for head in range(heads):
            s, h = divmod(head, local_heads)
            span = range(2 * per_shard * chip, 2 * per_shard * (chip + 1))
            mine = [u for u in span if owners[u][0] == head]
            assert len(mine) <= 2
            for n, u in enumerate(mine):
                home = u // per_shard
                slot = home if len(mine) == 1 else 2 * chip + n
                if slot == home:
                    keep[h, slot, s] = u % per_shard
                else:
                    give[h, home, s] = u % per_shard
                place[h, s, owners[u][1]] = slot
                held[h, slot, s] = owners[u][1]
                slot_of[u] = slot
    lends = [[[] for _ in range(segments)] for _ in range(local_heads)]
    back = np.zeros((segments, per_shard, 3), np.int32)
    for u, (head, _) in enumerate(owners):
        home = u // per_shard
        s, h = divmod(head, local_heads)
        back[home, u % per_shard] = (h, s, -1)
        if slot_of[u] != home:
            assert slot_of[u] == home ^ 1
            back[home, u % per_shard, 2] = len(lends[h][home ^ 1])
            lends[h][home ^ 1].append(s)
    most = max(1, max(len(t) for row in lends for t in row))
    lend = np.asarray(
        [[(t + [0] * most)[:most] for t in row] for row in lends], np.int32
    )
    fills = [[np.flatnonzero(back[t, :, 0] == h) for t in range(segments)] for h in range(local_heads)]
    longest = max(1, max(len(t) for row in fills for t in row))
    fill = np.zeros((local_heads, segments, longest), np.int32)
    for h in range(local_heads):
        for t in range(segments):
            assert len(fills[h][t]) > 0
            fill[h, t] = np.pad(fills[h][t], (0, longest - len(fills[h][t])), mode="edge")
    return keep, give, place, held, back, lend, fill


def tie(*values):
    return lax.optimization_barrier(values)


def place_kernel(sizes, aliased, target, source, *refs):
    out = refs[-1]
    code = source[pl.program_id(1)]
    at = 1 if aliased else 0
    for i, size in enumerate(sizes):
        pieces = refs[at : at + size]
        at += size

        @pl.when(code == i)
        def _(pieces=pieces):
            row = 0
            for piece in pieces:
                out[row : row + piece.shape[0], :] = piece[...].astype(F32)
                row += piece.shape[0]


def place_blocks(parts, target, source, shape, block, where, outer=1, into=None):
    flat = [t for part in parts for t in part]
    aliased = into is not None
    specs = [
        pl.BlockSpec((t.shape[0], t.shape[1] // outer), lambda o, n, target, source: (0, o))
        for t in flat
    ]
    if aliased:
        specs = [pl.BlockSpec(memory_space=pl.ANY)] + specs
        flat = [into] + flat
    return pl.pallas_call(
        functools.partial(place_kernel, [len(part) for part in parts], aliased),
        grid_spec=pltpu.PrefetchScalarGridSpec(
            num_scalar_prefetch=2,
            grid=(outer, target.shape[0]),
            in_specs=specs,
            out_specs=pl.BlockSpec(block, lambda o, n, target, source: where(o, target[n])),
        ),
        out_shape=jax.ShapeDtypeStruct(shape, F32),
        input_output_aliases={2: 0} if aliased else {},
        compiler_params=pltpu.CompilerParams(vmem_limit_bytes=40 * 2**20),
    )(target.astype(jnp.int32), source.astype(jnp.int32), *flat)


def local(
    tokens,
    cotangent,
    gain_attn,
    gain_ffn,
    mixer_in,
    mixer_out,
    ffn_in,
    ffn_out,
    segment_order,
    decay_index,
):
    rows, width = tokens.shape
    group = lax.axis_size("seq")
    segments = lax.axis_size("shard")
    heads = decay_index.shape[0]
    local_heads = heads // group
    seg_len = rows * group
    blk = min(512, seg_len)
    blocks = seg_len // blk
    vcols = local_heads * DV
    s = lax.axis_index("seq")
    j = lax.axis_index("shard")

    def swap(v, d):
        return lax.ppermute(v, "seq", [(i, i ^ d) for i in range(group)])

    def cross(v, d):
        return lax.ppermute(v, "shard", [(i, i ^ d) for i in range(segments)])

    def pick(v, i):
        return lax.dynamic_index_in_dim(v, i, 0, keepdims=False)

    def spread(v):
        if group == 4:
            h = v.shape[0] // 2
            r1 = swap(v, 1)
            r2 = swap(v, 2)
            return [(v,), (r1,), (r2,), (swap(r1[:h], 2), swap(r2[h:], 1))]
        return [(v,)] + [(swap(v, d),) for d in range(1, group)]

    def ordered(parts):
        r = parts[0][0].shape[0]
        out = jnp.zeros((group * r,) + parts[0][0].shape[1:], parts[0][0].dtype)
        for d, part in enumerate(parts):
            row = (s ^ d) * r
            for piece in part:
                out = lax.dynamic_update_slice_in_dim(out, piece, row, 0)
                row = row + piece.shape[0]
        return out

    def gather_near(v):
        return jnp.concatenate([piece for part in spread(v) for piece in part], axis=0)

    def gather_seq(v):
        return ordered(spread(v))

    def scatter_sum(blk_of, beside1=(), beside2=()):
        if group == 4:
            b0, b1, b2, b3 = (blk_of(d) for d in range(4))
            h = b0.shape[0] // 2
            b0 = b0.astype(F32)
            ra = swap(jnp.concatenate([b1[:h], b3[:h]], axis=0), 1)
            rb = swap(jnp.concatenate([b2[h:], b3[h:]], axis=0), 2)
            ra, rb, *beside1 = tie(ra, rb, *beside1)
            ra, rb = ra.astype(F32), rb.astype(F32)
            qa = swap((b2[:h].astype(F32) + ra[h:]).astype(BF16), 2)
            qb = swap((b1[h:].astype(F32) + rb[h:]).astype(BF16), 1)
            qa, qb, *beside2 = tie(qa, qb, *beside2)
            total = jnp.concatenate(
                [b0[:h] + ra[:h] + qa.astype(F32), b0[h:] + rb[:h] + qb.astype(F32)], axis=0
            )
            return (total, *beside1, *beside2)
        total = blk_of(0).astype(F32)
        for d in range(1, group):
            total = total + swap(blk_of(d), d).astype(F32)
        return (total, *beside1, *beside2)

    def scatter_near(v, beside1=(), beside2=()):
        return scatter_sum(lambda d: v[d * rows : (d + 1) * rows], beside1, beside2)

    def scatter_seq(v):
        return scatter_sum(lambda d: lax.dynamic_slice_in_dim(v, (s ^ d) * rows, rows, 0))[0]

    def gather_shard(v):
        return lax.all_gather(v, "shard", axis=0, tiled=True)

    def reduce_shard(v):
        return lax.psum_scatter(v, "shard", scatter_dimension=0, tiled=True)

    def sum_all(v):
        step = 1
        while step < group:
            v = v + swap(v, step)
            step *= 2
        step = 1
        while step < segments:
            v = v + cross(v, step)
            step *= 2
        return v

    keep, give, place, held, back, lend, fill = (
        jnp.asarray(t) for t in unit_tables(group, local_heads, segments)
    )
    units = mixer_in.reshape(-1, DK, width)

    def offered(h):
        kept = keep[h, j, s]
        given = cross(pick(units, give[h, j, s]), 1)
        return jnp.where(kept >= 0, pick(units, jnp.maximum(kept, 0)), given)

    sub = ffn_in.shape[0] // group
    ffn_out_cut = ffn_out.reshape(ffn_out.shape[0], segments // 2, group, sub)

    my_rank = jnp.sum(jnp.where(jnp.arange(segments) == j, segment_order, 0))
    all_logs = jnp.log1p(-jnp.exp2(-(5.0 + decay_index.astype(F32))))
    logs = lax.dynamic_slice_in_dim(all_logs, s * local_heads, local_heads)
    half = DK // 2
    inv_freq = jnp.exp(-jnp.log(10000.0) * jnp.arange(half).astype(F32) / half)
    positions = my_rank * seg_len + jnp.arange(seg_len, dtype=jnp.int32)
    angles = positions.astype(F32)[:, None] * inv_freq[None, :]
    cosine = jnp.cos(angles)
    sine = jnp.sin(angles)
    steps = jnp.arange(blk).astype(F32)
    gap = steps[:, None] - steps[None, :]
    masks = jnp.where(
        gap[None] >= 0.0, jnp.exp(jnp.maximum(gap, 0.0)[None] * logs[:, None, None]), 0.0
    )
    q_decays = jnp.exp((steps + 1.0)[None, :] * logs[:, None])[..., None]
    k_decays = jnp.exp((blk - 1.0 - steps)[None, :] * logs[:, None])[..., None]
    block_decays = jnp.exp(blk * logs)

    xf = tokens.astype(F32)
    normed = gather_seq(rms_scale(xf, gain_attn).astype(BF16))
    d_ffn = gather_near(cotangent)
    slots = [gather_shard(offered(0))]
    slots[0], normed, d_ffn, cosine, sine, masks, q_decays, k_decays = tie(
        slots[0], normed, d_ffn, cosine, sine, masks, q_decays, k_decays
    )
    for h in range(1, local_heads):
        slots.append(gather_shard(offered(h)))
    mixer_out_cut = lax.dynamic_slice_in_dim(mixer_out, s * vcols, vcols, 1)
    mixer_out_cut, slots[0] = tie(mixer_out_cut, slots[0])
    w_out = gather_shard(mixer_out_cut)
    later = [
        lax.dynamic_slice_in_dim(ffn_in, s * sub, sub, 0),
        lax.dynamic_index_in_dim(ffn_out_cut, s, 2, keepdims=False).reshape(ffn_out.shape[0], -1),
    ]
    inner_cols = later[1].shape[1]

    def rotate(v, sign):
        first = v[..., :half]
        second = v[..., half:]
        sn = sign * sine
        return jnp.concatenate(
            [first * cosine - second * sn, second * cosine + first * sn], axis=-1
        )

    def dots(pattern, left, right):
        return jnp.einsum(pattern, left, right, preferred_element_type=F32)

    def run_states(h, start, terms, reverse):
        found = [None] * blocks
        state = start
        for b in reversed(range(blocks)) if reverse else range(blocks):
            found[b] = state
            state = block_decays[h] * state + terms[b]
        return jnp.stack(found), state

    ranks = segment_order
    piece = DK // segments

    def exchange_states(h, total, reverse):
        cut = total.astype(BF16).reshape(segments, piece, DV)
        got = lax.all_to_all(cut, "shard", split_axis=0, concat_axis=0, tiled=True)
        if not reverse and h + 1 < local_heads:
            slots[h + 1], got, *later[:] = tie(slots[h + 1], got, *later)
        got = got.astype(F32)
        apart = ranks[:, None] - ranks[None, :] - 1
        if reverse:
            apart = -apart - 2
        distance = apart.astype(F32)
        coef = jnp.where(
            distance >= 0.0, jnp.exp(jnp.maximum(distance, 0.0) * seg_len * logs[h]), 0.0
        )
        joined = jnp.sum(coef[..., None, None] * got[None], axis=1).astype(BF16)
        back_cut = lax.all_to_all(joined, "shard", split_axis=0, concat_axis=0, tiled=True)
        if reverse and h == 0:
            back_cut, scattered["ffn_in"] = tie(back_cut, scattered["ffn_in"])
        return back_cut.reshape(DK, DV).astype(F32)

    kept = []
    zero_state = jnp.zeros((DK, DV), F32)
    for h in range(local_heads):
        proj = dot_nt(normed, slots[h])
        place_here = place[h, s]
        q_raw, k_raw, v_a, v_b, g_a, g_b = (
            lax.dynamic_slice_in_dim(proj, place_here[c] * DK, DK, 1) for c in range(6)
        )
        q = rotate(q_raw, 1.0).astype(BF16).reshape(blocks, blk, DK)
        k = rotate(k_raw, 1.0).astype(BF16).reshape(blocks, blk, DK)
        v = jnp.concatenate([v_a, v_b], axis=1).astype(BF16).reshape(blocks, blk, DV)
        gate = jnp.concatenate([g_a, g_b], axis=1)
        kd = (k.astype(F32) * k_decays[h]).astype(BF16)
        qd = (q.astype(F32) * q_decays[h]).astype(BF16)
        updates = dots("cmk,cmv->ckv", kd, v)
        ignored, total = run_states(h, zero_state, updates, False)
        state_in = exchange_states(h, total, False)
        states, ignored1 = run_states(h, state_in, updates, False)
        states = states.astype(BF16)
        weights = (dots("cnk,cmk->cnm", q, k) * masks[h]).astype(BF16)
        retained = dots("cnm,cmv->cnv", weights, v) + dots("cnk,ckv->cnv", qd, states)
        retained = retained.reshape(seg_len, DV)
        mixed = group_norm(retained).astype(BF16)
        hidden = gated_silu(gate, mixed.astype(F32)).astype(BF16)
        kept.append((q, k, v, qd, kd, gate, weights, states, retained, mixed, hidden))
    hidden = jnp.concatenate([t[-1] for t in kept], axis=1)
    w_ffn_in, w_ffn_out = (gather_shard(t) for t in later)

    resid = xf + scatter_seq(dot_nt(hidden, w_out, BF16))
    normed2 = gather_near(rms_scale(resid, gain_ffn).astype(BF16))
    proj2 = dot_nt(normed2, w_ffn_in)
    first, second = proj2[:, :inner_cols], proj2[:, inner_cols:]
    inner2 = gated_gelu(first, second).astype(BF16)

    d_inner2 = dot_nn(d_ffn, w_ffn_out)
    ignored2, gelu_back = jax.vjp(gated_gelu, first, second)
    d_first, d_second = gelu_back(d_inner2)
    dproj2 = jnp.concatenate([d_first, d_second], axis=1).astype(BF16)
    d_normed2, g_ffn_out, g_ffn_in = scatter_near(
        dot_nn(dproj2, w_ffn_in, BF16),
        (dot_tn(d_ffn, inner2, BF16),),
        (dot_tn(dproj2, normed2, BF16),),
    )
    scattered = {"ffn_out": reduce_shard(g_ffn_out), "ffn_in": reduce_shard(g_ffn_in)}
    ignored3, norm2_back = jax.vjp(rms_scale, resid, gain_ffn)
    d_resid_part, d_gain_ffn = norm2_back(d_normed2)
    d_resid = cotangent.astype(F32) + d_resid_part
    d_attn = gather_seq(d_resid.astype(BF16))
    inner2, d_attn, scattered["ffn_out"] = tie(inner2, d_attn, scattered["ffn_out"])
    parts_ffn_out = spread(scattered["ffn_out"])
    output = (resid + scatter_near(dot_nt(inner2, w_ffn_out, BF16))[0]).astype(BF16)
    d_hidden = dot_nn(d_attn, w_out)
    scattered["mixer_out"] = reduce_shard(dot_tn(d_attn, hidden, BF16))

    def tie_parts(v, parts):
        flat = tie(v, *(piece for part in parts for piece in part))
        rest = list(flat[1:])
        return flat[0], [tuple(rest.pop(0) for _ in part) for part in parts]

    g_slots = []
    d_normed = None
    for h in range(local_heads):
        q, k, v, qd, kd, gate, weights, states, retained, mixed, ignored = kept[h]
        ignored4, silu_back = jax.vjp(gated_silu, gate, mixed.astype(F32))
        d_gate, d_mixed = silu_back(d_hidden[:, h * DV : (h + 1) * DV])
        ignored5, group_back = jax.vjp(group_norm, retained)
        (d_retained,) = group_back(d_mixed.astype(BF16).astype(F32))
        d_out = d_retained.astype(BF16).reshape(blocks, blk, DV)
        cross_grads = dots("cnk,cnv->ckv", qd, d_out)
        ignored6, total = run_states(h, zero_state, cross_grads, True)
        grad_out = exchange_states(h, total, True)
        d_weights = dots("cnv,cmv->cnm", d_out, v).astype(BF16)
        d_scores = (d_weights.astype(F32) * masks[h]).astype(BF16)
        d_q = dots("cnm,cmk->cnk", d_scores, k)
        d_k = dots("cnm,cnk->cmk", d_scores, q)
        d_v = dots("cnm,cnv->cmv", weights, d_out)
        d_q_scaled = dots("cnv,ckv->cnk", d_out, states).astype(BF16)
        d_q = d_q + d_q_scaled.astype(F32) * q_decays[h]
        next_grads, ignored7 = run_states(h, grad_out, cross_grads, True)
        next_low = next_grads.astype(BF16)
        d_k_scaled = dots("cmv,ckv->cmk", v, next_low).astype(BF16)
        d_k = d_k + d_k_scaled.astype(F32) * k_decays[h]
        d_v = d_v + dots("cmk,ckv->cmv", kd, next_low)
        dq_raw = rotate(d_q.reshape(seg_len, DK).astype(BF16).astype(F32), -1.0)
        dk_raw = rotate(d_k.reshape(seg_len, DK).astype(BF16).astype(F32), -1.0)
        dproj = jnp.concatenate(
            [
                dq_raw.astype(BF16),
                dk_raw.astype(BF16),
                d_v.reshape(seg_len, DV).astype(BF16),
                d_gate.astype(BF16),
            ],
            axis=1,
        )
        held_here = held[h, :, s]
        by_slot = jnp.concatenate(
            [
                jnp.where(
                    held_here[c] >= 0,
                    lax.dynamic_slice_in_dim(dproj, jnp.maximum(held_here[c], 0) * DK, DK, 1),
                    jnp.zeros((), BF16),
                )
                for c in range(segments)
            ],
            axis=1,
        )
        if h == 0:
            by_slot, output = tie(by_slot, output)
            by_slot, parts_ffn_out = tie_parts(by_slot, parts_ffn_out)
            parts_ffn_in = spread(scattered["ffn_in"])
        if h == local_heads - 1:
            by_slot, parts_ffn_in = tie_parts(by_slot, parts_ffn_in)
            by_slot, scattered["mixer_out"] = tie(by_slot, scattered["mixer_out"])
            parts_mixer_out = spread(scattered["mixer_out"])
        g_slots.append(reduce_shard(dot_tn(by_slot, normed, BF16)))
        part = dot_nn(by_slot, slots[h])
        d_normed = part if d_normed is None else d_normed + part
    d_normed, parts_mixer_out = tie_parts(d_normed.astype(BF16), parts_mixer_out)
    d_normed = scatter_seq(d_normed)

    ignored8, norm1_back = jax.vjp(rms_scale, xf, gain_attn)
    d_x_part, d_gain_attn = norm1_back(d_normed)
    input_grad = (d_resid + d_x_part).astype(BF16)
    gain_ffn_grad = sum_all(d_gain_ffn)
    gain_attn_grad = sum_all(d_gain_attn)
    near = jnp.arange(group)
    g_ffn_in = place_blocks(
        parts_ffn_in, s ^ near, near, ffn_in.shape, (sub, width), lambda o, n: (n, 0)
    )
    g_mixer_out = place_blocks(
        parts_mixer_out,
        s ^ near,
        near,
        mixer_out.shape,
        (mixer_out.shape[0], vcols),
        lambda o, n: (0, n),
    )
    if sub % 128 == 0:
        g_ffn_out = place_blocks(
            parts_ffn_out,
            s ^ near,
            near,
            ffn_out.shape,
            (ffn_out.shape[0], sub),
            lambda o, n: (0, o * group + n),
            outer=segments // 2,
        )
    else:
        g_ffn_out = jnp.transpose(
            ordered(parts_ffn_out).reshape(group, ffn_out.shape[0], segments // 2, sub),
            (1, 2, 0, 3),
        ).reshape(ffn_out.shape).astype(F32)

    g_mixer_in = None
    for h in range(local_heads):
        if h == local_heads - 1:
            g_slots[h], output, input_grad, gain_attn_grad, gain_ffn_grad = tie(
                g_slots[h], output, input_grad, gain_attn_grad, gain_ffn_grad
            )
            g_slots[h], g_ffn_in, g_mixer_out, g_ffn_out = tie(
                g_slots[h], g_ffn_in, g_mixer_out, g_ffn_out
            )
            if g_mixer_in is not None:
                g_slots[h], g_mixer_in = tie(g_slots[h], g_mixer_in)
        parts = spread(g_slots[h])
        stack = jnp.stack([jnp.concatenate(part, axis=0) for part in parts])
        lent = cross(
            jnp.stack([pick(stack, s ^ lend[h, j, n]) for n in range(lend.shape[-1])]), 1
        )
        parts += [(lent[n],) for n in range(lend.shape[-1])]
        target = fill[h, j]
        found = back[j][target]
        source = jnp.where(found[:, 2] < 0, s ^ found[:, 1], group + found[:, 2])
        g_mixer_in = place_blocks(
            parts, target, source, mixer_in.shape, (DK, width), lambda o, n: (n, 0), into=g_mixer_in
        )
    return (
        output,
        input_grad,
        gain_attn_grad,
        gain_ffn_grad,
        g_mixer_in,
        g_mixer_out,
        g_ffn_in,
        g_ffn_out,
    )


def solution(mesh):
    return jax.shard_map(
        local,
        mesh=mesh,
        in_specs=(
            P(("shard", "seq"), None),
            P(("shard", "seq"), None),
            P(),
            P(),
            P("shard", None),
            P("shard", None),
            P("shard", None),
            P("shard", None),
            P(),
            P(),
        ),
        out_specs=(
            P(("shard", "seq"), None),
            P(("shard", "seq"), None),
            P(),
            P(),
            P("shard", None),
            P("shard", None),
            P("shard", None),
            P("shard", None),
        ),
        check_vma=False,
    )
```

```python
import functools

import jax
import jax.numpy as jnp
import numpy as np
from jax import lax
from jax.experimental import pallas as pl
from jax.experimental.pallas import tpu as pltpu
from jax.sharding import PartitionSpec as P

DK = 256
DV = 512
FF = 4096
QK = 2048
V = 4096


EPS_NORM = 1e-06
EPS_GROUP = 1e-05

F32 = jnp.float32
BF16 = jnp.bfloat16


def dot_nt(left, right, kind=F32):
    return lax.dot_general(
        left, right, (((1,), (1,)), ((), ())), preferred_element_type=F32
    ).astype(kind)


def dot_nn(left, right, kind=F32):
    return lax.dot_general(
        left, right, (((1,), (0,)), ((), ())), preferred_element_type=F32
    ).astype(kind)


def dot_tn(left, right, kind=F32):
    return lax.dot_general(
        left, right, (((0,), (0,)), ((), ())), preferred_element_type=F32
    ).astype(kind)


def rms_scale(v, gain):
    return v * lax.rsqrt(jnp.mean(v * v, axis=-1, keepdims=True) + EPS_NORM) * gain


def gated_gelu(first, second):
    return jax.nn.gelu(first) * second


def unit_tables(group, local_heads, segments):
    heads = group * local_heads
    owners = [(n, 0) for n in range(heads)] + [(n, 1) for n in range(heads)]
    for base in (2, 4):
        owners += [(n, base + half) for n in range(heads) for half in range(2)]
    per_shard = len(owners) // segments
    keep = np.full((local_heads, segments, group), -1, np.int32)
    give = np.zeros((local_heads, segments, group), np.int32)
    place = np.zeros((local_heads, group, 6), np.int32)
    held = np.full((local_heads, segments, group), -1, np.int32)
    slot_of = {}
    for chip in range(segments // 2):
        for head in range(heads):
            s, h = divmod(head, local_heads)
            span = range(2 * per_shard * chip, 2 * per_shard * (chip + 1))
            mine = [u for u in span if owners[u][0] == head]
            assert len(mine) <= 2
            for n, u in enumerate(mine):
                home = u // per_shard
                slot = home if len(mine) == 1 else 2 * chip + n
                if slot == home:
                    keep[h, slot, s] = u % per_shard
                else:
                    give[h, home, s] = u % per_shard
                place[h, s, owners[u][1]] = slot
                held[h, slot, s] = owners[u][1]
                slot_of[u] = slot
    lends = [[[] for _ in range(segments)] for _ in range(local_heads)]
    back = np.zeros((segments, per_shard, 3), np.int32)
    for u, (head, _) in enumerate(owners):
        home = u // per_shard
        s, h = divmod(head, local_heads)
        back[home, u % per_shard] = (h, s, -1)
        if slot_of[u] != home:
            assert slot_of[u] == home ^ 1
            back[home, u % per_shard, 2] = len(lends[h][home ^ 1])
            lends[h][home ^ 1].append(s)
    most = max(1, max(len(t) for row in lends for t in row))
    lend = np.asarray(
        [[(t + [0] * most)[:most] for t in row] for row in lends], np.int32
    )
    fills = [[np.flatnonzero(back[t, :, 0] == h) for t in range(segments)] for h in range(local_heads)]
    longest = max(1, max(len(t) for row in fills for t in row))
    fill = np.zeros((local_heads, segments, longest), np.int32)
    for h in range(local_heads):
        for t in range(segments):
            assert len(fills[h][t]) > 0
            fill[h, t] = np.pad(fills[h][t], (0, longest - len(fills[h][t])), mode="edge")
    return keep, give, place, held, back, lend, fill


def tie(*values):
    return lax.optimization_barrier(values)


def mm(left, right, dims):
    return lax.dot_general(left, right, (dims, ((), ())), preferred_element_type=F32)


NN = ((1,), (0,))
NT = ((1,), (1,))
TN = ((0,), (0,))


def turn(v, cosine, sine):
    half = v.shape[-1] // 2
    first, second = v[:, :half], v[:, half:]
    return jnp.concatenate(
        [first * cosine - second * sine, second * cosine + first * sine], axis=-1
    )


def scaled(v, decay):
    return (v.astype(F32) * decay).astype(BF16)


def project_kernel(blk, place, decay, x, w, cosine, sine, k_decay, q, k, v, gate, total, y):
    c = pl.program_id(0)
    rows = y.shape[0]
    for r in range(0, rows, blk):
        y[r : r + blk, :] = mm(x[r : r + blk, :], w[...], NT)

    @pl.when(c == 0)
    def _():
        q[...] = turn(y[...], cosine[...], sine[...]).astype(BF16)

    @pl.when(c == 1)
    def _():
        k[...] = turn(y[...], cosine[...], sine[...]).astype(BF16)

    @pl.when(c == 2)
    def _():
        v[:, :DK] = y[...].astype(BF16)

    @pl.when(c == 3)
    def _():
        v[:, DK:] = y[...].astype(BF16)
        state = jnp.zeros(total.shape, F32)
        for r in range(0, rows, blk):
            kd = scaled(k[r : r + blk, :], k_decay[...])
            state = decay[0] * state + mm(kd, v[r : r + blk, :], TN)
        total[...] = state.astype(BF16)

    @pl.when(c == 4)
    def _():
        gate[:, :DK] = y[...]

    @pl.when(c == 5)
    def _():
        gate[:, DK:] = y[...]


def retain_kernel(decay, q, k, v, gate, mask, q_decay, k_decay, start, hidden, mixed, kept, state):
    @pl.when(pl.program_id(0) == 0)
    def _():
        state[...] = start[...].astype(F32)

    weights = (mm(q[...], k[...], NT) * mask[...]).astype(BF16)
    o = mm(weights, v[...], NN)
    o += mm(scaled(q[...], q_decay[...]), state[...].astype(BF16), NN)
    state[...] = decay[0] * state[...] + mm(scaled(k[...], k_decay[...]), v[...], TN)
    kept[...] = o
    o = o - jnp.mean(o, axis=-1, keepdims=True)
    o = o * lax.rsqrt(jnp.mean(o * o, axis=-1, keepdims=True) + EPS_GROUP)
    low = o.astype(BF16)
    mixed[...] = low
    g = gate[...]
    hidden[...] = (g * jax.nn.sigmoid(g) * low.astype(F32)).astype(BF16)


def gate_back_kernel(decay, d_hidden, gate, mixed, kept, q, q_decay, d_gate, d_out, total, state):
    @pl.when(pl.program_id(0) == 0)
    def _():
        state[...] = jnp.zeros(state.shape, F32)

    g = gate[...]
    dh = d_hidden[...]
    sig = jax.nn.sigmoid(g)
    d_gate[...] = (dh * mixed[...].astype(F32) * (sig * (1.0 + g * (1.0 - sig)))).astype(BF16)
    dy = (dh * (g * sig)).astype(BF16).astype(F32)
    o = kept[...]
    o = o - jnp.mean(o, axis=-1, keepdims=True)
    inverse = lax.rsqrt(jnp.mean(o * o, axis=-1, keepdims=True) + EPS_GROUP)
    o = o * inverse
    do = inverse * (
        dy
        - jnp.mean(dy, axis=-1, keepdims=True)
        - o * jnp.mean(dy * o, axis=-1, keepdims=True)
    )
    do = do.astype(BF16)
    d_out[...] = do
    state[...] = decay[0] * state[...] + mm(scaled(q[...], q_decay[...]), do, TN)
    total[...] = state[...].astype(BF16)


def inner_back_kernel(
    decay, q, k, v, d_out, mask, q_decay, k_decay, start, cosine, sine, d_q, d_k, d_v, state
):
    @pl.when(pl.program_id(0) == 0)
    def _():
        state[...] = start[...].astype(F32)

    do = d_out[...]
    weights = (mm(q[...], k[...], NT) * mask[...]).astype(BF16)
    d_v[...] = mm(weights, do, TN)
    d_scores = mm(do, v[...], NT).astype(BF16).astype(F32)
    d_scores = (d_scores * mask[...]).astype(BF16)
    d_k[...] = mm(d_scores, q[...], TN)
    far = mm(do, state[...].astype(BF16), NT).astype(BF16).astype(F32)
    dq = mm(d_scores, k[...], NN) + far * q_decay[...]
    dq = dq.astype(BF16).astype(F32)
    d_q[...] = turn(dq, cosine[...], -sine[...]).astype(BF16)
    state[...] = decay[0] * state[...] + mm(scaled(k[...], k_decay[...]), v[...], TN)


def outer_back_kernel(
    place, decay, q, k, v, d_out, d_q, d_k, d_v, d_gate, q_decay, k_decay, start, cosine, sine,
    by_slot, state,
):
    @pl.when(pl.program_id(0) == 0)
    def _():
        state[...] = start[...].astype(F32)

    low = state[...].astype(BF16)
    far = mm(v[...], low, NT).astype(BF16).astype(F32)
    dk = (d_k[...] + far * k_decay[...]).astype(BF16).astype(F32)
    dk = turn(dk, cosine[...], -sine[...]).astype(BF16)
    dv = (d_v[...] + mm(scaled(k[...], k_decay[...]), low, NN)).astype(BF16)
    by_slot[...] = jnp.zeros(by_slot.shape, BF16)

    def put(c, value):
        by_slot[:, pl.ds(pl.multiple_of(place[c] * DK, DK), DK)] = value

    put(0, d_q[...])
    put(1, dk)
    put(2, dv[:, :DK])
    put(3, dv[:, DK:])
    put(4, d_gate[:, :DK])
    put(5, d_gate[:, DK:])
    state[...] = decay[0] * state[...] + mm(scaled(q[...], q_decay[...]), d_out[...], TN)


def head_call(kernel, grid, prefetch, operands, outputs, scratch, flops):
    arrays = [t[0] for t in operands]
    specs = [
        pl.BlockSpec(memory_space=pltpu.SMEM)
        if block is None
        else pl.BlockSpec(block, lambda n, *tables, where=where: where(n, *tables))
        for _, block, where in operands
    ]
    size = sum(t.size * t.dtype.itemsize for t in arrays + [t[0] for t in outputs])
    return pl.pallas_call(
        kernel,
        grid_spec=pltpu.PrefetchScalarGridSpec(
            num_scalar_prefetch=len(prefetch),
            grid=(grid,),
            in_specs=specs,
            out_specs=[
                pl.BlockSpec(block, lambda n, *tables, where=where: where(n, *tables))
                for _, block, where in outputs
            ],
            scratch_shapes=scratch,
        ),
        out_shape=[t[0] for t in outputs],
        compiler_params=pltpu.CompilerParams(vmem_limit_bytes=48 * 2**20),
        cost_estimate=pl.CostEstimate(flops=flops, bytes_accessed=size, transcendentals=0),
    )(*prefetch, *arrays)


def place_kernel(sizes, aliased, target, source, *refs):
    out = refs[-1]
    code = source[pl.program_id(1)]
    at = 1 if aliased else 0
    for i, size in enumerate(sizes):
        pieces = refs[at : at + size]
        at += size

        @pl.when(code == i)
        def _(pieces=pieces):
            row = 0
            for piece in pieces:
                out[row : row + piece.shape[0], :] = piece[...].astype(F32)
                row += piece.shape[0]


def place_blocks(parts, target, source, shape, block, where, outer=1, into=None):
    flat = [t for part in parts for t in part]
    aliased = into is not None
    specs = [
        pl.BlockSpec((t.shape[0], t.shape[1] // outer), lambda o, n, target, source: (0, o))
        for t in flat
    ]
    if aliased:
        specs = [pl.BlockSpec(memory_space=pl.ANY)] + specs
        flat = [into] + flat
    return pl.pallas_call(
        functools.partial(place_kernel, [len(part) for part in parts], aliased),
        grid_spec=pltpu.PrefetchScalarGridSpec(
            num_scalar_prefetch=2,
            grid=(outer, target.shape[0]),
            in_specs=specs,
            out_specs=pl.BlockSpec(block, lambda o, n, target, source: where(o, target[n])),
        ),
        out_shape=jax.ShapeDtypeStruct(shape, F32),
        input_output_aliases={2: 0} if aliased else {},
        compiler_params=pltpu.CompilerParams(vmem_limit_bytes=40 * 2**20),
    )(target.astype(jnp.int32), source.astype(jnp.int32), *flat)


def local(
    tokens,
    cotangent,
    gain_attn,
    gain_ffn,
    mixer_in,
    mixer_out,
    ffn_in,
    ffn_out,
    segment_order,
    decay_index,
):
    rows, width = tokens.shape
    group = lax.axis_size("seq")
    segments = lax.axis_size("shard")
    heads = decay_index.shape[0]
    local_heads = heads // group
    seg_len = rows * group
    blk = min(512, seg_len)
    blocks = seg_len // blk
    vcols = local_heads * DV
    s = lax.axis_index("seq")
    j = lax.axis_index("shard")

    def swap(v, d):
        return lax.ppermute(v, "seq", [(i, i ^ d) for i in range(group)])

    def cross(v, d):
        return lax.ppermute(v, "shard", [(i, i ^ d) for i in range(segments)])

    def pick(v, i):
        return lax.dynamic_index_in_dim(v, i, 0, keepdims=False)

    def spread(v):
        if group == 4:
            h = v.shape[0] // 2
            r1 = swap(v, 1)
            r2 = swap(v, 2)
            return [(v,), (r1,), (r2,), (swap(r1[:h], 2), swap(r2[h:], 1))]
        return [(v,)] + [(swap(v, d),) for d in range(1, group)]

    def ordered(parts):
        r = parts[0][0].shape[0]
        out = jnp.zeros((group * r,) + parts[0][0].shape[1:], parts[0][0].dtype)
        for d, part in enumerate(parts):
            row = (s ^ d) * r
            for piece in part:
                out = lax.dynamic_update_slice_in_dim(out, piece, row, 0)
                row = row + piece.shape[0]
        return out

    def gather_near(v):
        return jnp.concatenate([piece for part in spread(v) for piece in part], axis=0)

    def gather_seq(v):
        return ordered(spread(v))

    def scatter_sum(blk_of, beside1=(), beside2=()):
        if group == 4:
            b0, b1, b2, b3 = (blk_of(d) for d in range(4))
            h = b0.shape[0] // 2
            b0 = b0.astype(F32)
            ra = swap(jnp.concatenate([b1[:h], b3[:h]], axis=0), 1)
            rb = swap(jnp.concatenate([b2[h:], b3[h:]], axis=0), 2)
            ra, rb, *beside1 = tie(ra, rb, *beside1)
            ra, rb = ra.astype(F32), rb.astype(F32)
            qa = swap((b2[:h].astype(F32) + ra[h:]).astype(BF16), 2)
            qb = swap((b1[h:].astype(F32) + rb[h:]).astype(BF16), 1)
            qa, qb, *beside2 = tie(qa, qb, *beside2)
            total = jnp.concatenate(
                [b0[:h] + ra[:h] + qa.astype(F32), b0[h:] + rb[:h] + qb.astype(F32)], axis=0
            )
            return (total, *beside1, *beside2)
        total = blk_of(0).astype(F32)
        for d in range(1, group):
            total = total + swap(blk_of(d), d).astype(F32)
        return (total, *beside1, *beside2)

    def scatter_near(v, beside1=(), beside2=()):
        return scatter_sum(lambda d: v[d * rows : (d + 1) * rows], beside1, beside2)

    def scatter_seq(v):
        return scatter_sum(lambda d: lax.dynamic_slice_in_dim(v, (s ^ d) * rows, rows, 0))[0]

    def gather_shard(v):
        return lax.all_gather(v, "shard", axis=0, tiled=True)

    def reduce_shard(v):
        return lax.psum_scatter(v, "shard", scatter_dimension=0, tiled=True)

    def sum_all(v):
        step = 1
        while step < group:
            v = v + swap(v, step)
            step *= 2
        step = 1
        while step < segments:
            v = v + cross(v, step)
            step *= 2
        return v

    keep, give, place, held, back, lend, fill = (
        jnp.asarray(t) for t in unit_tables(group, local_heads, segments)
    )
    units = mixer_in.reshape(-1, DK, width)

    def offered(h):
        kept = keep[h, j, s]
        given = cross(pick(units, give[h, j, s]), 1)
        return jnp.where(kept >= 0, pick(units, jnp.maximum(kept, 0)), given)

    sub = ffn_in.shape[0] // group
    ffn_out_cut = ffn_out.reshape(ffn_out.shape[0], segments // 2, group, sub)

    my_rank = jnp.sum(jnp.where(jnp.arange(segments) == j, segment_order, 0))
    all_logs = jnp.log1p(-jnp.exp2(-(5.0 + decay_index.astype(F32))))
    logs = lax.dynamic_slice_in_dim(all_logs, s * local_heads, local_heads)
    half = DK // 2
    inv_freq = jnp.exp(-jnp.log(10000.0) * jnp.arange(half).astype(F32) / half)
    positions = my_rank * seg_len + jnp.arange(seg_len, dtype=jnp.int32)
    angles = positions.astype(F32)[:, None] * inv_freq[None, :]
    cosine = jnp.cos(angles)
    sine = jnp.sin(angles)
    steps = jnp.arange(blk).astype(F32)
    gap = steps[:, None] - steps[None, :]
    masks = jnp.where(
        gap[None] >= 0.0, jnp.exp(jnp.maximum(gap, 0.0)[None] * logs[:, None, None]), 0.0
    )
    q_decays = jnp.exp((steps + 1.0)[None, :] * logs[:, None])[..., None]
    k_decays = jnp.exp((blk - 1.0 - steps)[None, :] * logs[:, None])[..., None]
    block_decays = jnp.exp(blk * logs)

    xf = tokens.astype(F32)
    normed = gather_seq(rms_scale(xf, gain_attn).astype(BF16))
    d_ffn = gather_near(cotangent)
    slots = [gather_shard(offered(0))]
    slots[0], normed, d_ffn, cosine, sine, masks, q_decays, k_decays = tie(
        slots[0], normed, d_ffn, cosine, sine, masks, q_decays, k_decays
    )
    for h in range(1, local_heads):
        slots.append(gather_shard(offered(h)))
    mixer_out_cut = lax.dynamic_slice_in_dim(mixer_out, s * vcols, vcols, 1)
    mixer_out_cut, slots[0] = tie(mixer_out_cut, slots[0])
    w_out = gather_shard(mixer_out_cut)
    later = [
        lax.dynamic_slice_in_dim(ffn_in, s * sub, sub, 0),
        lax.dynamic_index_in_dim(ffn_out_cut, s, 2, keepdims=False).reshape(ffn_out.shape[0], -1),
    ]
    inner_cols = later[1].shape[1]

    ranks = segment_order
    piece = DK // segments

    def exchange_states(h, total, reverse):
        cut = total.reshape(segments, piece, DV)
        got = lax.all_to_all(cut, "shard", split_axis=0, concat_axis=0, tiled=True)
        if not reverse and h + 1 < local_heads:
            slots[h + 1], got, *later[:] = tie(slots[h + 1], got, *later)
        got = got.astype(F32)
        apart = ranks[:, None] - ranks[None, :] - 1
        if reverse:
            apart = -apart - 2
        distance = apart.astype(F32)
        coef = jnp.where(
            distance >= 0.0, jnp.exp(jnp.maximum(distance, 0.0) * seg_len * logs[h]), 0.0
        )
        joined = jnp.sum(coef[..., None, None] * got[None], axis=1).astype(BF16)
        back_cut = lax.all_to_all(joined, "shard", split_axis=0, concat_axis=0, tiled=True)
        if reverse and h == 0:
            back_cut, scattered["ffn_in"] = tie(back_cut, scattered["ffn_in"])
        return back_cut.reshape(DK, DV)

    def whole(n, *tables):
        return (0, 0)

    def ahead(n, *tables):
        return (n, 0)

    def behind(n, *tables):
        return (blocks - 1 - n, 0)

    def shaped(columns, kind, r=seg_len):
        return jax.ShapeDtypeStruct((r, columns), kind)

    kept = []
    state_scratch = [pltpu.VMEM((DK, DV), F32)]
    half_block = (blk, half)
    qk_block, v_block = (blk, DK), (blk, DV)
    ret_flops = 2 * seg_len * (DK + DV) * (blk + DK)
    for h in range(local_heads):
        decay = (block_decays[h : h + 1], None, None)
        mask = (masks[h], (blk, blk), whole)
        q_decay = (q_decays[h], (blk, 1), whole)
        k_decay = (k_decays[h], (blk, 1), whole)
        q, k, v, gate, total = head_call(
            functools.partial(project_kernel, blk),
            6,
            [place[h, s]],
            [
                decay,
                (normed, (seg_len, width), whole),
                (slots[h], (DK, width), lambda n, place: (place[n], 0)),
                (cosine, (seg_len, half), whole),
                (sine, (seg_len, half), whole),
                k_decay,
            ],
            [
                (shaped(DK, BF16), (seg_len, DK), whole),
                (shaped(DK, BF16), (seg_len, DK), whole),
                (shaped(DV, BF16), (seg_len, DV), whole),
                (shaped(DV, F32), (seg_len, DV), whole),
                (shaped(DV, BF16, DK), (DK, DV), whole),
            ],
            [pltpu.VMEM((seg_len, DK), F32)],
            2 * seg_len * width * 6 * DK,
        )
        state_in = exchange_states(h, total, False)
        hidden, mixed, retained = head_call(
            retain_kernel,
            blocks,
            [],
            [
                decay,
                (q, qk_block, ahead),
                (k, qk_block, ahead),
                (v, v_block, ahead),
                (gate, v_block, ahead),
                mask,
                q_decay,
                k_decay,
                (state_in, (DK, DV), whole),
            ],
            [
                (shaped(DV, BF16), v_block, ahead),
                (shaped(DV, BF16), v_block, ahead),
                (shaped(DV, F32), v_block, ahead),
            ],
            state_scratch,
            ret_flops,
        )
        kept.append((decay, mask, q_decay, k_decay, q, k, v, gate, state_in, retained, mixed, hidden))
    hidden = jnp.concatenate([t[-1] for t in kept], axis=1)
    w_ffn_in, w_ffn_out = (gather_shard(t) for t in later)

    resid = xf + scatter_seq(dot_nt(hidden, w_out, BF16))
    normed2 = gather_near(rms_scale(resid, gain_ffn).astype(BF16))
    proj2 = dot_nt(normed2, w_ffn_in)
    first, second = proj2[:, :inner_cols], proj2[:, inner_cols:]
    inner2 = gated_gelu(first, second).astype(BF16)

    d_inner2 = dot_nn(d_ffn, w_ffn_out)
    ignored2, gelu_back = jax.vjp(gated_gelu, first, second)
    d_first, d_second = gelu_back(d_inner2)
    dproj2 = jnp.concatenate([d_first, d_second], axis=1).astype(BF16)
    d_normed2, g_ffn_out, g_ffn_in = scatter_near(
        dot_nn(dproj2, w_ffn_in, BF16),
        (dot_tn(d_ffn, inner2, BF16),),
        (dot_tn(dproj2, normed2, BF16),),
    )
    scattered = {"ffn_out": reduce_shard(g_ffn_out), "ffn_in": reduce_shard(g_ffn_in)}
    ignored3, norm2_back = jax.vjp(rms_scale, resid, gain_ffn)
    d_resid_part, d_gain_ffn = norm2_back(d_normed2)
    d_resid = cotangent.astype(F32) + d_resid_part
    d_attn = gather_seq(d_resid.astype(BF16))
    inner2, d_attn, scattered["ffn_out"] = tie(inner2, d_attn, scattered["ffn_out"])
    parts_ffn_out = spread(scattered["ffn_out"])
    output = (resid + scatter_near(dot_nt(inner2, w_ffn_out, BF16))[0]).astype(BF16)
    d_hidden = dot_nn(d_attn, w_out)
    scattered["mixer_out"] = reduce_shard(dot_tn(d_attn, hidden, BF16))

    def tie_parts(v, parts):
        flat = tie(v, *(piece for part in parts for piece in part))
        rest = list(flat[1:])
        return flat[0], [tuple(rest.pop(0) for _ in part) for part in parts]

    g_slots = []
    d_normed = None
    turns = [(cosine, half_block), (sine, half_block)]
    firsts = []
    for h in range(local_heads):
        decay, mask, q_decay, k_decay, q, k, v, gate, state_in, retained, mixed, ignored = kept[h]
        firsts.append(
            head_call(
                gate_back_kernel,
                blocks,
                [],
                [
                    decay,
                    (d_hidden, v_block, lambda n, h=h: (blocks - 1 - n, h)),
                    (gate, v_block, behind),
                    (mixed, v_block, behind),
                    (retained, v_block, behind),
                    (q, qk_block, behind),
                    q_decay,
                ],
                [
                    (shaped(DV, BF16), v_block, behind),
                    (shaped(DV, BF16), v_block, behind),
                    (shaped(DV, BF16, DK), (DK, DV), whole),
                ],
                state_scratch,
                2 * seg_len * DK * DV,
            )
        )
    for h in range(local_heads):
        decay, mask, q_decay, k_decay, q, k, v, gate, state_in, retained, mixed, ignored = kept[h]
        d_gate, d_out, total = firsts[h]
        grad_out = exchange_states(h, total, True)
        d_q, d_k, d_v = head_call(
            inner_back_kernel,
            blocks,
            [],
            [
                decay,
                (q, qk_block, ahead),
                (k, qk_block, ahead),
                (v, v_block, ahead),
                (d_out, v_block, ahead),
                mask,
                q_decay,
                k_decay,
                (state_in, (DK, DV), whole),
                *((*t, ahead) for t in turns),
            ],
            [
                (shaped(DK, BF16), qk_block, ahead),
                (shaped(DK, F32), qk_block, ahead),
                (shaped(DV, F32), v_block, ahead),
            ],
            state_scratch,
            2 * ret_flops,
        )
        (by_slot,) = head_call(
            outer_back_kernel,
            blocks,
            [place[h, s]],
            [
                decay,
                (q, qk_block, behind),
                (k, qk_block, behind),
                (v, v_block, behind),
                (d_out, v_block, behind),
                (d_q, qk_block, behind),
                (d_k, qk_block, behind),
                (d_v, v_block, behind),
                (d_gate, v_block, behind),
                q_decay,
                k_decay,
                (grad_out, (DK, DV), whole),
                *((*t, behind) for t in turns),
            ],
            [(shaped(segments * DK, BF16), (blk, segments * DK), behind)],
            state_scratch,
            6 * seg_len * DK * DV,
        )
        if h == 0:
            by_slot, output = tie(by_slot, output)
            by_slot, parts_ffn_out = tie_parts(by_slot, parts_ffn_out)
            parts_ffn_in = spread(scattered["ffn_in"])
        if h == local_heads - 1:
            by_slot, parts_ffn_in = tie_parts(by_slot, parts_ffn_in)
            by_slot, scattered["mixer_out"] = tie(by_slot, scattered["mixer_out"])
            parts_mixer_out = spread(scattered["mixer_out"])
        g_slots.append(reduce_shard(dot_tn(by_slot, normed, BF16)))
        part = dot_nn(by_slot, slots[h])
        d_normed = part if d_normed is None else d_normed + part
    d_normed, parts_mixer_out = tie_parts(d_normed.astype(BF16), parts_mixer_out)
    d_normed = scatter_seq(d_normed)

    ignored8, norm1_back = jax.vjp(rms_scale, xf, gain_attn)
    d_x_part, d_gain_attn = norm1_back(d_normed)
    input_grad = (d_resid + d_x_part).astype(BF16)
    gain_ffn_grad = sum_all(d_gain_ffn)
    gain_attn_grad = sum_all(d_gain_attn)
    near = jnp.arange(group)
    g_ffn_in = place_blocks(
        parts_ffn_in, s ^ near, near, ffn_in.shape, (sub, width), lambda o, n: (n, 0)
    )
    g_mixer_out = place_blocks(
        parts_mixer_out,
        s ^ near,
        near,
        mixer_out.shape,
        (mixer_out.shape[0], vcols),
        lambda o, n: (0, n),
    )
    if sub % 128 == 0:
        g_ffn_out = place_blocks(
            parts_ffn_out,
            s ^ near,
            near,
            ffn_out.shape,
            (ffn_out.shape[0], sub),
            lambda o, n: (0, o * group + n),
            outer=segments // 2,
        )
    else:
        g_ffn_out = jnp.transpose(
            ordered(parts_ffn_out).reshape(group, ffn_out.shape[0], segments // 2, sub),
            (1, 2, 0, 3),
        ).reshape(ffn_out.shape).astype(F32)

    g_mixer_in = None
    for h in range(local_heads):
        if h == local_heads - 1:
            g_slots[h], output, input_grad, gain_attn_grad, gain_ffn_grad = tie(
                g_slots[h], output, input_grad, gain_attn_grad, gain_ffn_grad
            )
            g_slots[h], g_ffn_in, g_mixer_out, g_ffn_out = tie(
                g_slots[h], g_ffn_in, g_mixer_out, g_ffn_out
            )
            if g_mixer_in is not None:
                g_slots[h], g_mixer_in = tie(g_slots[h], g_mixer_in)
        parts = spread(g_slots[h])
        stack = jnp.stack([jnp.concatenate(part, axis=0) for part in parts])
        lent = cross(
            jnp.stack([pick(stack, s ^ lend[h, j, n]) for n in range(lend.shape[-1])]), 1
        )
        parts += [(lent[n],) for n in range(lend.shape[-1])]
        target = fill[h, j]
        found = back[j][target]
        source = jnp.where(found[:, 2] < 0, s ^ found[:, 1], group + found[:, 2])
        g_mixer_in = place_blocks(
            parts, target, source, mixer_in.shape, (DK, width), lambda o, n: (n, 0), into=g_mixer_in
        )
    return (
        output,
        input_grad,
        gain_attn_grad,
        gain_ffn_grad,
        g_mixer_in,
        g_mixer_out,
        g_ffn_in,
        g_ffn_out,
    )


def solution(mesh):
    return jax.shard_map(
        local,
        mesh=mesh,
        in_specs=(
            P(("shard", "seq"), None),
            P(("shard", "seq"), None),
            P(),
            P(),
            P("shard", None),
            P("shard", None),
            P("shard", None),
            P("shard", None),
            P(),
            P(),
        ),
        out_specs=(
            P(("shard", "seq"), None),
            P(("shard", "seq"), None),
            P(),
            P(),
            P("shard", None),
            P("shard", None),
            P("shard", None),
            P("shard", None),
        ),
        check_vma=False,
    )
```

```python
import functools

import jax
import jax.numpy as jnp
import numpy as np
from jax import lax
from jax.experimental import pallas as pl
from jax.experimental.pallas import tpu as pltpu
from jax.sharding import PartitionSpec as P

DK = 256
DV = 512
FF = 4096
QK = 2048
V = 4096


EPS_NORM = 1e-06
EPS_GROUP = 1e-05

F32 = jnp.float32
BF16 = jnp.bfloat16


def dot_nt(left, right, kind=F32):
    return lax.dot_general(
        left, right, (((1,), (1,)), ((), ())), preferred_element_type=F32
    ).astype(kind)


def dot_nn(left, right, kind=F32):
    return lax.dot_general(
        left, right, (((1,), (0,)), ((), ())), preferred_element_type=F32
    ).astype(kind)


def dot_tn(left, right, kind=F32):
    return lax.dot_general(
        left, right, (((0,), (0,)), ((), ())), preferred_element_type=F32
    ).astype(kind)


def rms_scale(v, gain):
    return v * lax.rsqrt(jnp.mean(v * v, axis=-1, keepdims=True) + EPS_NORM) * gain


def gated_gelu(first, second):
    return jax.nn.gelu(first) * second


def unit_owners(heads):
    owners = [(n, 0) for n in range(heads)] + [(n, 1) for n in range(heads)]
    for base in (2, 4):
        owners += [(n, base + half) for n in range(heads) for half in range(2)]
    return owners


def balanced_tables():
    group, segments, per_shard = 4, 8, 6
    number = {owner: u for u, owner in enumerate(unit_owners(8))}
    keep = np.full((2, segments, group), -1, np.int32)
    give = np.zeros((2, segments, group), np.int32)
    back = np.zeros((segments, per_shard, 2), np.int32)
    lend = [[] for _ in range(segments)]
    seen = set()
    for s in range(group):
        a, b = s, s + 4
        if s < 2:
            gates = [(a, 4), (b, 4), (b, 5)], (b + 2, 5)
        else:
            gates = [(a - 2, 5), (a, 4), (a, 5)], (b, 4)
        first = [(a, 0), (a, 1), (a, 2), (a, 3), (b, 2)] + gates[0]
        second = [(b, 0), (b, 1), (b, 3), gates[1]]
        for slot, owner in enumerate(first):
            home, index = divmod(number[owner], per_shard)
            seen.add(number[owner])
            assert home // 2 == slot // 2
            if home == slot:
                keep[0, slot, s] = index
                back[home, index] = (0, s)
            else:
                give[0, home, s] = index
                back[home, index] = (1, len(lend[slot]))
                lend[slot].append(s)
        for chip, owner in enumerate(second):
            home, index = divmod(number[owner], per_shard)
            seen.add(number[owner])
            assert home // 2 == chip
            keep[1, home, s] = index
            give[1, home, s] = index
            back[home, index] = (2, s)
    assert len(seen) == segments * per_shard
    most = max(len(t) for t in lend)
    return keep, give, back, np.asarray([(t + [0] * most)[:most] for t in lend], np.int32)


def unit_tables(group, local_heads, segments):
    heads = group * local_heads
    owners = unit_owners(heads)
    per_shard = len(owners) // segments
    keep = np.full((local_heads, segments, group), -1, np.int32)
    give = np.zeros((local_heads, segments, group), np.int32)
    place = np.zeros((local_heads, group, 6), np.int32)
    held = np.full((local_heads, segments, group), -1, np.int32)
    slot_of = {}
    for chip in range(segments // 2):
        for head in range(heads):
            h, s = divmod(head, group)
            span = range(2 * per_shard * chip, 2 * per_shard * (chip + 1))
            mine = [u for u in span if owners[u][0] == head]
            assert len(mine) <= 2
            for n, u in enumerate(mine):
                home = u // per_shard
                slot = home if len(mine) == 1 else 2 * chip + n
                if slot == home:
                    keep[h, slot, s] = u % per_shard
                else:
                    give[h, home, s] = u % per_shard
                place[h, s, owners[u][1]] = slot
                held[h, slot, s] = owners[u][1]
                slot_of[u] = slot
    lends = [[[] for _ in range(segments)] for _ in range(local_heads)]
    back = np.zeros((segments, per_shard, 3), np.int32)
    for u, (head, _) in enumerate(owners):
        home = u // per_shard
        h, s = divmod(head, group)
        back[home, u % per_shard] = (h, s, -1)
        if slot_of[u] != home:
            assert slot_of[u] == home ^ 1
            back[home, u % per_shard, 2] = len(lends[h][home ^ 1])
            lends[h][home ^ 1].append(s)
    most = max(1, max(len(t) for row in lends for t in row))
    lend = np.asarray(
        [[(t + [0] * most)[:most] for t in row] for row in lends], np.int32
    )
    return keep, give, place, held, back, lend


def tie(*values):
    return lax.optimization_barrier(values)


def mm(left, right, dims):
    return lax.dot_general(left, right, (dims, ((), ())), preferred_element_type=F32)


NN = ((1,), (0,))
NT = ((1,), (1,))
TN = ((0,), (0,))


def turn(v, cosine, sine):
    half = v.shape[-1] // 2
    first, second = v[:, :half], v[:, half:]
    return jnp.concatenate(
        [first * cosine - second * sine, second * cosine + first * sine], axis=-1
    )


def scaled(v, decay):
    return (v.astype(F32) * decay).astype(BF16)


def project_kernel(blk, roles, carried, params, x, w, cosine, sine, k_decay, *refs):
    if carried:
        v_a, *refs = refs
    q, k, v, total, gates, *rest = refs
    y = rest[-1]
    rows = y.shape[0]
    y[...] = mm(x[...], w[...], NT)

    def put(role, part, gate_at):
        value = y[:, part * DK : (part + 1) * DK]
        if role == "q":
            q[...] = turn(value, cosine[...], sine[...]).astype(BF16)
        elif role == "k":
            k[...] = turn(value, cosine[...], sine[...]).astype(BF16)
        elif role == "va":
            v[:, :DK] = value.astype(BF16)
        elif role == "vb":
            v[:, DK:] = value.astype(BF16)
        elif role == "xv":
            rest[0][...] = value.astype(BF16)
        else:
            gates[:, gate_at * DK : (gate_at + 1) * DK] = value

    for step in range(len(roles) // 2):

        @pl.when(pl.program_id(0) == step)
        def _(step=step):
            for part in range(2):
                at = 2 * step + part
                put(roles[at], part, roles[:at].count("g"))
            if step == 1:
                if carried:
                    v[:, :DK] = v_a[...]
                state = jnp.zeros(total.shape, F32)
                for r in range(0, rows, blk):
                    kd = scaled(k[r : r + blk, :], k_decay[...])
                    state = params[0] * state + mm(kd, v[r : r + blk, :], TN)
                total[...] = state.astype(BF16)


def select(params, low, high):
    return jnp.where(params[1] > 0.5, low[...].astype(F32), high[...].astype(F32))


def retain_kernel(
    params, q, k, v, low_a, high_a, low_b, high_b, mask, q_decay, k_decay, start,
    hidden, mixed, kept, state,
):
    @pl.when(pl.program_id(0) == 0)
    def _():
        state[...] = start[...].astype(F32)

    weights = (mm(q[...], k[...], NT) * mask[...]).astype(BF16)
    o = mm(weights, v[...], NN)
    o += mm(scaled(q[...], q_decay[...]), state[...].astype(BF16), NN)
    state[...] = params[0] * state[...] + mm(scaled(k[...], k_decay[...]), v[...], TN)
    kept[...] = o
    o = o - jnp.mean(o, axis=-1, keepdims=True)
    o = o * lax.rsqrt(jnp.mean(o * o, axis=-1, keepdims=True) + EPS_GROUP)
    low = o.astype(BF16)
    mixed[...] = low
    for n, (one, two) in enumerate(((low_a, high_a), (low_b, high_b))):
        columns = slice(n * DK, (n + 1) * DK)
        g = select(params, one, two)
        hidden[:, columns] = (g * jax.nn.sigmoid(g) * low[:, columns].astype(F32)).astype(BF16)


def gate_back_kernel(
    params, d_hidden, low_a, high_a, low_b, high_b, mixed, kept, q, q_decay,
    d_gate, d_out, total, state,
):
    @pl.when(pl.program_id(0) == 0)
    def _():
        state[...] = jnp.zeros(state.shape, F32)

    g = jnp.concatenate([select(params, low_a, high_a), select(params, low_b, high_b)], axis=1)
    dh = d_hidden[...]
    sig = jax.nn.sigmoid(g)
    d_gate[...] = (dh * mixed[...].astype(F32) * (sig * (1.0 + g * (1.0 - sig)))).astype(BF16)
    dy = (dh * (g * sig)).astype(BF16).astype(F32)
    o = kept[...]
    o = o - jnp.mean(o, axis=-1, keepdims=True)
    inverse = lax.rsqrt(jnp.mean(o * o, axis=-1, keepdims=True) + EPS_GROUP)
    o = o * inverse
    do = inverse * (
        dy
        - jnp.mean(dy, axis=-1, keepdims=True)
        - o * jnp.mean(dy * o, axis=-1, keepdims=True)
    )
    do = do.astype(BF16)
    d_out[...] = do
    state[...] = params[0] * state[...] + mm(scaled(q[...], q_decay[...]), do, TN)
    total[...] = state[...].astype(BF16)


def inner_back_kernel(
    params, q, k, v, d_out, mask, q_decay, k_decay, start, cosine, sine, d_q, d_k, d_v, state
):
    @pl.when(pl.program_id(0) == 0)
    def _():
        state[...] = start[...].astype(F32)

    do = d_out[...]
    weights = (mm(q[...], k[...], NT) * mask[...]).astype(BF16)
    d_v[...] = mm(weights, do, TN)
    d_scores = mm(do, v[...], NT).astype(BF16).astype(F32)
    d_scores = (d_scores * mask[...]).astype(BF16)
    d_k[...] = mm(d_scores, q[...], TN)
    far = mm(do, state[...].astype(BF16), NT).astype(BF16).astype(F32)
    dq = mm(d_scores, k[...], NN) + far * q_decay[...]
    dq = dq.astype(BF16).astype(F32)
    d_q[...] = turn(dq, cosine[...], -sine[...]).astype(BF16)
    state[...] = params[0] * state[...] + mm(scaled(k[...], k_decay[...]), v[...], TN)


def outer_back_kernel(
    roles, params, q, k, v, d_out, d_q, d_k, d_v, q_decay, k_decay, start, cosine, sine, *refs
):
    refs = list(refs)
    state = refs.pop()
    v_a = None if "va" in roles else refs.pop()
    by_unit = refs.pop()

    @pl.when(pl.program_id(0) == 0)
    def _():
        state[...] = start[...].astype(F32)

    low = state[...].astype(BF16)
    far = mm(v[...], low, NT).astype(BF16).astype(F32)
    dk = (d_k[...] + far * k_decay[...]).astype(BF16).astype(F32)
    dk = turn(dk, cosine[...], -sine[...]).astype(BF16)
    dv = (d_v[...] + mm(scaled(k[...], k_decay[...]), low, NN)).astype(BF16)
    for n, role in enumerate(roles):
        if role == "q":
            value = d_q[...]
        elif role == "k":
            value = dk
        elif role == "va":
            value = dv[:, :DK]
        elif role == "vb":
            value = dv[:, DK:]
        elif role == "xv":
            value = refs.pop(0)[...]
        else:
            value = select(params, refs.pop(0), refs.pop(0)).astype(BF16)
        by_unit[:, n * DK : (n + 1) * DK] = value
    if v_a is not None:
        v_a[...] = dv[:, :DK]
    state[...] = params[0] * state[...] + mm(scaled(q[...], q_decay[...]), d_out[...], TN)


def head_call(kernel, grid, operands, outputs, scratch, flops):
    arrays = [t[0] for t in operands]
    size = sum(t.size * t.dtype.itemsize for t in arrays + [t[0] for t in outputs])
    return pl.pallas_call(
        kernel,
        grid=(grid,),
        in_specs=[
            pl.BlockSpec(memory_space=pltpu.SMEM) if block is None else pl.BlockSpec(block, where)
            for _, block, where in operands
        ],
        out_specs=[pl.BlockSpec(block, where) for _, block, where in outputs],
        scratch_shapes=scratch,
        out_shape=[t[0] for t in outputs],
        compiler_params=pltpu.CompilerParams(vmem_limit_bytes=56 * 2**20),
        cost_estimate=pl.CostEstimate(flops=flops, bytes_accessed=size, transcendentals=0),
    )(*arrays)


def place_kernel(parts, target, source, *refs):
    out = refs[-1]
    code = source[pl.program_id(1)]
    for i, part in enumerate(parts):

        @pl.when(code == i)
        def _(part=part):
            row = 0
            for n in part:
                piece = refs[n]
                out[row : row + piece.shape[0], :] = piece[...].astype(F32)
                row += piece.shape[0]


def place_blocks(parts, target, source, shape, block, where, outer=1):
    flat, index = [], []
    for part in parts:
        for piece in part:
            if not any(piece is t for t in flat):
                flat.append(piece)
        index.append([next(n for n, t in enumerate(flat) if t is piece) for piece in part])
    return pl.pallas_call(
        functools.partial(place_kernel, index),
        grid_spec=pltpu.PrefetchScalarGridSpec(
            num_scalar_prefetch=2,
            grid=(outer, target.shape[0]),
            in_specs=[
                pl.BlockSpec((t.shape[0], t.shape[1] // outer), lambda o, n, target, source: (0, o))
                for t in flat
            ],
            out_specs=pl.BlockSpec(block, lambda o, n, target, source: where(o, target[n])),
        ),
        out_shape=jax.ShapeDtypeStruct(shape, F32),
        compiler_params=pltpu.CompilerParams(vmem_limit_bytes=48 * 2**20),
    )(target.astype(jnp.int32), source.astype(jnp.int32), *flat)


def local(
    tokens,
    cotangent,
    gain_attn,
    gain_ffn,
    mixer_in,
    mixer_out,
    ffn_in,
    ffn_out,
    segment_order,
    decay_index,
):
    rows, width = tokens.shape
    group = lax.axis_size("seq")
    segments = lax.axis_size("shard")
    heads = decay_index.shape[0]
    local_heads = heads // group
    seg_len = rows * group
    blk = min(512, seg_len)
    blocks = seg_len // blk
    vcols = local_heads * DV
    s = lax.axis_index("seq")
    j = lax.axis_index("shard")

    def swap(v, d):
        return lax.ppermute(v, "seq", [(i, i ^ d) for i in range(group)])

    def cross(v, d):
        return lax.ppermute(v, "shard", [(i, i ^ d) for i in range(segments)])

    def pick(v, i):
        return lax.dynamic_index_in_dim(v, i, 0, keepdims=False)

    def spread(v):
        if group == 4:
            h = v.shape[0] // 2
            r1 = swap(v, 1)
            r2 = swap(v, 2)
            return [(v,), (r1,), (r2,), (swap(r1[:h], 2), swap(r2[h:], 1))]
        return [(v,)] + [(swap(v, d),) for d in range(1, group)]

    def ordered(parts):
        r = parts[0][0].shape[0]
        out = jnp.zeros((group * r,) + parts[0][0].shape[1:], parts[0][0].dtype)
        for d, part in enumerate(parts):
            row = (s ^ d) * r
            for piece in part:
                out = lax.dynamic_update_slice_in_dim(out, piece, row, 0)
                row = row + piece.shape[0]
        return out

    def gather_near(v):
        return jnp.concatenate([piece for part in spread(v) for piece in part], axis=0)

    def gather_seq(v):
        return ordered(spread(v))

    def scatter_sum(blk_of, beside1=(), beside2=()):
        if group == 4:
            b0, b1, b2, b3 = (blk_of(d) for d in range(4))
            h = b0.shape[0] // 2
            b0 = b0.astype(F32)
            ra = swap(jnp.concatenate([b1[:h], b3[:h]], axis=0), 1)
            rb = swap(jnp.concatenate([b2[h:], b3[h:]], axis=0), 2)
            ra, rb, *beside1 = tie(ra, rb, *beside1)
            ra, rb = ra.astype(F32), rb.astype(F32)
            qa = swap((b2[:h].astype(F32) + ra[h:]).astype(BF16), 2)
            qb = swap((b1[h:].astype(F32) + rb[h:]).astype(BF16), 1)
            qa, qb, *beside2 = tie(qa, qb, *beside2)
            total = jnp.concatenate(
                [b0[:h] + ra[:h] + qa.astype(F32), b0[h:] + rb[:h] + qb.astype(F32)], axis=0
            )
            return (total, *beside1, *beside2)
        total = blk_of(0).astype(F32)
        for d in range(1, group):
            total = total + swap(blk_of(d), d).astype(F32)
        return (total, *beside1, *beside2)

    def scatter_near(v, beside1=(), beside2=()):
        return scatter_sum(lambda d: v[d * rows : (d + 1) * rows], beside1, beside2)

    def scatter_seq(v):
        return scatter_sum(lambda d: lax.dynamic_slice_in_dim(v, (s ^ d) * rows, rows, 0))[0]

    def gather_shard(v):
        return lax.all_gather(v, "shard", axis=0, tiled=True)

    def reduce_shard(v):
        return lax.psum_scatter(v, "shard", scatter_dimension=0, tiled=True)

    def sum_all(v):
        step = 1
        while step < group:
            v = v + swap(v, step)
            step *= 2
        step = 1
        while step < segments:
            v = v + cross(v, step)
            step *= 2
        return v

    balanced = group == 4 and local_heads == 2 and segments == 8
    units = mixer_in.reshape(-1, DK, width)
    if balanced:
        keep, give, back, lend = (jnp.asarray(t) for t in balanced_tables())
        core = j % 2
    else:
        keep, give, place, held, back, lend = (
            jnp.asarray(t) for t in unit_tables(group, local_heads, segments)
        )

    def offered(h):
        kept, given = keep[h, j, s], give[h, j, s]
        if balanced and h == 1:
            cut = mixer_in.reshape(-1, DK // 2, width)
            own = pick(cut, 2 * jnp.maximum(kept, 0) + core)
            given = cross(pick(cut, 2 * given + 1 - core), 1)
        else:
            own = pick(units, jnp.maximum(kept, 0))
            given = cross(pick(units, given), 1)
        return jnp.where(kept >= 0, own, given)

    sub = ffn_in.shape[0] // group
    ffn_out_cut = ffn_out.reshape(ffn_out.shape[0], segments // 2, group, sub)

    my_rank = jnp.sum(jnp.where(jnp.arange(segments) == j, segment_order, 0))
    all_logs = jnp.log1p(-jnp.exp2(-(5.0 + decay_index.astype(F32))))
    logs = lax.dynamic_index_in_dim(all_logs.reshape(local_heads, group), s, 1, keepdims=False)
    half = DK // 2
    inv_freq = jnp.exp(-jnp.log(10000.0) * jnp.arange(half).astype(F32) / half)
    positions = my_rank * seg_len + jnp.arange(seg_len, dtype=jnp.int32)
    angles = positions.astype(F32)[:, None] * inv_freq[None, :]
    cosine = jnp.cos(angles)
    sine = jnp.sin(angles)
    steps = jnp.arange(blk).astype(F32)
    gap = steps[:, None] - steps[None, :]
    masks = jnp.where(
        gap[None] >= 0.0, jnp.exp(jnp.maximum(gap, 0.0)[None] * logs[:, None, None]), 0.0
    )
    q_decays = jnp.exp((steps + 1.0)[None, :] * logs[:, None])[..., None]
    k_decays = jnp.exp((blk - 1.0 - steps)[None, :] * logs[:, None])[..., None]
    block_decays = jnp.exp(blk * logs)

    xf = tokens.astype(F32)
    normed = gather_seq(rms_scale(xf, gain_attn).astype(BF16))
    d_ffn = gather_near(cotangent)
    slots = [gather_shard(offered(0))]
    slots[0], normed, d_ffn, cosine, sine, masks, q_decays, k_decays = tie(
        slots[0], normed, d_ffn, cosine, sine, masks, q_decays, k_decays
    )
    for h in range(1, local_heads):
        slots.append(gather_shard(offered(h)))
    mixer_out_cut = jnp.concatenate(
        [
            lax.dynamic_slice_in_dim(mixer_out, (h * group + s) * DV, DV, 1)
            for h in range(local_heads)
        ],
        axis=1,
    )
    mixer_out_cut, slots[0] = tie(mixer_out_cut, slots[0])
    w_out = gather_shard(mixer_out_cut)
    later = [
        lax.dynamic_slice_in_dim(ffn_in, s * sub, sub, 0),
        lax.dynamic_index_in_dim(ffn_out_cut, s, 2, keepdims=False).reshape(ffn_out.shape[0], -1),
    ]
    inner_cols = later[1].shape[1]

    ranks = segment_order
    piece = DK // segments

    def exchange_states(h, total, reverse):
        cut = total.reshape(segments, piece, DV)
        got = lax.all_to_all(cut, "shard", split_axis=0, concat_axis=0, tiled=True)
        if not reverse and h + 1 < local_heads:
            slots[h + 1], got, *later[:] = tie(slots[h + 1], got, *later)
        got = got.astype(F32)
        apart = ranks[:, None] - ranks[None, :] - 1
        if reverse:
            apart = -apart - 2
        distance = apart.astype(F32)
        coef = jnp.where(
            distance >= 0.0, jnp.exp(jnp.maximum(distance, 0.0) * seg_len * logs[h]), 0.0
        )
        joined = jnp.sum(coef[..., None, None] * got[None], axis=1).astype(BF16)
        back_cut = lax.all_to_all(joined, "shard", split_axis=0, concat_axis=0, tiled=True)
        if reverse and h == 0:
            back_cut, scattered["ffn_in"] = tie(back_cut, scattered["ffn_in"])
        return back_cut.reshape(DK, DV)

    def whole(n):
        return (0, 0)

    def ahead(n):
        return (n, 0)

    def behind(n):
        return (blocks - 1 - n, 0)

    def shaped(columns, kind, r=seg_len):
        return jax.ShapeDtypeStruct((r, columns), kind)

    state_scratch = [pltpu.VMEM((DK, DV), F32)]
    half_block = (blk, half)
    unit_block, v_block = (blk, DK), (blk, DV)
    ret_flops = 2 * seg_len * (DK + DV) * (blk + DK)
    low = s < group // 2
    if balanced:
        roles = [["q", "k", "va", "vb", "xv", "g", "g", "g"], ["q", "k", "vb", "g"]]
    else:
        roles = [["q", "k", "va", "vb", "g", "g"]] * local_heads
    params = [
        (jnp.stack([block_decays[h], low.astype(F32)]), None, None) for h in range(local_heads)
    ]
    heads_kept = []
    extra_v = None
    for h in range(local_heads):
        if balanced:
            weights = slots[h]
        else:
            cut = slots[h].reshape(-1, DK, width)
            weights = jnp.concatenate([pick(cut, place[h, s, c]) for c in range(6)], axis=0)
        carried = "va" not in roles[h]
        gate_count = roles[h].count("g")
        q, k, v, total, gates, *extra = head_call(
            functools.partial(project_kernel, blk, roles[h], carried),
            len(roles[h]) // 2,
            [
                params[h],
                (normed, (seg_len, width), whole),
                (weights, (2 * DK, width), ahead),
                (cosine, (seg_len, half), whole),
                (sine, (seg_len, half), whole),
                (k_decays[h], (blk, 1), whole),
            ]
            + ([(extra_v, (seg_len, DK), whole)] if carried else []),
            [
                (shaped(DK, BF16), (seg_len, DK), whole),
                (shaped(DK, BF16), (seg_len, DK), whole),
                (shaped(DV, BF16), (seg_len, DV), whole),
                (shaped(DV, BF16, DK), (DK, DV), whole),
                (shaped(gate_count * DK, F32), (seg_len, gate_count * DK), whole),
            ]
            + ([(shaped(DK, BF16), (seg_len, DK), whole)] if "xv" in roles[h] else []),
            [pltpu.VMEM((seg_len, 2 * DK), F32)],
            2 * seg_len * width * len(roles[h]) * DK,
        )
        extra_v = extra[0] if extra else None
        state_in = exchange_states(h, total, False)
        heads_kept.append((weights, q, k, v, gates, state_in))

    def columns(v, c, order):
        return (v, unit_block, lambda n, c=c: (order(n)[0], c))

    if balanced:
        gates0, gates1 = heads_kept[0][4], heads_kept[1][4]
        swapped = swap(jnp.where(low, gates1, gates0[:, :DK]).astype(BF16), 2)

        def gate_operands(h, order):
            if h == 0:
                four = (gates0, 0), (gates0, 1), (swapped, 0), (gates0, 2)
            else:
                four = (gates0, 1), (gates1, 0), (gates0, 2), (swapped, 0)
            return [columns(v, c, order) for v, c in four]

    else:

        def gate_operands(h, order):
            return [columns(heads_kept[h][4], c, order) for c in (0, 0, 1, 1)]

    kept = []
    for h in range(local_heads):
        weights, q, k, v, gates, state_in = heads_kept[h]
        hidden, mixed, retained = head_call(
            retain_kernel,
            blocks,
            [
                params[h],
                (q, unit_block, ahead),
                (k, unit_block, ahead),
                (v, v_block, ahead),
                *gate_operands(h, ahead),
                (masks[h], (blk, blk), whole),
                (q_decays[h], (blk, 1), whole),
                (k_decays[h], (blk, 1), whole),
                (state_in, (DK, DV), whole),
            ],
            [
                (shaped(DV, BF16), v_block, ahead),
                (shaped(DV, BF16), v_block, ahead),
                (shaped(DV, F32), v_block, ahead),
            ],
            state_scratch,
            ret_flops,
        )
        kept.append((retained, mixed, hidden))
    hidden = jnp.concatenate([t[-1] for t in kept], axis=1)
    w_ffn_in, w_ffn_out = (gather_shard(t) for t in later)

    resid = xf + scatter_seq(dot_nt(hidden, w_out, BF16))
    normed2 = gather_near(rms_scale(resid, gain_ffn).astype(BF16))
    proj2 = dot_nt(normed2, w_ffn_in)
    first, second = proj2[:, :inner_cols], proj2[:, inner_cols:]
    inner2 = gated_gelu(first, second).astype(BF16)

    g_ffn_out, d_ffn = tie(dot_tn(d_ffn, inner2, BF16), d_ffn)
    scattered = {"ffn_out": reduce_shard(g_ffn_out)}
    d_inner2 = dot_nn(d_ffn, w_ffn_out)
    ignored2, gelu_back = jax.vjp(gated_gelu, first, second)
    d_first, d_second = gelu_back(d_inner2)
    dproj2 = jnp.concatenate([d_first, d_second], axis=1).astype(BF16)
    d_normed2, g_ffn_in = scatter_near(
        dot_nn(dproj2, w_ffn_in, BF16), (dot_tn(dproj2, normed2, BF16),)
    )
    scattered["ffn_in"] = reduce_shard(g_ffn_in)
    ignored3, norm2_back = jax.vjp(rms_scale, resid, gain_ffn)
    d_resid_part, d_gain_ffn = norm2_back(d_normed2)
    d_resid = cotangent.astype(F32) + d_resid_part
    d_attn = gather_seq(d_resid.astype(BF16))
    inner2, d_attn, scattered["ffn_out"] = tie(inner2, d_attn, scattered["ffn_out"])
    parts_ffn_out = spread(scattered["ffn_out"])
    output = (resid + scatter_near(dot_nt(inner2, w_ffn_out, BF16))[0]).astype(BF16)
    d_hidden = dot_nn(d_attn, w_out)
    scattered["mixer_out"] = reduce_shard(dot_tn(d_attn, hidden, BF16))

    def tie_parts(v, parts):
        flat = tie(v, *(piece for part in parts for piece in part))
        rest = list(flat[1:])
        return flat[0], [tuple(rest.pop(0) for _ in part) for part in parts]

    turns = [(cosine, half_block), (sine, half_block)]
    firsts = []
    for h in range(local_heads):
        weights, q, k, v, gates, state_in = heads_kept[h]
        retained, mixed, ignored4 = kept[h]
        firsts.append(
            head_call(
                gate_back_kernel,
                blocks,
                [
                    params[h],
                    (d_hidden, v_block, lambda n, h=h: (blocks - 1 - n, h)),
                    *gate_operands(h, behind),
                    (mixed, v_block, behind),
                    (retained, v_block, behind),
                    (q, unit_block, behind),
                    (q_decays[h], (blk, 1), whole),
                ],
                [
                    (shaped(DV, BF16), v_block, behind),
                    (shaped(DV, BF16), v_block, behind),
                    (shaped(DV, BF16, DK), (DK, DV), whole),
                ],
                state_scratch,
                2 * seg_len * DK * DV,
            )
        )
    d_gates = [t[0] for t in firsts]
    if balanced:
        d_swapped = swap(jnp.where(low, d_gates[0][:, DK:], d_gates[1][:, DK:]), 2)
        d_gate_pairs = [
            [
                ((d_gates[0], 0), (d_swapped, 0)),
                ((d_gates[1], 0), (d_gates[0], 0)),
                ((d_gates[1], 1), (d_gates[0], 1)),
            ],
            [((d_swapped, 0), (d_gates[1], 0))],
        ]
    else:
        d_gate_pairs = [[((t, 0), (t, 0)), ((t, 1), (t, 1))] for t in d_gates]
    grads_out = {h: exchange_states(h, firsts[h][2], True) for h in reversed(range(local_heads))}
    by_units = [None] * local_heads
    extra_v = None
    for h in reversed(range(local_heads)):
        weights, q, k, v, gates, state_in = heads_kept[h]
        d_out = firsts[h][1]
        d_q, d_k, d_v = head_call(
            inner_back_kernel,
            blocks,
            [
                params[h],
                (q, unit_block, ahead),
                (k, unit_block, ahead),
                (v, v_block, ahead),
                (d_out, v_block, ahead),
                (masks[h], (blk, blk), whole),
                (q_decays[h], (blk, 1), whole),
                (k_decays[h], (blk, 1), whole),
                (state_in, (DK, DV), whole),
                *((*t, ahead) for t in turns),
            ],
            [
                (shaped(DK, BF16), unit_block, ahead),
                (shaped(DK, F32), unit_block, ahead),
                (shaped(DV, F32), v_block, ahead),
            ],
            state_scratch,
            2 * ret_flops,
        )
        count = len(roles[h])
        lone = "va" not in roles[h]
        by_units[h], *extra = head_call(
            functools.partial(outer_back_kernel, roles[h]),
            blocks,
            [
                params[h],
                (q, unit_block, behind),
                (k, unit_block, behind),
                (v, v_block, behind),
                (d_out, v_block, behind),
                (d_q, unit_block, behind),
                (d_k, unit_block, behind),
                (d_v, v_block, behind),
                (q_decays[h], (blk, 1), whole),
                (k_decays[h], (blk, 1), whole),
                (grads_out[h], (DK, DV), whole),
                *((*t, behind) for t in turns),
            ]
            + ([(extra_v, unit_block, behind)] if "xv" in roles[h] else [])
            + [columns(v, c, behind) for pair in d_gate_pairs[h] for v, c in pair],
            [(shaped(count * DK, BF16), (blk, count * DK), behind)]
            + ([(shaped(DK, BF16), unit_block, behind)] if lone else []),
            state_scratch,
            6 * seg_len * DK * DV,
        )
        extra_v = extra[0] if extra else None

    by_units[0], output = tie(by_units[0], output)
    by_units[0], parts_ffn_out = tie_parts(by_units[0], parts_ffn_out)
    parts_ffn_in = spread(scattered["ffn_in"])
    by_units[-1], parts_ffn_in = tie_parts(by_units[-1], parts_ffn_in)
    parts_mixer_out = spread(scattered["mixer_out"])
    g_slots = []
    d_normed = None
    for h in range(local_heads):
        g_unit = dot_tn(by_units[h], normed, BF16)
        if not balanced:
            cut = g_unit.reshape(-1, DK, width)
            g_unit = jnp.concatenate(
                [pick(cut, jnp.maximum(held[h, c, s], 0)) for c in range(segments)], axis=0
            )
        g_slots.append(reduce_shard(g_unit))
        part = dot_nn(by_units[h], heads_kept[h][0])
        d_normed = part if d_normed is None else d_normed + part
    d_normed, parts_mixer_out = tie_parts(d_normed.astype(BF16), parts_mixer_out)
    d_normed = scatter_seq(d_normed)

    ignored8, norm1_back = jax.vjp(rms_scale, xf, gain_attn)
    d_x_part, d_gain_attn = norm1_back(d_normed)
    input_grad = (d_resid + d_x_part).astype(BF16)
    gain_ffn_grad = sum_all(d_gain_ffn)
    gain_attn_grad = sum_all(d_gain_attn)
    near = jnp.arange(group)
    g_ffn_in = place_blocks(
        parts_ffn_in, s ^ near, near, ffn_in.shape, (sub, width), lambda o, n: (n, 0)
    )
    g_mixer_out = place_blocks(
        parts_mixer_out,
        s ^ near,
        near,
        mixer_out.shape,
        (mixer_out.shape[0], DV),
        lambda o, n: (0, o * group + n),
        outer=local_heads,
    )
    if sub % 128 == 0:
        g_ffn_out = place_blocks(
            parts_ffn_out,
            s ^ near,
            near,
            ffn_out.shape,
            (ffn_out.shape[0], sub),
            lambda o, n: (0, o * group + n),
            outer=segments // 2,
        )
    else:
        g_ffn_out = jnp.transpose(
            ordered(parts_ffn_out).reshape(group, ffn_out.shape[0], segments // 2, sub),
            (1, 2, 0, 3),
        ).reshape(ffn_out.shape).astype(F32)

    parts = []
    for h in range(local_heads):
        last = h == local_heads - 1
        if last:
            g_slots[h], output, input_grad, gain_attn_grad, gain_ffn_grad = tie(
                g_slots[h], output, input_grad, gain_attn_grad, gain_ffn_grad
            )
            g_slots[h], g_ffn_in, g_mixer_out, g_ffn_out = tie(
                g_slots[h], g_ffn_in, g_mixer_out, g_ffn_out
            )
            g_slots[h], parts = tie_parts(g_slots[h], parts)
        here = spread(g_slots[h])
        if balanced and last:
            there = [tuple(cross(piece, 1) for piece in part) for part in here]
            parts += [a + b for a, b in zip(here, there)] + [b + a for a, b in zip(here, there)]
        else:
            lend_here = lend[j] if balanced else lend[h, j]
            stack = jnp.stack([jnp.concatenate(part, axis=0) for part in here])
            lent = cross(
                jnp.stack([pick(stack, s ^ lend_here[n]) for n in range(lend_here.shape[0])]), 1
            )
            parts += here + [(lent[n],) for n in range(lend_here.shape[0])]
    found = back[j]
    if balanced:
        spare = lend.shape[-1]
        source = jnp.where(
            found[:, 0] == 0,
            s ^ found[:, 1],
            jnp.where(
                found[:, 0] == 1,
                group + found[:, 1],
                group + spare + core * group + (s ^ found[:, 1]),
            ),
        )
    else:
        source = found[:, 0] * (group + lend.shape[-1]) + jnp.where(
            found[:, 2] < 0, s ^ found[:, 1], group + found[:, 2]
        )
    g_mixer_in = place_blocks(
        parts,
        jnp.arange(source.shape[0]),
        source,
        mixer_in.shape,
        (DK, width),
        lambda o, n: (n, 0),
    )
    return (
        output,
        input_grad,
        gain_attn_grad,
        gain_ffn_grad,
        g_mixer_in,
        g_mixer_out,
        g_ffn_in,
        g_ffn_out,
    )


def solution(mesh):
    return jax.shard_map(
        local,
        mesh=mesh,
        in_specs=(
            P(("shard", "seq"), None),
            P(("shard", "seq"), None),
            P(),
            P(),
            P("shard", None),
            P("shard", None),
            P("shard", None),
            P("shard", None),
            P(),
            P(),
        ),
        out_specs=(
            P(("shard", "seq"), None),
            P(("shard", "seq"), None),
            P(),
            P(),
            P("shard", None),
            P("shard", None),
            P("shard", None),
            P("shard", None),
        ),
        check_vma=False,
    )
```

```python
import functools

import jax
import jax.numpy as jnp
import numpy as np
from jax import lax
from jax.experimental import pallas as pl
from jax.experimental.pallas import tpu as pltpu
from jax.sharding import PartitionSpec as P

DK = 256
DV = 512
FF = 4096
QK = 2048
V = 4096


EPS_NORM = 1e-06
EPS_GROUP = 1e-05

F32 = jnp.float32
BF16 = jnp.bfloat16


def dot_nt(left, right, kind=F32):
    return lax.dot_general(
        left, right, (((1,), (1,)), ((), ())), preferred_element_type=F32
    ).astype(kind)


def dot_nn(left, right, kind=F32):
    return lax.dot_general(
        left, right, (((1,), (0,)), ((), ())), preferred_element_type=F32
    ).astype(kind)


def dot_tn(left, right, kind=F32):
    return lax.dot_general(
        left, right, (((0,), (0,)), ((), ())), preferred_element_type=F32
    ).astype(kind)


def rms_scale(v, gain):
    return v * lax.rsqrt(jnp.mean(v * v, axis=-1, keepdims=True) + EPS_NORM) * gain


def gated_gelu(first, second):
    return jax.nn.gelu(first) * second


def unit_owners(heads):
    owners = [(n, 0) for n in range(heads)] + [(n, 1) for n in range(heads)]
    for base in (2, 4):
        owners += [(n, base + half) for n in range(heads) for half in range(2)]
    return owners


def balanced_tables():
    group, segments, per_shard = 4, 8, 6
    number = {owner: u for u, owner in enumerate(unit_owners(8))}
    keep = np.full((2, segments, group), -1, np.int32)
    give = np.zeros((2, segments, group), np.int32)
    back = np.zeros((segments, per_shard, 2), np.int32)
    lend = [[] for _ in range(segments)]
    seen = set()
    for s in range(group):
        a, b = s, s + 4
        if s < 2:
            gates = [(a, 4), (b, 4), (b, 5)], (b + 2, 5)
        else:
            gates = [(a - 2, 5), (a, 4), (a, 5)], (b, 4)
        first = [(a, 0), (a, 1), (a, 2), (a, 3), (b, 2)] + gates[0]
        second = [(b, 0), (b, 1), (b, 3), gates[1]]
        for slot, owner in enumerate(first):
            home, index = divmod(number[owner], per_shard)
            seen.add(number[owner])
            assert home // 2 == slot // 2
            if home == slot:
                keep[0, slot, s] = index
                back[home, index] = (0, s)
            else:
                give[0, home, s] = index
                back[home, index] = (1, len(lend[slot]))
                lend[slot].append(s)
        for chip, owner in enumerate(second):
            home, index = divmod(number[owner], per_shard)
            seen.add(number[owner])
            assert home // 2 == chip
            keep[1, home, s] = index
            give[1, home, s] = index
            back[home, index] = (2, s)
    assert len(seen) == segments * per_shard
    most = max(len(t) for t in lend)
    return keep, give, back, np.asarray([(t + [0] * most)[:most] for t in lend], np.int32)


def unit_tables(group, local_heads, segments):
    heads = group * local_heads
    owners = unit_owners(heads)
    per_shard = len(owners) // segments
    keep = np.full((local_heads, segments, group), -1, np.int32)
    give = np.zeros((local_heads, segments, group), np.int32)
    place = np.zeros((local_heads, group, 6), np.int32)
    held = np.full((local_heads, segments, group), -1, np.int32)
    slot_of = {}
    for chip in range(segments // 2):
        for head in range(heads):
            h, s = divmod(head, group)
            span = range(2 * per_shard * chip, 2 * per_shard * (chip + 1))
            mine = [u for u in span if owners[u][0] == head]
            assert len(mine) <= 2
            for n, u in enumerate(mine):
                home = u // per_shard
                slot = home if len(mine) == 1 else 2 * chip + n
                if slot == home:
                    keep[h, slot, s] = u % per_shard
                else:
                    give[h, home, s] = u % per_shard
                place[h, s, owners[u][1]] = slot
                held[h, slot, s] = owners[u][1]
                slot_of[u] = slot
    lends = [[[] for _ in range(segments)] for _ in range(local_heads)]
    back = np.zeros((segments, per_shard, 3), np.int32)
    for u, (head, _) in enumerate(owners):
        home = u // per_shard
        h, s = divmod(head, group)
        back[home, u % per_shard] = (h, s, -1)
        if slot_of[u] != home:
            assert slot_of[u] == home ^ 1
            back[home, u % per_shard, 2] = len(lends[h][home ^ 1])
            lends[h][home ^ 1].append(s)
    most = max(1, max(len(t) for row in lends for t in row))
    lend = np.asarray(
        [[(t + [0] * most)[:most] for t in row] for row in lends], np.int32
    )
    return keep, give, place, held, back, lend


def tie(*values):
    return lax.optimization_barrier(values)


def mm(left, right, dims):
    return lax.dot_general(left, right, (dims, ((), ())), preferred_element_type=F32)


NN = ((1,), (0,))
NT = ((1,), (1,))
TN = ((0,), (0,))


def turn(v, cosine, sine):
    half = v.shape[-1] // 2
    first, second = v[:, :half], v[:, half:]
    return jnp.concatenate(
        [first * cosine - second * sine, second * cosine + first * sine], axis=-1
    )


def scaled(v, decay):
    return (v.astype(F32) * decay).astype(BF16)


def project_kernel(blk, roles, carried, params, x, w, cosine, sine, k_decay, *refs):
    if carried:
        v_a, *refs = refs
    q, k, v, total, gates, *rest = refs
    y = rest[-1]
    rows = y.shape[0]
    y[...] = mm(x[...], w[...], NT)

    def put(role, part, gate_at):
        value = y[:, part * DK : (part + 1) * DK]
        if role == "q":
            q[...] = turn(value, cosine[...], sine[...]).astype(BF16)
        elif role == "k":
            k[...] = turn(value, cosine[...], sine[...]).astype(BF16)
        elif role == "va":
            v[:, :DK] = value.astype(BF16)
        elif role == "vb":
            v[:, DK:] = value.astype(BF16)
        elif role == "xv":
            rest[0][...] = value.astype(BF16)
        else:
            gates[:, gate_at * DK : (gate_at + 1) * DK] = value

    for step in range(len(roles) // 2):

        @pl.when(pl.program_id(0) == step)
        def _(step=step):
            for part in range(2):
                at = 2 * step + part
                put(roles[at], part, roles[:at].count("g"))
            if step == 1:
                if carried:
                    v[:, :DK] = v_a[...]
                state = jnp.zeros(total.shape, F32)
                for r in range(0, rows, blk):
                    kd = scaled(k[r : r + blk, :], k_decay[...])
                    state = params[0] * state + mm(kd, v[r : r + blk, :], TN)
                total[...] = state.astype(BF16)


def select(params, low, high):
    return jnp.where(params[1] > 0.5, low[...].astype(F32), high[...].astype(F32))


def retain_kernel(
    params, q, k, v, low_a, high_a, low_b, high_b, mask, q_decay, k_decay, start,
    hidden, mixed, kept, state,
):
    @pl.when(pl.program_id(0) == 0)
    def _():
        state[...] = start[...].astype(F32)

    weights = (mm(q[...], k[...], NT) * mask[...]).astype(BF16)
    o = mm(weights, v[...], NN)
    o += mm(scaled(q[...], q_decay[...]), state[...].astype(BF16), NN)
    state[...] = params[0] * state[...] + mm(scaled(k[...], k_decay[...]), v[...], TN)
    kept[...] = o
    o = o - jnp.mean(o, axis=-1, keepdims=True)
    o = o * lax.rsqrt(jnp.mean(o * o, axis=-1, keepdims=True) + EPS_GROUP)
    low = o.astype(BF16)
    mixed[...] = low
    for n, (one, two) in enumerate(((low_a, high_a), (low_b, high_b))):
        columns = slice(n * DK, (n + 1) * DK)
        g = select(params, one, two)
        hidden[:, columns] = (g * jax.nn.sigmoid(g) * low[:, columns].astype(F32)).astype(BF16)


def gate_back_kernel(
    params, d_hidden, low_a, high_a, low_b, high_b, mixed, kept, q, q_decay,
    d_gate, d_out, total, state,
):
    @pl.when(pl.program_id(0) == 0)
    def _():
        state[...] = jnp.zeros(state.shape, F32)

    g = jnp.concatenate([select(params, low_a, high_a), select(params, low_b, high_b)], axis=1)
    dh = d_hidden[...]
    sig = jax.nn.sigmoid(g)
    d_gate[...] = (dh * mixed[...].astype(F32) * (sig * (1.0 + g * (1.0 - sig)))).astype(BF16)
    dy = (dh * (g * sig)).astype(BF16).astype(F32)
    o = kept[...]
    o = o - jnp.mean(o, axis=-1, keepdims=True)
    inverse = lax.rsqrt(jnp.mean(o * o, axis=-1, keepdims=True) + EPS_GROUP)
    o = o * inverse
    do = inverse * (
        dy
        - jnp.mean(dy, axis=-1, keepdims=True)
        - o * jnp.mean(dy * o, axis=-1, keepdims=True)
    )
    do = do.astype(BF16)
    d_out[...] = do
    state[...] = params[0] * state[...] + mm(scaled(q[...], q_decay[...]), do, TN)
    total[...] = state[...].astype(BF16)


def inner_back_kernel(
    params, q, k, v, d_out, mask, q_decay, k_decay, start, cosine, sine, d_q, d_k, d_v, state
):
    @pl.when(pl.program_id(0) == 0)
    def _():
        state[...] = start[...].astype(F32)

    do = d_out[...]
    weights = (mm(q[...], k[...], NT) * mask[...]).astype(BF16)
    d_v[...] = mm(weights, do, TN)
    d_scores = mm(do, v[...], NT).astype(BF16).astype(F32)
    d_scores = (d_scores * mask[...]).astype(BF16)
    d_k[...] = mm(d_scores, q[...], TN)
    far = mm(do, state[...].astype(BF16), NT).astype(BF16).astype(F32)
    dq = mm(d_scores, k[...], NN) + far * q_decay[...]
    dq = dq.astype(BF16).astype(F32)
    d_q[...] = turn(dq, cosine[...], -sine[...]).astype(BF16)
    state[...] = params[0] * state[...] + mm(scaled(k[...], k_decay[...]), v[...], TN)


def outer_back_kernel(
    roles, params, q, k, v, d_out, d_q, d_k, d_v, q_decay, k_decay, start, cosine, sine, *refs
):
    refs = list(refs)
    state = refs.pop()
    v_a = None if "va" in roles else refs.pop()
    by_unit = refs.pop()

    @pl.when(pl.program_id(0) == 0)
    def _():
        state[...] = start[...].astype(F32)

    low = state[...].astype(BF16)
    far = mm(v[...], low, NT).astype(BF16).astype(F32)
    dk = (d_k[...] + far * k_decay[...]).astype(BF16).astype(F32)
    dk = turn(dk, cosine[...], -sine[...]).astype(BF16)
    dv = (d_v[...] + mm(scaled(k[...], k_decay[...]), low, NN)).astype(BF16)
    for n, role in enumerate(roles):
        if role == "q":
            value = d_q[...]
        elif role == "k":
            value = dk
        elif role == "va":
            value = dv[:, :DK]
        elif role == "vb":
            value = dv[:, DK:]
        elif role == "xv":
            value = refs.pop(0)[...]
        else:
            value = select(params, refs.pop(0), refs.pop(0)).astype(BF16)
        by_unit[:, n * DK : (n + 1) * DK] = value
    if v_a is not None:
        v_a[...] = dv[:, :DK]
    state[...] = params[0] * state[...] + mm(scaled(q[...], q_decay[...]), d_out[...], TN)


def head_call(kernel, grid, operands, outputs, scratch, flops):
    arrays = [t[0] for t in operands]
    size = sum(t.size * t.dtype.itemsize for t in arrays + [t[0] for t in outputs])
    return pl.pallas_call(
        kernel,
        grid=(grid,),
        in_specs=[
            pl.BlockSpec(memory_space=pltpu.SMEM) if block is None else pl.BlockSpec(block, where)
            for _, block, where in operands
        ],
        out_specs=[pl.BlockSpec(block, where) for _, block, where in outputs],
        scratch_shapes=scratch,
        out_shape=[t[0] for t in outputs],
        compiler_params=pltpu.CompilerParams(vmem_limit_bytes=56 * 2**20),
        cost_estimate=pl.CostEstimate(flops=flops, bytes_accessed=size, transcendentals=0),
    )(*arrays)


def place_kernel(parts, target, source, *refs):
    out = refs[-1]
    code = source[pl.program_id(1)]
    for i, part in enumerate(parts):

        @pl.when(code == i)
        def _(part=part):
            row = 0
            for n in part:
                piece = refs[n]
                out[row : row + piece.shape[0], :] = piece[...].astype(F32)
                row += piece.shape[0]


def place_blocks(parts, target, source, shape, block, where, outer=1):
    flat, index = [], []
    for part in parts:
        for piece in part:
            if not any(piece is t for t in flat):
                flat.append(piece)
        index.append([next(n for n, t in enumerate(flat) if t is piece) for piece in part])
    return pl.pallas_call(
        functools.partial(place_kernel, index),
        grid_spec=pltpu.PrefetchScalarGridSpec(
            num_scalar_prefetch=2,
            grid=(outer, target.shape[0]),
            in_specs=[
                pl.BlockSpec((t.shape[0], t.shape[1] // outer), lambda o, n, target, source: (0, o))
                for t in flat
            ],
            out_specs=pl.BlockSpec(block, lambda o, n, target, source: where(o, target[n])),
        ),
        out_shape=jax.ShapeDtypeStruct(shape, F32),
        compiler_params=pltpu.CompilerParams(vmem_limit_bytes=48 * 2**20),
    )(target.astype(jnp.int32), source.astype(jnp.int32), *flat)


def local(
    tokens,
    cotangent,
    gain_attn,
    gain_ffn,
    mixer_in,
    mixer_out,
    ffn_in,
    ffn_out,
    segment_order,
    decay_index,
):
    rows, width = tokens.shape
    group = lax.axis_size("seq")
    segments = lax.axis_size("shard")
    heads = decay_index.shape[0]
    local_heads = heads // group
    seg_len = rows * group
    blk = min(512, seg_len)
    blocks = seg_len // blk
    vcols = local_heads * DV
    s = lax.axis_index("seq")
    j = lax.axis_index("shard")

    def swap(v, d):
        return lax.ppermute(v, "seq", [(i, i ^ d) for i in range(group)])

    def cross(v, d):
        return lax.ppermute(v, "shard", [(i, i ^ d) for i in range(segments)])

    def pick(v, i):
        return lax.dynamic_index_in_dim(v, i, 0, keepdims=False)

    def spread(v):
        if group == 4:
            h = v.shape[0] // 2
            r1 = swap(v, 1)
            r2 = swap(v, 2)
            return [(v,), (r1,), (r2,), (swap(r1[:h], 2), swap(r2[h:], 1))]
        return [(v,)] + [(swap(v, d),) for d in range(1, group)]

    def ordered(parts):
        r = parts[0][0].shape[0]
        out = jnp.zeros((group * r,) + parts[0][0].shape[1:], parts[0][0].dtype)
        for d, part in enumerate(parts):
            row = (s ^ d) * r
            for piece in part:
                out = lax.dynamic_update_slice_in_dim(out, piece, row, 0)
                row = row + piece.shape[0]
        return out

    def gather_near(v):
        return jnp.concatenate([piece for part in spread(v) for piece in part], axis=0)

    def gather_seq(v):
        return ordered(spread(v))

    def scatter_sum(blk_of, beside1=(), beside2=()):
        if group == 4:
            b0, b1, b2, b3 = (blk_of(d) for d in range(4))
            h = b0.shape[0] // 2
            b0 = b0.astype(F32)
            ra = swap(jnp.concatenate([b1[:h], b3[:h]], axis=0), 1)
            rb = swap(jnp.concatenate([b2[h:], b3[h:]], axis=0), 2)
            ra, rb, *beside1 = tie(ra, rb, *beside1)
            ra, rb = ra.astype(F32), rb.astype(F32)
            qa = swap((b2[:h].astype(F32) + ra[h:]).astype(BF16), 2)
            qb = swap((b1[h:].astype(F32) + rb[h:]).astype(BF16), 1)
            qa, qb, *beside2 = tie(qa, qb, *beside2)
            total = jnp.concatenate(
                [b0[:h] + ra[:h] + qa.astype(F32), b0[h:] + rb[:h] + qb.astype(F32)], axis=0
            )
            return (total, *beside1, *beside2)
        total = blk_of(0).astype(F32)
        for d in range(1, group):
            total = total + swap(blk_of(d), d).astype(F32)
        return (total, *beside1, *beside2)

    def scatter_near(v, beside1=(), beside2=()):
        return scatter_sum(lambda d: v[d * rows : (d + 1) * rows], beside1, beside2)

    def scatter_seq(v):
        return scatter_sum(lambda d: lax.dynamic_slice_in_dim(v, (s ^ d) * rows, rows, 0))[0]

    def gather_shard(v):
        return lax.all_gather(v, "shard", axis=0, tiled=True)

    def reduce_shard(v):
        return lax.psum_scatter(v, "shard", scatter_dimension=0, tiled=True)

    def sum_all(v):
        step = 1
        while step < group:
            v = v + swap(v, step)
            step *= 2
        step = 1
        while step < segments:
            v = v + cross(v, step)
            step *= 2
        return v

    balanced = group == 4 and local_heads == 2 and segments == 8
    units = mixer_in.reshape(-1, DK, width)
    if balanced:
        keep, give, back, lend = (jnp.asarray(t) for t in balanced_tables())
        core = j % 2
    else:
        keep, give, place, held, back, lend = (
            jnp.asarray(t) for t in unit_tables(group, local_heads, segments)
        )

    def offered(h):
        kept, given = keep[h, j, s], give[h, j, s]
        if balanced and h == 1:
            cut = mixer_in.reshape(-1, DK // 2, width)
            own = pick(cut, 2 * jnp.maximum(kept, 0) + core)
            given = cross(pick(cut, 2 * given + 1 - core), 1)
        else:
            own = pick(units, jnp.maximum(kept, 0))
            given = cross(pick(units, given), 1)
        return jnp.where(kept >= 0, own, given)

    sub = ffn_in.shape[0] // group
    ffn_out_cut = ffn_out.reshape(ffn_out.shape[0], segments // 2, group, sub)

    my_rank = jnp.sum(jnp.where(jnp.arange(segments) == j, segment_order, 0))
    all_logs = jnp.log1p(-jnp.exp2(-(5.0 + decay_index.astype(F32))))
    logs = lax.dynamic_index_in_dim(all_logs.reshape(local_heads, group), s, 1, keepdims=False)
    half = DK // 2
    inv_freq = jnp.exp(-jnp.log(10000.0) * jnp.arange(half).astype(F32) / half)
    positions = my_rank * seg_len + jnp.arange(seg_len, dtype=jnp.int32)
    angles = positions.astype(F32)[:, None] * inv_freq[None, :]
    cosine = jnp.cos(angles)
    sine = jnp.sin(angles)
    steps = jnp.arange(blk).astype(F32)
    gap = steps[:, None] - steps[None, :]
    masks = jnp.where(
        gap[None] >= 0.0, jnp.exp(jnp.maximum(gap, 0.0)[None] * logs[:, None, None]), 0.0
    )
    q_decays = jnp.exp((steps + 1.0)[None, :] * logs[:, None])[..., None]
    k_decays = jnp.exp((blk - 1.0 - steps)[None, :] * logs[:, None])[..., None]
    block_decays = jnp.exp(blk * logs)

    xf = tokens.astype(F32)
    normed = gather_seq(rms_scale(xf, gain_attn).astype(BF16))
    d_ffn = gather_near(cotangent)
    slots = [gather_shard(offered(0))]
    slots[0], normed, d_ffn, cosine, sine, masks, q_decays, k_decays = tie(
        slots[0], normed, d_ffn, cosine, sine, masks, q_decays, k_decays
    )
    for h in range(1, local_heads):
        slots.append(gather_shard(offered(h)))
    mixer_out_cut = jnp.concatenate(
        [
            lax.dynamic_slice_in_dim(mixer_out, (h * group + s) * DV, DV, 1)
            for h in range(local_heads)
        ],
        axis=1,
    )
    mixer_out_cut, slots[0] = tie(mixer_out_cut, slots[0])
    w_out = gather_shard(mixer_out_cut)
    later = [
        lax.dynamic_slice_in_dim(ffn_in, s * sub, sub, 0),
        lax.dynamic_index_in_dim(ffn_out_cut, s, 2, keepdims=False).reshape(ffn_out.shape[0], -1),
    ]
    inner_cols = later[1].shape[1]

    ranks = segment_order
    piece = DK // segments

    def exchange_states(hs, totals, reverse, beside=()):
        cut = jnp.concatenate([t.reshape(segments, piece, DV) for t in totals], axis=1)
        got = lax.all_to_all(cut, "shard", split_axis=0, concat_axis=0, tiled=True)
        got, *beside = tie(got, *beside)
        apart = ranks[:, None] - ranks[None, :] - 1
        if reverse:
            apart = -apart - 2
        distance = apart.astype(F32)
        joined = []
        for n, h in enumerate(hs):
            coef = jnp.where(
                distance >= 0.0, jnp.exp(jnp.maximum(distance, 0.0) * seg_len * logs[h]), 0.0
            )
            part = got[:, n * piece : (n + 1) * piece].astype(F32)
            joined.append(jnp.sum(coef[..., None, None] * part[None], axis=1).astype(BF16))
        joined = jnp.concatenate(joined, axis=1)
        back_cut = lax.all_to_all(joined, "shard", split_axis=0, concat_axis=0, tiled=True)
        states = [
            back_cut[:, n * piece : (n + 1) * piece].reshape(DK, DV) for n in range(len(hs))
        ]
        return (states, *beside)

    def whole(n):
        return (0, 0)

    def ahead(n):
        return (n, 0)

    def behind(n):
        return (blocks - 1 - n, 0)

    def shaped(columns, kind, r=seg_len):
        return jax.ShapeDtypeStruct((r, columns), kind)

    state_scratch = [pltpu.VMEM((DK, DV), F32)]
    half_block = (blk, half)
    unit_block, v_block = (blk, DK), (blk, DV)
    ret_flops = 2 * seg_len * (DK + DV) * (blk + DK)
    low = s < group // 2
    if balanced:
        roles = [["q", "k", "va", "vb", "xv", "g", "g", "g"], ["q", "k", "vb", "g"]]
    else:
        roles = [["q", "k", "va", "vb", "g", "g"]] * local_heads
    params = [
        (jnp.stack([block_decays[h], low.astype(F32)]), None, None) for h in range(local_heads)
    ]
    heads_kept = []
    extra_v = None
    for h in range(local_heads):
        if balanced:
            weights = slots[h]
        else:
            cut = slots[h].reshape(-1, DK, width)
            weights = jnp.concatenate([pick(cut, place[h, s, c]) for c in range(6)], axis=0)
        carried = "va" not in roles[h]
        gate_count = roles[h].count("g")
        q, k, v, total, gates, *extra = head_call(
            functools.partial(project_kernel, blk, roles[h], carried),
            len(roles[h]) // 2,
            [
                params[h],
                (normed, (seg_len, width), whole),
                (weights, (2 * DK, width), ahead),
                (cosine, (seg_len, half), whole),
                (sine, (seg_len, half), whole),
                (k_decays[h], (blk, 1), whole),
            ]
            + ([(extra_v, (seg_len, DK), whole)] if carried else []),
            [
                (shaped(DK, BF16), (seg_len, DK), whole),
                (shaped(DK, BF16), (seg_len, DK), whole),
                (shaped(DV, BF16), (seg_len, DV), whole),
                (shaped(DV, BF16, DK), (DK, DV), whole),
                (shaped(gate_count * DK, F32), (seg_len, gate_count * DK), whole),
            ]
            + ([(shaped(DK, BF16), (seg_len, DK), whole)] if "xv" in roles[h] else []),
            [pltpu.VMEM((seg_len, 2 * DK), F32)],
            2 * seg_len * width * len(roles[h]) * DK,
        )
        extra_v = extra[0] if extra else None
        (state_in,) = exchange_states([h], [total], False)[0]
        if h + 1 < local_heads:
            slots[h + 1], state_in, *later[:] = tie(slots[h + 1], state_in, *later)
        heads_kept.append((weights, q, k, v, gates, state_in))

    def columns(v, c, order):
        return (v, unit_block, lambda n, c=c: (order(n)[0], c))

    if balanced:
        gates0, gates1 = heads_kept[0][4], heads_kept[1][4]
        swapped = swap(jnp.where(low, gates1, gates0[:, :DK]).astype(BF16), 2)

        def gate_operands(h, order):
            if h == 0:
                four = (gates0, 0), (gates0, 1), (swapped, 0), (gates0, 2)
            else:
                four = (gates0, 1), (gates1, 0), (gates0, 2), (swapped, 0)
            return [columns(v, c, order) for v, c in four]

    else:

        def gate_operands(h, order):
            return [columns(heads_kept[h][4], c, order) for c in (0, 0, 1, 1)]

    kept = []
    for h in range(local_heads):
        weights, q, k, v, gates, state_in = heads_kept[h]
        hidden, mixed, retained = head_call(
            retain_kernel,
            blocks,
            [
                params[h],
                (q, unit_block, ahead),
                (k, unit_block, ahead),
                (v, v_block, ahead),
                *gate_operands(h, ahead),
                (masks[h], (blk, blk), whole),
                (q_decays[h], (blk, 1), whole),
                (k_decays[h], (blk, 1), whole),
                (state_in, (DK, DV), whole),
            ],
            [
                (shaped(DV, BF16), v_block, ahead),
                (shaped(DV, BF16), v_block, ahead),
                (shaped(DV, F32), v_block, ahead),
            ],
            state_scratch,
            ret_flops,
        )
        kept.append((retained, mixed, hidden))
    hidden = jnp.concatenate([t[-1] for t in kept], axis=1)
    w_ffn_in, w_ffn_out = (gather_shard(t) for t in later)

    resid = xf + scatter_seq(dot_nt(hidden, w_out, BF16))
    normed2 = gather_near(rms_scale(resid, gain_ffn).astype(BF16))
    proj2 = dot_nt(normed2, w_ffn_in)
    first, second = proj2[:, :inner_cols], proj2[:, inner_cols:]
    inner2 = gated_gelu(first, second).astype(BF16)

    g_ffn_out, d_ffn = tie(dot_tn(d_ffn, inner2, BF16), d_ffn)
    scattered = {"ffn_out": reduce_shard(g_ffn_out)}
    d_inner2 = dot_nn(d_ffn, w_ffn_out)
    ignored2, gelu_back = jax.vjp(gated_gelu, first, second)
    d_first, d_second = gelu_back(d_inner2)
    dproj2 = jnp.concatenate([d_first, d_second], axis=1).astype(BF16)
    d_normed2, g_ffn_in = scatter_near(
        dot_nn(dproj2, w_ffn_in, BF16), (dot_tn(dproj2, normed2, BF16),)
    )
    scattered["ffn_in"] = reduce_shard(g_ffn_in)
    ignored3, norm2_back = jax.vjp(rms_scale, resid, gain_ffn)
    d_resid_part, d_gain_ffn = norm2_back(d_normed2)
    d_resid = cotangent.astype(F32) + d_resid_part
    d_attn = gather_seq(d_resid.astype(BF16))
    d_attn, scattered["ffn_out"] = tie(d_attn, scattered["ffn_out"])
    parts_ffn_out = spread(scattered["ffn_out"])
    d_hidden = dot_nn(d_attn, w_out)
    inner2, hidden, d_hidden, d_gain_ffn = tie(inner2, hidden, d_hidden, d_gain_ffn)
    output = (resid + scatter_near(dot_nt(inner2, w_ffn_out, BF16))[0]).astype(BF16)
    g_mixer_out = dot_tn(d_attn, hidden, BF16)

    def tie_parts(v, parts):
        flat = tie(v, *(piece for part in parts for piece in part))
        rest = list(flat[1:])
        return flat[0], [tuple(rest.pop(0) for _ in part) for part in parts]

    turns = [(cosine, half_block), (sine, half_block)]
    firsts = []
    for h in range(local_heads):
        weights, q, k, v, gates, state_in = heads_kept[h]
        retained, mixed, ignored4 = kept[h]
        firsts.append(
            head_call(
                gate_back_kernel,
                blocks,
                [
                    params[h],
                    (d_hidden, v_block, lambda n, h=h: (blocks - 1 - n, h)),
                    *gate_operands(h, behind),
                    (mixed, v_block, behind),
                    (retained, v_block, behind),
                    (q, unit_block, behind),
                    (q_decays[h], (blk, 1), whole),
                ],
                [
                    (shaped(DV, BF16), v_block, behind),
                    (shaped(DV, BF16), v_block, behind),
                    (shaped(DV, BF16, DK), (DK, DV), whole),
                ],
                state_scratch,
                2 * seg_len * DK * DV,
            )
        )
    d_gates = [t[0] for t in firsts]
    if balanced:
        d_swapped = swap(jnp.where(low, d_gates[0][:, DK:], d_gates[1][:, DK:]), 2)
        d_gate_pairs = [
            [
                ((d_gates[0], 0), (d_swapped, 0)),
                ((d_gates[1], 0), (d_gates[0], 0)),
                ((d_gates[1], 1), (d_gates[0], 1)),
            ],
            [((d_swapped, 0), (d_gates[1], 0))],
        ]
    else:
        d_gate_pairs = [[((t, 0), (t, 0)), ((t, 1), (t, 1))] for t in d_gates]
    inners = []
    for h in range(local_heads):
        weights, q, k, v, gates, state_in = heads_kept[h]
        inners.append(
            head_call(
                inner_back_kernel,
                blocks,
                [
                    params[h],
                    (q, unit_block, ahead),
                    (k, unit_block, ahead),
                    (v, v_block, ahead),
                    (firsts[h][1], v_block, ahead),
                    (masks[h], (blk, blk), whole),
                    (q_decays[h], (blk, 1), whole),
                    (k_decays[h], (blk, 1), whole),
                    (state_in, (DK, DV), whole),
                    *((*t, ahead) for t in turns),
                ],
                [
                    (shaped(DK, BF16), unit_block, ahead),
                    (shaped(DK, F32), unit_block, ahead),
                    (shaped(DV, F32), v_block, ahead),
                ],
                state_scratch,
                2 * ret_flops,
            )
        )
    g_mixer_out, *totals = tie(g_mixer_out, *(t[2] for t in firsts))
    scattered["mixer_out"] = reduce_shard(g_mixer_out)
    grads_out, scattered["ffn_in"], *flat = exchange_states(
        range(local_heads),
        totals,
        True,
        (scattered["ffn_in"], *(t for inner in inners for t in inner)),
    )
    inners = [flat[3 * h : 3 * h + 3] for h in range(local_heads)]
    parts_ffn_in = spread(scattered["ffn_in"])
    by_units = [None] * local_heads
    extra_v = None
    for h in reversed(range(local_heads)):
        weights, q, k, v, gates, state_in = heads_kept[h]
        d_out = firsts[h][1]
        d_q, d_k, d_v = inners[h]
        count = len(roles[h])
        lone = "va" not in roles[h]
        by_units[h], *extra = head_call(
            functools.partial(outer_back_kernel, roles[h]),
            blocks,
            [
                params[h],
                (q, unit_block, behind),
                (k, unit_block, behind),
                (v, v_block, behind),
                (d_out, v_block, behind),
                (d_q, unit_block, behind),
                (d_k, unit_block, behind),
                (d_v, v_block, behind),
                (q_decays[h], (blk, 1), whole),
                (k_decays[h], (blk, 1), whole),
                (grads_out[h], (DK, DV), whole),
                *((*t, behind) for t in turns),
            ]
            + ([(extra_v, unit_block, behind)] if "xv" in roles[h] else [])
            + [columns(v, c, behind) for pair in d_gate_pairs[h] for v, c in pair],
            [(shaped(count * DK, BF16), (blk, count * DK), behind)]
            + ([(shaped(DK, BF16), unit_block, behind)] if lone else []),
            state_scratch,
            6 * seg_len * DK * DV,
        )
        extra_v = extra[0] if extra else None

    gain_ffn_grad = sum_all(d_gain_ffn)
    by_units[0], output, gain_ffn_grad = tie(by_units[0], output, gain_ffn_grad)
    by_units[0], parts_ffn_out = tie_parts(by_units[0], parts_ffn_out)
    by_units[-1], parts_ffn_in = tie_parts(by_units[-1], parts_ffn_in)
    by_units[-1], scattered["mixer_out"] = tie(by_units[-1], scattered["mixer_out"])
    parts_mixer_out = spread(scattered["mixer_out"])
    g_slots = []
    d_normed = None
    for h in range(local_heads):
        g_unit = dot_tn(by_units[h], normed, BF16)
        if not balanced:
            cut = g_unit.reshape(-1, DK, width)
            g_unit = jnp.concatenate(
                [pick(cut, jnp.maximum(held[h, c, s], 0)) for c in range(segments)], axis=0
            )
        part = dot_nn(by_units[h], heads_kept[h][0])
        d_normed = part if d_normed is None else d_normed + part
        if h == local_heads - 1:
            g_unit, d_normed = tie(g_unit, d_normed.astype(BF16))
        g_slots.append(reduce_shard(g_unit))
    d_normed = scatter_seq(d_normed)

    ignored8, norm1_back = jax.vjp(rms_scale, xf, gain_attn)
    d_x_part, d_gain_attn = norm1_back(d_normed)
    input_grad = (d_resid + d_x_part).astype(BF16)
    gain_attn_grad = sum_all(d_gain_attn)
    near = jnp.arange(group)
    g_ffn_in = place_blocks(
        parts_ffn_in, s ^ near, near, ffn_in.shape, (sub, width), lambda o, n: (n, 0)
    )
    if sub % 128 == 0:
        g_ffn_out = place_blocks(
            parts_ffn_out,
            s ^ near,
            near,
            ffn_out.shape,
            (ffn_out.shape[0], sub),
            lambda o, n: (0, o * group + n),
            outer=segments // 2,
        )
    else:
        g_ffn_out = jnp.transpose(
            ordered(parts_ffn_out).reshape(group, ffn_out.shape[0], segments // 2, sub),
            (1, 2, 0, 3),
        ).reshape(ffn_out.shape).astype(F32)

    parts = []
    for h in range(local_heads):
        last = h == local_heads - 1
        if h == 0:
            g_slots[h], g_ffn_in, g_ffn_out, input_grad = tie(
                g_slots[h], g_ffn_in, g_ffn_out, input_grad
            )
        if last:
            pieces = parts_mixer_out[0]
            pieces0, parts = tie_parts(pieces[0], parts)
            parts_mixer_out[0] = (pieces0, *pieces[1:])
            g_mixer_out = place_blocks(
                parts_mixer_out,
                s ^ near,
                near,
                mixer_out.shape,
                (mixer_out.shape[0], DV),
                lambda o, n: (0, o * group + n),
                outer=local_heads,
            )
            g_slots[h], gain_attn_grad, g_mixer_out = tie(g_slots[h], gain_attn_grad, g_mixer_out)
        here = spread(g_slots[h])
        if balanced and last:
            there = [tuple(cross(piece, 1) for piece in part) for part in here]
            parts += [a + b for a, b in zip(here, there)] + [b + a for a, b in zip(here, there)]
        else:
            lend_here = lend[j] if balanced else lend[h, j]
            stack = jnp.stack([jnp.concatenate(part, axis=0) for part in here])
            parts += here + [
                (cross(pick(stack, s ^ lend_here[n]), 1),) for n in range(lend_here.shape[0])
            ]
    found = back[j]
    if balanced:
        spare = lend.shape[-1]
        source = jnp.where(
            found[:, 0] == 0,
            s ^ found[:, 1],
            jnp.where(
                found[:, 0] == 1,
                group + found[:, 1],
                group + spare + core * group + (s ^ found[:, 1]),
            ),
        )
    else:
        source = found[:, 0] * (group + lend.shape[-1]) + jnp.where(
            found[:, 2] < 0, s ^ found[:, 1], group + found[:, 2]
        )
    g_mixer_in = place_blocks(
        parts,
        jnp.arange(source.shape[0]),
        source,
        mixer_in.shape,
        (DK, width),
        lambda o, n: (n, 0),
    )
    return (
        output,
        input_grad,
        gain_attn_grad,
        gain_ffn_grad,
        g_mixer_in,
        g_mixer_out,
        g_ffn_in,
        g_ffn_out,
    )


def solution(mesh):
    return jax.shard_map(
        local,
        mesh=mesh,
        in_specs=(
            P(("shard", "seq"), None),
            P(("shard", "seq"), None),
            P(),
            P(),
            P("shard", None),
            P("shard", None),
            P("shard", None),
            P("shard", None),
            P(),
            P(),
        ),
        out_specs=(
            P(("shard", "seq"), None),
            P(("shard", "seq"), None),
            P(),
            P(),
            P("shard", None),
            P("shard", None),
            P("shard", None),
            P("shard", None),
        ),
        check_vma=False,
    )
```

```python
import functools

import jax
import jax.numpy as jnp
import numpy as np
from jax import lax
from jax.experimental import pallas as pl
from jax.experimental.pallas import tpu as pltpu
from jax.sharding import PartitionSpec as P

DK = 256
DV = 512
FF = 4096
QK = 2048
V = 4096


EPS_NORM = 1e-06
EPS_GROUP = 1e-05

F32 = jnp.float32
BF16 = jnp.bfloat16


def dot_nt(left, right, kind=F32):
    return lax.dot_general(
        left, right, (((1,), (1,)), ((), ())), preferred_element_type=F32
    ).astype(kind)


def dot_nn(left, right, kind=F32):
    return lax.dot_general(
        left, right, (((1,), (0,)), ((), ())), preferred_element_type=F32
    ).astype(kind)


def dot_tn(left, right, kind=F32):
    return lax.dot_general(
        left, right, (((0,), (0,)), ((), ())), preferred_element_type=F32
    ).astype(kind)


def rms_scale(v, gain):
    return v * lax.rsqrt(jnp.mean(v * v, axis=-1, keepdims=True) + EPS_NORM) * gain


def gated_gelu(first, second):
    return jax.nn.gelu(first) * second


def unit_owners(heads):
    owners = [(n, 0) for n in range(heads)] + [(n, 1) for n in range(heads)]
    for base in (2, 4):
        owners += [(n, base + half) for n in range(heads) for half in range(2)]
    return owners


def balanced_tables():
    group, segments, per_shard = 4, 8, 6
    number = {owner: u for u, owner in enumerate(unit_owners(8))}
    keep = np.full((2, segments, group), -1, np.int32)
    give = np.zeros((2, segments, group), np.int32)
    back = np.zeros((segments, per_shard, 2), np.int32)
    lend = [[] for _ in range(segments)]
    seen = set()
    for s in range(group):
        a, b = s, s + 4
        if s < 2:
            gates = [(a, 4), (b, 4), (b, 5)], (b + 2, 5)
        else:
            gates = [(a - 2, 5), (a, 4), (a, 5)], (b, 4)
        first = [(a, 0), (a, 1), (a, 2), (a, 3), (b, 2)] + gates[0]
        second = [(b, 0), (b, 1), (b, 3), gates[1]]
        for slot, owner in enumerate(first):
            home, index = divmod(number[owner], per_shard)
            seen.add(number[owner])
            assert home // 2 == slot // 2
            if home == slot:
                keep[0, slot, s] = index
                back[home, index] = (0, s)
            else:
                give[0, home, s] = index
                back[home, index] = (1, len(lend[slot]))
                lend[slot].append(s)
        for chip, owner in enumerate(second):
            home, index = divmod(number[owner], per_shard)
            seen.add(number[owner])
            assert home // 2 == chip
            keep[1, home, s] = index
            give[1, home, s] = index
            back[home, index] = (2, s)
    assert len(seen) == segments * per_shard
    most = max(len(t) for t in lend)
    return keep, give, back, np.asarray([(t + [0] * most)[:most] for t in lend], np.int32)


def unit_tables(group, local_heads, segments):
    heads = group * local_heads
    owners = unit_owners(heads)
    per_shard = len(owners) // segments
    keep = np.full((local_heads, segments, group), -1, np.int32)
    give = np.zeros((local_heads, segments, group), np.int32)
    place = np.zeros((local_heads, group, 6), np.int32)
    held = np.full((local_heads, segments, group), -1, np.int32)
    slot_of = {}
    for chip in range(segments // 2):
        for head in range(heads):
            h, s = divmod(head, group)
            span = range(2 * per_shard * chip, 2 * per_shard * (chip + 1))
            mine = [u for u in span if owners[u][0] == head]
            assert len(mine) <= 2
            for n, u in enumerate(mine):
                home = u // per_shard
                slot = home if len(mine) == 1 else 2 * chip + n
                if slot == home:
                    keep[h, slot, s] = u % per_shard
                else:
                    give[h, home, s] = u % per_shard
                place[h, s, owners[u][1]] = slot
                held[h, slot, s] = owners[u][1]
                slot_of[u] = slot
    lends = [[[] for _ in range(segments)] for _ in range(local_heads)]
    back = np.zeros((segments, per_shard, 3), np.int32)
    for u, (head, _) in enumerate(owners):
        home = u // per_shard
        h, s = divmod(head, group)
        back[home, u % per_shard] = (h, s, -1)
        if slot_of[u] != home:
            assert slot_of[u] == home ^ 1
            back[home, u % per_shard, 2] = len(lends[h][home ^ 1])
            lends[h][home ^ 1].append(s)
    most = max(1, max(len(t) for row in lends for t in row))
    lend = np.asarray(
        [[(t + [0] * most)[:most] for t in row] for row in lends], np.int32
    )
    return keep, give, place, held, back, lend


def tie(*values):
    return lax.optimization_barrier(values)


def mm(left, right, dims):
    return lax.dot_general(left, right, (dims, ((), ())), preferred_element_type=F32)


NN = ((1,), (0,))
NT = ((1,), (1,))
TN = ((0,), (0,))


def turn(v, cosine, sine):
    half = v.shape[-1] // 2
    first, second = v[:, :half], v[:, half:]
    return jnp.concatenate(
        [first * cosine - second * sine, second * cosine + first * sine], axis=-1
    )


def scaled(v, decay):
    return (v.astype(F32) * decay).astype(BF16)


def project_kernel(blk, roles, carried, params, x, w, cosine, sine, k_decay, *refs):
    if carried:
        v_a, *refs = refs
    q, k, v, total, gates, *rest = refs
    y = rest[-1]
    rows = y.shape[0]
    y[...] = mm(x[...], w[...], NT)

    def put(role, part, gate_at):
        value = y[:, part * DK : (part + 1) * DK]
        if role == "q":
            q[...] = turn(value, cosine[...], sine[...]).astype(BF16)
        elif role == "k":
            k[...] = turn(value, cosine[...], sine[...]).astype(BF16)
        elif role == "va":
            v[:, :DK] = value.astype(BF16)
        elif role == "vb":
            v[:, DK:] = value.astype(BF16)
        elif role == "xv":
            rest[0][...] = value.astype(BF16)
        else:
            gates[:, gate_at * DK : (gate_at + 1) * DK] = value

    for step in range(len(roles) // 2):

        @pl.when(pl.program_id(0) == step)
        def _(step=step):
            for part in range(2):
                at = 2 * step + part
                put(roles[at], part, roles[:at].count("g"))
            if step == 1:
                if carried:
                    v[:, :DK] = v_a[...]
                state = jnp.zeros(total.shape, F32)
                for r in range(0, rows, blk):
                    kd = scaled(k[r : r + blk, :], k_decay[...])
                    state = params[0] * state + mm(kd, v[r : r + blk, :], TN)
                total[...] = state.astype(BF16)


def join_kernel(count, *refs):
    out = refs[-1]
    total = mm(refs[0][...], refs[count][...], NN)
    for n in range(1, count):
        total += mm(refs[n][...], refs[count + n][...], NN)
    out[...] = total.astype(out.dtype)


def select(params, low, high):
    return jnp.where(params[1] > 0.5, low[...].astype(F32), high[...].astype(F32))


def retain_kernel(
    params, q, k, v, low_a, high_a, low_b, high_b, mask, q_decay, k_decay, start,
    hidden, mixed, kept, state,
):
    @pl.when(pl.program_id(0) == 0)
    def _():
        state[...] = start[...].astype(F32)

    weights = (mm(q[...], k[...], NT) * mask[...]).astype(BF16)
    o = mm(weights, v[...], NN)
    o += mm(scaled(q[...], q_decay[...]), state[...].astype(BF16), NN)
    state[...] = params[0] * state[...] + mm(scaled(k[...], k_decay[...]), v[...], TN)
    kept[...] = o
    o = o - jnp.mean(o, axis=-1, keepdims=True)
    o = o * lax.rsqrt(jnp.mean(o * o, axis=-1, keepdims=True) + EPS_GROUP)
    low = o.astype(BF16)
    mixed[...] = low
    for n, (one, two) in enumerate(((low_a, high_a), (low_b, high_b))):
        columns = slice(n * DK, (n + 1) * DK)
        g = select(params, one, two)
        hidden[:, columns] = (g * jax.nn.sigmoid(g) * low[:, columns].astype(F32)).astype(BF16)


def gate_back_kernel(
    params, d_hidden, low_a, high_a, low_b, high_b, mixed, kept, q, q_decay,
    d_gate, d_out, total, state,
):
    @pl.when(pl.program_id(0) == 0)
    def _():
        state[...] = jnp.zeros(state.shape, F32)

    g = jnp.concatenate([select(params, low_a, high_a), select(params, low_b, high_b)], axis=1)
    dh = d_hidden[...]
    sig = jax.nn.sigmoid(g)
    d_gate[...] = (dh * mixed[...].astype(F32) * (sig * (1.0 + g * (1.0 - sig)))).astype(BF16)
    dy = (dh * (g * sig)).astype(BF16).astype(F32)
    o = kept[...]
    o = o - jnp.mean(o, axis=-1, keepdims=True)
    inverse = lax.rsqrt(jnp.mean(o * o, axis=-1, keepdims=True) + EPS_GROUP)
    o = o * inverse
    do = inverse * (
        dy
        - jnp.mean(dy, axis=-1, keepdims=True)
        - o * jnp.mean(dy * o, axis=-1, keepdims=True)
    )
    do = do.astype(BF16)
    d_out[...] = do
    state[...] = params[0] * state[...] + mm(scaled(q[...], q_decay[...]), do, TN)
    total[...] = state[...].astype(BF16)


def inner_back_kernel(
    params, q, k, v, d_out, mask, q_decay, k_decay, start, cosine, sine, d_q, d_k, d_v, state
):
    @pl.when(pl.program_id(0) == 0)
    def _():
        state[...] = start[...].astype(F32)

    do = d_out[...]
    weights = (mm(q[...], k[...], NT) * mask[...]).astype(BF16)
    d_v[...] = mm(weights, do, TN)
    d_scores = mm(do, v[...], NT).astype(BF16).astype(F32)
    d_scores = (d_scores * mask[...]).astype(BF16)
    d_k[...] = mm(d_scores, q[...], TN)
    far = mm(do, state[...].astype(BF16), NT).astype(BF16).astype(F32)
    dq = mm(d_scores, k[...], NN) + far * q_decay[...]
    dq = dq.astype(BF16).astype(F32)
    d_q[...] = turn(dq, cosine[...], -sine[...]).astype(BF16)
    state[...] = params[0] * state[...] + mm(scaled(k[...], k_decay[...]), v[...], TN)


def outer_back_kernel(
    roles, params, q, k, v, d_out, d_q, d_k, d_v, q_decay, k_decay, start, cosine, sine, *refs
):
    refs = list(refs)
    state = refs.pop()
    v_a = None if "va" in roles else refs.pop()
    by_unit = refs.pop()

    @pl.when(pl.program_id(0) == 0)
    def _():
        state[...] = start[...].astype(F32)

    low = state[...].astype(BF16)
    far = mm(v[...], low, NT).astype(BF16).astype(F32)
    dk = (d_k[...] + far * k_decay[...]).astype(BF16).astype(F32)
    dk = turn(dk, cosine[...], -sine[...]).astype(BF16)
    dv = (d_v[...] + mm(scaled(k[...], k_decay[...]), low, NN)).astype(BF16)
    for n, role in enumerate(roles):
        if role == "q":
            value = d_q[...]
        elif role == "k":
            value = dk
        elif role == "va":
            value = dv[:, :DK]
        elif role == "vb":
            value = dv[:, DK:]
        elif role == "xv":
            value = refs.pop(0)[...]
        else:
            value = select(params, refs.pop(0), refs.pop(0)).astype(BF16)
        by_unit[:, n * DK : (n + 1) * DK] = value
    if v_a is not None:
        v_a[...] = dv[:, :DK]
    state[...] = params[0] * state[...] + mm(scaled(q[...], q_decay[...]), d_out[...], TN)


def head_call(kernel, grid, operands, outputs, scratch, flops):
    arrays = [t[0] for t in operands]
    size = sum(t.size * t.dtype.itemsize for t in arrays + [t[0] for t in outputs])
    return pl.pallas_call(
        kernel,
        grid=(grid,),
        in_specs=[
            pl.BlockSpec(memory_space=pltpu.SMEM) if block is None else pl.BlockSpec(block, where)
            for _, block, where in operands
        ],
        out_specs=[pl.BlockSpec(block, where) for _, block, where in outputs],
        scratch_shapes=scratch,
        out_shape=[t[0] for t in outputs],
        compiler_params=pltpu.CompilerParams(vmem_limit_bytes=56 * 2**20),
        cost_estimate=pl.CostEstimate(flops=flops, bytes_accessed=size, transcendentals=0),
    )(*arrays)


def place_kernel(parts, target, source, *refs):
    out = refs[-1]
    code = source[pl.program_id(1)]
    for i, part in enumerate(parts):

        @pl.when(code == i)
        def _(part=part):
            row = 0
            for n in part:
                piece = refs[n]
                out[row : row + piece.shape[0], :] = piece[...].astype(F32)
                row += piece.shape[0]


def place_blocks(parts, target, source, shape, block, where, outer=1):
    flat, index = [], []
    for part in parts:
        for piece in part:
            if not any(piece is t for t in flat):
                flat.append(piece)
        index.append([next(n for n, t in enumerate(flat) if t is piece) for piece in part])
    return pl.pallas_call(
        functools.partial(place_kernel, index),
        grid_spec=pltpu.PrefetchScalarGridSpec(
            num_scalar_prefetch=2,
            grid=(outer, target.shape[0]),
            in_specs=[
                pl.BlockSpec((t.shape[0], t.shape[1] // outer), lambda o, n, target, source: (0, o))
                for t in flat
            ],
            out_specs=pl.BlockSpec(block, lambda o, n, target, source: where(o, target[n])),
        ),
        out_shape=jax.ShapeDtypeStruct(shape, F32),
        compiler_params=pltpu.CompilerParams(vmem_limit_bytes=48 * 2**20),
    )(target.astype(jnp.int32), source.astype(jnp.int32), *flat)


def local(
    tokens,
    cotangent,
    gain_attn,
    gain_ffn,
    mixer_in,
    mixer_out,
    ffn_in,
    ffn_out,
    segment_order,
    decay_index,
):
    rows, width = tokens.shape
    group = lax.axis_size("seq")
    segments = lax.axis_size("shard")
    heads = decay_index.shape[0]
    local_heads = heads // group
    seg_len = rows * group
    blk = min(512, seg_len)
    blocks = seg_len // blk
    vcols = local_heads * DV
    s = lax.axis_index("seq")
    j = lax.axis_index("shard")

    def swap(v, d):
        return lax.ppermute(v, "seq", [(i, i ^ d) for i in range(group)])

    def cross(v, d):
        return lax.ppermute(v, "shard", [(i, i ^ d) for i in range(segments)])

    def pick(v, i):
        return lax.dynamic_index_in_dim(v, i, 0, keepdims=False)

    def spread(v):
        if group == 4:
            h = v.shape[0] // 2
            r1 = swap(v, 1)
            r2 = swap(v, 2)
            return [(v,), (r1,), (r2,), (swap(r1[:h], 2), swap(r2[h:], 1))]
        return [(v,)] + [(swap(v, d),) for d in range(1, group)]

    def ordered(parts):
        r = parts[0][0].shape[0]
        out = jnp.zeros((group * r,) + parts[0][0].shape[1:], parts[0][0].dtype)
        for d, part in enumerate(parts):
            row = (s ^ d) * r
            for piece in part:
                out = lax.dynamic_update_slice_in_dim(out, piece, row, 0)
                row = row + piece.shape[0]
        return out

    def gather_near(v):
        return jnp.concatenate([piece for part in spread(v) for piece in part], axis=0)

    def gather_seq(v):
        return ordered(spread(v))

    def scatter_sum(blk_of, beside1=(), beside2=()):
        if group == 4:
            b0, b1, b2, b3 = (blk_of(d) for d in range(4))
            h = b0.shape[0] // 2
            b0 = b0.astype(F32)
            ra = swap(jnp.concatenate([b1[:h], b3[:h]], axis=0), 1)
            rb = swap(jnp.concatenate([b2[h:], b3[h:]], axis=0), 2)
            ra, rb, *beside1 = tie(ra, rb, *beside1)
            ra, rb = ra.astype(F32), rb.astype(F32)
            qa = swap((b2[:h].astype(F32) + ra[h:]).astype(BF16), 2)
            qb = swap((b1[h:].astype(F32) + rb[h:]).astype(BF16), 1)
            qa, qb, *beside2 = tie(qa, qb, *beside2)
            total = jnp.concatenate(
                [b0[:h] + ra[:h] + qa.astype(F32), b0[h:] + rb[:h] + qb.astype(F32)], axis=0
            )
            return (total, *beside1, *beside2)
        total = blk_of(0).astype(F32)
        for d in range(1, group):
            total = total + swap(blk_of(d), d).astype(F32)
        return (total, *beside1, *beside2)

    def scatter_near(v, beside1=(), beside2=()):
        return scatter_sum(lambda d: v[d * rows : (d + 1) * rows], beside1, beside2)

    def scatter_seq(v):
        return scatter_sum(lambda d: lax.dynamic_slice_in_dim(v, (s ^ d) * rows, rows, 0))[0]

    def gather_shard(v):
        return lax.all_gather(v, "shard", axis=0, tiled=True)

    def reduce_shard(v):
        return lax.psum_scatter(v, "shard", scatter_dimension=0, tiled=True)

    balanced = group == 4 and local_heads == 2 and segments == 8
    units = mixer_in.reshape(-1, DK, width)
    if balanced:
        keep, give, back, lend = (jnp.asarray(t) for t in balanced_tables())
        core = j % 2
    else:
        keep, give, place, held, back, lend = (
            jnp.asarray(t) for t in unit_tables(group, local_heads, segments)
        )

    def offered(h):
        kept, given = keep[h, j, s], give[h, j, s]
        if balanced and h == 1:
            cut = mixer_in.reshape(-1, DK // 2, width)
            own = pick(cut, 2 * jnp.maximum(kept, 0) + core)
            given = cross(pick(cut, 2 * given + 1 - core), 1)
        else:
            own = pick(units, jnp.maximum(kept, 0))
            given = cross(pick(units, given), 1)
        return jnp.where(kept >= 0, own, given)

    sub = ffn_in.shape[0] // group
    ffn_out_cut = ffn_out.reshape(ffn_out.shape[0], segments // 2, group, sub)

    my_rank = jnp.sum(jnp.where(jnp.arange(segments) == j, segment_order, 0))
    all_logs = jnp.log1p(-jnp.exp2(-(5.0 + decay_index.astype(F32))))
    logs = lax.dynamic_index_in_dim(all_logs.reshape(local_heads, group), s, 1, keepdims=False)
    half = DK // 2
    inv_freq = jnp.exp(-jnp.log(10000.0) * jnp.arange(half).astype(F32) / half)
    positions = my_rank * seg_len + jnp.arange(seg_len, dtype=jnp.int32)
    angles = positions.astype(F32)[:, None] * inv_freq[None, :]
    cosine = jnp.cos(angles)
    sine = jnp.sin(angles)
    steps = jnp.arange(blk).astype(F32)
    gap = steps[:, None] - steps[None, :]
    masks = jnp.where(
        gap[None] >= 0.0, jnp.exp(jnp.maximum(gap, 0.0)[None] * logs[:, None, None]), 0.0
    )
    q_decays = jnp.exp((steps + 1.0)[None, :] * logs[:, None])[..., None]
    k_decays = jnp.exp((blk - 1.0 - steps)[None, :] * logs[:, None])[..., None]
    block_decays = jnp.exp(blk * logs)

    xf = tokens.astype(F32)
    normed = gather_seq(rms_scale(xf, gain_attn).astype(BF16))
    d_ffn = gather_near(cotangent)
    slots = [gather_shard(offered(0))]
    slots[0], normed, d_ffn, cosine, sine, masks, q_decays, k_decays = tie(
        slots[0], normed, d_ffn, cosine, sine, masks, q_decays, k_decays
    )
    for h in range(1, local_heads):
        slots.append(gather_shard(offered(h)))
    mixer_out_cut = jnp.concatenate(
        [
            lax.dynamic_slice_in_dim(mixer_out, (h * group + s) * DV, DV, 1)
            for h in range(local_heads)
        ],
        axis=1,
    )
    mixer_out_cut, slots[0] = tie(mixer_out_cut, slots[0])
    w_out = gather_shard(mixer_out_cut)
    later = [
        lax.dynamic_slice_in_dim(ffn_in, s * sub, sub, 0),
        lax.dynamic_index_in_dim(ffn_out_cut, s, 2, keepdims=False).reshape(ffn_out.shape[0], -1),
    ]
    inner_cols = later[1].shape[1]

    ranks = segment_order
    piece = DK // segments

    def exchange_states(hs, totals, reverse, beside=()):
        cut = jnp.concatenate([t.reshape(segments, piece, DV) for t in totals], axis=1)
        got = lax.all_to_all(cut, "shard", split_axis=0, concat_axis=0, tiled=True)
        got, *beside = tie(got, *beside)
        apart = ranks[:, None] - ranks[None, :] - 1
        if reverse:
            apart = -apart - 2
        distance = apart.astype(F32)
        joined = []
        for n, h in enumerate(hs):
            coef = jnp.where(
                distance >= 0.0, jnp.exp(jnp.maximum(distance, 0.0) * seg_len * logs[h]), 0.0
            )
            part = got[:, n * piece : (n + 1) * piece].astype(F32)
            joined.append(jnp.sum(coef[..., None, None] * part[None], axis=1).astype(BF16))
        joined = jnp.concatenate(joined, axis=1)
        back_cut = lax.all_to_all(joined, "shard", split_axis=0, concat_axis=0, tiled=True)
        states = [
            back_cut[:, n * piece : (n + 1) * piece].reshape(DK, DV) for n in range(len(hs))
        ]
        return (states, *beside)

    def whole(n):
        return (0, 0)

    def ahead(n):
        return (n, 0)

    def behind(n):
        return (blocks - 1 - n, 0)

    def shaped(columns, kind, r=seg_len):
        return jax.ShapeDtypeStruct((r, columns), kind)

    state_scratch = [pltpu.VMEM((DK, DV), F32)]
    half_block = (blk, half)
    unit_block, v_block = (blk, DK), (blk, DV)
    ret_flops = 2 * seg_len * (DK + DV) * (blk + DK)
    low = s < group // 2
    if balanced:
        roles = [["q", "k", "va", "vb", "xv", "g", "g", "g"], ["q", "k", "vb", "g"]]
    else:
        roles = [["q", "k", "va", "vb", "g", "g"]] * local_heads
    params = [
        (jnp.stack([block_decays[h], low.astype(F32)]), None, None) for h in range(local_heads)
    ]
    heads_kept = []
    extra_v = None
    for h in range(local_heads):
        if balanced:
            weights = slots[h]
        else:
            cut = slots[h].reshape(-1, DK, width)
            weights = jnp.concatenate([pick(cut, place[h, s, c]) for c in range(6)], axis=0)
        carried = "va" not in roles[h]
        gate_count = roles[h].count("g")
        q, k, v, total, gates, *extra = head_call(
            functools.partial(project_kernel, blk, roles[h], carried),
            len(roles[h]) // 2,
            [
                params[h],
                (normed, (seg_len, width), whole),
                (weights, (2 * DK, width), ahead),
                (cosine, (seg_len, half), whole),
                (sine, (seg_len, half), whole),
                (k_decays[h], (blk, 1), whole),
            ]
            + ([(extra_v, (seg_len, DK), whole)] if carried else []),
            [
                (shaped(DK, BF16), (seg_len, DK), whole),
                (shaped(DK, BF16), (seg_len, DK), whole),
                (shaped(DV, BF16), (seg_len, DV), whole),
                (shaped(DV, BF16, DK), (DK, DV), whole),
                (shaped(gate_count * DK, F32), (seg_len, gate_count * DK), whole),
            ]
            + ([(shaped(DK, BF16), (seg_len, DK), whole)] if "xv" in roles[h] else []),
            [pltpu.VMEM((seg_len, 2 * DK), F32)],
            2 * seg_len * width * len(roles[h]) * DK,
        )
        extra_v = extra[0] if extra else None
        (state_in,) = exchange_states([h], [total], False)[0]
        if h + 1 < local_heads:
            slots[h + 1], state_in, *later[:] = tie(slots[h + 1], state_in, *later)
        heads_kept.append((weights, q, k, v, gates, state_in))

    def columns(v, c, order):
        return (v, unit_block, lambda n, c=c: (order(n)[0], c))

    if balanced:
        gates0, gates1 = heads_kept[0][4], heads_kept[1][4]
        swapped = swap(jnp.where(low, gates1, gates0[:, :DK]).astype(BF16), 2)

        def gate_operands(h, order):
            if h == 0:
                four = (gates0, 0), (gates0, 1), (swapped, 0), (gates0, 2)
            else:
                four = (gates0, 1), (gates1, 0), (gates0, 2), (swapped, 0)
            return [columns(v, c, order) for v, c in four]

    else:

        def gate_operands(h, order):
            return [columns(heads_kept[h][4], c, order) for c in (0, 0, 1, 1)]

    kept = []
    for h in range(local_heads):
        weights, q, k, v, gates, state_in = heads_kept[h]
        hidden, mixed, retained = head_call(
            retain_kernel,
            blocks,
            [
                params[h],
                (q, unit_block, ahead),
                (k, unit_block, ahead),
                (v, v_block, ahead),
                *gate_operands(h, ahead),
                (masks[h], (blk, blk), whole),
                (q_decays[h], (blk, 1), whole),
                (k_decays[h], (blk, 1), whole),
                (state_in, (DK, DV), whole),
            ],
            [
                (shaped(DV, BF16), v_block, ahead),
                (shaped(DV, BF16), v_block, ahead),
                (shaped(DV, F32), v_block, ahead),
            ],
            state_scratch,
            ret_flops,
        )
        kept.append((retained, mixed, hidden))
    hidden = jnp.concatenate([t[-1] for t in kept], axis=1)
    w_ffn_in, w_ffn_out = (gather_shard(t) for t in later)

    resid = xf + scatter_seq(dot_nt(hidden, w_out, BF16))
    normed2 = gather_near(rms_scale(resid, gain_ffn).astype(BF16))
    proj2 = dot_nt(normed2, w_ffn_in)
    first, second = proj2[:, :inner_cols], proj2[:, inner_cols:]
    inner2 = gated_gelu(first, second).astype(BF16)

    g_ffn_out, d_ffn = tie(dot_tn(d_ffn, inner2, BF16), d_ffn)
    scattered = {"ffn_out": reduce_shard(g_ffn_out)}
    d_inner2 = dot_nn(d_ffn, w_ffn_out)
    ignored2, gelu_back = jax.vjp(gated_gelu, first, second)
    d_first, d_second = gelu_back(d_inner2)
    dproj2 = jnp.concatenate([d_first, d_second], axis=1).astype(BF16)
    d_normed2, g_ffn_in = scatter_near(
        dot_nn(dproj2, w_ffn_in, BF16), (dot_tn(dproj2, normed2, BF16),)
    )
    scattered["ffn_in"] = reduce_shard(g_ffn_in)
    ignored3, norm2_back = jax.vjp(rms_scale, resid, gain_ffn)
    d_resid_part, d_gain_ffn = norm2_back(d_normed2)
    d_resid = cotangent.astype(F32) + d_resid_part
    d_attn = gather_seq(d_resid.astype(BF16))
    d_attn, scattered["ffn_out"] = tie(d_attn, scattered["ffn_out"])
    parts_ffn_out = spread(scattered["ffn_out"])
    d_hidden = dot_nn(d_attn, w_out)
    hidden, d_hidden = tie(hidden, d_hidden)
    g_mixer_out = dot_tn(d_attn, hidden, BF16)

    def tie_parts(v, parts):
        flat = tie(v, *(piece for part in parts for piece in part))
        rest = list(flat[1:])
        return flat[0], [tuple(rest.pop(0) for _ in part) for part in parts]

    turns = [(cosine, half_block), (sine, half_block)]
    firsts = []
    for h in range(local_heads):
        weights, q, k, v, gates, state_in = heads_kept[h]
        retained, mixed, ignored4 = kept[h]
        firsts.append(
            head_call(
                gate_back_kernel,
                blocks,
                [
                    params[h],
                    (d_hidden, v_block, lambda n, h=h: (blocks - 1 - n, h)),
                    *gate_operands(h, behind),
                    (mixed, v_block, behind),
                    (retained, v_block, behind),
                    (q, unit_block, behind),
                    (q_decays[h], (blk, 1), whole),
                ],
                [
                    (shaped(DV, BF16), v_block, behind),
                    (shaped(DV, BF16), v_block, behind),
                    (shaped(DV, BF16, DK), (DK, DV), whole),
                ],
                state_scratch,
                2 * seg_len * DK * DV,
            )
        )
    d_gates = [t[0] for t in firsts]
    if balanced:
        d_swapped = swap(jnp.where(low, d_gates[0][:, DK:], d_gates[1][:, DK:]), 2)
        d_gate_pairs = [
            [
                ((d_gates[0], 0), (d_swapped, 0)),
                ((d_gates[1], 0), (d_gates[0], 0)),
                ((d_gates[1], 1), (d_gates[0], 1)),
            ],
            [((d_swapped, 0), (d_gates[1], 0))],
        ]
    else:
        d_gate_pairs = [[((t, 0), (t, 0)), ((t, 1), (t, 1))] for t in d_gates]
    inners = []
    for h in range(local_heads):
        weights, q, k, v, gates, state_in = heads_kept[h]
        inners.append(
            head_call(
                inner_back_kernel,
                blocks,
                [
                    params[h],
                    (q, unit_block, ahead),
                    (k, unit_block, ahead),
                    (v, v_block, ahead),
                    (firsts[h][1], v_block, ahead),
                    (masks[h], (blk, blk), whole),
                    (q_decays[h], (blk, 1), whole),
                    (k_decays[h], (blk, 1), whole),
                    (state_in, (DK, DV), whole),
                    *((*t, ahead) for t in turns),
                ],
                [
                    (shaped(DK, BF16), unit_block, ahead),
                    (shaped(DK, F32), unit_block, ahead),
                    (shaped(DV, F32), v_block, ahead),
                ],
                state_scratch,
                2 * ret_flops,
            )
        )
    g_mixer_out, *totals = tie(g_mixer_out, *(t[2] for t in firsts))
    scattered["mixer_out"] = reduce_shard(g_mixer_out)
    grads_out, inner2, scattered["ffn_in"], *flat = exchange_states(
        range(local_heads),
        totals,
        True,
        (inner2, scattered["ffn_in"], *(t for inner in inners for t in inner)),
    )
    inners = [flat[3 * h : 3 * h + 3] for h in range(local_heads)]
    parts_ffn_in = spread(scattered["ffn_in"])
    if group == 4:
        grads_out[-1], *pieces = tie(grads_out[-1], *(parts_ffn_in[d][0] for d in range(3)))
        parts_ffn_in[:3] = [(t,) for t in pieces]
    output = (resid + scatter_near(dot_nt(inner2, w_ffn_out, BF16))[0]).astype(BF16)
    by_units = [None] * local_heads
    extra_v = None
    for h in reversed(range(local_heads)):
        weights, q, k, v, gates, state_in = heads_kept[h]
        d_out = firsts[h][1]
        d_q, d_k, d_v = inners[h]
        count = len(roles[h])
        lone = "va" not in roles[h]
        by_units[h], *extra = head_call(
            functools.partial(outer_back_kernel, roles[h]),
            blocks,
            [
                params[h],
                (q, unit_block, behind),
                (k, unit_block, behind),
                (v, v_block, behind),
                (d_out, v_block, behind),
                (d_q, unit_block, behind),
                (d_k, unit_block, behind),
                (d_v, v_block, behind),
                (q_decays[h], (blk, 1), whole),
                (k_decays[h], (blk, 1), whole),
                (grads_out[h], (DK, DV), whole),
                *((*t, behind) for t in turns),
            ]
            + ([(extra_v, unit_block, behind)] if "xv" in roles[h] else [])
            + [columns(v, c, behind) for pair in d_gate_pairs[h] for v, c in pair],
            [(shaped(count * DK, BF16), (blk, count * DK), behind)]
            + ([(shaped(DK, BF16), unit_block, behind)] if lone else []),
            state_scratch,
            6 * seg_len * DK * DV,
        )
        extra_v = extra[0] if extra else None

    by_units[0], parts_ffn_out = tie_parts(by_units[0], parts_ffn_out)
    by_units[-1], parts_ffn_in = tie_parts(by_units[-1], parts_ffn_in)
    by_units[-1], scattered["mixer_out"] = tie(by_units[-1], scattered["mixer_out"])
    parts_mixer_out = spread(scattered["mixer_out"])
    g_slots = []
    for h in range(local_heads):
        g_unit = dot_tn(by_units[h], normed, BF16)
        if not balanced:
            cut = g_unit.reshape(-1, DK, width)
            g_unit = jnp.concatenate(
                [pick(cut, jnp.maximum(held[h, c, s], 0)) for c in range(segments)], axis=0
            )
        if h == local_heads - 1:
            tile = 512
            rights = [t[0] for t in heads_kept]
            (d_normed,) = head_call(
                functools.partial(join_kernel, local_heads),
                width // tile,
                [(t, t.shape, whole) for t in by_units]
                + [(t, (t.shape[0], tile), lambda n: (0, n)) for t in rights],
                [(shaped(width, BF16), (seg_len, tile), lambda n: (0, n))],
                [],
                2 * seg_len * width * sum(t.shape[0] for t in rights),
            )
            g_unit, d_normed = tie(g_unit, d_normed)
        g_slots.append(reduce_shard(g_unit))
    d_normed = scatter_seq(d_normed)

    ignored8, norm1_back = jax.vjp(rms_scale, xf, gain_attn)
    d_x_part, d_gain_attn = norm1_back(d_normed)
    input_grad = (d_resid + d_x_part).astype(BF16)
    gains = jnp.concatenate([d_gain_attn, d_gain_ffn])[None]
    near = jnp.arange(group)
    g_ffn_in = place_blocks(
        parts_ffn_in, s ^ near, near, ffn_in.shape, (sub, width), lambda o, n: (n, 0)
    )
    if sub % 128 == 0:
        g_ffn_out = place_blocks(
            parts_ffn_out,
            s ^ near,
            near,
            ffn_out.shape,
            (ffn_out.shape[0], sub),
            lambda o, n: (0, o * group + n),
            outer=segments // 2,
        )
    else:
        g_ffn_out = jnp.transpose(
            ordered(parts_ffn_out).reshape(group, ffn_out.shape[0], segments // 2, sub),
            (1, 2, 0, 3),
        ).reshape(ffn_out.shape).astype(F32)

    parts = []
    for h in range(local_heads):
        last = h == local_heads - 1
        if h == 0:
            g_slots[h], g_ffn_in, g_ffn_out, input_grad = tie(
                g_slots[h], g_ffn_in, g_ffn_out, input_grad
            )
        if last:
            pieces = parts_mixer_out[0]
            pieces0, parts = tie_parts(pieces[0], parts)
            parts_mixer_out[0] = (pieces0, *pieces[1:])
            g_mixer_out = place_blocks(
                parts_mixer_out,
                s ^ near,
                near,
                mixer_out.shape,
                (mixer_out.shape[0], DV),
                lambda o, n: (0, o * group + n),
                outer=local_heads,
            )
            g_slots[h], g_mixer_out, output = tie(g_slots[h], g_mixer_out, output)
            gains, g_slots[h] = tie(gains, g_slots[h])
            gains = jnp.sum(lax.all_gather(gains, ("shard", "seq"), axis=0, tiled=True), axis=0)
            gain_attn_grad, gain_ffn_grad = gains[:width], gains[width:]
        here = spread(g_slots[h])
        if balanced and last:
            there = [tuple(cross(piece, 1) for piece in part) for part in here]
            parts += [a + b for a, b in zip(here, there)] + [b + a for a, b in zip(here, there)]
        else:
            lend_here = lend[j] if balanced else lend[h, j]
            stack = jnp.stack([jnp.concatenate(part, axis=0) for part in here])
            parts += here + [
                (cross(pick(stack, s ^ lend_here[n]), 1),) for n in range(lend_here.shape[0])
            ]
    found = back[j]
    if balanced:
        spare = lend.shape[-1]
        source = jnp.where(
            found[:, 0] == 0,
            s ^ found[:, 1],
            jnp.where(
                found[:, 0] == 1,
                group + found[:, 1],
                group + spare + core * group + (s ^ found[:, 1]),
            ),
        )
    else:
        source = found[:, 0] * (group + lend.shape[-1]) + jnp.where(
            found[:, 2] < 0, s ^ found[:, 1], group + found[:, 2]
        )
    g_mixer_in = place_blocks(
        parts,
        jnp.arange(source.shape[0]),
        source,
        mixer_in.shape,
        (DK, width),
        lambda o, n: (n, 0),
    )
    return (
        output,
        input_grad,
        gain_attn_grad,
        gain_ffn_grad,
        g_mixer_in,
        g_mixer_out,
        g_ffn_in,
        g_ffn_out,
    )


def solution(mesh):
    return jax.shard_map(
        local,
        mesh=mesh,
        in_specs=(
            P(("shard", "seq"), None),
            P(("shard", "seq"), None),
            P(),
            P(),
            P("shard", None),
            P("shard", None),
            P("shard", None),
            P("shard", None),
            P(),
            P(),
        ),
        out_specs=(
            P(("shard", "seq"), None),
            P(("shard", "seq"), None),
            P(),
            P(),
            P("shard", None),
            P("shard", None),
            P("shard", None),
            P("shard", None),
        ),
        check_vma=False,
    )
```

```python
import functools

import jax
import jax.numpy as jnp
import numpy as np
from jax import lax
from jax.experimental import pallas as pl
from jax.experimental.pallas import tpu as pltpu
from jax.sharding import PartitionSpec as P

DK = 256
DV = 512
FF = 4096
QK = 2048
V = 4096


EPS_NORM = 1e-06
EPS_GROUP = 1e-05

F32 = jnp.float32
BF16 = jnp.bfloat16


def dot_nt(left, right, kind=F32):
    return lax.dot_general(
        left, right, (((1,), (1,)), ((), ())), preferred_element_type=F32
    ).astype(kind)


def dot_nn(left, right, kind=F32):
    return lax.dot_general(
        left, right, (((1,), (0,)), ((), ())), preferred_element_type=F32
    ).astype(kind)


def dot_tn(left, right, kind=F32):
    return lax.dot_general(
        left, right, (((0,), (0,)), ((), ())), preferred_element_type=F32
    ).astype(kind)


def rms_scale(v, gain):
    return v * lax.rsqrt(jnp.mean(v * v, axis=-1, keepdims=True) + EPS_NORM) * gain


def gated_gelu(first, second):
    return jax.nn.gelu(first) * second


def unit_owners(heads):
    owners = [(n, 0) for n in range(heads)] + [(n, 1) for n in range(heads)]
    for base in (2, 4):
        owners += [(n, base + half) for n in range(heads) for half in range(2)]
    return owners


def balanced_tables():
    group, segments, per_shard = 4, 8, 6
    number = {owner: u for u, owner in enumerate(unit_owners(8))}
    keep = np.full((2, segments, group), -1, np.int32)
    give = np.zeros((2, segments, group), np.int32)
    back = np.zeros((segments, per_shard, 2), np.int32)
    lend = [[] for _ in range(segments)]
    seen = set()
    for s in range(group):
        a, b = s, s + 4
        if s < 2:
            gates = [(a, 4), (b, 4), (b, 5)], (b + 2, 5)
        else:
            gates = [(a - 2, 5), (a, 4), (a, 5)], (b, 4)
        first = [(a, 0), (a, 1), (a, 2), (a, 3), (b, 2)] + gates[0]
        second = [(b, 0), (b, 1), (b, 3), gates[1]]
        for slot, owner in enumerate(first):
            home, index = divmod(number[owner], per_shard)
            seen.add(number[owner])
            assert home // 2 == slot // 2
            if home == slot:
                keep[0, slot, s] = index
                back[home, index] = (0, s)
            else:
                give[0, home, s] = index
                back[home, index] = (1, len(lend[slot]))
                lend[slot].append(s)
        for chip, owner in enumerate(second):
            home, index = divmod(number[owner], per_shard)
            seen.add(number[owner])
            assert home // 2 == chip
            keep[1, home, s] = index
            give[1, home, s] = index
            back[home, index] = (2, s)
    assert len(seen) == segments * per_shard
    most = max(len(t) for t in lend)
    return keep, give, back, np.asarray([(t + [0] * most)[:most] for t in lend], np.int32)


def unit_tables(group, local_heads, segments):
    heads = group * local_heads
    owners = unit_owners(heads)
    per_shard = len(owners) // segments
    keep = np.full((local_heads, segments, group), -1, np.int32)
    give = np.zeros((local_heads, segments, group), np.int32)
    place = np.zeros((local_heads, group, 6), np.int32)
    held = np.full((local_heads, segments, group), -1, np.int32)
    slot_of = {}
    for chip in range(segments // 2):
        for head in range(heads):
            h, s = divmod(head, group)
            span = range(2 * per_shard * chip, 2 * per_shard * (chip + 1))
            mine = [u for u in span if owners[u][0] == head]
            assert len(mine) <= 2
            for n, u in enumerate(mine):
                home = u // per_shard
                slot = home if len(mine) == 1 else 2 * chip + n
                if slot == home:
                    keep[h, slot, s] = u % per_shard
                else:
                    give[h, home, s] = u % per_shard
                place[h, s, owners[u][1]] = slot
                held[h, slot, s] = owners[u][1]
                slot_of[u] = slot
    lends = [[[] for _ in range(segments)] for _ in range(local_heads)]
    back = np.zeros((segments, per_shard, 3), np.int32)
    for u, (head, _) in enumerate(owners):
        home = u // per_shard
        h, s = divmod(head, group)
        back[home, u % per_shard] = (h, s, -1)
        if slot_of[u] != home:
            assert slot_of[u] == home ^ 1
            back[home, u % per_shard, 2] = len(lends[h][home ^ 1])
            lends[h][home ^ 1].append(s)
    most = max(1, max(len(t) for row in lends for t in row))
    lend = np.asarray(
        [[(t + [0] * most)[:most] for t in row] for row in lends], np.int32
    )
    return keep, give, place, held, back, lend


def tie(*values):
    return lax.optimization_barrier(values)


def mm(left, right, dims):
    return lax.dot_general(left, right, (dims, ((), ())), preferred_element_type=F32)


NN = ((1,), (0,))
NT = ((1,), (1,))
TN = ((0,), (0,))


def turn(v, cosine, sine):
    half = v.shape[-1] // 2
    first, second = v[:, :half], v[:, half:]
    return jnp.concatenate(
        [first * cosine - second * sine, second * cosine + first * sine], axis=-1
    )


def scaled(v, decay):
    return (v.astype(F32) * decay).astype(BF16)


def project_kernel(blk, roles, carried, params, x, w, cosine, sine, k_decay, *refs):
    if carried:
        v_a, *refs = refs
    q, k, v, total, gates, *rest = refs
    y = rest[-1]
    rows = y.shape[0]
    y[...] = mm(x[...], w[...], NT)

    def put(role, part, gate_at):
        value = y[:, part * DK : (part + 1) * DK]
        if role == "q":
            q[...] = turn(value, cosine[...], sine[...]).astype(BF16)
        elif role == "k":
            k[...] = turn(value, cosine[...], sine[...]).astype(BF16)
        elif role == "va":
            v[:, :DK] = value.astype(BF16)
        elif role == "vb":
            v[:, DK:] = value.astype(BF16)
        elif role == "xv":
            rest[0][...] = value.astype(BF16)
        else:
            gates[:, gate_at * DK : (gate_at + 1) * DK] = value

    for step in range(len(roles) // 2):

        @pl.when(pl.program_id(0) == step)
        def _(step=step):
            for part in range(2):
                at = 2 * step + part
                put(roles[at], part, roles[:at].count("g"))
            if step == 1:
                if carried:
                    v[:, :DK] = v_a[...]
                state = jnp.zeros(total.shape, F32)
                for r in range(0, rows, blk):
                    kd = scaled(k[r : r + blk, :], k_decay[...])
                    state = params[0] * state + mm(kd, v[r : r + blk, :], TN)
                total[...] = state.astype(BF16)


def join_kernel(count, *refs):
    out = refs[-1]
    total = mm(refs[0][...], refs[count][...], NN)
    for n in range(1, count):
        total += mm(refs[n][...], refs[count + n][...], NN)
    out[...] = total.astype(out.dtype)


def select(params, low, high):
    return jnp.where(params[1] > 0.5, low[...].astype(F32), high[...].astype(F32))


def retain_kernel(
    params, q, k, v, low_a, high_a, low_b, high_b, mask, q_decay, k_decay, start,
    hidden, mixed, kept, state,
):
    @pl.when(pl.program_id(0) == 0)
    def _():
        state[...] = start[...].astype(F32)

    weights = (mm(q[...], k[...], NT) * mask[...]).astype(BF16)
    o = mm(weights, v[...], NN)
    o += mm(scaled(q[...], q_decay[...]), state[...].astype(BF16), NN)
    state[...] = params[0] * state[...] + mm(scaled(k[...], k_decay[...]), v[...], TN)
    kept[...] = o
    o = o - jnp.mean(o, axis=-1, keepdims=True)
    o = o * lax.rsqrt(jnp.mean(o * o, axis=-1, keepdims=True) + EPS_GROUP)
    low = o.astype(BF16)
    mixed[...] = low
    for n, (one, two) in enumerate(((low_a, high_a), (low_b, high_b))):
        columns = slice(n * DK, (n + 1) * DK)
        g = select(params, one, two)
        hidden[:, columns] = (g * jax.nn.sigmoid(g) * low[:, columns].astype(F32)).astype(BF16)


def gate_back_kernel(
    params, d_hidden, low_a, high_a, low_b, high_b, mixed, kept, q, q_decay,
    d_gate, d_out, total, state,
):
    @pl.when(pl.program_id(0) == 0)
    def _():
        state[...] = jnp.zeros(state.shape, F32)

    g = jnp.concatenate([select(params, low_a, high_a), select(params, low_b, high_b)], axis=1)
    dh = d_hidden[...]
    sig = jax.nn.sigmoid(g)
    d_gate[...] = (dh * mixed[...].astype(F32) * (sig * (1.0 + g * (1.0 - sig)))).astype(BF16)
    dy = (dh * (g * sig)).astype(BF16).astype(F32)
    o = kept[...]
    o = o - jnp.mean(o, axis=-1, keepdims=True)
    inverse = lax.rsqrt(jnp.mean(o * o, axis=-1, keepdims=True) + EPS_GROUP)
    o = o * inverse
    do = inverse * (
        dy
        - jnp.mean(dy, axis=-1, keepdims=True)
        - o * jnp.mean(dy * o, axis=-1, keepdims=True)
    )
    do = do.astype(BF16)
    d_out[...] = do
    state[...] = params[0] * state[...] + mm(scaled(q[...], q_decay[...]), do, TN)
    total[...] = state[...].astype(BF16)


def inner_back_kernel(
    params, q, k, v, d_out, mask, q_decay, k_decay, start, cosine, sine, d_q, d_k, d_v, state
):
    @pl.when(pl.program_id(0) == 0)
    def _():
        state[...] = start[...].astype(F32)

    do = d_out[...]
    weights = (mm(q[...], k[...], NT) * mask[...]).astype(BF16)
    d_v[...] = mm(weights, do, TN)
    d_scores = mm(do, v[...], NT).astype(BF16).astype(F32)
    d_scores = (d_scores * mask[...]).astype(BF16)
    d_k[...] = mm(d_scores, q[...], TN)
    far = mm(do, state[...].astype(BF16), NT).astype(BF16).astype(F32)
    dq = mm(d_scores, k[...], NN) + far * q_decay[...]
    dq = dq.astype(BF16).astype(F32)
    d_q[...] = turn(dq, cosine[...], -sine[...]).astype(BF16)
    state[...] = params[0] * state[...] + mm(scaled(k[...], k_decay[...]), v[...], TN)


def outer_back_kernel(
    roles, params, q, k, v, d_out, d_q, d_k, d_v, q_decay, k_decay, start, cosine, sine, *refs
):
    refs = list(refs)
    state = refs.pop()
    v_a = None if "va" in roles else refs.pop()
    by_unit = refs.pop()

    @pl.when(pl.program_id(0) == 0)
    def _():
        state[...] = start[...].astype(F32)

    low = state[...].astype(BF16)
    far = mm(v[...], low, NT).astype(BF16).astype(F32)
    dk = (d_k[...] + far * k_decay[...]).astype(BF16).astype(F32)
    dk = turn(dk, cosine[...], -sine[...]).astype(BF16)
    dv = (d_v[...] + mm(scaled(k[...], k_decay[...]), low, NN)).astype(BF16)
    for n, role in enumerate(roles):
        if role == "q":
            value = d_q[...]
        elif role == "k":
            value = dk
        elif role == "va":
            value = dv[:, :DK]
        elif role == "vb":
            value = dv[:, DK:]
        elif role == "xv":
            value = refs.pop(0)[...]
        else:
            value = select(params, refs.pop(0), refs.pop(0)).astype(BF16)
        by_unit[:, n * DK : (n + 1) * DK] = value
    if v_a is not None:
        v_a[...] = dv[:, :DK]
    state[...] = params[0] * state[...] + mm(scaled(q[...], q_decay[...]), d_out[...], TN)


def head_call(kernel, grid, operands, outputs, scratch, flops):
    arrays = [t[0] for t in operands]
    size = sum(t.size * t.dtype.itemsize for t in arrays + [t[0] for t in outputs])
    return pl.pallas_call(
        kernel,
        grid=(grid,),
        in_specs=[
            pl.BlockSpec(memory_space=pltpu.SMEM) if block is None else pl.BlockSpec(block, where)
            for _, block, where in operands
        ],
        out_specs=[pl.BlockSpec(block, where) for _, block, where in outputs],
        scratch_shapes=scratch,
        out_shape=[t[0] for t in outputs],
        compiler_params=pltpu.CompilerParams(vmem_limit_bytes=56 * 2**20),
        cost_estimate=pl.CostEstimate(flops=flops, bytes_accessed=size, transcendentals=0),
    )(*arrays)


def place_kernel(parts, target, source, *refs):
    out = refs[-1]
    code = source[pl.program_id(1)]
    for i, part in enumerate(parts):

        @pl.when(code == i)
        def _(part=part):
            row = 0
            for n in part:
                piece = refs[n]
                out[row : row + piece.shape[0], :] = piece[...].astype(F32)
                row += piece.shape[0]


def place_blocks(parts, target, source, shape, block, where, outer=1):
    flat, index = [], []
    for part in parts:
        for piece in part:
            if not any(piece is t for t in flat):
                flat.append(piece)
        index.append([next(n for n, t in enumerate(flat) if t is piece) for piece in part])
    return pl.pallas_call(
        functools.partial(place_kernel, index),
        grid_spec=pltpu.PrefetchScalarGridSpec(
            num_scalar_prefetch=2,
            grid=(outer, target.shape[0]),
            in_specs=[
                pl.BlockSpec((t.shape[0], t.shape[1] // outer), lambda o, n, target, source: (0, o))
                for t in flat
            ],
            out_specs=pl.BlockSpec(block, lambda o, n, target, source: where(o, target[n])),
        ),
        out_shape=jax.ShapeDtypeStruct(shape, F32),
        compiler_params=pltpu.CompilerParams(vmem_limit_bytes=48 * 2**20),
    )(target.astype(jnp.int32), source.astype(jnp.int32), *flat)


def local(
    tokens,
    cotangent,
    gain_attn,
    gain_ffn,
    mixer_in,
    mixer_out,
    ffn_in,
    ffn_out,
    segment_order,
    decay_index,
):
    rows, width = tokens.shape
    group = lax.axis_size("seq")
    segments = lax.axis_size("shard")
    heads = decay_index.shape[0]
    local_heads = heads // group
    seg_len = rows * group
    blk = min(512, seg_len)
    blocks = seg_len // blk
    vcols = local_heads * DV
    s = lax.axis_index("seq")
    j = lax.axis_index("shard")

    def swap(v, d):
        return lax.ppermute(v, "seq", [(i, i ^ d) for i in range(group)])

    def cross(v, d):
        return lax.ppermute(v, "shard", [(i, i ^ d) for i in range(segments)])

    def pick(v, i):
        return lax.dynamic_index_in_dim(v, i, 0, keepdims=False)

    def spread(v):
        if group == 4:
            h = v.shape[0] // 2
            r1 = swap(v, 1)
            r2 = swap(v, 2)
            return [(v,), (r1,), (r2,), (swap(r1[:h], 2), swap(r2[h:], 1))]
        return [(v,)] + [(swap(v, d),) for d in range(1, group)]

    def ordered(parts):
        r = parts[0][0].shape[0]
        out = jnp.zeros((group * r,) + parts[0][0].shape[1:], parts[0][0].dtype)
        for d, part in enumerate(parts):
            row = (s ^ d) * r
            for piece in part:
                out = lax.dynamic_update_slice_in_dim(out, piece, row, 0)
                row = row + piece.shape[0]
        return out

    def gather_near(v):
        return jnp.concatenate([piece for part in spread(v) for piece in part], axis=0)

    def gather_seq(v):
        return ordered(spread(v))

    def first_step(blk_of):
        b = [blk_of(d) for d in range(4)]
        h = b[0].shape[0] // 2
        ra = swap(jnp.concatenate([b[1][:h], b[3][:h]], axis=0), 1)
        rb = swap(jnp.concatenate([b[2][h:], b[3][h:]], axis=0), 2)
        return b, ra, rb

    def second_step(b, ra, rb):
        h = b[0].shape[0] // 2
        ra, rb = ra.astype(F32), rb.astype(F32)
        qa = swap((b[2][:h].astype(F32) + ra[h:]).astype(BF16), 2)
        qb = swap((b[1][h:].astype(F32) + rb[h:]).astype(BF16), 1)
        top = b[0][:h].astype(F32) + ra[:h] + qa.astype(F32)
        return jnp.concatenate([top, b[0][h:].astype(F32) + rb[:h] + qb.astype(F32)], axis=0)

    def send_blocks(make):
        order = list(range(group - 1, 0, -1))
        got = [swap(make(d).astype(BF16), d) for d in order]
        return make(0), got

    def add_blocks(own, got):
        for t in got:
            own = own + t.astype(F32)
        return own

    def near_rows(v):
        return lambda d: v[d * rows : (d + 1) * rows]

    def seq_rows(v):
        return lambda d: lax.dynamic_slice_in_dim(v, (s ^ d) * rows, rows, 0)

    def gather_shard(v):
        return lax.all_gather(v, "shard", axis=0, tiled=True)

    def reduce_shard(v):
        return lax.psum_scatter(v, "shard", scatter_dimension=0, tiled=True)

    balanced = group == 4 and local_heads == 2 and segments == 8
    units = mixer_in.reshape(-1, DK, width)
    if balanced:
        keep, give, back, lend = (jnp.asarray(t) for t in balanced_tables())
        core = j % 2
    else:
        keep, give, place, held, back, lend = (
            jnp.asarray(t) for t in unit_tables(group, local_heads, segments)
        )

    def offered(h):
        kept, given = keep[h, j, s], give[h, j, s]
        if balanced and h == 1:
            cut = mixer_in.reshape(-1, DK // 2, width)
            own = pick(cut, 2 * jnp.maximum(kept, 0) + core)
            given = cross(pick(cut, 2 * given + 1 - core), 1)
        else:
            own = pick(units, jnp.maximum(kept, 0))
            given = cross(pick(units, given), 1)
        return jnp.where(kept >= 0, own, given)

    sub = ffn_in.shape[0] // group
    ffn_out_cut = ffn_out.reshape(ffn_out.shape[0], segments // 2, group, sub)

    my_rank = jnp.sum(jnp.where(jnp.arange(segments) == j, segment_order, 0))
    all_logs = jnp.log1p(-jnp.exp2(-(5.0 + decay_index.astype(F32))))
    logs = lax.dynamic_index_in_dim(all_logs.reshape(local_heads, group), s, 1, keepdims=False)
    half = DK // 2
    inv_freq = jnp.exp(-jnp.log(10000.0) * jnp.arange(half).astype(F32) / half)
    positions = my_rank * seg_len + jnp.arange(seg_len, dtype=jnp.int32)
    angles = positions.astype(F32)[:, None] * inv_freq[None, :]
    cosine = jnp.cos(angles)
    sine = jnp.sin(angles)
    steps = jnp.arange(blk).astype(F32)
    gap = steps[:, None] - steps[None, :]
    masks = jnp.where(
        gap[None] >= 0.0, jnp.exp(jnp.maximum(gap, 0.0)[None] * logs[:, None, None]), 0.0
    )
    q_decays = jnp.exp((steps + 1.0)[None, :] * logs[:, None])[..., None]
    k_decays = jnp.exp((blk - 1.0 - steps)[None, :] * logs[:, None])[..., None]
    block_decays = jnp.exp(blk * logs)

    xf = tokens.astype(F32)
    normed = gather_seq(rms_scale(xf, gain_attn).astype(BF16))
    d_ffn = gather_near(cotangent)
    slots = [gather_shard(offered(0))]
    slots[0], normed, d_ffn, cosine, sine, masks, q_decays, k_decays = tie(
        slots[0], normed, d_ffn, cosine, sine, masks, q_decays, k_decays
    )
    for h in range(1, local_heads):
        slots.append(gather_shard(offered(h)))
    mixer_out_cut = jnp.concatenate(
        [
            lax.dynamic_slice_in_dim(mixer_out, (h * group + s) * DV, DV, 1)
            for h in range(local_heads)
        ],
        axis=1,
    )
    mixer_out_cut, slots[0] = tie(mixer_out_cut, slots[0])
    w_out = gather_shard(mixer_out_cut)
    later = [
        lax.dynamic_slice_in_dim(ffn_in, s * sub, sub, 0),
        lax.dynamic_index_in_dim(ffn_out_cut, s, 2, keepdims=False).reshape(ffn_out.shape[0], -1),
    ]
    inner_cols = later[1].shape[1]

    ranks = segment_order
    piece = DK // segments

    def exchange_states(hs, totals, reverse, beside=()):
        cut = jnp.concatenate([t.reshape(segments, piece, DV) for t in totals], axis=1)
        got = lax.all_to_all(cut, "shard", split_axis=0, concat_axis=0, tiled=True)
        got, *beside = tie(got, *beside)
        apart = ranks[:, None] - ranks[None, :] - 1
        if reverse:
            apart = -apart - 2
        distance = apart.astype(F32)
        joined = []
        for n, h in enumerate(hs):
            coef = jnp.where(
                distance >= 0.0, jnp.exp(jnp.maximum(distance, 0.0) * seg_len * logs[h]), 0.0
            )
            part = got[:, n * piece : (n + 1) * piece].astype(F32)
            joined.append(jnp.sum(coef[..., None, None] * part[None], axis=1).astype(BF16))
        joined = jnp.concatenate(joined, axis=1)
        back_cut = lax.all_to_all(joined, "shard", split_axis=0, concat_axis=0, tiled=True)
        states = [
            back_cut[:, n * piece : (n + 1) * piece].reshape(DK, DV) for n in range(len(hs))
        ]
        return (states, *beside)

    def whole(n):
        return (0, 0)

    def ahead(n):
        return (n, 0)

    def behind(n):
        return (blocks - 1 - n, 0)

    def shaped(columns, kind, r=seg_len):
        return jax.ShapeDtypeStruct((r, columns), kind)

    state_scratch = [pltpu.VMEM((DK, DV), F32)]
    half_block = (blk, half)
    unit_block, v_block = (blk, DK), (blk, DV)
    ret_flops = 2 * seg_len * (DK + DV) * (blk + DK)
    low = s < group // 2
    if balanced:
        roles = [["q", "k", "va", "vb", "xv", "g", "g", "g"], ["q", "k", "vb", "g"]]
    else:
        roles = [["q", "k", "va", "vb", "g", "g"]] * local_heads
    params = [
        (jnp.stack([block_decays[h], low.astype(F32)]), None, None) for h in range(local_heads)
    ]
    heads_kept = []
    extra_v = None
    for h in range(local_heads):
        if balanced:
            weights = slots[h]
        else:
            cut = slots[h].reshape(-1, DK, width)
            weights = jnp.concatenate([pick(cut, place[h, s, c]) for c in range(6)], axis=0)
        carried = "va" not in roles[h]
        gate_count = roles[h].count("g")
        q, k, v, total, gates, *extra = head_call(
            functools.partial(project_kernel, blk, roles[h], carried),
            len(roles[h]) // 2,
            [
                params[h],
                (normed, (seg_len, width), whole),
                (weights, (2 * DK, width), ahead),
                (cosine, (seg_len, half), whole),
                (sine, (seg_len, half), whole),
                (k_decays[h], (blk, 1), whole),
            ]
            + ([(extra_v, (seg_len, DK), whole)] if carried else []),
            [
                (shaped(DK, BF16), (seg_len, DK), whole),
                (shaped(DK, BF16), (seg_len, DK), whole),
                (shaped(DV, BF16), (seg_len, DV), whole),
                (shaped(DV, BF16, DK), (DK, DV), whole),
                (shaped(gate_count * DK, F32), (seg_len, gate_count * DK), whole),
            ]
            + ([(shaped(DK, BF16), (seg_len, DK), whole)] if "xv" in roles[h] else []),
            [pltpu.VMEM((seg_len, 2 * DK), F32)],
            2 * seg_len * width * len(roles[h]) * DK,
        )
        extra_v = extra[0] if extra else None
        (state_in,) = exchange_states([h], [total], False)[0]
        if h + 1 < local_heads:
            slots[h + 1], state_in, *later[:] = tie(slots[h + 1], state_in, *later)
        heads_kept.append((weights, q, k, v, gates, state_in))

    def columns(v, c, order):
        return (v, unit_block, lambda n, c=c: (order(n)[0], c))

    if balanced:
        gates0, gates1 = heads_kept[0][4], heads_kept[1][4]
        swapped = swap(jnp.where(low, gates1, gates0[:, :DK]).astype(BF16), 2)

        def gate_operands(h, order):
            if h == 0:
                four = (gates0, 0), (gates0, 1), (swapped, 0), (gates0, 2)
            else:
                four = (gates0, 1), (gates1, 0), (gates0, 2), (swapped, 0)
            return [columns(v, c, order) for v, c in four]

    else:

        def gate_operands(h, order):
            return [columns(heads_kept[h][4], c, order) for c in (0, 0, 1, 1)]

    kept = []
    for h in range(local_heads):
        weights, q, k, v, gates, state_in = heads_kept[h]
        hidden, mixed, retained = head_call(
            retain_kernel,
            blocks,
            [
                params[h],
                (q, unit_block, ahead),
                (k, unit_block, ahead),
                (v, v_block, ahead),
                *gate_operands(h, ahead),
                (masks[h], (blk, blk), whole),
                (q_decays[h], (blk, 1), whole),
                (k_decays[h], (blk, 1), whole),
                (state_in, (DK, DV), whole),
            ],
            [
                (shaped(DV, BF16), v_block, ahead),
                (shaped(DV, BF16), v_block, ahead),
                (shaped(DV, F32), v_block, ahead),
            ],
            state_scratch,
            ret_flops,
        )
        kept.append((retained, mixed, hidden))
    hidden = jnp.concatenate([t[-1] for t in kept], axis=1)
    w_ffn_in, w_ffn_out = (gather_shard(t) for t in later)

    hidden_rows = seq_rows(hidden)
    resid = xf + add_blocks(*send_blocks(lambda d: dot_nt(hidden_rows(d), w_out)))
    normed2 = gather_near(rms_scale(resid, gain_ffn).astype(BF16))
    proj2 = dot_nt(normed2, w_ffn_in)
    first, second = proj2[:, :inner_cols], proj2[:, inner_cols:]
    inner2 = gated_gelu(first, second).astype(BF16)

    g_ffn_out, d_ffn = tie(dot_tn(d_ffn, inner2, BF16), d_ffn)
    scattered = {"ffn_out": reduce_shard(g_ffn_out)}
    d_inner2 = dot_nn(d_ffn, w_ffn_out)
    ignored2, gelu_back = jax.vjp(gated_gelu, first, second)
    d_first, d_second = gelu_back(d_inner2)
    dproj2 = jnp.concatenate([d_first, d_second], axis=1).astype(BF16)
    dproj2_rows = near_rows(dproj2)
    own, got = send_blocks(lambda d: dot_nn(dproj2_rows(d), w_ffn_in))
    g_ffn_in, own, *got = tie(dot_tn(dproj2, normed2, BF16), own, *got)
    d_normed2 = add_blocks(own, got)
    scattered["ffn_in"] = reduce_shard(g_ffn_in)
    ignored3, norm2_back = jax.vjp(rms_scale, resid, gain_ffn)
    d_resid_part, d_gain_ffn = norm2_back(d_normed2)
    d_resid = cotangent.astype(F32) + d_resid_part
    d_attn = gather_seq(d_resid.astype(BF16))
    d_attn, scattered["ffn_out"] = tie(d_attn, scattered["ffn_out"])
    parts_ffn_out = spread(scattered["ffn_out"])
    d_hidden = dot_nn(d_attn, w_out)
    hidden, d_hidden = tie(hidden, d_hidden)
    g_mixer_out = dot_tn(d_attn, hidden, BF16)

    def tie_parts(v, parts):
        flat = tie(v, *(piece for part in parts for piece in part))
        rest = list(flat[1:])
        return flat[0], [tuple(rest.pop(0) for _ in part) for part in parts]

    turns = [(cosine, half_block), (sine, half_block)]
    firsts = []
    for h in range(local_heads):
        weights, q, k, v, gates, state_in = heads_kept[h]
        retained, mixed, ignored4 = kept[h]
        firsts.append(
            head_call(
                gate_back_kernel,
                blocks,
                [
                    params[h],
                    (d_hidden, v_block, lambda n, h=h: (blocks - 1 - n, h)),
                    *gate_operands(h, behind),
                    (mixed, v_block, behind),
                    (retained, v_block, behind),
                    (q, unit_block, behind),
                    (q_decays[h], (blk, 1), whole),
                ],
                [
                    (shaped(DV, BF16), v_block, behind),
                    (shaped(DV, BF16), v_block, behind),
                    (shaped(DV, BF16, DK), (DK, DV), whole),
                ],
                state_scratch,
                2 * seg_len * DK * DV,
            )
        )
    d_gates = [t[0] for t in firsts]
    if balanced:
        d_swapped = swap(jnp.where(low, d_gates[0][:, DK:], d_gates[1][:, DK:]), 2)
    inners = []
    for h in range(local_heads):
        weights, q, k, v, gates, state_in = heads_kept[h]
        inners.append(
            head_call(
                inner_back_kernel,
                blocks,
                [
                    params[h],
                    (q, unit_block, ahead),
                    (k, unit_block, ahead),
                    (v, v_block, ahead),
                    (firsts[h][1], v_block, ahead),
                    (masks[h], (blk, blk), whole),
                    (q_decays[h], (blk, 1), whole),
                    (k_decays[h], (blk, 1), whole),
                    (state_in, (DK, DV), whole),
                    *((*t, ahead) for t in turns),
                ],
                [
                    (shaped(DK, BF16), unit_block, ahead),
                    (shaped(DK, F32), unit_block, ahead),
                    (shaped(DV, F32), v_block, ahead),
                ],
                state_scratch,
                2 * ret_flops,
            )
        )
    totals = [t[2] for t in firsts]
    if balanced:
        d_swapped, *totals = tie(d_swapped, *totals)
    g_mixer_out, *totals = tie(g_mixer_out, *totals)
    scattered["mixer_out"] = reduce_shard(g_mixer_out)
    grads_out, inner2, scattered["ffn_in"], *flat = exchange_states(
        range(local_heads),
        totals,
        True,
        (inner2, scattered["ffn_in"], *(t for inner in inners for t in inner)),
    )
    inners = [flat[3 * h : 3 * h + 3] for h in range(local_heads)]
    parts_ffn_in = spread(scattered["ffn_in"])
    if balanced:
        d_gate_pairs = [
            [
                ((d_gates[0], 0), (d_swapped, 0)),
                ((d_gates[1], 0), (d_gates[0], 0)),
                ((d_gates[1], 1), (d_gates[0], 1)),
            ],
            [((d_swapped, 0), (d_gates[1], 0))],
        ]
    else:
        d_gate_pairs = [[((t, 0), (t, 0)), ((t, 1), (t, 1))] for t in d_gates]
    by_units = [None] * local_heads
    extra_v = None
    for h in reversed(range(local_heads)):
        weights, q, k, v, gates, state_in = heads_kept[h]
        d_out = firsts[h][1]
        d_q, d_k, d_v = inners[h]
        count = len(roles[h])
        lone = "va" not in roles[h]
        by_units[h], *extra = head_call(
            functools.partial(outer_back_kernel, roles[h]),
            blocks,
            [
                params[h],
                (q, unit_block, behind),
                (k, unit_block, behind),
                (v, v_block, behind),
                (d_out, v_block, behind),
                (d_q, unit_block, behind),
                (d_k, unit_block, behind),
                (d_v, v_block, behind),
                (q_decays[h], (blk, 1), whole),
                (k_decays[h], (blk, 1), whole),
                (grads_out[h], (DK, DV), whole),
                *((*t, behind) for t in turns),
            ]
            + ([(extra_v, unit_block, behind)] if "xv" in roles[h] else [])
            + [columns(v, c, behind) for pair in d_gate_pairs[h] for v, c in pair],
            [(shaped(count * DK, BF16), (blk, count * DK), behind)]
            + ([(shaped(DK, BF16), unit_block, behind)] if lone else []),
            state_scratch,
            6 * seg_len * DK * DV,
        )
        extra_v = extra[0] if extra else None

    by_units[0], parts_ffn_out = tie_parts(by_units[0], parts_ffn_out)
    by_units[0], parts_ffn_in[:3] = tie_parts(by_units[0], parts_ffn_in[:3])
    by_units[-1], parts_ffn_in = tie_parts(by_units[-1], parts_ffn_in)
    by_units[-1], scattered["mixer_out"] = tie(by_units[-1], scattered["mixer_out"])
    parts_mixer_out = spread(scattered["mixer_out"])
    by_units[0], inner2 = tie(by_units[0], inner2)
    if group == 4:
        late = first_step(near_rows(dot_nt(inner2, w_ffn_out, BF16)))
    else:
        inner2_rows = near_rows(inner2)
        late = send_blocks(lambda d: dot_nt(inner2_rows(d), w_ffn_out))
    g_slots = []
    for h in range(local_heads):
        g_unit = dot_tn(by_units[h], normed, BF16)
        if not balanced:
            cut = g_unit.reshape(-1, DK, width)
            g_unit = jnp.concatenate(
                [pick(cut, jnp.maximum(held[h, c, s], 0)) for c in range(segments)], axis=0
            )
        if h == local_heads - 1:
            tile = 512
            rights = [t[0] for t in heads_kept]
            (d_normed,) = head_call(
                functools.partial(join_kernel, local_heads),
                width // tile,
                [(t, t.shape, whole) for t in by_units]
                + [(t, (t.shape[0], tile), lambda n: (0, n)) for t in rights],
                [(shaped(width, BF16), (seg_len, tile), lambda n: (0, n))],
                [],
                2 * seg_len * width * sum(t.shape[0] for t in rights),
            )
            g_unit, d_normed = tie(g_unit, d_normed)
        g_slots.append(reduce_shard(g_unit))
    if group == 4:
        blocks_late, ra, rb = late
        d_normed, ra, rb = tie(d_normed, ra, rb)
        late = blocks_late, ra, rb
        d_normed, parts_mixer_out[:3] = tie_parts(d_normed, parts_mixer_out[:3])
        d_normed = second_step(*first_step(seq_rows(d_normed)))
        output = (resid + second_step(*late)).astype(BF16)
    else:
        d_normed_rows = seq_rows(d_normed)
        d_normed = add_blocks(*send_blocks(lambda d: d_normed_rows(d).astype(F32)))
        output = (resid + add_blocks(*late)).astype(BF16)

    ignored8, norm1_back = jax.vjp(rms_scale, xf, gain_attn)
    d_x_part, d_gain_attn = norm1_back(d_normed)
    input_grad = (d_resid + d_x_part).astype(BF16)
    gains = jnp.concatenate([d_gain_attn, d_gain_ffn])[None]
    step = 1
    while step < group:
        gains = gains + swap(gains, step)
        step *= 2
    gains = lax.all_to_all(
        jnp.broadcast_to(gains, (segments, 2 * width)),
        "shard",
        split_axis=0,
        concat_axis=0,
        tiled=True,
    )
    gains = jnp.sum(gains, axis=0)
    gain_attn_grad, gain_ffn_grad = gains[:width], gains[width:]
    near = jnp.arange(group)
    g_ffn_in = place_blocks(
        parts_ffn_in, s ^ near, near, ffn_in.shape, (sub, width), lambda o, n: (n, 0)
    )
    if sub % 128 == 0:
        g_ffn_out = place_blocks(
            parts_ffn_out,
            s ^ near,
            near,
            ffn_out.shape,
            (ffn_out.shape[0], sub),
            lambda o, n: (0, o * group + n),
            outer=segments // 2,
        )
    else:
        g_ffn_out = jnp.transpose(
            ordered(parts_ffn_out).reshape(group, ffn_out.shape[0], segments // 2, sub),
            (1, 2, 0, 3),
        ).reshape(ffn_out.shape).astype(F32)

    parts = []
    for h in range(local_heads):
        last = h == local_heads - 1
        if h == 0:
            g_slots[h], g_ffn_in, g_ffn_out, input_grad, output = tie(
                g_slots[h], g_ffn_in, g_ffn_out, input_grad, output
            )
            g_slots[h], parts_mixer_out = tie_parts(g_slots[h], parts_mixer_out)
        if last:
            pieces = parts_mixer_out[0]
            pieces0, parts = tie_parts(pieces[0], parts)
            parts_mixer_out[0] = (pieces0, *pieces[1:])
            g_mixer_out = place_blocks(
                parts_mixer_out,
                s ^ near,
                near,
                mixer_out.shape,
                (mixer_out.shape[0], DV),
                lambda o, n: (0, o * group + n),
                outer=local_heads,
            )
            g_slots[h], g_mixer_out = tie(g_slots[h], g_mixer_out)
        here = spread(g_slots[h])
        if balanced and last:
            there = [tuple(cross(piece, 1) for piece in part) for part in here]
            parts += [a + b for a, b in zip(here, there)] + [b + a for a, b in zip(here, there)]
        else:
            lend_here = lend[j] if balanced else lend[h, j]
            stack = jnp.stack([jnp.concatenate(part, axis=0) for part in here])
            parts += here + [
                (cross(pick(stack, s ^ lend_here[n]), 1),) for n in range(lend_here.shape[0])
            ]
    found = back[j]
    if balanced:
        spare = lend.shape[-1]
        source = jnp.where(
            found[:, 0] == 0,
            s ^ found[:, 1],
            jnp.where(
                found[:, 0] == 1,
                group + found[:, 1],
                group + spare + core * group + (s ^ found[:, 1]),
            ),
        )
    else:
        source = found[:, 0] * (group + lend.shape[-1]) + jnp.where(
            found[:, 2] < 0, s ^ found[:, 1], group + found[:, 2]
        )
    g_mixer_in = place_blocks(
        parts,
        jnp.arange(source.shape[0]),
        source,
        mixer_in.shape,
        (DK, width),
        lambda o, n: (n, 0),
    )
    return (
        output,
        input_grad,
        gain_attn_grad,
        gain_ffn_grad,
        g_mixer_in,
        g_mixer_out,
        g_ffn_in,
        g_ffn_out,
    )


def solution(mesh):
    return jax.shard_map(
        local,
        mesh=mesh,
        in_specs=(
            P(("shard", "seq"), None),
            P(("shard", "seq"), None),
            P(),
            P(),
            P("shard", None),
            P("shard", None),
            P("shard", None),
            P("shard", None),
            P(),
            P(),
        ),
        out_specs=(
            P(("shard", "seq"), None),
            P(("shard", "seq"), None),
            P(),
            P(),
            P("shard", None),
            P("shard", None),
            P("shard", None),
            P("shard", None),
        ),
        check_vma=False,
    )
```

```python
import functools

import jax
import jax.numpy as jnp
import numpy as np
from jax import lax
from jax.experimental import pallas as pl
from jax.experimental.pallas import tpu as pltpu
from jax.sharding import PartitionSpec as P

DK = 256
DV = 512
FF = 4096
QK = 2048
V = 4096


EPS_NORM = 1e-06
EPS_GROUP = 1e-05

F32 = jnp.float32
BF16 = jnp.bfloat16


def dot_nt(left, right, kind=F32):
    return lax.dot_general(
        left, right, (((1,), (1,)), ((), ())), preferred_element_type=F32
    ).astype(kind)


def dot_nn(left, right, kind=F32):
    return lax.dot_general(
        left, right, (((1,), (0,)), ((), ())), preferred_element_type=F32
    ).astype(kind)


def dot_tn(left, right, kind=F32):
    return lax.dot_general(
        left, right, (((0,), (0,)), ((), ())), preferred_element_type=F32
    ).astype(kind)


def rms_scale(v, gain):
    return v * lax.rsqrt(jnp.mean(v * v, axis=-1, keepdims=True) + EPS_NORM) * gain


def gated_gelu(first, second):
    return jax.nn.gelu(first) * second


def unit_owners(heads):
    owners = [(n, 0) for n in range(heads)] + [(n, 1) for n in range(heads)]
    for base in (2, 4):
        owners += [(n, base + half) for n in range(heads) for half in range(2)]
    return owners


def balanced_tables():
    group, segments, per_shard = 4, 8, 6
    number = {owner: u for u, owner in enumerate(unit_owners(8))}
    keep = np.full((2, segments, group), -1, np.int32)
    give = np.zeros((2, segments, group), np.int32)
    back = np.zeros((segments, per_shard, 2), np.int32)
    lend = [[] for _ in range(segments)]
    seen = set()
    for s in range(group):
        a, b = s, s + 4
        if s < 2:
            gates = [(a, 4), (b, 4), (b, 5)], (b + 2, 5)
        else:
            gates = [(a - 2, 5), (a, 4), (a, 5)], (b, 4)
        first = [(a, 0), (a, 1), (a, 2), (a, 3), (b, 2)] + gates[0]
        second = [(b, 0), (b, 1), (b, 3), gates[1]]
        for slot, owner in enumerate(first):
            home, index = divmod(number[owner], per_shard)
            seen.add(number[owner])
            assert home // 2 == slot // 2
            if home == slot:
                keep[0, slot, s] = index
                back[home, index] = (0, s)
            else:
                give[0, home, s] = index
                back[home, index] = (1, len(lend[slot]))
                lend[slot].append(s)
        for chip, owner in enumerate(second):
            home, index = divmod(number[owner], per_shard)
            seen.add(number[owner])
            assert home // 2 == chip
            keep[1, home, s] = index
            give[1, home, s] = index
            back[home, index] = (2, s)
    assert len(seen) == segments * per_shard
    most = max(len(t) for t in lend)
    return keep, give, back, np.asarray([(t + [0] * most)[:most] for t in lend], np.int32)


def unit_tables(group, local_heads, segments):
    heads = group * local_heads
    owners = unit_owners(heads)
    per_shard = len(owners) // segments
    keep = np.full((local_heads, segments, group), -1, np.int32)
    give = np.zeros((local_heads, segments, group), np.int32)
    place = np.zeros((local_heads, group, 6), np.int32)
    held = np.full((local_heads, segments, group), -1, np.int32)
    slot_of = {}
    for chip in range(segments // 2):
        for head in range(heads):
            h, s = divmod(head, group)
            span = range(2 * per_shard * chip, 2 * per_shard * (chip + 1))
            mine = [u for u in span if owners[u][0] == head]
            assert len(mine) <= 2
            for n, u in enumerate(mine):
                home = u // per_shard
                slot = home if len(mine) == 1 else 2 * chip + n
                if slot == home:
                    keep[h, slot, s] = u % per_shard
                else:
                    give[h, home, s] = u % per_shard
                place[h, s, owners[u][1]] = slot
                held[h, slot, s] = owners[u][1]
                slot_of[u] = slot
    lends = [[[] for _ in range(segments)] for _ in range(local_heads)]
    back = np.zeros((segments, per_shard, 3), np.int32)
    for u, (head, _) in enumerate(owners):
        home = u // per_shard
        h, s = divmod(head, group)
        back[home, u % per_shard] = (h, s, -1)
        if slot_of[u] != home:
            assert slot_of[u] == home ^ 1
            back[home, u % per_shard, 2] = len(lends[h][home ^ 1])
            lends[h][home ^ 1].append(s)
    most = max(1, max(len(t) for row in lends for t in row))
    lend = np.asarray(
        [[(t + [0] * most)[:most] for t in row] for row in lends], np.int32
    )
    return keep, give, place, held, back, lend


def tie(*values):
    return lax.optimization_barrier(values)


def mm(left, right, dims):
    return lax.dot_general(left, right, (dims, ((), ())), preferred_element_type=F32)


NN = ((1,), (0,))
NT = ((1,), (1,))
TN = ((0,), (0,))


def turn(v, cosine, sine):
    half = v.shape[-1] // 2
    first, second = v[:, :half], v[:, half:]
    return jnp.concatenate(
        [first * cosine - second * sine, second * cosine + first * sine], axis=-1
    )


def scaled(v, decay):
    return (v.astype(F32) * decay).astype(BF16)


def project_kernel(blk, roles, carried, params, x, w, cosine, sine, k_decay, *refs):
    if carried:
        v_a, *refs = refs
    q, k, v, total, gates, *rest = refs
    y = rest[-1]
    rows = y.shape[0]
    y[...] = mm(x[...], w[...], NT)

    def put(role, part, gate_at):
        value = y[:, part * DK : (part + 1) * DK]
        if role == "q":
            q[...] = turn(value, cosine[...], sine[...]).astype(BF16)
        elif role == "k":
            k[...] = turn(value, cosine[...], sine[...]).astype(BF16)
        elif role == "va":
            v[:, :DK] = value.astype(BF16)
        elif role == "vb":
            v[:, DK:] = value.astype(BF16)
        elif role == "xv":
            rest[0][...] = value.astype(BF16)
        else:
            gates[:, gate_at * DK : (gate_at + 1) * DK] = value

    for step in range(len(roles) // 2):

        @pl.when(pl.program_id(0) == step)
        def _(step=step):
            for part in range(2):
                at = 2 * step + part
                put(roles[at], part, roles[:at].count("g"))
            if step == 1:
                if carried:
                    v[:, :DK] = v_a[...]
                state = jnp.zeros(total.shape, F32)
                for r in range(0, rows, blk):
                    kd = scaled(k[r : r + blk, :], k_decay[...])
                    state = params[0] * state + mm(kd, v[r : r + blk, :], TN)
                total[...] = state.astype(BF16)


def join_kernel(count, *refs):
    out = refs[-1]
    total = mm(refs[0][...], refs[count][...], NN)
    for n in range(1, count):
        total += mm(refs[n][...], refs[count + n][...], NN)
    out[...] = total.astype(out.dtype)


def select(params, low, high):
    return jnp.where(params[1] > 0.5, low[...].astype(F32), high[...].astype(F32))


def retain_kernel(
    params, q, k, v, low_a, high_a, low_b, high_b, mask, q_decay, k_decay, start,
    hidden, mixed, kept, state,
):
    @pl.when(pl.program_id(0) == 0)
    def _():
        state[...] = start[...].astype(F32)

    weights = (mm(q[...], k[...], NT) * mask[...]).astype(BF16)
    o = mm(weights, v[...], NN)
    o += mm(scaled(q[...], q_decay[...]), state[...].astype(BF16), NN)
    state[...] = params[0] * state[...] + mm(scaled(k[...], k_decay[...]), v[...], TN)
    kept[...] = o
    o = o - jnp.mean(o, axis=-1, keepdims=True)
    o = o * lax.rsqrt(jnp.mean(o * o, axis=-1, keepdims=True) + EPS_GROUP)
    low = o.astype(BF16)
    mixed[...] = low
    for n, (one, two) in enumerate(((low_a, high_a), (low_b, high_b))):
        columns = slice(n * DK, (n + 1) * DK)
        g = select(params, one, two)
        hidden[:, columns] = (g * jax.nn.sigmoid(g) * low[:, columns].astype(F32)).astype(BF16)


def gate_back_kernel(
    params, d_hidden, low_a, high_a, low_b, high_b, mixed, kept, q, q_decay,
    d_gate, d_out, total, state,
):
    @pl.when(pl.program_id(0) == 0)
    def _():
        state[...] = jnp.zeros(state.shape, F32)

    g = jnp.concatenate([select(params, low_a, high_a), select(params, low_b, high_b)], axis=1)
    dh = d_hidden[...]
    sig = jax.nn.sigmoid(g)
    d_gate[...] = (dh * mixed[...].astype(F32) * (sig * (1.0 + g * (1.0 - sig)))).astype(BF16)
    dy = (dh * (g * sig)).astype(BF16).astype(F32)
    o = kept[...]
    o = o - jnp.mean(o, axis=-1, keepdims=True)
    inverse = lax.rsqrt(jnp.mean(o * o, axis=-1, keepdims=True) + EPS_GROUP)
    o = o * inverse
    do = inverse * (
        dy
        - jnp.mean(dy, axis=-1, keepdims=True)
        - o * jnp.mean(dy * o, axis=-1, keepdims=True)
    )
    do = do.astype(BF16)
    d_out[...] = do
    state[...] = params[0] * state[...] + mm(scaled(q[...], q_decay[...]), do, TN)
    total[...] = state[...].astype(BF16)


def inner_back_kernel(
    params, q, k, v, d_out, mask, q_decay, k_decay, start, cosine, sine, d_q, d_k, d_v, state
):
    @pl.when(pl.program_id(0) == 0)
    def _():
        state[...] = start[...].astype(F32)

    do = d_out[...]
    weights = (mm(q[...], k[...], NT) * mask[...]).astype(BF16)
    d_v[...] = mm(weights, do, TN)
    d_scores = mm(do, v[...], NT).astype(BF16).astype(F32)
    d_scores = (d_scores * mask[...]).astype(BF16)
    d_k[...] = mm(d_scores, q[...], TN)
    far = mm(do, state[...].astype(BF16), NT).astype(BF16).astype(F32)
    dq = mm(d_scores, k[...], NN) + far * q_decay[...]
    dq = dq.astype(BF16).astype(F32)
    d_q[...] = turn(dq, cosine[...], -sine[...]).astype(BF16)
    state[...] = params[0] * state[...] + mm(scaled(k[...], k_decay[...]), v[...], TN)


def outer_back_kernel(
    roles, params, q, k, v, d_out, d_q, d_k, d_v, q_decay, k_decay, start, cosine, sine, *refs
):
    refs = list(refs)
    state = refs.pop()
    v_a = None if "va" in roles else refs.pop()
    by_unit = refs.pop()

    @pl.when(pl.program_id(0) == 0)
    def _():
        state[...] = start[...].astype(F32)

    low = state[...].astype(BF16)
    far = mm(v[...], low, NT).astype(BF16).astype(F32)
    dk = (d_k[...] + far * k_decay[...]).astype(BF16).astype(F32)
    dk = turn(dk, cosine[...], -sine[...]).astype(BF16)
    dv = (d_v[...] + mm(scaled(k[...], k_decay[...]), low, NN)).astype(BF16)
    for n, role in enumerate(roles):
        if role == "q":
            value = d_q[...]
        elif role == "k":
            value = dk
        elif role == "va":
            value = dv[:, :DK]
        elif role == "vb":
            value = dv[:, DK:]
        elif role == "xv":
            value = refs.pop(0)[...]
        else:
            value = select(params, refs.pop(0), refs.pop(0)).astype(BF16)
        by_unit[:, n * DK : (n + 1) * DK] = value
    if v_a is not None:
        v_a[...] = dv[:, :DK]
    state[...] = params[0] * state[...] + mm(scaled(q[...], q_decay[...]), d_out[...], TN)


def head_call(kernel, grid, operands, outputs, scratch, flops):
    arrays = [t[0] for t in operands]
    size = sum(t.size * t.dtype.itemsize for t in arrays + [t[0] for t in outputs])
    return pl.pallas_call(
        kernel,
        grid=(grid,),
        in_specs=[
            pl.BlockSpec(memory_space=pltpu.SMEM) if block is None else pl.BlockSpec(block, where)
            for _, block, where in operands
        ],
        out_specs=[pl.BlockSpec(block, where) for _, block, where in outputs],
        scratch_shapes=scratch,
        out_shape=[t[0] for t in outputs],
        compiler_params=pltpu.CompilerParams(vmem_limit_bytes=56 * 2**20),
        cost_estimate=pl.CostEstimate(flops=flops, bytes_accessed=size, transcendentals=0),
    )(*arrays)


def place_kernel(parts, target, source, *refs):
    out = refs[-1]
    code = source[pl.program_id(1)]
    for i, part in enumerate(parts):

        @pl.when(code == i)
        def _(part=part):
            row = 0
            for n in part:
                piece = refs[n]
                out[row : row + piece.shape[0], :] = piece[...].astype(F32)
                row += piece.shape[0]


def place_blocks(parts, target, source, shape, block, where, outer=1):
    flat, index = [], []
    for part in parts:
        for piece in part:
            if not any(piece is t for t in flat):
                flat.append(piece)
        index.append([next(n for n, t in enumerate(flat) if t is piece) for piece in part])
    return pl.pallas_call(
        functools.partial(place_kernel, index),
        grid_spec=pltpu.PrefetchScalarGridSpec(
            num_scalar_prefetch=2,
            grid=(outer, target.shape[0]),
            in_specs=[
                pl.BlockSpec((t.shape[0], t.shape[1] // outer), lambda o, n, target, source: (0, o))
                for t in flat
            ],
            out_specs=pl.BlockSpec(block, lambda o, n, target, source: where(o, target[n])),
        ),
        out_shape=jax.ShapeDtypeStruct(shape, F32),
        compiler_params=pltpu.CompilerParams(vmem_limit_bytes=48 * 2**20),
    )(target.astype(jnp.int32), source.astype(jnp.int32), *flat)


def local(
    tokens,
    cotangent,
    gain_attn,
    gain_ffn,
    mixer_in,
    mixer_out,
    ffn_in,
    ffn_out,
    segment_order,
    decay_index,
):
    rows, width = tokens.shape
    group = lax.axis_size("seq")
    segments = lax.axis_size("shard")
    heads = decay_index.shape[0]
    local_heads = heads // group
    seg_len = rows * group
    blk = min(512, seg_len)
    blocks = seg_len // blk
    vcols = local_heads * DV
    s = lax.axis_index("seq")
    j = lax.axis_index("shard")

    def swap(v, d):
        return lax.ppermute(v, "seq", [(i, i ^ d) for i in range(group)])

    def cross(v, d):
        return lax.ppermute(v, "shard", [(i, i ^ d) for i in range(segments)])

    def pick(v, i):
        return lax.dynamic_index_in_dim(v, i, 0, keepdims=False)

    def spread(v):
        if group == 4:
            h = v.shape[0] // 2
            r1 = swap(v, 1)
            r2 = swap(v, 2)
            return [(v,), (r1,), (r2,), (swap(r1[:h], 2), swap(r2[h:], 1))]
        return [(v,)] + [(swap(v, d),) for d in range(1, group)]

    def ordered(parts):
        r = parts[0][0].shape[0]
        out = jnp.zeros((group * r,) + parts[0][0].shape[1:], parts[0][0].dtype)
        for d, part in enumerate(parts):
            row = (s ^ d) * r
            for piece in part:
                out = lax.dynamic_update_slice_in_dim(out, piece, row, 0)
                row = row + piece.shape[0]
        return out

    def gather_near(v):
        return jnp.concatenate([piece for part in spread(v) for piece in part], axis=0)

    def gather_seq(v):
        return ordered(spread(v))

    def first_step(blk_of):
        b = [blk_of(d) for d in range(4)]
        h = b[0].shape[0] // 2
        sa = jnp.concatenate([b[1][:h], b[3][:h]], axis=0)
        sb = jnp.concatenate([b[2][h:], b[3][h:]], axis=0)
        sa, sb = tie(sa, sb)
        return b, swap(sa, 1), swap(sb, 2)

    def second_step(b, ra, rb):
        h = b[0].shape[0] // 2
        ra, rb = ra.astype(F32), rb.astype(F32)
        qa = (b[2][:h].astype(F32) + ra[h:]).astype(BF16)
        qb = (b[1][h:].astype(F32) + rb[h:]).astype(BF16)
        qa, qb = tie(qa, qb)
        qa, qb = swap(qa, 2), swap(qb, 1)
        top = b[0][:h].astype(F32) + ra[:h] + qa.astype(F32)
        return jnp.concatenate([top, b[0][h:].astype(F32) + rb[:h] + qb.astype(F32)], axis=0)

    def send_blocks(blk_of):
        sent = tie(*(blk_of(d) for d in range(group)))
        return sent[0], [swap(sent[d], d) for d in range(group - 1, 0, -1)]

    def add_blocks(own, got):
        own = own.astype(F32)
        for t in got:
            own = own + t.astype(F32)
        return own

    def near_rows(v):
        return lambda d: v[d * rows : (d + 1) * rows]

    def seq_rows(v):
        return lambda d: lax.dynamic_slice_in_dim(v, (s ^ d) * rows, rows, 0)

    def gather_shard(v):
        return lax.all_gather(v, "shard", axis=0, tiled=True)

    def reduce_shard(v):
        return lax.psum_scatter(v, "shard", scatter_dimension=0, tiled=True)

    balanced = group == 4 and local_heads == 2 and segments == 8
    units = mixer_in.reshape(-1, DK, width)
    if balanced:
        keep, give, back, lend = (jnp.asarray(t) for t in balanced_tables())
        core = j % 2
    else:
        keep, give, place, held, back, lend = (
            jnp.asarray(t) for t in unit_tables(group, local_heads, segments)
        )

    def offered(h):
        kept, given = keep[h, j, s], give[h, j, s]
        if balanced and h == 1:
            cut = mixer_in.reshape(-1, DK // 2, width)
            own = pick(cut, 2 * jnp.maximum(kept, 0) + core)
            given = cross(pick(cut, 2 * given + 1 - core), 1)
        else:
            own = pick(units, jnp.maximum(kept, 0))
            given = cross(pick(units, given), 1)
        return jnp.where(kept >= 0, own, given)

    sub = ffn_in.shape[0] // group
    ffn_out_cut = ffn_out.reshape(ffn_out.shape[0], segments // 2, group, sub)

    my_rank = jnp.sum(jnp.where(jnp.arange(segments) == j, segment_order, 0))
    all_logs = jnp.log1p(-jnp.exp2(-(5.0 + decay_index.astype(F32))))
    logs = lax.dynamic_index_in_dim(all_logs.reshape(local_heads, group), s, 1, keepdims=False)
    half = DK // 2
    inv_freq = jnp.exp(-jnp.log(10000.0) * jnp.arange(half).astype(F32) / half)
    positions = my_rank * seg_len + jnp.arange(seg_len, dtype=jnp.int32)
    angles = positions.astype(F32)[:, None] * inv_freq[None, :]
    cosine = jnp.cos(angles)
    sine = jnp.sin(angles)
    steps = jnp.arange(blk).astype(F32)
    gap = steps[:, None] - steps[None, :]
    masks = jnp.where(
        gap[None] >= 0.0, jnp.exp(jnp.maximum(gap, 0.0)[None] * logs[:, None, None]), 0.0
    )
    q_decays = jnp.exp((steps + 1.0)[None, :] * logs[:, None])[..., None]
    k_decays = jnp.exp((blk - 1.0 - steps)[None, :] * logs[:, None])[..., None]
    block_decays = jnp.exp(blk * logs)

    xf = tokens.astype(F32)
    normed = gather_seq(rms_scale(xf, gain_attn).astype(BF16))
    d_ffn = gather_near(cotangent)
    slots = [gather_shard(offered(0))]
    slots[0], normed, d_ffn, cosine, sine, masks, q_decays, k_decays = tie(
        slots[0], normed, d_ffn, cosine, sine, masks, q_decays, k_decays
    )
    for h in range(1, local_heads):
        slots.append(gather_shard(offered(h)))
    mixer_out_cut = jnp.concatenate(
        [
            lax.dynamic_slice_in_dim(mixer_out, (h * group + s) * DV, DV, 1)
            for h in range(local_heads)
        ],
        axis=1,
    )
    mixer_out_cut, slots[0] = tie(mixer_out_cut, slots[0])
    w_out = gather_shard(mixer_out_cut)
    later = [
        lax.dynamic_slice_in_dim(ffn_in, s * sub, sub, 0),
        lax.dynamic_index_in_dim(ffn_out_cut, s, 2, keepdims=False).reshape(ffn_out.shape[0], -1),
    ]
    inner_cols = later[1].shape[1]

    ranks = segment_order
    piece = DK // segments

    def exchange_states(hs, totals, reverse, beside=()):
        cut = jnp.concatenate([t.reshape(segments, piece, DV) for t in totals], axis=1)
        got = lax.all_to_all(cut, "shard", split_axis=0, concat_axis=0, tiled=True)
        got, *beside = tie(got, *beside)
        apart = ranks[:, None] - ranks[None, :] - 1
        if reverse:
            apart = -apart - 2
        distance = apart.astype(F32)
        joined = []
        for n, h in enumerate(hs):
            coef = jnp.where(
                distance >= 0.0, jnp.exp(jnp.maximum(distance, 0.0) * seg_len * logs[h]), 0.0
            )
            part = got[:, n * piece : (n + 1) * piece].astype(F32)
            joined.append(jnp.sum(coef[..., None, None] * part[None], axis=1).astype(BF16))
        joined = jnp.concatenate(joined, axis=1)
        back_cut = lax.all_to_all(joined, "shard", split_axis=0, concat_axis=0, tiled=True)
        states = [
            back_cut[:, n * piece : (n + 1) * piece].reshape(DK, DV) for n in range(len(hs))
        ]
        return (states, *beside)

    def whole(n):
        return (0, 0)

    def ahead(n):
        return (n, 0)

    def behind(n):
        return (blocks - 1 - n, 0)

    def shaped(columns, kind, r=seg_len):
        return jax.ShapeDtypeStruct((r, columns), kind)

    state_scratch = [pltpu.VMEM((DK, DV), F32)]
    half_block = (blk, half)
    unit_block, v_block = (blk, DK), (blk, DV)
    ret_flops = 2 * seg_len * (DK + DV) * (blk + DK)
    low = s < group // 2
    if balanced:
        roles = [["q", "k", "va", "vb", "xv", "g", "g", "g"], ["q", "k", "vb", "g"]]
    else:
        roles = [["q", "k", "va", "vb", "g", "g"]] * local_heads
    params = [
        (jnp.stack([block_decays[h], low.astype(F32)]), None, None) for h in range(local_heads)
    ]
    heads_kept = []
    extra_v = None
    for h in range(local_heads):
        if balanced:
            weights = slots[h]
        else:
            cut = slots[h].reshape(-1, DK, width)
            weights = jnp.concatenate([pick(cut, place[h, s, c]) for c in range(6)], axis=0)
        carried = "va" not in roles[h]
        gate_count = roles[h].count("g")
        q, k, v, total, gates, *extra = head_call(
            functools.partial(project_kernel, blk, roles[h], carried),
            len(roles[h]) // 2,
            [
                params[h],
                (normed, (seg_len, width), whole),
                (weights, (2 * DK, width), ahead),
                (cosine, (seg_len, half), whole),
                (sine, (seg_len, half), whole),
                (k_decays[h], (blk, 1), whole),
            ]
            + ([(extra_v, (seg_len, DK), whole)] if carried else []),
            [
                (shaped(DK, BF16), (seg_len, DK), whole),
                (shaped(DK, BF16), (seg_len, DK), whole),
                (shaped(DV, BF16), (seg_len, DV), whole),
                (shaped(DV, BF16, DK), (DK, DV), whole),
                (shaped(gate_count * DK, F32), (seg_len, gate_count * DK), whole),
            ]
            + ([(shaped(DK, BF16), (seg_len, DK), whole)] if "xv" in roles[h] else []),
            [pltpu.VMEM((seg_len, 2 * DK), F32)],
            2 * seg_len * width * len(roles[h]) * DK,
        )
        extra_v = extra[0] if extra else None
        (state_in,) = exchange_states([h], [total], False)[0]
        if h + 1 < local_heads:
            slots[h + 1], state_in, *later[:] = tie(slots[h + 1], state_in, *later)
        heads_kept.append((weights, q, k, v, gates, state_in))

    def columns(v, c, order):
        return (v, unit_block, lambda n, c=c: (order(n)[0], c))

    if balanced:
        gates0, gates1 = heads_kept[0][4], heads_kept[1][4]
        swapped = swap(jnp.where(low, gates1, gates0[:, :DK]).astype(BF16), 2)

        def gate_operands(h, order):
            if h == 0:
                four = (gates0, 0), (gates0, 1), (swapped, 0), (gates0, 2)
            else:
                four = (gates0, 1), (gates1, 0), (gates0, 2), (swapped, 0)
            return [columns(v, c, order) for v, c in four]

    else:

        def gate_operands(h, order):
            return [columns(heads_kept[h][4], c, order) for c in (0, 0, 1, 1)]

    kept = []
    for h in range(local_heads):
        weights, q, k, v, gates, state_in = heads_kept[h]
        hidden, mixed, retained = head_call(
            retain_kernel,
            blocks,
            [
                params[h],
                (q, unit_block, ahead),
                (k, unit_block, ahead),
                (v, v_block, ahead),
                *gate_operands(h, ahead),
                (masks[h], (blk, blk), whole),
                (q_decays[h], (blk, 1), whole),
                (k_decays[h], (blk, 1), whole),
                (state_in, (DK, DV), whole),
            ],
            [
                (shaped(DV, BF16), v_block, ahead),
                (shaped(DV, BF16), v_block, ahead),
                (shaped(DV, F32), v_block, ahead),
            ],
            state_scratch,
            ret_flops,
        )
        kept.append((retained, mixed, hidden))
    hidden = jnp.concatenate([t[-1] for t in kept], axis=1)
    w_ffn_in, w_ffn_out = (gather_shard(t) for t in later)

    resid = xf + add_blocks(*send_blocks(seq_rows(dot_nt(hidden, w_out, BF16))))
    normed2 = gather_near(rms_scale(resid, gain_ffn).astype(BF16))
    proj2 = dot_nt(normed2, w_ffn_in)
    first, second = proj2[:, :inner_cols], proj2[:, inner_cols:]
    inner2 = gated_gelu(first, second).astype(BF16)

    g_ffn_out, d_ffn = tie(dot_tn(d_ffn, inner2, BF16), d_ffn)
    scattered = {"ffn_out": reduce_shard(g_ffn_out)}
    d_inner2 = dot_nn(d_ffn, w_ffn_out)
    ignored2, gelu_back = jax.vjp(gated_gelu, first, second)
    d_first, d_second = gelu_back(d_inner2)
    dproj2 = jnp.concatenate([d_first, d_second], axis=1).astype(BF16)
    d_normed2 = dot_nn(dproj2, w_ffn_in, BF16)
    g_ffn_in = dot_tn(dproj2, normed2, BF16)
    if group == 4:
        terms, ra, rb = first_step(near_rows(d_normed2))
        ra, rb, g_ffn_in = tie(ra, rb, g_ffn_in)
        d_normed2 = second_step(terms, ra, rb)
    else:
        d_normed2 = add_blocks(*send_blocks(near_rows(d_normed2)))
    scattered["ffn_in"] = reduce_shard(g_ffn_in)
    ignored3, norm2_back = jax.vjp(rms_scale, resid, gain_ffn)
    d_resid_part, d_gain_ffn = norm2_back(d_normed2)
    d_resid = cotangent.astype(F32) + d_resid_part
    d_attn = gather_seq(d_resid.astype(BF16))
    d_attn, scattered["ffn_out"] = tie(d_attn, scattered["ffn_out"])
    parts_ffn_out = spread(scattered["ffn_out"])
    d_hidden = dot_nn(d_attn, w_out)
    hidden, d_hidden = tie(hidden, d_hidden)
    g_mixer_out = dot_tn(d_attn, hidden, BF16)

    def tie_parts(v, parts):
        flat = tie(v, *(piece for part in parts for piece in part))
        rest = list(flat[1:])
        return flat[0], [tuple(rest.pop(0) for _ in part) for part in parts]

    turns = [(cosine, half_block), (sine, half_block)]
    firsts = []
    for h in range(local_heads):
        weights, q, k, v, gates, state_in = heads_kept[h]
        retained, mixed, ignored4 = kept[h]
        firsts.append(
            head_call(
                gate_back_kernel,
                blocks,
                [
                    params[h],
                    (d_hidden, v_block, lambda n, h=h: (blocks - 1 - n, h)),
                    *gate_operands(h, behind),
                    (mixed, v_block, behind),
                    (retained, v_block, behind),
                    (q, unit_block, behind),
                    (q_decays[h], (blk, 1), whole),
                ],
                [
                    (shaped(DV, BF16), v_block, behind),
                    (shaped(DV, BF16), v_block, behind),
                    (shaped(DV, BF16, DK), (DK, DV), whole),
                ],
                state_scratch,
                2 * seg_len * DK * DV,
            )
        )
    d_gates = [t[0] for t in firsts]
    if balanced:
        d_swapped = swap(jnp.where(low, d_gates[0][:, DK:], d_gates[1][:, DK:]), 2)
    inners = []
    for h in range(local_heads):
        weights, q, k, v, gates, state_in = heads_kept[h]
        inners.append(
            head_call(
                inner_back_kernel,
                blocks,
                [
                    params[h],
                    (q, unit_block, ahead),
                    (k, unit_block, ahead),
                    (v, v_block, ahead),
                    (firsts[h][1], v_block, ahead),
                    (masks[h], (blk, blk), whole),
                    (q_decays[h], (blk, 1), whole),
                    (k_decays[h], (blk, 1), whole),
                    (state_in, (DK, DV), whole),
                    *((*t, ahead) for t in turns),
                ],
                [
                    (shaped(DK, BF16), unit_block, ahead),
                    (shaped(DK, F32), unit_block, ahead),
                    (shaped(DV, F32), v_block, ahead),
                ],
                state_scratch,
                2 * ret_flops,
            )
        )
    totals = [t[2] for t in firsts]
    if group == 4:
        totals[0], parts_ffn_out[:3] = tie_parts(totals[0], parts_ffn_out[:3])
    if not balanced:
        d_swapped = totals[0]
    flat_ffn_out = [piece for part in parts_ffn_out for piece in part]
    grads_out, d_swapped, g_mixer_out, inner2, scattered["ffn_in"], *flat = exchange_states(
        range(local_heads),
        totals,
        True,
        (
            d_swapped,
            g_mixer_out,
            inner2,
            scattered["ffn_in"],
            *(t for inner in inners for t in inner),
            *flat_ffn_out,
        ),
    )
    scattered["mixer_out"] = reduce_shard(g_mixer_out)
    inners = [flat[3 * h : 3 * h + 3] for h in range(local_heads)]
    rest = flat[3 * local_heads :]
    parts_ffn_out = [tuple(rest.pop(0) for _ in part) for part in parts_ffn_out]
    parts_ffn_in = spread(scattered["ffn_in"])
    if balanced:
        d_gate_pairs = [
            [
                ((d_gates[0], 0), (d_swapped, 0)),
                ((d_gates[1], 0), (d_gates[0], 0)),
                ((d_gates[1], 1), (d_gates[0], 1)),
            ],
            [((d_swapped, 0), (d_gates[1], 0))],
        ]
    else:
        d_gate_pairs = [[((t, 0), (t, 0)), ((t, 1), (t, 1))] for t in d_gates]
    by_units = [None] * local_heads
    extra_v = None
    for h in reversed(range(local_heads)):
        weights, q, k, v, gates, state_in = heads_kept[h]
        d_out = firsts[h][1]
        d_q, d_k, d_v = inners[h]
        count = len(roles[h])
        lone = "va" not in roles[h]
        by_units[h], *extra = head_call(
            functools.partial(outer_back_kernel, roles[h]),
            blocks,
            [
                params[h],
                (q, unit_block, behind),
                (k, unit_block, behind),
                (v, v_block, behind),
                (d_out, v_block, behind),
                (d_q, unit_block, behind),
                (d_k, unit_block, behind),
                (d_v, v_block, behind),
                (q_decays[h], (blk, 1), whole),
                (k_decays[h], (blk, 1), whole),
                (grads_out[h], (DK, DV), whole),
                *((*t, behind) for t in turns),
            ]
            + ([(extra_v, unit_block, behind)] if "xv" in roles[h] else [])
            + [columns(v, c, behind) for pair in d_gate_pairs[h] for v, c in pair],
            [(shaped(count * DK, BF16), (blk, count * DK), behind)]
            + ([(shaped(DK, BF16), unit_block, behind)] if lone else []),
            state_scratch,
            6 * seg_len * DK * DV,
        )
        extra_v = extra[0] if extra else None

    by_units[0], parts_ffn_in[:3] = tie_parts(by_units[0], parts_ffn_in[:3])
    by_units[-1], parts_ffn_in = tie_parts(by_units[-1], parts_ffn_in)
    by_units[-1], scattered["mixer_out"] = tie(by_units[-1], scattered["mixer_out"])
    parts_mixer_out = spread(scattered["mixer_out"])
    by_units[0], inner2 = tie(by_units[0], inner2)
    if group == 4:
        late = first_step(near_rows(dot_nt(inner2, w_ffn_out, BF16)))
    else:
        late = send_blocks(near_rows(dot_nt(inner2, w_ffn_out, BF16)))
    g_slots = []
    for h in range(local_heads):
        g_unit = dot_tn(by_units[h], normed, BF16)
        if not balanced:
            cut = g_unit.reshape(-1, DK, width)
            g_unit = jnp.concatenate(
                [pick(cut, jnp.maximum(held[h, c, s], 0)) for c in range(segments)], axis=0
            )
        if h == local_heads - 1:
            tile = 512
            rights = [t[0] for t in heads_kept]
            (d_normed,) = head_call(
                functools.partial(join_kernel, local_heads),
                width // tile,
                [(t, t.shape, whole) for t in by_units]
                + [(t, (t.shape[0], tile), lambda n: (0, n)) for t in rights],
                [(shaped(width, BF16), (seg_len, tile), lambda n: (0, n))],
                [],
                2 * seg_len * width * sum(t.shape[0] for t in rights),
            )
            g_unit, d_normed = tie(g_unit, d_normed)
        g_slots.append(reduce_shard(g_unit))
    if group == 4:
        blocks_late, ra, rb = late
        d_normed, ra, rb = tie(d_normed, ra, rb)
        late = blocks_late, ra, rb
        d_normed, parts_mixer_out[:3] = tie_parts(d_normed, parts_mixer_out[:3])
        d_normed = second_step(*first_step(seq_rows(d_normed)))
        output = (resid + second_step(*late)).astype(BF16)
    else:
        d_normed = add_blocks(*send_blocks(seq_rows(d_normed)))
        output = (resid + add_blocks(*late)).astype(BF16)

    ignored8, norm1_back = jax.vjp(rms_scale, xf, gain_attn)
    d_x_part, d_gain_attn = norm1_back(d_normed)
    input_grad = (d_resid + d_x_part).astype(BF16)
    gains = jnp.concatenate([d_gain_attn, d_gain_ffn])[None]
    step = 1
    while step < group:
        gains = gains + swap(gains, step)
        step *= 2
    gains = lax.all_to_all(
        jnp.broadcast_to(gains, (segments, 2 * width)),
        "shard",
        split_axis=0,
        concat_axis=0,
        tiled=True,
    )
    gains = jnp.sum(gains, axis=0)
    near = jnp.arange(group)
    g_ffn_in = place_blocks(
        parts_ffn_in, s ^ near, near, ffn_in.shape, (sub, width), lambda o, n: (n, 0)
    )
    if sub % 128 == 0:
        g_ffn_out = place_blocks(
            parts_ffn_out,
            s ^ near,
            near,
            ffn_out.shape,
            (ffn_out.shape[0], sub),
            lambda o, n: (0, o * group + n),
            outer=segments // 2,
        )
    else:
        g_ffn_out = jnp.transpose(
            ordered(parts_ffn_out).reshape(group, ffn_out.shape[0], segments // 2, sub),
            (1, 2, 0, 3),
        ).reshape(ffn_out.shape).astype(F32)

    parts = []
    for h in range(local_heads):
        last = h == local_heads - 1
        if h == 0:
            g_slots[h], g_ffn_in, g_ffn_out, input_grad, output = tie(
                g_slots[h], g_ffn_in, g_ffn_out, input_grad, output
            )
            g_slots[h], parts_mixer_out = tie_parts(g_slots[h], parts_mixer_out)
            g_slots[h], gains = tie(g_slots[h], gains)
        if last:
            pieces = parts_mixer_out[0]
            pieces0, parts = tie_parts(pieces[0], parts)
            parts_mixer_out[0] = (pieces0, *pieces[1:])
            g_mixer_out = place_blocks(
                parts_mixer_out,
                s ^ near,
                near,
                mixer_out.shape,
                (mixer_out.shape[0], DV),
                lambda o, n: (0, o * group + n),
                outer=local_heads,
            )
            g_slots[h], g_mixer_out = tie(g_slots[h], g_mixer_out)
        here = spread(g_slots[h])
        if balanced and last:
            there = [tuple(cross(piece, 1) for piece in part) for part in here]
            parts += [a + b for a, b in zip(here, there)] + [b + a for a, b in zip(here, there)]
        else:
            lend_here = lend[j] if balanced else lend[h, j]
            stack = jnp.stack([jnp.concatenate(part, axis=0) for part in here])
            parts += here + [
                (cross(pick(stack, s ^ lend_here[n]), 1),) for n in range(lend_here.shape[0])
            ]
    gain_attn_grad, gain_ffn_grad = gains[:width], gains[width:]
    found = back[j]
    if balanced:
        spare = lend.shape[-1]
        source = jnp.where(
            found[:, 0] == 0,
            s ^ found[:, 1],
            jnp.where(
                found[:, 0] == 1,
                group + found[:, 1],
                group + spare + core * group + (s ^ found[:, 1]),
            ),
        )
    else:
        source = found[:, 0] * (group + lend.shape[-1]) + jnp.where(
            found[:, 2] < 0, s ^ found[:, 1], group + found[:, 2]
        )
    g_mixer_in = place_blocks(
        parts,
        jnp.arange(source.shape[0]),
        source,
        mixer_in.shape,
        (DK, width),
        lambda o, n: (n, 0),
    )
    return (
        output,
        input_grad,
        gain_attn_grad,
        gain_ffn_grad,
        g_mixer_in,
        g_mixer_out,
        g_ffn_in,
        g_ffn_out,
    )


def solution(mesh):
    return jax.shard_map(
        local,
        mesh=mesh,
        in_specs=(
            P(("shard", "seq"), None),
            P(("shard", "seq"), None),
            P(),
            P(),
            P("shard", None),
            P("shard", None),
            P("shard", None),
            P("shard", None),
            P(),
            P(),
        ),
        out_specs=(
            P(("shard", "seq"), None),
            P(("shard", "seq"), None),
            P(),
            P(),
            P("shard", None),
            P("shard", None),
            P("shard", None),
            P("shard", None),
        ),
        check_vma=False,
    )
```

```python
import functools

import jax
import jax.numpy as jnp
import numpy as np
from jax import lax
from jax.experimental import pallas as pl
from jax.experimental.pallas import tpu as pltpu
from jax.sharding import PartitionSpec as P

DK = 256
DV = 512
FF = 4096
QK = 2048
V = 4096


EPS_NORM = 1e-06
EPS_GROUP = 1e-05

F32 = jnp.float32
BF16 = jnp.bfloat16


def dot_nt(left, right, kind=F32):
    return lax.dot_general(
        left, right, (((1,), (1,)), ((), ())), preferred_element_type=F32
    ).astype(kind)


def dot_nn(left, right, kind=F32):
    return lax.dot_general(
        left, right, (((1,), (0,)), ((), ())), preferred_element_type=F32
    ).astype(kind)


def dot_tn(left, right, kind=F32):
    return lax.dot_general(
        left, right, (((0,), (0,)), ((), ())), preferred_element_type=F32
    ).astype(kind)


def rms_scale(v, gain):
    return v * lax.rsqrt(jnp.mean(v * v, axis=-1, keepdims=True) + EPS_NORM) * gain


def gated_gelu(first, second):
    return jax.nn.gelu(first) * second


def unit_owners(heads):
    owners = [(n, 0) for n in range(heads)] + [(n, 1) for n in range(heads)]
    for base in (2, 4):
        owners += [(n, base + half) for n in range(heads) for half in range(2)]
    return owners


def balanced_tables():
    group, segments, per_shard = 4, 8, 6
    number = {owner: u for u, owner in enumerate(unit_owners(8))}
    keep = np.full((2, segments, group), -1, np.int32)
    give = np.zeros((2, segments, group), np.int32)
    back = np.zeros((segments, per_shard, 2), np.int32)
    lend = [[] for _ in range(segments)]
    seen = set()
    for s in range(group):
        a, b = s, s + 4
        if s < 2:
            gates = [(a, 4), (b, 4), (b, 5)], (b + 2, 5)
        else:
            gates = [(a - 2, 5), (a, 4), (a, 5)], (b, 4)
        first = [(a, 0), (a, 1), (a, 2), (a, 3), (b, 2)] + gates[0]
        second = [(b, 0), (b, 1), (b, 3), gates[1]]
        for slot, owner in enumerate(first):
            home, index = divmod(number[owner], per_shard)
            seen.add(number[owner])
            assert home // 2 == slot // 2
            if home == slot:
                keep[0, slot, s] = index
                back[home, index] = (0, s)
            else:
                give[0, home, s] = index
                back[home, index] = (1, len(lend[slot]))
                lend[slot].append(s)
        for chip, owner in enumerate(second):
            home, index = divmod(number[owner], per_shard)
            seen.add(number[owner])
            assert home // 2 == chip
            keep[1, home, s] = index
            give[1, home, s] = index
            back[home, index] = (2, s)
    assert len(seen) == segments * per_shard
    most = max(len(t) for t in lend)
    return keep, give, back, np.asarray([(t + [0] * most)[:most] for t in lend], np.int32)


def unit_tables(group, local_heads, segments):
    heads = group * local_heads
    owners = unit_owners(heads)
    per_shard = len(owners) // segments
    keep = np.full((local_heads, segments, group), -1, np.int32)
    give = np.zeros((local_heads, segments, group), np.int32)
    place = np.zeros((local_heads, group, 6), np.int32)
    held = np.full((local_heads, segments, group), -1, np.int32)
    slot_of = {}
    for chip in range(segments // 2):
        for head in range(heads):
            h, s = divmod(head, group)
            span = range(2 * per_shard * chip, 2 * per_shard * (chip + 1))
            mine = [u for u in span if owners[u][0] == head]
            assert len(mine) <= 2
            for n, u in enumerate(mine):
                home = u // per_shard
                slot = home if len(mine) == 1 else 2 * chip + n
                if slot == home:
                    keep[h, slot, s] = u % per_shard
                else:
                    give[h, home, s] = u % per_shard
                place[h, s, owners[u][1]] = slot
                held[h, slot, s] = owners[u][1]
                slot_of[u] = slot
    lends = [[[] for _ in range(segments)] for _ in range(local_heads)]
    back = np.zeros((segments, per_shard, 3), np.int32)
    for u, (head, _) in enumerate(owners):
        home = u // per_shard
        h, s = divmod(head, group)
        back[home, u % per_shard] = (h, s, -1)
        if slot_of[u] != home:
            assert slot_of[u] == home ^ 1
            back[home, u % per_shard, 2] = len(lends[h][home ^ 1])
            lends[h][home ^ 1].append(s)
    most = max(1, max(len(t) for row in lends for t in row))
    lend = np.asarray(
        [[(t + [0] * most)[:most] for t in row] for row in lends], np.int32
    )
    return keep, give, place, held, back, lend


def tie(*values):
    return lax.optimization_barrier(values)


def mm(left, right, dims):
    return lax.dot_general(left, right, (dims, ((), ())), preferred_element_type=F32)


NN = ((1,), (0,))
NT = ((1,), (1,))
TN = ((0,), (0,))


def turn(v, cosine, sine):
    half = v.shape[-1] // 2
    first, second = v[:, :half], v[:, half:]
    return jnp.concatenate(
        [first * cosine - second * sine, second * cosine + first * sine], axis=-1
    )


def scaled(v, decay):
    return (v.astype(F32) * decay).astype(BF16)


def project_kernel(blk, roles, carried, params, x, w, cosine, sine, k_decay, *refs):
    if carried:
        v_a, *refs = refs
    q, k, v, total, gates, *rest = refs
    y = rest[-1]
    rows = y.shape[0]
    y[...] = mm(x[...], w[...], NT)

    def put(role, part, gate_at):
        value = y[:, part * DK : (part + 1) * DK]
        if role == "q":
            q[...] = turn(value, cosine[...], sine[...]).astype(BF16)
        elif role == "k":
            k[...] = turn(value, cosine[...], sine[...]).astype(BF16)
        elif role == "va":
            v[:, :DK] = value.astype(BF16)
        elif role == "vb":
            v[:, DK:] = value.astype(BF16)
        elif role == "xv":
            rest[0][...] = value.astype(BF16)
        else:
            gates[:, gate_at * DK : (gate_at + 1) * DK] = value.astype(BF16)

    for step in range(len(roles) // 2):

        @pl.when(pl.program_id(0) == step)
        def _(step=step):
            for part in range(2):
                at = 2 * step + part
                put(roles[at], part, roles[:at].count("g"))
            if step == 1:
                if carried:
                    v[:, :DK] = v_a[...]
                state = jnp.zeros(total.shape, F32)
                for r in range(0, rows, blk):
                    kd = scaled(k[r : r + blk, :], k_decay[...])
                    state = params[0] * state + mm(kd, v[r : r + blk, :], TN)
                total[...] = state.astype(BF16)


def join_kernel(count, *refs):
    out = refs[-1]
    total = mm(refs[0][...], refs[count][...], NN)
    for n in range(1, count):
        total += mm(refs[n][...], refs[count + n][...], NN)
    out[...] = total.astype(out.dtype)


def select(params, low, high):
    return jnp.where(params[1] > 0.5, low[...].astype(F32), high[...].astype(F32))


def retain_kernel(
    params, q, k, v, low_a, high_a, low_b, high_b, mask, q_decay, k_decay, start,
    hidden, mixed, kept, state,
):
    @pl.when(pl.program_id(0) == 0)
    def _():
        state[...] = start[...].astype(F32)

    weights = (mm(q[...], k[...], NT) * mask[...]).astype(BF16)
    o = mm(weights, v[...], NN)
    o += mm(scaled(q[...], q_decay[...]), state[...].astype(BF16), NN)
    state[...] = params[0] * state[...] + mm(scaled(k[...], k_decay[...]), v[...], TN)
    o = o - jnp.mean(o, axis=-1, keepdims=True)
    inverse = lax.rsqrt(jnp.mean(o * o, axis=-1, keepdims=True) + EPS_GROUP)
    kept[...] = inverse
    low = (o * inverse).astype(BF16)
    mixed[...] = low
    for n, (one, two) in enumerate(((low_a, high_a), (low_b, high_b))):
        columns = slice(n * DK, (n + 1) * DK)
        g = select(params, one, two)
        hidden[:, columns] = (g * jax.nn.sigmoid(g) * low[:, columns].astype(F32)).astype(BF16)


def take(refs, counts):
    pieces, at = [], 0
    for count in counts:
        pieces.append(refs[at : at + count])
        at += count
    return pieces


def gate_back_kernel(heads, params, d_attn, w_out, *refs):
    inputs = take(refs, [8] * heads)
    outputs = take(refs[8 * heads :], [3] * heads)
    states = refs[11 * heads :]

    @pl.when(pl.program_id(0) == 0)
    def _():
        for state in states:
            state[...] = jnp.zeros(state.shape, F32)

    d_hidden = mm(d_attn[...], w_out[...], NN)
    for h in range(heads):
        low_a, high_a, low_b, high_b, mixed, inverse, q, q_decay = inputs[h]
        d_gate, d_out, total = outputs[h]
        g = jnp.concatenate(
            [select(params, low_a, high_a), select(params, low_b, high_b)], axis=1
        )
        dh = d_hidden[:, h * DV : (h + 1) * DV]
        sig = jax.nn.sigmoid(g)
        o = mixed[...].astype(F32)
        d_gate[...] = (dh * o * (sig * (1.0 + g * (1.0 - sig)))).astype(BF16)
        dy = (dh * (g * sig)).astype(BF16).astype(F32)
        do = inverse[...] * (
            dy
            - jnp.mean(dy, axis=-1, keepdims=True)
            - o * jnp.mean(dy * o, axis=-1, keepdims=True)
        )
        do = do.astype(BF16)
        d_out[...] = do
        state = states[h]
        state[...] = params[2 + h] * state[...] + mm(scaled(q[...], q_decay[...]), do, TN)
        total[...] = state[...].astype(BF16)


def inner_back_kernel(heads, params, cosine, sine, *refs):
    inputs = take(refs, [8] * heads)
    outputs = take(refs[8 * heads :], [3] * heads)
    states = refs[11 * heads :]

    @pl.when(pl.program_id(0) == 0)
    def _():
        for h in range(heads):
            states[h][...] = inputs[h][7][...].astype(F32)

    for h in range(heads):
        q, k, v, d_out, mask, q_decay, k_decay, ignored = inputs[h]
        d_q, d_k, d_v = outputs[h]
        state = states[h]
        do = d_out[...]
        weights = (mm(q[...], k[...], NT) * mask[...]).astype(BF16)
        d_v[...] = mm(weights, do, TN)
        d_scores = mm(do, v[...], NT).astype(BF16).astype(F32)
        d_scores = (d_scores * mask[...]).astype(BF16)
        d_k[...] = mm(d_scores, q[...], TN)
        far = mm(do, state[...].astype(BF16), NT).astype(BF16).astype(F32)
        dq = mm(d_scores, k[...], NN) + far * q_decay[...]
        dq = dq.astype(BF16).astype(F32)
        d_q[...] = turn(dq, cosine[...], -sine[...]).astype(BF16)
        state[...] = params[2 + h] * state[...] + mm(scaled(k[...], k_decay[...]), v[...], TN)


def outer_back_kernel(roles, params, cosine, sine, *refs):
    heads = len(roles)
    counts = [10 + 2 * t.count("g") for t in roles]
    inputs = take(refs, counts)
    outputs = refs[sum(counts) : sum(counts) + heads]
    states = refs[sum(counts) + heads :]

    @pl.when(pl.program_id(0) == 0)
    def _():
        for h in range(heads):
            states[h][...] = inputs[h][9][...].astype(F32)

    other = None
    for h in reversed(range(heads)):
        q, k, v, d_out, d_q, d_k, d_v, q_decay, k_decay, ignored, *gates = inputs[h]
        state = states[h]
        low = state[...].astype(BF16)
        far = mm(v[...], low, NT).astype(BF16).astype(F32)
        dk = (d_k[...] + far * k_decay[...]).astype(BF16).astype(F32)
        dk = turn(dk, cosine[...], -sine[...]).astype(BF16)
        dv = (d_v[...] + mm(scaled(k[...], k_decay[...]), low, NN)).astype(BF16)
        for n, role in enumerate(roles[h]):
            if role == "q":
                value = d_q[...]
            elif role == "k":
                value = dk
            elif role == "va":
                value = dv[:, :DK]
            elif role == "vb":
                value = dv[:, DK:]
            elif role == "xv":
                value = other
            else:
                value = select(params, gates.pop(0), gates.pop(0)).astype(BF16)
            outputs[h][:, n * DK : (n + 1) * DK] = value
        other = dv[:, :DK]
        state[...] = params[2 + h] * state[...] + mm(scaled(q[...], q_decay[...]), d_out[...], TN)


def head_call(kernel, grid, operands, outputs, scratch, flops):
    arrays = [t[0] for t in operands]
    size = sum(t.size * t.dtype.itemsize for t in arrays + [t[0] for t in outputs])
    call = pl.pallas_call(
        kernel,
        grid=(grid,),
        in_specs=[
            pl.BlockSpec(memory_space=pltpu.SMEM) if block is None else pl.BlockSpec(block, where)
            for _, block, where in operands
        ],
        out_specs=[pl.BlockSpec(block, where) for _, block, where in outputs],
        scratch_shapes=scratch,
        out_shape=[t[0] for t in outputs],
        compiler_params=pltpu.CompilerParams(vmem_limit_bytes=56 * 2**20),
        cost_estimate=pl.CostEstimate(flops=flops, bytes_accessed=size, transcendentals=0),
    )
    return list(call(*arrays))


def place_kernel(parts, target, source, *refs):
    out = refs[-1]
    code = source[pl.program_id(1)]
    for i, part in enumerate(parts):

        @pl.when(code == i)
        def _(part=part):
            row = 0
            for n in part:
                piece = refs[n]
                out[row : row + piece.shape[0], :] = piece[...].astype(F32)
                row += piece.shape[0]


def place_blocks(parts, target, source, shape, block, where, outer=1):
    flat, index = [], []
    for part in parts:
        for piece in part:
            if not any(piece is t for t in flat):
                flat.append(piece)
        index.append([next(n for n, t in enumerate(flat) if t is piece) for piece in part])
    return pl.pallas_call(
        functools.partial(place_kernel, index),
        grid_spec=pltpu.PrefetchScalarGridSpec(
            num_scalar_prefetch=2,
            grid=(outer, target.shape[0]),
            in_specs=[
                pl.BlockSpec((t.shape[0], t.shape[1] // outer), lambda o, n, target, source: (0, o))
                for t in flat
            ],
            out_specs=pl.BlockSpec(block, lambda o, n, target, source: where(o, target[n])),
        ),
        out_shape=jax.ShapeDtypeStruct(shape, F32),
        compiler_params=pltpu.CompilerParams(vmem_limit_bytes=48 * 2**20),
    )(target.astype(jnp.int32), source.astype(jnp.int32), *flat)


def local(
    tokens,
    cotangent,
    gain_attn,
    gain_ffn,
    mixer_in,
    mixer_out,
    ffn_in,
    ffn_out,
    segment_order,
    decay_index,
):
    rows, width = tokens.shape
    group = lax.axis_size("seq")
    segments = lax.axis_size("shard")
    heads = decay_index.shape[0]
    local_heads = heads // group
    seg_len = rows * group
    blk = min(512, seg_len)
    blocks = seg_len // blk
    vcols = local_heads * DV
    s = lax.axis_index("seq")
    j = lax.axis_index("shard")

    def swap(v, d):
        return lax.ppermute(v, "seq", [(i, i ^ d) for i in range(group)])

    def cross(v, d):
        return lax.ppermute(v, "shard", [(i, i ^ d) for i in range(segments)])

    def pick(v, i):
        return lax.dynamic_index_in_dim(v, i, 0, keepdims=False)

    def spread(v):
        if group == 4:
            h = v.shape[0] // 2
            r1 = swap(v, 1)
            r2 = swap(v, 2)
            return [(v,), (r1,), (r2,), (swap(r1[:h], 2), swap(r2[h:], 1))]
        return [(v,)] + [(swap(v, d),) for d in range(1, group)]

    def ordered(parts):
        r = parts[0][0].shape[0]
        out = jnp.zeros((group * r,) + parts[0][0].shape[1:], parts[0][0].dtype)
        for d, part in enumerate(parts):
            row = (s ^ d) * r
            for piece in part:
                out = lax.dynamic_update_slice_in_dim(out, piece, row, 0)
                row = row + piece.shape[0]
        return out

    def gather_near(v):
        return jnp.concatenate([piece for part in spread(v) for piece in part], axis=0)

    def gather_seq(v):
        return ordered(spread(v))

    def first_step(blk_of):
        b = [blk_of(d) for d in range(4)]
        h = b[0].shape[0] // 2
        sa = jnp.concatenate([b[1][:h], b[3][:h]], axis=0)
        sb = jnp.concatenate([b[2][h:], b[3][h:]], axis=0)
        sa, sb = tie(sa, sb)
        return b, swap(sa, 1), swap(sb, 2)

    def second_step(b, ra, rb):
        h = b[0].shape[0] // 2
        ra, rb = ra.astype(F32), rb.astype(F32)
        qa = (b[2][:h].astype(F32) + ra[h:]).astype(BF16)
        qb = (b[1][h:].astype(F32) + rb[h:]).astype(BF16)
        qa, qb = tie(qa, qb)
        qa, qb = swap(qa, 2), swap(qb, 1)
        top = b[0][:h].astype(F32) + ra[:h] + qa.astype(F32)
        return jnp.concatenate([top, b[0][h:].astype(F32) + rb[:h] + qb.astype(F32)], axis=0)

    def send_blocks(blk_of):
        sent = tie(*(blk_of(d) for d in range(group)))
        return sent[0], [swap(sent[d], d) for d in range(group - 1, 0, -1)]

    def add_blocks(own, got):
        own = own.astype(F32)
        for t in got:
            own = own + t.astype(F32)
        return own

    def near_rows(v):
        return lambda d: v[d * rows : (d + 1) * rows]

    def seq_rows(v):
        return lambda d: lax.dynamic_slice_in_dim(v, (s ^ d) * rows, rows, 0)

    def gather_shard(v):
        return lax.all_gather(v, "shard", axis=0, tiled=True)

    def reduce_shard(v):
        return lax.psum_scatter(v, "shard", scatter_dimension=0, tiled=True)

    balanced = group == 4 and local_heads == 2 and segments == 8
    units = mixer_in.reshape(-1, DK, width)
    if balanced:
        keep, give, back, lend = (jnp.asarray(t) for t in balanced_tables())
        core = j % 2
    else:
        keep, give, place, held, back, lend = (
            jnp.asarray(t) for t in unit_tables(group, local_heads, segments)
        )

    def offered(h):
        kept, given = keep[h, j, s], give[h, j, s]
        if balanced and h == 1:
            cut = mixer_in.reshape(-1, DK // 2, width)
            own = pick(cut, 2 * jnp.maximum(kept, 0) + core)
            given = cross(pick(cut, 2 * given + 1 - core), 1)
        else:
            own = pick(units, jnp.maximum(kept, 0))
            given = cross(pick(units, given), 1)
        return jnp.where(kept >= 0, own, given)

    sub = ffn_in.shape[0] // group
    ffn_out_cut = ffn_out.reshape(ffn_out.shape[0], segments // 2, group, sub)

    my_rank = jnp.sum(jnp.where(jnp.arange(segments) == j, segment_order, 0))
    all_logs = jnp.log1p(-jnp.exp2(-(5.0 + decay_index.astype(F32))))
    logs = lax.dynamic_index_in_dim(all_logs.reshape(local_heads, group), s, 1, keepdims=False)
    half = DK // 2
    inv_freq = jnp.exp(-jnp.log(10000.0) * jnp.arange(half).astype(F32) / half)
    positions = my_rank * seg_len + jnp.arange(seg_len, dtype=jnp.int32)
    angles = positions.astype(F32)[:, None] * inv_freq[None, :]
    cosine = jnp.cos(angles)
    sine = jnp.sin(angles)
    steps = jnp.arange(blk).astype(F32)
    gap = steps[:, None] - steps[None, :]
    masks = jnp.where(
        gap[None] >= 0.0, jnp.exp(jnp.maximum(gap, 0.0)[None] * logs[:, None, None]), 0.0
    )
    q_decays = jnp.exp((steps + 1.0)[None, :] * logs[:, None])[..., None]
    k_decays = jnp.exp((blk - 1.0 - steps)[None, :] * logs[:, None])[..., None]
    block_decays = jnp.exp(blk * logs)

    xf = tokens.astype(F32)
    normed = gather_seq(rms_scale(xf, gain_attn).astype(BF16))
    d_ffn = gather_near(cotangent)
    slots = [gather_shard(offered(0))]
    slots[0], normed, d_ffn, cosine, sine, masks, q_decays, k_decays = tie(
        slots[0], normed, d_ffn, cosine, sine, masks, q_decays, k_decays
    )
    for h in range(1, local_heads):
        slots.append(gather_shard(offered(h)))
    mixer_out_cut = jnp.concatenate(
        [
            lax.dynamic_slice_in_dim(mixer_out, (h * group + s) * DV, DV, 1)
            for h in range(local_heads)
        ],
        axis=1,
    )
    mixer_out_cut, slots[0] = tie(mixer_out_cut, slots[0])
    w_out = gather_shard(mixer_out_cut)
    later = [
        lax.dynamic_slice_in_dim(ffn_in, s * sub, sub, 0),
        lax.dynamic_index_in_dim(ffn_out_cut, s, 2, keepdims=False).reshape(ffn_out.shape[0], -1),
    ]
    inner_cols = later[1].shape[1]

    ranks = segment_order
    piece = DK // segments

    def exchange_states(hs, totals, reverse, beside=()):
        cut = jnp.concatenate([t.reshape(segments, piece, DV) for t in totals], axis=1)
        got = lax.all_to_all(cut, "shard", split_axis=0, concat_axis=0, tiled=True)
        got, *beside = tie(got, *beside)
        apart = ranks[:, None] - ranks[None, :] - 1
        if reverse:
            apart = -apart - 2
        distance = apart.astype(F32)
        joined = []
        for n, h in enumerate(hs):
            coef = jnp.where(
                distance >= 0.0, jnp.exp(jnp.maximum(distance, 0.0) * seg_len * logs[h]), 0.0
            )
            part = got[:, n * piece : (n + 1) * piece].astype(F32)
            joined.append(jnp.sum(coef[..., None, None] * part[None], axis=1).astype(BF16))
        joined = jnp.concatenate(joined, axis=1)
        back_cut = lax.all_to_all(joined, "shard", split_axis=0, concat_axis=0, tiled=True)
        states = [
            back_cut[:, n * piece : (n + 1) * piece].reshape(DK, DV) for n in range(len(hs))
        ]
        return (states, *beside)

    def whole(n):
        return (0, 0)

    def ahead(n):
        return (n, 0)

    def behind(n):
        return (blocks - 1 - n, 0)

    def shaped(columns, kind, r=seg_len):
        return jax.ShapeDtypeStruct((r, columns), kind)

    state_scratch = [pltpu.VMEM((DK, DV), F32)]
    half_block = (blk, half)
    unit_block, v_block = (blk, DK), (blk, DV)
    ret_flops = 2 * seg_len * (DK + DV) * (blk + DK)
    low = s < group // 2
    if balanced:
        roles = [["q", "k", "va", "vb", "xv", "g", "g", "g"], ["q", "k", "vb", "g"]]
    else:
        roles = [["q", "k", "va", "vb", "g", "g"]] * local_heads
    params = [
        (jnp.stack([block_decays[h], low.astype(F32)]), None, None) for h in range(local_heads)
    ]
    heads_kept = []
    extra_v = None
    for h in range(local_heads):
        if balanced:
            weights = slots[h]
        else:
            cut = slots[h].reshape(-1, DK, width)
            weights = jnp.concatenate([pick(cut, place[h, s, c]) for c in range(6)], axis=0)
        carried = "va" not in roles[h]
        gate_count = roles[h].count("g")
        q, k, v, total, gates, *extra = head_call(
            functools.partial(project_kernel, blk, roles[h], carried),
            len(roles[h]) // 2,
            [
                params[h],
                (normed, (seg_len, width), whole),
                (weights, (2 * DK, width), ahead),
                (cosine, (seg_len, half), whole),
                (sine, (seg_len, half), whole),
                (k_decays[h], (blk, 1), whole),
            ]
            + ([(extra_v, (seg_len, DK), whole)] if carried else []),
            [
                (shaped(DK, BF16), (seg_len, DK), whole),
                (shaped(DK, BF16), (seg_len, DK), whole),
                (shaped(DV, BF16), (seg_len, DV), whole),
                (shaped(DV, BF16, DK), (DK, DV), whole),
                (shaped(gate_count * DK, BF16), (seg_len, gate_count * DK), whole),
            ]
            + ([(shaped(DK, BF16), (seg_len, DK), whole)] if "xv" in roles[h] else []),
            [pltpu.VMEM((seg_len, 2 * DK), F32)],
            2 * seg_len * width * len(roles[h]) * DK,
        )
        extra_v = extra[0] if extra else None
        (state_in,) = exchange_states([h], [total], False)[0]
        if h + 1 < local_heads:
            slots[h + 1], state_in, *later[:] = tie(slots[h + 1], state_in, *later)
        heads_kept.append((weights, q, k, v, gates, state_in))

    def columns(v, c, order):
        return (v, unit_block, lambda n, c=c: (order(n)[0], c))

    if balanced:
        gates0, gates1 = heads_kept[0][4], heads_kept[1][4]
        swapped = swap(jnp.where(low, gates1, gates0[:, :DK]), 2)

        def gate_operands(h, order):
            if h == 0:
                four = (gates0, 0), (gates0, 1), (swapped, 0), (gates0, 2)
            else:
                four = (gates0, 1), (gates1, 0), (gates0, 2), (swapped, 0)
            return [columns(v, c, order) for v, c in four]

    else:

        def gate_operands(h, order):
            return [columns(heads_kept[h][4], c, order) for c in (0, 0, 1, 1)]

    kept = []
    for h in range(local_heads):
        weights, q, k, v, gates, state_in = heads_kept[h]
        hidden, mixed, retained = head_call(
            retain_kernel,
            blocks,
            [
                params[h],
                (q, unit_block, ahead),
                (k, unit_block, ahead),
                (v, v_block, ahead),
                *gate_operands(h, ahead),
                (masks[h], (blk, blk), whole),
                (q_decays[h], (blk, 1), whole),
                (k_decays[h], (blk, 1), whole),
                (state_in, (DK, DV), whole),
            ],
            [
                (shaped(DV, BF16), v_block, ahead),
                (shaped(DV, BF16), v_block, ahead),
                (shaped(1, F32), (blk, 1), ahead),
            ],
            state_scratch,
            ret_flops,
        )
        kept.append((retained, mixed, hidden))
    hidden = jnp.concatenate([t[-1] for t in kept], axis=1)
    w_ffn_in, w_ffn_out = (gather_shard(t) for t in later)

    resid = xf + add_blocks(*send_blocks(seq_rows(dot_nt(hidden, w_out, BF16))))
    normed2 = gather_near(rms_scale(resid, gain_ffn).astype(BF16))
    proj2 = dot_nt(normed2, w_ffn_in)
    first, second = proj2[:, :inner_cols], proj2[:, inner_cols:]
    inner2 = gated_gelu(first, second).astype(BF16)

    g_ffn_out, d_ffn = tie(dot_tn(d_ffn, inner2, BF16), d_ffn)
    scattered = {"ffn_out": reduce_shard(g_ffn_out)}
    d_inner2 = dot_nn(d_ffn, w_ffn_out)
    ignored2, gelu_back = jax.vjp(gated_gelu, first, second)
    d_first, d_second = gelu_back(d_inner2)
    dproj2 = jnp.concatenate([d_first, d_second], axis=1).astype(BF16)
    d_normed2 = dot_nn(dproj2, w_ffn_in, BF16)
    g_ffn_in = dot_tn(dproj2, normed2, BF16)
    if group == 4:
        terms, ra, rb = first_step(near_rows(d_normed2))
        ra, rb, g_ffn_in = tie(ra, rb, g_ffn_in)
        d_normed2 = second_step(terms, ra, rb)
    else:
        d_normed2 = add_blocks(*send_blocks(near_rows(d_normed2)))
    scattered["ffn_in"] = reduce_shard(g_ffn_in)
    ignored3, norm2_back = jax.vjp(rms_scale, resid, gain_ffn)
    d_resid_part, d_gain_ffn = norm2_back(d_normed2)
    d_resid = cotangent.astype(F32) + d_resid_part
    (d_attn,) = tie(d_resid.astype(BF16))
    d_attn = gather_seq(d_attn)
    d_attn, scattered["ffn_out"] = tie(d_attn, scattered["ffn_out"])
    parts_ffn_out = spread(scattered["ffn_out"])

    def tie_parts(v, parts):
        flat = tie(v, *(piece for part in parts for piece in part))
        rest = list(flat[1:])
        return flat[0], [tuple(rest.pop(0) for _ in part) for part in parts]

    all_params = (
        jnp.concatenate([jnp.stack([jnp.float32(0.0), low.astype(F32)]), block_decays]),
        None,
        None,
    )
    outs = head_call(
        functools.partial(gate_back_kernel, local_heads),
        blocks,
        [
            all_params,
            (d_attn, (blk, width), behind),
            (w_out, (width, vcols), whole),
        ]
        + [
            t
            for h in range(local_heads)
            for t in (
                *gate_operands(h, behind),
                (kept[h][1], v_block, behind),
                (kept[h][0], (blk, 1), behind),
                (heads_kept[h][1], unit_block, behind),
                (q_decays[h], (blk, 1), whole),
            )
        ],
        [
            (shaped(DV, BF16), v_block, behind),
            (shaped(DV, BF16), v_block, behind),
            (shaped(DV, BF16, DK), (DK, DV), whole),
        ]
        * local_heads,
        state_scratch * local_heads,
        2 * seg_len * (DK * DV * local_heads + width * vcols),
    )
    d_gates, d_outs, totals = outs[0::3], outs[1::3], outs[2::3]
    if balanced:
        d_swapped = swap(jnp.where(low, d_gates[0][:, DK:], d_gates[1][:, DK:]), 2)
    else:
        d_swapped = totals[0]
    if group == 4:
        totals[0], parts_ffn_out[:3] = tie_parts(totals[0], parts_ffn_out[:3])
    hidden, totals[0] = tie(hidden, totals[0])
    g_mixer_out = dot_tn(d_attn, hidden, BF16)
    inners = head_call(
        functools.partial(inner_back_kernel, local_heads),
        blocks,
        [all_params, (cosine, half_block, ahead), (sine, half_block, ahead)]
        + [
            t
            for h in range(local_heads)
            for t in (
                (heads_kept[h][1], unit_block, ahead),
                (heads_kept[h][2], unit_block, ahead),
                (heads_kept[h][3], v_block, ahead),
                (d_outs[h], v_block, ahead),
                (masks[h], (blk, blk), whole),
                (q_decays[h], (blk, 1), whole),
                (k_decays[h], (blk, 1), whole),
                (heads_kept[h][5], (DK, DV), whole),
            )
        ],
        [
            (shaped(DK, BF16), unit_block, ahead),
            (shaped(DK, F32), unit_block, ahead),
            (shaped(DV, F32), v_block, ahead),
        ]
        * local_heads,
        state_scratch * local_heads,
        2 * local_heads * ret_flops,
    )
    flat_ffn_out = [piece for part in parts_ffn_out for piece in part]
    grads_out, d_swapped, g_mixer_out, inner2, scattered["ffn_in"], *flat = exchange_states(
        range(local_heads),
        totals,
        True,
        (d_swapped, g_mixer_out, inner2, scattered["ffn_in"], *inners, *flat_ffn_out),
    )
    scattered["mixer_out"] = reduce_shard(g_mixer_out)
    inners = flat[: 3 * local_heads]
    rest = flat[3 * local_heads :]
    parts_ffn_out = [tuple(rest.pop(0) for _ in part) for part in parts_ffn_out]
    parts_ffn_in = spread(scattered["ffn_in"])
    ffn_terms, *grads_out = tie(dot_nt(inner2, w_ffn_out, BF16), *grads_out)
    if balanced:
        d_gate_pairs = [
            [
                ((d_gates[0], 0), (d_swapped, 0)),
                ((d_gates[1], 0), (d_gates[0], 0)),
                ((d_gates[1], 1), (d_gates[0], 1)),
            ],
            [((d_swapped, 0), (d_gates[1], 0))],
        ]
    else:
        d_gate_pairs = [[((t, 0), (t, 0)), ((t, 1), (t, 1))] for t in d_gates]
    by_units = head_call(
        functools.partial(outer_back_kernel, roles),
        blocks,
        [all_params, (cosine, half_block, behind), (sine, half_block, behind)]
        + [
            t
            for h in range(local_heads)
            for t in (
                (heads_kept[h][1], unit_block, behind),
                (heads_kept[h][2], unit_block, behind),
                (heads_kept[h][3], v_block, behind),
                (d_outs[h], v_block, behind),
                (inners[3 * h], unit_block, behind),
                (inners[3 * h + 1], unit_block, behind),
                (inners[3 * h + 2], v_block, behind),
                (q_decays[h], (blk, 1), whole),
                (k_decays[h], (blk, 1), whole),
                (grads_out[h], (DK, DV), whole),
                *(columns(v, c, behind) for pair in d_gate_pairs[h] for v, c in pair),
            )
        ],
        [(shaped(len(t) * DK, BF16), (blk, len(t) * DK), behind) for t in roles],
        state_scratch * local_heads,
        6 * local_heads * seg_len * DK * DV,
    )

    if group == 4:
        late = first_step(near_rows(ffn_terms))
    else:
        late = send_blocks(near_rows(ffn_terms))
    by_units[0], parts_ffn_in[:3] = tie_parts(by_units[0], parts_ffn_in[:3])
    g_units = [dot_tn(by_units[0], normed, BF16)]
    by_units[-1], g_units[0] = tie(by_units[-1], g_units[0])
    by_units[-1], scattered["mixer_out"] = tie(by_units[-1], scattered["mixer_out"])
    tile = 512
    rights = [t[0] for t in heads_kept]
    (d_normed,) = head_call(
        functools.partial(join_kernel, local_heads),
        width // tile,
        [(t, t.shape, whole) for t in by_units]
        + [(t, (t.shape[0], tile), lambda n: (0, n)) for t in rights],
        [(shaped(width, BF16), (seg_len, tile), lambda n: (0, n))],
        [],
        2 * seg_len * width * sum(t.shape[0] for t in rights),
    )
    d_normed, parts_ffn_in = tie_parts(d_normed, parts_ffn_in)
    if group == 4:
        ffn_own, ra, rb = late
        d_normed, ra, rb = tie(d_normed, ra, rb)
        first = first_step(seq_rows(d_normed))
        output = (resid + second_step(ffn_own, ra, rb)).astype(BF16)
    else:
        output = (resid + add_blocks(*late)).astype(BF16)
    output, scattered["mixer_out"] = tie(output, scattered["mixer_out"])
    parts_mixer_out = spread(scattered["mixer_out"])
    for h in range(1, local_heads):
        by_units[h], d_normed = tie(by_units[h], d_normed)
        g_units.append(dot_tn(by_units[h], normed, BF16))
    if group == 4:
        own, ra, rb = first
        ra, rb, g_units[-1] = tie(ra, rb, g_units[-1])
        d_normed = second_step(own, ra, rb)
    else:
        d_normed = add_blocks(*send_blocks(seq_rows(d_normed)))
    g_slots = []
    for h in range(local_heads):
        if not balanced:
            cut = g_units[h].reshape(-1, DK, width)
            g_units[h] = jnp.concatenate(
                [pick(cut, jnp.maximum(held[h, c, s], 0)) for c in range(segments)], axis=0
            )
        g_slots.append(reduce_shard(g_units[h]))

    ignored8, norm1_back = jax.vjp(rms_scale, xf, gain_attn)
    d_x_part, d_gain_attn = norm1_back(d_normed)
    input_grad = (d_resid + d_x_part).astype(BF16)
    gains = jnp.concatenate([d_gain_attn, d_gain_ffn])[None]
    step = 1
    while step < group:
        gains = gains + swap(gains, step)
        step *= 2
    gains = lax.all_to_all(
        jnp.broadcast_to(gains, (segments, 2 * width)),
        "shard",
        split_axis=0,
        concat_axis=0,
        tiled=True,
    )
    gains = jnp.sum(gains, axis=0)
    parts = []
    for h in range(local_heads):
        last = h == local_heads - 1
        if h == 0:
            g_slots[h], input_grad, output = tie(g_slots[h], input_grad, output)
            g_slots[h], parts_mixer_out = tie_parts(g_slots[h], parts_mixer_out)
            g_slots[h], gains = tie(g_slots[h], gains)
            parts_ffn_in[0], parts_ffn_out[0], g_slots[h] = tie(
                parts_ffn_in[0], parts_ffn_out[0], g_slots[h]
            )
            near = jnp.arange(group)
            g_ffn_in = place_blocks(
                parts_ffn_in, s ^ near, near, ffn_in.shape, (sub, width), lambda o, n: (n, 0)
            )
            if sub % 128 == 0:
                g_ffn_out = place_blocks(
                    parts_ffn_out,
                    s ^ near,
                    near,
                    ffn_out.shape,
                    (ffn_out.shape[0], sub),
                    lambda o, n: (0, o * group + n),
                    outer=segments // 2,
                )
            else:
                g_ffn_out = jnp.transpose(
                    ordered(parts_ffn_out).reshape(group, ffn_out.shape[0], segments // 2, sub),
                    (1, 2, 0, 3),
                ).reshape(ffn_out.shape).astype(F32)
        if last:
            pieces = parts_mixer_out[0]
            pieces0, parts = tie_parts(pieces[0], parts)
            parts_mixer_out[0] = (pieces0, *pieces[1:])
            g_mixer_out = place_blocks(
                parts_mixer_out,
                s ^ near,
                near,
                mixer_out.shape,
                (mixer_out.shape[0], DV),
                lambda o, n: (0, o * group + n),
                outer=local_heads,
            )
            g_slots[h], g_mixer_out, g_ffn_in, g_ffn_out = tie(
                g_slots[h], g_mixer_out, g_ffn_in, g_ffn_out
            )
        here = spread(g_slots[h])
        if balanced and last:
            there = [tuple(cross(piece, 1) for piece in part) for part in here]
            parts += [a + b for a, b in zip(here, there)] + [b + a for a, b in zip(here, there)]
        else:
            lend_here = lend[j] if balanced else lend[h, j]
            stack = jnp.stack([jnp.concatenate(part, axis=0) for part in here])
            parts += here + [
                (cross(pick(stack, s ^ lend_here[n]), 1),) for n in range(lend_here.shape[0])
            ]
    gain_attn_grad, gain_ffn_grad = gains[:width], gains[width:]
    found = back[j]
    if balanced:
        spare = lend.shape[-1]
        source = jnp.where(
            found[:, 0] == 0,
            s ^ found[:, 1],
            jnp.where(
                found[:, 0] == 1,
                group + found[:, 1],
                group + spare + core * group + (s ^ found[:, 1]),
            ),
        )
    else:
        source = found[:, 0] * (group + lend.shape[-1]) + jnp.where(
            found[:, 2] < 0, s ^ found[:, 1], group + found[:, 2]
        )
    g_mixer_in = place_blocks(
        parts,
        jnp.arange(source.shape[0]),
        source,
        mixer_in.shape,
        (DK, width),
        lambda o, n: (n, 0),
    )
    return (
        output,
        input_grad,
        gain_attn_grad,
        gain_ffn_grad,
        g_mixer_in,
        g_mixer_out,
        g_ffn_in,
        g_ffn_out,
    )


def solution(mesh):
    return jax.shard_map(
        local,
        mesh=mesh,
        in_specs=(
            P(("shard", "seq"), None),
            P(("shard", "seq"), None),
            P(),
            P(),
            P("shard", None),
            P("shard", None),
            P("shard", None),
            P("shard", None),
            P(),
            P(),
        ),
        out_specs=(
            P(("shard", "seq"), None),
            P(("shard", "seq"), None),
            P(),
            P(),
            P("shard", None),
            P("shard", None),
            P("shard", None),
            P("shard", None),
        ),
        check_vma=False,
    )
```

```python
import functools

import jax
import jax.numpy as jnp
import numpy as np
from jax import lax
from jax.experimental import pallas as pl
from jax.experimental.pallas import tpu as pltpu
from jax.sharding import PartitionSpec as P

DK = 256
DV = 512
FF = 4096
QK = 2048
V = 4096


EPS_NORM = 1e-06
EPS_GROUP = 1e-05

F32 = jnp.float32
BF16 = jnp.bfloat16


def dot_nt(left, right, kind=F32):
    return lax.dot_general(
        left, right, (((1,), (1,)), ((), ())), preferred_element_type=F32
    ).astype(kind)


def dot_nn(left, right, kind=F32):
    return lax.dot_general(
        left, right, (((1,), (0,)), ((), ())), preferred_element_type=F32
    ).astype(kind)


def dot_tn(left, right, kind=F32):
    return lax.dot_general(
        left, right, (((0,), (0,)), ((), ())), preferred_element_type=F32
    ).astype(kind)


def rms_scale(v, gain):
    return v * lax.rsqrt(jnp.mean(v * v, axis=-1, keepdims=True) + EPS_NORM) * gain


def gated_gelu(first, second):
    return jax.nn.gelu(first) * second


def unit_owners(heads):
    owners = [(n, 0) for n in range(heads)] + [(n, 1) for n in range(heads)]
    for base in (2, 4):
        owners += [(n, base + half) for n in range(heads) for half in range(2)]
    return owners


def balanced_tables():
    group, segments, per_shard = 4, 8, 6
    number = {owner: u for u, owner in enumerate(unit_owners(8))}
    keep = np.full((2, segments, group), -1, np.int32)
    give = np.zeros((2, segments, group), np.int32)
    back = np.zeros((segments, per_shard, 2), np.int32)
    lend = [[] for _ in range(segments)]
    seen = set()
    for s in range(group):
        a, b = s, s + 4
        if s < 2:
            gates = [(a, 4), (b, 4), (b, 5)], (b + 2, 5)
        else:
            gates = [(a - 2, 5), (a, 4), (a, 5)], (b, 4)
        first = [(a, 0), (a, 1), (a, 2), (a, 3), (b, 2)] + gates[0]
        second = [(b, 0), (b, 1), (b, 3), gates[1]]
        for slot, owner in enumerate(first):
            home, index = divmod(number[owner], per_shard)
            seen.add(number[owner])
            assert home // 2 == slot // 2
            if home == slot:
                keep[0, slot, s] = index
                back[home, index] = (0, s)
            else:
                give[0, home, s] = index
                back[home, index] = (1, len(lend[slot]))
                lend[slot].append(s)
        for chip, owner in enumerate(second):
            home, index = divmod(number[owner], per_shard)
            seen.add(number[owner])
            assert home // 2 == chip
            keep[1, home, s] = index
            give[1, home, s] = index
            back[home, index] = (2, s)
    assert len(seen) == segments * per_shard
    most = max(len(t) for t in lend)
    return keep, give, back, np.asarray([(t + [0] * most)[:most] for t in lend], np.int32)


def unit_tables(group, local_heads, segments):
    heads = group * local_heads
    owners = unit_owners(heads)
    per_shard = len(owners) // segments
    keep = np.full((local_heads, segments, group), -1, np.int32)
    give = np.zeros((local_heads, segments, group), np.int32)
    place = np.zeros((local_heads, group, 6), np.int32)
    held = np.full((local_heads, segments, group), -1, np.int32)
    slot_of = {}
    for chip in range(segments // 2):
        for head in range(heads):
            h, s = divmod(head, group)
            span = range(2 * per_shard * chip, 2 * per_shard * (chip + 1))
            mine = [u for u in span if owners[u][0] == head]
            assert len(mine) <= 2
            for n, u in enumerate(mine):
                home = u // per_shard
                slot = home if len(mine) == 1 else 2 * chip + n
                if slot == home:
                    keep[h, slot, s] = u % per_shard
                else:
                    give[h, home, s] = u % per_shard
                place[h, s, owners[u][1]] = slot
                held[h, slot, s] = owners[u][1]
                slot_of[u] = slot
    lends = [[[] for _ in range(segments)] for _ in range(local_heads)]
    back = np.zeros((segments, per_shard, 3), np.int32)
    for u, (head, _) in enumerate(owners):
        home = u // per_shard
        h, s = divmod(head, group)
        back[home, u % per_shard] = (h, s, -1)
        if slot_of[u] != home:
            assert slot_of[u] == home ^ 1
            back[home, u % per_shard, 2] = len(lends[h][home ^ 1])
            lends[h][home ^ 1].append(s)
    most = max(1, max(len(t) for row in lends for t in row))
    lend = np.asarray(
        [[(t + [0] * most)[:most] for t in row] for row in lends], np.int32
    )
    return keep, give, place, held, back, lend


def tie(*values):
    return lax.optimization_barrier(values)


def mm(left, right, dims):
    return lax.dot_general(left, right, (dims, ((), ())), preferred_element_type=F32)


NN = ((1,), (0,))
NT = ((1,), (1,))
TN = ((0,), (0,))


def turn(v, cosine, sine):
    half = v.shape[-1] // 2
    first, second = v[:, :half], v[:, half:]
    return jnp.concatenate(
        [first * cosine - second * sine, second * cosine + first * sine], axis=-1
    )


def scaled(v, decay):
    return (v.astype(F32) * decay).astype(BF16)


def project_kernel(blk, roles, carried, params, x, w, cosine, sine, k_decay, *refs):
    if carried:
        v_a, *refs = refs
    q, k, v, total, gates, *rest = refs
    y = rest[-1]
    rows = y.shape[0]
    y[...] = mm(x[...], w[...], NT)

    def put(role, part, gate_at):
        value = y[:, part * DK : (part + 1) * DK]
        if role == "q":
            q[...] = turn(value, cosine[...], sine[...]).astype(BF16)
        elif role == "k":
            k[...] = turn(value, cosine[...], sine[...]).astype(BF16)
        elif role == "va":
            v[:, :DK] = value.astype(BF16)
        elif role == "vb":
            v[:, DK:] = value.astype(BF16)
        elif role == "xv":
            rest[0][...] = value.astype(BF16)
        else:
            gates[:, gate_at * DK : (gate_at + 1) * DK] = value.astype(BF16)

    for step in range(len(roles) // 2):

        @pl.when(pl.program_id(0) == step)
        def _(step=step):
            for part in range(2):
                at = 2 * step + part
                put(roles[at], part, roles[:at].count("g"))
            if step == 1:
                if carried:
                    v[:, :DK] = v_a[...]
                state = jnp.zeros(total.shape, F32)
                for r in range(0, rows, blk):
                    kd = scaled(k[r : r + blk, :], k_decay[...])
                    state = params[0] * state + mm(kd, v[r : r + blk, :], TN)
                total[...] = state.astype(BF16)


def join_kernel(count, *refs):
    out = refs[-1]
    total = mm(refs[0][...], refs[count][...], NN)
    for n in range(1, count):
        total += mm(refs[n][...], refs[count + n][...], NN)
    out[...] = total.astype(out.dtype)


def select(params, low, high):
    return jnp.where(params[1] > 0.5, low[...].astype(F32), high[...].astype(F32))


def retain_kernel(
    params, q, k, v, low_a, high_a, low_b, high_b, mask, q_decay, k_decay, start,
    hidden, mixed, kept, state,
):
    @pl.when(pl.program_id(0) == 0)
    def _():
        state[...] = start[...].astype(F32)

    weights = (mm(q[...], k[...], NT) * mask[...]).astype(BF16)
    o = mm(weights, v[...], NN)
    o += mm(scaled(q[...], q_decay[...]), state[...].astype(BF16), NN)
    state[...] = params[0] * state[...] + mm(scaled(k[...], k_decay[...]), v[...], TN)
    o = o - jnp.mean(o, axis=-1, keepdims=True)
    inverse = lax.rsqrt(jnp.mean(o * o, axis=-1, keepdims=True) + EPS_GROUP)
    kept[...] = inverse
    low = (o * inverse).astype(BF16)
    mixed[...] = low
    for n, (one, two) in enumerate(((low_a, high_a), (low_b, high_b))):
        columns = slice(n * DK, (n + 1) * DK)
        g = select(params, one, two)
        hidden[:, columns] = (g * jax.nn.sigmoid(g) * low[:, columns].astype(F32)).astype(BF16)


def take(refs, counts):
    pieces, at = [], 0
    for count in counts:
        pieces.append(refs[at : at + count])
        at += count
    return pieces


def gate_back_kernel(heads, params, d_attn, w_out, *refs):
    inputs = take(refs, [8] * heads)
    outputs = take(refs[8 * heads :], [3] * heads)
    states = refs[11 * heads :]

    @pl.when(pl.program_id(0) == 0)
    def _():
        for state in states:
            state[...] = jnp.zeros(state.shape, F32)

    d_hidden = mm(d_attn[...], w_out[...], NN)
    for h in range(heads):
        low_a, high_a, low_b, high_b, mixed, inverse, q, q_decay = inputs[h]
        d_gate, d_out, total = outputs[h]
        g = jnp.concatenate(
            [select(params, low_a, high_a), select(params, low_b, high_b)], axis=1
        )
        dh = d_hidden[:, h * DV : (h + 1) * DV]
        sig = jax.nn.sigmoid(g)
        o = mixed[...].astype(F32)
        d_gate[...] = (dh * o * (sig * (1.0 + g * (1.0 - sig)))).astype(BF16)
        dy = (dh * (g * sig)).astype(BF16).astype(F32)
        do = inverse[...] * (
            dy
            - jnp.mean(dy, axis=-1, keepdims=True)
            - o * jnp.mean(dy * o, axis=-1, keepdims=True)
        )
        do = do.astype(BF16)
        d_out[...] = do
        state = states[h]
        state[...] = params[2 + h] * state[...] + mm(scaled(q[...], q_decay[...]), do, TN)
        total[...] = state[...].astype(BF16)


def inner_back_kernel(heads, params, cosine, sine, *refs):
    inputs = take(refs, [8] * heads)
    outputs = take(refs[8 * heads :], [3] * heads)
    states = refs[11 * heads :]

    @pl.when(pl.program_id(0) == 0)
    def _():
        for h in range(heads):
            states[h][...] = inputs[h][7][...].astype(F32)

    for h in range(heads):
        q, k, v, d_out, mask, q_decay, k_decay, ignored = inputs[h]
        d_q, d_k, d_v = outputs[h]
        state = states[h]
        do = d_out[...]
        weights = (mm(q[...], k[...], NT) * mask[...]).astype(BF16)
        d_v[...] = mm(weights, do, TN)
        d_scores = mm(do, v[...], NT).astype(BF16).astype(F32)
        d_scores = (d_scores * mask[...]).astype(BF16)
        d_k[...] = mm(d_scores, q[...], TN)
        far = mm(do, state[...].astype(BF16), NT).astype(BF16).astype(F32)
        dq = mm(d_scores, k[...], NN) + far * q_decay[...]
        dq = dq.astype(BF16).astype(F32)
        d_q[...] = turn(dq, cosine[...], -sine[...]).astype(BF16)
        state[...] = params[2 + h] * state[...] + mm(scaled(k[...], k_decay[...]), v[...], TN)


def outer_back_kernel(roles, params, cosine, sine, *refs):
    heads = len(roles)
    counts = [10 + 2 * t.count("g") for t in roles]
    inputs = take(refs, counts)
    outputs = refs[sum(counts) : sum(counts) + heads]
    states = refs[sum(counts) + heads :]

    @pl.when(pl.program_id(0) == 0)
    def _():
        for h in range(heads):
            states[h][...] = inputs[h][9][...].astype(F32)

    other = None
    for h in reversed(range(heads)):
        q, k, v, d_out, d_q, d_k, d_v, q_decay, k_decay, ignored, *gates = inputs[h]
        state = states[h]
        low = state[...].astype(BF16)
        far = mm(v[...], low, NT).astype(BF16).astype(F32)
        dk = (d_k[...] + far * k_decay[...]).astype(BF16).astype(F32)
        dk = turn(dk, cosine[...], -sine[...]).astype(BF16)
        dv = (d_v[...] + mm(scaled(k[...], k_decay[...]), low, NN)).astype(BF16)
        for n, role in enumerate(roles[h]):
            if role == "q":
                value = d_q[...]
            elif role == "k":
                value = dk
            elif role == "va":
                value = dv[:, :DK]
            elif role == "vb":
                value = dv[:, DK:]
            elif role == "xv":
                value = other
            else:
                value = select(params, gates.pop(0), gates.pop(0)).astype(BF16)
            outputs[h][:, n * DK : (n + 1) * DK] = value
        other = dv[:, :DK]
        state[...] = params[2 + h] * state[...] + mm(scaled(q[...], q_decay[...]), d_out[...], TN)


def head_call(kernel, grid, operands, outputs, scratch, flops):
    arrays = [t[0] for t in operands]
    size = sum(t.size * t.dtype.itemsize for t in arrays + [t[0] for t in outputs])
    call = pl.pallas_call(
        kernel,
        grid=(grid,),
        in_specs=[
            pl.BlockSpec(memory_space=pltpu.SMEM) if block is None else pl.BlockSpec(block, where)
            for _, block, where in operands
        ],
        out_specs=[pl.BlockSpec(block, where) for _, block, where in outputs],
        scratch_shapes=scratch,
        out_shape=[t[0] for t in outputs],
        compiler_params=pltpu.CompilerParams(vmem_limit_bytes=56 * 2**20),
        cost_estimate=pl.CostEstimate(flops=flops, bytes_accessed=size, transcendentals=0),
    )
    return list(call(*arrays))


def place_kernel(parts, target, source, *refs):
    out = refs[-1]
    code = source[pl.program_id(1)]
    for i, part in enumerate(parts):

        @pl.when(code == i)
        def _(part=part):
            row = 0
            for n in part:
                piece = refs[n]
                out[row : row + piece.shape[0], :] = piece[...].astype(F32)
                row += piece.shape[0]


def place_blocks(parts, target, source, shape, block, where, outer=1):
    flat, index = [], []
    for part in parts:
        for piece in part:
            if not any(piece is t for t in flat):
                flat.append(piece)
        index.append([next(n for n, t in enumerate(flat) if t is piece) for piece in part])
    return pl.pallas_call(
        functools.partial(place_kernel, index),
        grid_spec=pltpu.PrefetchScalarGridSpec(
            num_scalar_prefetch=2,
            grid=(outer, target.shape[0]),
            in_specs=[
                pl.BlockSpec((t.shape[0], t.shape[1] // outer), lambda o, n, target, source: (0, o))
                for t in flat
            ],
            out_specs=pl.BlockSpec(block, lambda o, n, target, source: where(o, target[n])),
        ),
        out_shape=jax.ShapeDtypeStruct(shape, F32),
        compiler_params=pltpu.CompilerParams(vmem_limit_bytes=48 * 2**20),
    )(target.astype(jnp.int32), source.astype(jnp.int32), *flat)


def local(
    tokens,
    cotangent,
    gain_attn,
    gain_ffn,
    mixer_in,
    mixer_out,
    ffn_in,
    ffn_out,
    segment_order,
    decay_index,
):
    rows, width = tokens.shape
    group = lax.axis_size("seq")
    segments = lax.axis_size("shard")
    heads = decay_index.shape[0]
    local_heads = heads // group
    seg_len = rows * group
    blk = min(512, seg_len)
    blocks = seg_len // blk
    vcols = local_heads * DV
    s = lax.axis_index("seq")
    j = lax.axis_index("shard")

    def swap(v, d):
        return lax.ppermute(v, "seq", [(i, i ^ d) for i in range(group)])

    def cross(v, d):
        return lax.ppermute(v, "shard", [(i, i ^ d) for i in range(segments)])

    def pick(v, i):
        return lax.dynamic_index_in_dim(v, i, 0, keepdims=False)

    def spread(v, beside=None):
        if group == 4:
            h = v.shape[0] // 2
            r1 = swap(v, 1)
            r2 = swap(v, 2)
            if beside is not None:
                r1, r2, beside[:] = tie(r1, r2, list(beside))
            return [(v,), (r1,), (r2,), (swap(r1[:h], 2), swap(r2[h:], 1))]
        return [(v,)] + [(swap(v, d),) for d in range(1, group)]

    def ordered(parts):
        r = parts[0][0].shape[0]
        out = jnp.zeros((group * r,) + parts[0][0].shape[1:], parts[0][0].dtype)
        for d, part in enumerate(parts):
            row = (s ^ d) * r
            for piece in part:
                out = lax.dynamic_update_slice_in_dim(out, piece, row, 0)
                row = row + piece.shape[0]
        return out

    def gather_near(v):
        return jnp.concatenate([piece for part in spread(v) for piece in part], axis=0)

    def gather_seq(v):
        return ordered(spread(v))

    def first_step(blk_of):
        b = [blk_of(d) for d in range(4)]
        h = b[0].shape[0] // 2
        sa = jnp.concatenate([b[1][:h], b[3][:h]], axis=0)
        sb = jnp.concatenate([b[2][h:], b[3][h:]], axis=0)
        sa, sb = tie(sa, sb)
        return b, swap(sa, 1), swap(sb, 2)

    def second_step(b, ra, rb):
        h = b[0].shape[0] // 2
        ra, rb = ra.astype(F32), rb.astype(F32)
        qa = (b[2][:h].astype(F32) + ra[h:]).astype(BF16)
        qb = (b[1][h:].astype(F32) + rb[h:]).astype(BF16)
        qa, qb = tie(qa, qb)
        qa, qb = swap(qa, 2), swap(qb, 1)
        top = b[0][:h].astype(F32) + ra[:h] + qa.astype(F32)
        return jnp.concatenate([top, b[0][h:].astype(F32) + rb[:h] + qb.astype(F32)], axis=0)

    def send_blocks(blk_of):
        sent = tie(*(blk_of(d) for d in range(group)))
        return sent[0], [swap(sent[d], d) for d in range(group - 1, 0, -1)]

    def add_blocks(own, got):
        own = own.astype(F32)
        for t in got:
            own = own + t.astype(F32)
        return own

    def near_rows(v):
        return lambda d: v[d * rows : (d + 1) * rows]

    def seq_rows(v):
        return lambda d: lax.dynamic_slice_in_dim(v, (s ^ d) * rows, rows, 0)

    def gather_shard(v):
        return lax.all_gather(v, "shard", axis=0, tiled=True)

    def reduce_shard(v):
        return lax.psum_scatter(v, "shard", scatter_dimension=0, tiled=True)

    balanced = group == 4 and local_heads == 2 and segments == 8
    units = mixer_in.reshape(-1, DK, width)
    if balanced:
        keep, give, back, lend = (jnp.asarray(t) for t in balanced_tables())
        core = j % 2
    else:
        keep, give, place, held, back, lend = (
            jnp.asarray(t) for t in unit_tables(group, local_heads, segments)
        )

    def offered(h):
        kept, given = keep[h, j, s], give[h, j, s]
        if balanced and h == 1:
            cut = mixer_in.reshape(-1, DK // 2, width)
            own = pick(cut, 2 * jnp.maximum(kept, 0) + core)
            given = cross(pick(cut, 2 * given + 1 - core), 1)
        else:
            own = pick(units, jnp.maximum(kept, 0))
            given = cross(pick(units, given), 1)
        return jnp.where(kept >= 0, own, given)

    sub = ffn_in.shape[0] // group
    ffn_out_cut = ffn_out.reshape(ffn_out.shape[0], segments // 2, group, sub)

    my_rank = jnp.sum(jnp.where(jnp.arange(segments) == j, segment_order, 0))
    all_logs = jnp.log1p(-jnp.exp2(-(5.0 + decay_index.astype(F32))))
    logs = lax.dynamic_index_in_dim(all_logs.reshape(local_heads, group), s, 1, keepdims=False)
    half = DK // 2
    inv_freq = jnp.exp(-jnp.log(10000.0) * jnp.arange(half).astype(F32) / half)
    positions = my_rank * seg_len + jnp.arange(seg_len, dtype=jnp.int32)
    angles = positions.astype(F32)[:, None] * inv_freq[None, :]
    cosine = jnp.cos(angles)
    sine = jnp.sin(angles)
    steps = jnp.arange(blk).astype(F32)
    gap = steps[:, None] - steps[None, :]
    masks = jnp.where(
        gap[None] >= 0.0, jnp.exp(jnp.maximum(gap, 0.0)[None] * logs[:, None, None]), 0.0
    )
    q_decays = jnp.exp((steps + 1.0)[None, :] * logs[:, None])[..., None]
    k_decays = jnp.exp((blk - 1.0 - steps)[None, :] * logs[:, None])[..., None]
    block_decays = jnp.exp(blk * logs)

    xf = tokens.astype(F32)
    normed = gather_seq(rms_scale(xf, gain_attn).astype(BF16))
    d_ffn = gather_near(cotangent)
    slots = [gather_shard(offered(0))]
    slots[0], normed, d_ffn, cosine, sine, masks, q_decays, k_decays = tie(
        slots[0], normed, d_ffn, cosine, sine, masks, q_decays, k_decays
    )
    for h in range(1, local_heads):
        slots.append(gather_shard(offered(h)))
    mixer_out_cut = jnp.concatenate(
        [
            lax.dynamic_slice_in_dim(mixer_out, (h * group + s) * DV, DV, 1)
            for h in range(local_heads)
        ],
        axis=1,
    )
    mixer_out_cut, slots[0] = tie(mixer_out_cut, slots[0])
    w_out = gather_shard(mixer_out_cut)
    later = [
        lax.dynamic_slice_in_dim(ffn_in, s * sub, sub, 0),
        lax.dynamic_index_in_dim(ffn_out_cut, s, 2, keepdims=False).reshape(ffn_out.shape[0], -1),
    ]
    inner_cols = later[1].shape[1]

    ranks = segment_order
    piece = DK // segments

    def exchange_states(hs, totals, reverse, beside=()):
        cut = jnp.concatenate([t.reshape(segments, piece, DV) for t in totals], axis=1)
        got = lax.all_to_all(cut, "shard", split_axis=0, concat_axis=0, tiled=True)
        got, *beside = tie(got, *beside)
        apart = ranks[:, None] - ranks[None, :] - 1
        if reverse:
            apart = -apart - 2
        distance = apart.astype(F32)
        joined = []
        for n, h in enumerate(hs):
            coef = jnp.where(
                distance >= 0.0, jnp.exp(jnp.maximum(distance, 0.0) * seg_len * logs[h]), 0.0
            )
            part = got[:, n * piece : (n + 1) * piece].astype(F32)
            joined.append(jnp.sum(coef[..., None, None] * part[None], axis=1).astype(BF16))
        joined = jnp.concatenate(joined, axis=1)
        back_cut = lax.all_to_all(joined, "shard", split_axis=0, concat_axis=0, tiled=True)
        states = [
            back_cut[:, n * piece : (n + 1) * piece].reshape(DK, DV) for n in range(len(hs))
        ]
        return (states, *beside)

    def whole(n):
        return (0, 0)

    def ahead(n):
        return (n, 0)

    def behind(n):
        return (blocks - 1 - n, 0)

    def shaped(columns, kind, r=seg_len):
        return jax.ShapeDtypeStruct((r, columns), kind)

    state_scratch = [pltpu.VMEM((DK, DV), F32)]
    half_block = (blk, half)
    unit_block, v_block = (blk, DK), (blk, DV)
    ret_flops = 2 * seg_len * (DK + DV) * (blk + DK)
    low = s < group // 2
    if balanced:
        roles = [["q", "k", "va", "vb", "xv", "g", "g", "g"], ["q", "k", "vb", "g"]]
    else:
        roles = [["q", "k", "va", "vb", "g", "g"]] * local_heads
    params = [
        (jnp.stack([block_decays[h], low.astype(F32)]), None, None) for h in range(local_heads)
    ]
    heads_kept = []
    extra_v = None
    for h in range(local_heads):
        if balanced:
            weights = slots[h]
        else:
            cut = slots[h].reshape(-1, DK, width)
            weights = jnp.concatenate([pick(cut, place[h, s, c]) for c in range(6)], axis=0)
        carried = "va" not in roles[h]
        gate_count = roles[h].count("g")
        q, k, v, total, gates, *extra = head_call(
            functools.partial(project_kernel, blk, roles[h], carried),
            len(roles[h]) // 2,
            [
                params[h],
                (normed, (seg_len, width), whole),
                (weights, (2 * DK, width), ahead),
                (cosine, (seg_len, half), whole),
                (sine, (seg_len, half), whole),
                (k_decays[h], (blk, 1), whole),
            ]
            + ([(extra_v, (seg_len, DK), whole)] if carried else []),
            [
                (shaped(DK, BF16), (seg_len, DK), whole),
                (shaped(DK, BF16), (seg_len, DK), whole),
                (shaped(DV, BF16), (seg_len, DV), whole),
                (shaped(DV, BF16, DK), (DK, DV), whole),
                (shaped(gate_count * DK, BF16), (seg_len, gate_count * DK), whole),
            ]
            + ([(shaped(DK, BF16), (seg_len, DK), whole)] if "xv" in roles[h] else []),
            [pltpu.VMEM((seg_len, 2 * DK), F32)],
            2 * seg_len * width * len(roles[h]) * DK,
        )
        extra_v = extra[0] if extra else None
        (state_in,) = exchange_states([h], [total], False)[0]
        if h + 1 < local_heads:
            slots[h + 1], state_in, *later[:] = tie(slots[h + 1], state_in, *later)
        heads_kept.append((weights, q, k, v, gates, state_in))

    def columns(v, c, order):
        return (v, unit_block, lambda n, c=c: (order(n)[0], c))

    if balanced:
        gates0, gates1 = heads_kept[0][4], heads_kept[1][4]
        swapped = swap(jnp.where(low, gates1, gates0[:, :DK]), 2)

        def gate_operands(h, order):
            if h == 0:
                four = (gates0, 0), (gates0, 1), (swapped, 0), (gates0, 2)
            else:
                four = (gates0, 1), (gates1, 0), (gates0, 2), (swapped, 0)
            return [columns(v, c, order) for v, c in four]

    else:

        def gate_operands(h, order):
            return [columns(heads_kept[h][4], c, order) for c in (0, 0, 1, 1)]

    kept = []
    for h in range(local_heads):
        weights, q, k, v, gates, state_in = heads_kept[h]
        hidden, mixed, retained = head_call(
            retain_kernel,
            blocks,
            [
                params[h],
                (q, unit_block, ahead),
                (k, unit_block, ahead),
                (v, v_block, ahead),
                *gate_operands(h, ahead),
                (masks[h], (blk, blk), whole),
                (q_decays[h], (blk, 1), whole),
                (k_decays[h], (blk, 1), whole),
                (state_in, (DK, DV), whole),
            ],
            [
                (shaped(DV, BF16), v_block, ahead),
                (shaped(DV, BF16), v_block, ahead),
                (shaped(1, F32), (blk, 1), ahead),
            ],
            state_scratch,
            ret_flops,
        )
        kept.append((retained, mixed, hidden))
    hidden = jnp.concatenate([t[-1] for t in kept], axis=1)
    w_ffn_in, w_ffn_out = (gather_shard(t) for t in later)

    resid = xf + add_blocks(*send_blocks(seq_rows(dot_nt(hidden, w_out, BF16))))
    normed2 = gather_near(rms_scale(resid, gain_ffn).astype(BF16))
    proj2 = dot_nt(normed2, w_ffn_in)
    first, second = proj2[:, :inner_cols], proj2[:, inner_cols:]
    inner2 = gated_gelu(first, second).astype(BF16)

    g_ffn_out, d_ffn = tie(dot_tn(d_ffn, inner2, BF16), d_ffn)
    scattered = {"ffn_out": reduce_shard(g_ffn_out)}
    d_inner2 = dot_nn(d_ffn, w_ffn_out)
    ignored2, gelu_back = jax.vjp(gated_gelu, first, second)
    d_first, d_second = gelu_back(d_inner2)
    dproj2 = jnp.concatenate([d_first, d_second], axis=1).astype(BF16)
    d_normed2 = dot_nn(dproj2, w_ffn_in, BF16)
    g_ffn_in = dot_tn(dproj2, normed2, BF16)
    if group == 4:
        terms, ra, rb = first_step(near_rows(d_normed2))
        ra, rb, g_ffn_in = tie(ra, rb, g_ffn_in)
        d_normed2 = second_step(terms, ra, rb)
    else:
        d_normed2 = add_blocks(*send_blocks(near_rows(d_normed2)))
    scattered["ffn_in"] = reduce_shard(g_ffn_in)
    ignored3, norm2_back = jax.vjp(rms_scale, resid, gain_ffn)
    d_resid_part, d_gain_ffn = norm2_back(d_normed2)
    d_resid = cotangent.astype(F32) + d_resid_part
    (d_attn,) = tie(d_resid.astype(BF16))
    d_attn = gather_seq(d_attn)
    d_attn, scattered["ffn_out"] = tie(d_attn, scattered["ffn_out"])
    parts_ffn_out = spread(scattered["ffn_out"])

    def tie_parts(v, parts):
        flat = tie(v, *(piece for part in parts for piece in part))
        rest = list(flat[1:])
        return flat[0], [tuple(rest.pop(0) for _ in part) for part in parts]

    all_params = (
        jnp.concatenate([jnp.stack([jnp.float32(0.0), low.astype(F32)]), block_decays]),
        None,
        None,
    )
    outs = head_call(
        functools.partial(gate_back_kernel, local_heads),
        blocks,
        [
            all_params,
            (d_attn, (blk, width), behind),
            (w_out, (width, vcols), whole),
        ]
        + [
            t
            for h in range(local_heads)
            for t in (
                *gate_operands(h, behind),
                (kept[h][1], v_block, behind),
                (kept[h][0], (blk, 1), behind),
                (heads_kept[h][1], unit_block, behind),
                (q_decays[h], (blk, 1), whole),
            )
        ],
        [
            (shaped(DV, BF16), v_block, behind),
            (shaped(DV, BF16), v_block, behind),
            (shaped(DV, BF16, DK), (DK, DV), whole),
        ]
        * local_heads,
        state_scratch * local_heads,
        2 * seg_len * (DK * DV * local_heads + width * vcols),
    )
    d_gates, d_outs, totals = outs[0::3], outs[1::3], outs[2::3]
    if balanced:
        d_swapped = swap(jnp.where(low, d_gates[0][:, DK:], d_gates[1][:, DK:]), 2)
    else:
        d_swapped = totals[0]
    if group == 4:
        totals[0], parts_ffn_out[:3] = tie_parts(totals[0], parts_ffn_out[:3])
    hidden, totals[0] = tie(hidden, totals[0])
    g_mixer_out = dot_tn(d_attn, hidden, BF16)
    inners = head_call(
        functools.partial(inner_back_kernel, local_heads),
        blocks,
        [all_params, (cosine, half_block, ahead), (sine, half_block, ahead)]
        + [
            t
            for h in range(local_heads)
            for t in (
                (heads_kept[h][1], unit_block, ahead),
                (heads_kept[h][2], unit_block, ahead),
                (heads_kept[h][3], v_block, ahead),
                (d_outs[h], v_block, ahead),
                (masks[h], (blk, blk), whole),
                (q_decays[h], (blk, 1), whole),
                (k_decays[h], (blk, 1), whole),
                (heads_kept[h][5], (DK, DV), whole),
            )
        ],
        [
            (shaped(DK, BF16), unit_block, ahead),
            (shaped(DK, F32), unit_block, ahead),
            (shaped(DV, F32), v_block, ahead),
        ]
        * local_heads,
        state_scratch * local_heads,
        2 * local_heads * ret_flops,
    )
    flat_ffn_out = [piece for part in parts_ffn_out for piece in part]
    grads_out, d_swapped, g_mixer_out, inner2, scattered["ffn_in"], *flat = exchange_states(
        range(local_heads),
        totals,
        True,
        (d_swapped, g_mixer_out, inner2, scattered["ffn_in"], *inners, *flat_ffn_out),
    )
    scattered["mixer_out"] = reduce_shard(g_mixer_out)
    inners = flat[: 3 * local_heads]
    rest = flat[3 * local_heads :]
    parts_ffn_out = [tuple(rest.pop(0) for _ in part) for part in parts_ffn_out]
    parts_ffn_in = spread(scattered["ffn_in"])
    near = jnp.arange(group)
    if sub % 128 == 0:
        g_ffn_out = place_blocks(
            parts_ffn_out,
            s ^ near,
            near,
            ffn_out.shape,
            (ffn_out.shape[0], sub),
            lambda o, n: (0, o * group + n),
            outer=segments // 2,
        )
    else:
        g_ffn_out = jnp.transpose(
            ordered(parts_ffn_out).reshape(group, ffn_out.shape[0], segments // 2, sub),
            (1, 2, 0, 3),
        ).reshape(ffn_out.shape).astype(F32)
    ffn_terms, g_ffn_out, *grads_out = tie(
        dot_nt(inner2, w_ffn_out, BF16), g_ffn_out, *grads_out
    )
    if balanced:
        d_gate_pairs = [
            [
                ((d_gates[0], 0), (d_swapped, 0)),
                ((d_gates[1], 0), (d_gates[0], 0)),
                ((d_gates[1], 1), (d_gates[0], 1)),
            ],
            [((d_swapped, 0), (d_gates[1], 0))],
        ]
    else:
        d_gate_pairs = [[((t, 0), (t, 0)), ((t, 1), (t, 1))] for t in d_gates]
    by_units = head_call(
        functools.partial(outer_back_kernel, roles),
        blocks,
        [all_params, (cosine, half_block, behind), (sine, half_block, behind)]
        + [
            t
            for h in range(local_heads)
            for t in (
                (heads_kept[h][1], unit_block, behind),
                (heads_kept[h][2], unit_block, behind),
                (heads_kept[h][3], v_block, behind),
                (d_outs[h], v_block, behind),
                (inners[3 * h], unit_block, behind),
                (inners[3 * h + 1], unit_block, behind),
                (inners[3 * h + 2], v_block, behind),
                (q_decays[h], (blk, 1), whole),
                (k_decays[h], (blk, 1), whole),
                (grads_out[h], (DK, DV), whole),
                *(columns(v, c, behind) for pair in d_gate_pairs[h] for v, c in pair),
            )
        ],
        [(shaped(len(t) * DK, BF16), (blk, len(t) * DK), behind) for t in roles],
        state_scratch * local_heads,
        seg_len * DK * DV,
    )

    if group == 4:
        late = first_step(near_rows(ffn_terms))
    else:
        late = send_blocks(near_rows(ffn_terms))
    by_units[0], parts_ffn_in[:3] = tie_parts(by_units[0], parts_ffn_in[:3])
    g_units = [dot_tn(by_units[0], normed, BF16)]
    by_units[-1], g_units[0] = tie(by_units[-1], g_units[0])
    by_units[-1], scattered["mixer_out"] = tie(by_units[-1], scattered["mixer_out"])
    tile = 512
    rights = [t[0] for t in heads_kept]
    (d_normed,) = head_call(
        functools.partial(join_kernel, local_heads),
        width // tile,
        [(t, t.shape, whole) for t in by_units]
        + [(t, (t.shape[0], tile), lambda n: (0, n)) for t in rights],
        [(shaped(width, BF16), (seg_len, tile), lambda n: (0, n))],
        [],
        seg_len * width,
    )
    d_normed, parts_ffn_in = tie_parts(d_normed, parts_ffn_in)
    if group == 4:
        ffn_own, ra, rb = late
        d_normed, ra, rb = tie(d_normed, ra, rb)
        first = first_step(seq_rows(d_normed))
        output = (resid + second_step(ffn_own, ra, rb)).astype(BF16)
    else:
        output = (resid + add_blocks(*late)).astype(BF16)
    parts_mixer_out = spread(scattered["mixer_out"])
    for h in range(1, local_heads):
        by_units[h], d_normed = tie(by_units[h], d_normed)
        g_units.append(dot_tn(by_units[h], normed, BF16))
    g_ffn_in = place_blocks(
        parts_ffn_in, s ^ near, near, ffn_in.shape, (sub, width), lambda o, n: (n, 0)
    )
    if group == 4:
        own, ra, rb = first
        ra, rb, g_units[-1], g_ffn_in = tie(ra, rb, g_units[-1], g_ffn_in)
        d_normed = second_step(own, ra, rb)
    else:
        d_normed = add_blocks(*send_blocks(seq_rows(d_normed)))
    g_slots = []
    for h in range(local_heads):
        if not balanced:
            cut = g_units[h].reshape(-1, DK, width)
            g_units[h] = jnp.concatenate(
                [pick(cut, jnp.maximum(held[h, c, s], 0)) for c in range(segments)], axis=0
            )
        g_slots.append(reduce_shard(g_units[h]))

    ignored8, norm1_back = jax.vjp(rms_scale, xf, gain_attn)
    d_x_part, d_gain_attn = norm1_back(d_normed)
    input_grad = (d_resid + d_x_part).astype(BF16)
    gains = jnp.concatenate([d_gain_attn, d_gain_ffn])[None]
    step = 1
    while step < group:
        gains = gains + swap(gains, step)
        step *= 2
    g_slots[0], gains = tie(g_slots[0], gains)
    gains = lax.all_to_all(
        jnp.broadcast_to(gains, (segments, 2 * width)),
        "shard",
        split_axis=0,
        concat_axis=0,
        tiled=True,
    )
    gains = jnp.sum(gains, axis=0)
    parts = []
    for h in range(local_heads):
        last = h == local_heads - 1
        beside = None
        if h == 0:
            g_slots[h], input_grad = tie(g_slots[h], input_grad)
            g_slots[h], parts_mixer_out = tie_parts(g_slots[h], parts_mixer_out)
            g_mixer_out = place_blocks(
                parts_mixer_out,
                s ^ near,
                near,
                mixer_out.shape,
                (mixer_out.shape[0], DV),
                lambda o, n: (0, o * group + n),
                outer=local_heads,
            )
            beside = [g_mixer_out, output, gains]
        if last and h > 0:
            g_slots[h], gains, g_mixer_out = tie(g_slots[h], gains, g_mixer_out)
            g_slots[h], parts = tie_parts(g_slots[h], parts)
        here = spread(g_slots[h], beside)
        if group == 4 and h == 0:
            g_mixer_out, output, gains = beside
        if balanced and last:
            there = [tuple(cross(piece, 1) for piece in part) for part in here]
            parts += [a + b for a, b in zip(here, there)] + [b + a for a, b in zip(here, there)]
        else:
            lend_here = lend[j] if balanced else lend[h, j]
            stack = jnp.stack([jnp.concatenate(part, axis=0) for part in here])
            parts += here + [
                (cross(pick(stack, s ^ lend_here[n]), 1),) for n in range(lend_here.shape[0])
            ]
    gain_attn_grad, gain_ffn_grad = gains[:width], gains[width:]
    found = back[j]
    if balanced:
        spare = lend.shape[-1]
        source = jnp.where(
            found[:, 0] == 0,
            s ^ found[:, 1],
            jnp.where(
                found[:, 0] == 1,
                group + found[:, 1],
                group + spare + core * group + (s ^ found[:, 1]),
            ),
        )
    else:
        source = found[:, 0] * (group + lend.shape[-1]) + jnp.where(
            found[:, 2] < 0, s ^ found[:, 1], group + found[:, 2]
        )
    g_mixer_in = place_blocks(
        parts,
        jnp.arange(source.shape[0]),
        source,
        mixer_in.shape,
        (DK, width),
        lambda o, n: (n, 0),
    )
    return (
        output,
        input_grad,
        gain_attn_grad,
        gain_ffn_grad,
        g_mixer_in,
        g_mixer_out,
        g_ffn_in,
        g_ffn_out,
    )


def solution(mesh):
    return jax.shard_map(
        local,
        mesh=mesh,
        in_specs=(
            P(("shard", "seq"), None),
            P(("shard", "seq"), None),
            P(),
            P(),
            P("shard", None),
            P("shard", None),
            P("shard", None),
            P("shard", None),
            P(),
            P(),
        ),
        out_specs=(
            P(("shard", "seq"), None),
            P(("shard", "seq"), None),
            P(),
            P(),
            P("shard", None),
            P("shard", None),
            P("shard", None),
            P("shard", None),
        ),
        check_vma=False,
    )
```

```python
import functools

import jax
import jax.numpy as jnp
import numpy as np
from jax import lax
from jax.experimental import pallas as pl
from jax.experimental.pallas import tpu as pltpu
from jax.sharding import PartitionSpec as P

DK = 256
DV = 512
FF = 4096
QK = 2048
V = 4096


EPS_NORM = 1e-06
EPS_GROUP = 1e-05

F32 = jnp.float32
BF16 = jnp.bfloat16


def dot_nt(left, right, kind=F32):
    return lax.dot_general(
        left, right, (((1,), (1,)), ((), ())), preferred_element_type=F32
    ).astype(kind)


def dot_nn(left, right, kind=F32):
    return lax.dot_general(
        left, right, (((1,), (0,)), ((), ())), preferred_element_type=F32
    ).astype(kind)


def dot_tn(left, right, kind=F32):
    return lax.dot_general(
        left, right, (((0,), (0,)), ((), ())), preferred_element_type=F32
    ).astype(kind)


def rms_scale(v, gain):
    return v * lax.rsqrt(jnp.mean(v * v, axis=-1, keepdims=True) + EPS_NORM) * gain


def gated_gelu(first, second):
    return jax.nn.gelu(first) * second


def unit_owners(heads):
    owners = [(n, 0) for n in range(heads)] + [(n, 1) for n in range(heads)]
    for base in (2, 4):
        owners += [(n, base + half) for n in range(heads) for half in range(2)]
    return owners


def balanced_tables():
    group, segments, per_shard = 4, 8, 6
    number = {owner: u for u, owner in enumerate(unit_owners(8))}
    keep = np.full((2, segments, group), -1, np.int32)
    give = np.zeros((2, segments, group), np.int32)
    back = np.zeros((segments, per_shard, 2), np.int32)
    lend = [[] for _ in range(segments)]
    seen = set()
    for s in range(group):
        a, b = s, s + 4
        if s < 2:
            gates = [(a, 4), (b, 4), (b, 5)], (b + 2, 5)
        else:
            gates = [(a - 2, 5), (a, 4), (a, 5)], (b, 4)
        first = [(a, 0), (a, 1), (a, 2), (a, 3), (b, 2)] + gates[0]
        second = [(b, 0), (b, 1), (b, 3), gates[1]]
        for slot, owner in enumerate(first):
            home, index = divmod(number[owner], per_shard)
            seen.add(number[owner])
            assert home // 2 == slot // 2
            if home == slot:
                keep[0, slot, s] = index
                back[home, index] = (0, s)
            else:
                give[0, home, s] = index
                back[home, index] = (1, len(lend[slot]))
                lend[slot].append(s)
        for chip, owner in enumerate(second):
            home, index = divmod(number[owner], per_shard)
            seen.add(number[owner])
            assert home // 2 == chip
            keep[1, home, s] = index
            give[1, home, s] = index
            back[home, index] = (2, s)
    assert len(seen) == segments * per_shard
    most = max(len(t) for t in lend)
    return keep, give, back, np.asarray([(t + [0] * most)[:most] for t in lend], np.int32)


def unit_tables(group, local_heads, segments):
    heads = group * local_heads
    owners = unit_owners(heads)
    per_shard = len(owners) // segments
    keep = np.full((local_heads, segments, group), -1, np.int32)
    give = np.zeros((local_heads, segments, group), np.int32)
    place = np.zeros((local_heads, group, 6), np.int32)
    held = np.full((local_heads, segments, group), -1, np.int32)
    slot_of = {}
    for chip in range(segments // 2):
        for head in range(heads):
            h, s = divmod(head, group)
            span = range(2 * per_shard * chip, 2 * per_shard * (chip + 1))
            mine = [u for u in span if owners[u][0] == head]
            assert len(mine) <= 2
            for n, u in enumerate(mine):
                home = u // per_shard
                slot = home if len(mine) == 1 else 2 * chip + n
                if slot == home:
                    keep[h, slot, s] = u % per_shard
                else:
                    give[h, home, s] = u % per_shard
                place[h, s, owners[u][1]] = slot
                held[h, slot, s] = owners[u][1]
                slot_of[u] = slot
    lends = [[[] for _ in range(segments)] for _ in range(local_heads)]
    back = np.zeros((segments, per_shard, 3), np.int32)
    for u, (head, _) in enumerate(owners):
        home = u // per_shard
        h, s = divmod(head, group)
        back[home, u % per_shard] = (h, s, -1)
        if slot_of[u] != home:
            assert slot_of[u] == home ^ 1
            back[home, u % per_shard, 2] = len(lends[h][home ^ 1])
            lends[h][home ^ 1].append(s)
    most = max(1, max(len(t) for row in lends for t in row))
    lend = np.asarray(
        [[(t + [0] * most)[:most] for t in row] for row in lends], np.int32
    )
    return keep, give, place, held, back, lend


def tie(*values):
    return lax.optimization_barrier(values)


def mm(left, right, dims):
    return lax.dot_general(left, right, (dims, ((), ())), preferred_element_type=F32)


NN = ((1,), (0,))
NT = ((1,), (1,))
TN = ((0,), (0,))


def turn(v, cosine, sine):
    half = v.shape[-1] // 2
    first, second = v[:, :half], v[:, half:]
    return jnp.concatenate(
        [first * cosine - second * sine, second * cosine + first * sine], axis=-1
    )


def scaled(v, decay):
    return (v.astype(F32) * decay).astype(BF16)


def project_kernel(blk, roles, carried, params, x, w, cosine, sine, k_decay, *refs):
    if carried:
        v_a, *refs = refs
    q, k, v, total, gates, *rest = refs
    y = rest[-1]
    rows = y.shape[0]
    y[...] = mm(x[...], w[...], NT)

    def put(role, part, gate_at):
        value = y[:, part * DK : (part + 1) * DK]
        if role == "q":
            q[...] = turn(value, cosine[...], sine[...]).astype(BF16)
        elif role == "k":
            k[...] = turn(value, cosine[...], sine[...]).astype(BF16)
        elif role == "va":
            v[:, :DK] = value.astype(BF16)
        elif role == "vb":
            v[:, DK:] = value.astype(BF16)
        elif role == "xv":
            rest[0][...] = value.astype(BF16)
        else:
            gates[:, gate_at * DK : (gate_at + 1) * DK] = value.astype(BF16)

    for step in range(len(roles) // 2):

        @pl.when(pl.program_id(0) == step)
        def _(step=step):
            for part in range(2):
                at = 2 * step + part
                put(roles[at], part, roles[:at].count("g"))
            if step == 1:
                if carried:
                    v[:, :DK] = v_a[...]
                state = jnp.zeros(total.shape, F32)
                for r in range(0, rows, blk):
                    kd = scaled(k[r : r + blk, :], k_decay[...])
                    state = params[0] * state + mm(kd, v[r : r + blk, :], TN)
                total[...] = state.astype(BF16)


def join_kernel(count, *refs):
    out = refs[-1]
    total = mm(refs[0][...], refs[count][...], NN)
    for n in range(1, count):
        total += mm(refs[n][...], refs[count + n][...], NN)
    out[...] = total.astype(out.dtype)


def select(params, low, high):
    return jnp.where(params[1] > 0.5, low[...].astype(F32), high[...].astype(F32))


def retain_kernel(
    params, q, k, v, low_a, high_a, low_b, high_b, mask, q_decay, k_decay, start,
    hidden, mixed, kept, state,
):
    @pl.when(pl.program_id(0) == 0)
    def _():
        state[...] = start[...].astype(F32)

    weights = (mm(q[...], k[...], NT) * mask[...]).astype(BF16)
    o = mm(weights, v[...], NN)
    o += mm(scaled(q[...], q_decay[...]), state[...].astype(BF16), NN)
    state[...] = params[0] * state[...] + mm(scaled(k[...], k_decay[...]), v[...], TN)
    o = o - jnp.mean(o, axis=-1, keepdims=True)
    inverse = lax.rsqrt(jnp.mean(o * o, axis=-1, keepdims=True) + EPS_GROUP)
    kept[...] = inverse
    low = (o * inverse).astype(BF16)
    mixed[...] = low
    for n, (one, two) in enumerate(((low_a, high_a), (low_b, high_b))):
        columns = slice(n * DK, (n + 1) * DK)
        g = select(params, one, two)
        hidden[:, columns] = (g * jax.nn.sigmoid(g) * low[:, columns].astype(F32)).astype(BF16)


def take(refs, counts):
    pieces, at = [], 0
    for count in counts:
        pieces.append(refs[at : at + count])
        at += count
    return pieces


def gate_back_kernel(heads, params, d_attn, w_out, *refs):
    inputs = take(refs, [8] * heads)
    outputs = take(refs[8 * heads :], [3] * heads)
    states = refs[11 * heads :]

    @pl.when(pl.program_id(0) == 0)
    def _():
        for state in states:
            state[...] = jnp.zeros(state.shape, F32)

    d_hidden = mm(d_attn[...], w_out[...], NN)
    for h in range(heads):
        low_a, high_a, low_b, high_b, mixed, inverse, q, q_decay = inputs[h]
        d_gate, d_out, total = outputs[h]
        g = jnp.concatenate(
            [select(params, low_a, high_a), select(params, low_b, high_b)], axis=1
        )
        dh = d_hidden[:, h * DV : (h + 1) * DV]
        sig = jax.nn.sigmoid(g)
        o = mixed[...].astype(F32)
        d_gate[...] = (dh * o * (sig * (1.0 + g * (1.0 - sig)))).astype(BF16)
        dy = (dh * (g * sig)).astype(BF16).astype(F32)
        do = inverse[...] * (
            dy
            - jnp.mean(dy, axis=-1, keepdims=True)
            - o * jnp.mean(dy * o, axis=-1, keepdims=True)
        )
        do = do.astype(BF16)
        d_out[...] = do
        state = states[h]
        state[...] = params[2 + h] * state[...] + mm(scaled(q[...], q_decay[...]), do, TN)
        total[...] = state[...].astype(BF16)


def inner_back_kernel(heads, params, cosine, sine, *refs):
    inputs = take(refs, [8] * heads)
    outputs = take(refs[8 * heads :], [3] * heads)
    states = refs[11 * heads :]

    @pl.when(pl.program_id(0) == 0)
    def _():
        for h in range(heads):
            states[h][...] = inputs[h][7][...].astype(F32)

    for h in range(heads):
        q, k, v, d_out, mask, q_decay, k_decay, ignored = inputs[h]
        d_q, d_k, d_v = outputs[h]
        state = states[h]
        do = d_out[...]
        weights = (mm(q[...], k[...], NT) * mask[...]).astype(BF16)
        d_v[...] = mm(weights, do, TN)
        d_scores = mm(do, v[...], NT).astype(BF16).astype(F32)
        d_scores = (d_scores * mask[...]).astype(BF16)
        d_k[...] = mm(d_scores, q[...], TN)
        far = mm(do, state[...].astype(BF16), NT).astype(BF16).astype(F32)
        dq = mm(d_scores, k[...], NN) + far * q_decay[...]
        dq = dq.astype(BF16).astype(F32)
        d_q[...] = turn(dq, cosine[...], -sine[...]).astype(BF16)
        state[...] = params[2 + h] * state[...] + mm(scaled(k[...], k_decay[...]), v[...], TN)


def outer_back_kernel(roles, params, cosine, sine, *refs):
    heads = len(roles)
    counts = [10 + 2 * t.count("g") for t in roles]
    inputs = take(refs, counts)
    outputs = refs[sum(counts) : sum(counts) + heads]
    states = refs[sum(counts) + heads :]

    @pl.when(pl.program_id(0) == 0)
    def _():
        for h in range(heads):
            states[h][...] = inputs[h][9][...].astype(F32)

    other = None
    for h in reversed(range(heads)):
        q, k, v, d_out, d_q, d_k, d_v, q_decay, k_decay, ignored, *gates = inputs[h]
        state = states[h]
        low = state[...].astype(BF16)
        far = mm(v[...], low, NT).astype(BF16).astype(F32)
        dk = (d_k[...] + far * k_decay[...]).astype(BF16).astype(F32)
        dk = turn(dk, cosine[...], -sine[...]).astype(BF16)
        dv = (d_v[...] + mm(scaled(k[...], k_decay[...]), low, NN)).astype(BF16)
        for n, role in enumerate(roles[h]):
            if role == "q":
                value = d_q[...]
            elif role == "k":
                value = dk
            elif role == "va":
                value = dv[:, :DK]
            elif role == "vb":
                value = dv[:, DK:]
            elif role == "xv":
                value = other
            else:
                value = select(params, gates.pop(0), gates.pop(0)).astype(BF16)
            outputs[h][:, n * DK : (n + 1) * DK] = value
        other = dv[:, :DK]
        state[...] = params[2 + h] * state[...] + mm(scaled(q[...], q_decay[...]), d_out[...], TN)


def head_call(kernel, grid, operands, outputs, scratch, flops):
    arrays = [t[0] for t in operands]
    size = sum(t.size * t.dtype.itemsize for t in arrays + [t[0] for t in outputs])
    call = pl.pallas_call(
        kernel,
        grid=(grid,),
        in_specs=[
            pl.BlockSpec(memory_space=pltpu.SMEM) if block is None else pl.BlockSpec(block, where)
            for _, block, where in operands
        ],
        out_specs=[pl.BlockSpec(block, where) for _, block, where in outputs],
        scratch_shapes=scratch,
        out_shape=[t[0] for t in outputs],
        compiler_params=pltpu.CompilerParams(vmem_limit_bytes=56 * 2**20),
        cost_estimate=pl.CostEstimate(flops=flops, bytes_accessed=size, transcendentals=0),
    )
    return list(call(*arrays))


def place_kernel(parts, target, source, *refs):
    out = refs[-1]
    code = source[pl.program_id(1)]
    for i, part in enumerate(parts):

        @pl.when(code == i)
        def _(part=part):
            row = 0
            for n in part:
                piece = refs[n]
                out[row : row + piece.shape[0], :] = piece[...].astype(F32)
                row += piece.shape[0]


def place_blocks(parts, target, source, shape, block, where, outer=1):
    flat, index = [], []
    for part in parts:
        for piece in part:
            if not any(piece is t for t in flat):
                flat.append(piece)
        index.append([next(n for n, t in enumerate(flat) if t is piece) for piece in part])
    return pl.pallas_call(
        functools.partial(place_kernel, index),
        grid_spec=pltpu.PrefetchScalarGridSpec(
            num_scalar_prefetch=2,
            grid=(outer, target.shape[0]),
            in_specs=[
                pl.BlockSpec((t.shape[0], t.shape[1] // outer), lambda o, n, target, source: (0, o))
                for t in flat
            ],
            out_specs=pl.BlockSpec(block, lambda o, n, target, source: where(o, target[n])),
        ),
        out_shape=jax.ShapeDtypeStruct(shape, F32),
        compiler_params=pltpu.CompilerParams(vmem_limit_bytes=48 * 2**20),
    )(target.astype(jnp.int32), source.astype(jnp.int32), *flat)


def local(
    tokens,
    cotangent,
    gain_attn,
    gain_ffn,
    mixer_in,
    mixer_out,
    ffn_in,
    ffn_out,
    segment_order,
    decay_index,
):
    rows, width = tokens.shape
    group = lax.axis_size("seq")
    segments = lax.axis_size("shard")
    heads = decay_index.shape[0]
    local_heads = heads // group
    seg_len = rows * group
    blk = min(512, seg_len)
    blocks = seg_len // blk
    vcols = local_heads * DV
    s = lax.axis_index("seq")
    j = lax.axis_index("shard")

    def swap(v, d):
        return lax.ppermute(v, "seq", [(i, i ^ d) for i in range(group)])

    def cross(v, d):
        return lax.ppermute(v, "shard", [(i, i ^ d) for i in range(segments)])

    def pick(v, i):
        return lax.dynamic_index_in_dim(v, i, 0, keepdims=False)

    def spread(v, beside=None):
        if group == 4:
            h = v.shape[0] // 2
            r1 = swap(v, 1)
            r2 = swap(v, 2)
            if beside:
                r1, r2, beside[:] = tie(r1, r2, list(beside))
            return [(v,), (r1,), (r2,), (swap(r1[:h], 2), swap(r2[h:], 1))]
        return [(v,)] + [(swap(v, d),) for d in range(1, group)]

    def ordered(parts):
        r = parts[0][0].shape[0]
        out = jnp.zeros((group * r,) + parts[0][0].shape[1:], parts[0][0].dtype)
        for d, part in enumerate(parts):
            row = (s ^ d) * r
            for piece in part:
                out = lax.dynamic_update_slice_in_dim(out, piece, row, 0)
                row = row + piece.shape[0]
        return out

    def gather_near(v):
        return jnp.concatenate([piece for part in spread(v) for piece in part], axis=0)

    def gather_seq(v):
        return ordered(spread(v))

    def first_step(blk_of):
        b = [blk_of(d) for d in range(4)]
        h = b[0].shape[0] // 2
        sa = jnp.concatenate([b[1][:h], b[3][:h]], axis=0)
        sb = jnp.concatenate([b[2][h:], b[3][h:]], axis=0)
        sa, sb = tie(sa, sb)
        return b, swap(sa, 1), swap(sb, 2)

    def second_step(b, ra, rb):
        h = b[0].shape[0] // 2
        ra, rb = ra.astype(F32), rb.astype(F32)
        qa = (b[2][:h].astype(F32) + ra[h:]).astype(BF16)
        qb = (b[1][h:].astype(F32) + rb[h:]).astype(BF16)
        qa, qb = tie(qa, qb)
        qa, qb = swap(qa, 2), swap(qb, 1)
        top = b[0][:h].astype(F32) + ra[:h] + qa.astype(F32)
        return jnp.concatenate([top, b[0][h:].astype(F32) + rb[:h] + qb.astype(F32)], axis=0)

    def send_blocks(blk_of):
        sent = tie(*(blk_of(d) for d in range(group)))
        return sent[0], [swap(sent[d], d) for d in range(group - 1, 0, -1)]

    def add_blocks(own, got):
        own = own.astype(F32)
        for t in got:
            own = own + t.astype(F32)
        return own

    def near_rows(v):
        return lambda d: v[d * rows : (d + 1) * rows]

    def seq_rows(v):
        return lambda d: lax.dynamic_slice_in_dim(v, (s ^ d) * rows, rows, 0)

    def gather_shard(v):
        return lax.all_gather(v, "shard", axis=0, tiled=True)

    def reduce_shard(v):
        return lax.psum_scatter(v, "shard", scatter_dimension=0, tiled=True)

    balanced = group == 4 and local_heads == 2 and segments == 8
    units = mixer_in.reshape(-1, DK, width)
    if balanced:
        keep, give, back, lend = (jnp.asarray(t) for t in balanced_tables())
        core = j % 2
    else:
        keep, give, place, held, back, lend = (
            jnp.asarray(t) for t in unit_tables(group, local_heads, segments)
        )

    def offered(h):
        kept, given = keep[h, j, s], give[h, j, s]
        if balanced and h == 1:
            cut = mixer_in.reshape(-1, DK // 2, width)
            own = pick(cut, 2 * jnp.maximum(kept, 0) + core)
            given = cross(pick(cut, 2 * given + 1 - core), 1)
        else:
            own = pick(units, jnp.maximum(kept, 0))
            given = cross(pick(units, given), 1)
        return jnp.where(kept >= 0, own, given)

    sub = ffn_in.shape[0] // group
    ffn_out_cut = ffn_out.reshape(ffn_out.shape[0], segments // 2, group, sub)

    my_rank = jnp.sum(jnp.where(jnp.arange(segments) == j, segment_order, 0))
    all_logs = jnp.log1p(-jnp.exp2(-(5.0 + decay_index.astype(F32))))
    logs = lax.dynamic_index_in_dim(all_logs.reshape(local_heads, group), s, 1, keepdims=False)
    half = DK // 2
    inv_freq = jnp.exp(-jnp.log(10000.0) * jnp.arange(half).astype(F32) / half)
    positions = my_rank * seg_len + jnp.arange(seg_len, dtype=jnp.int32)
    angles = positions.astype(F32)[:, None] * inv_freq[None, :]
    cosine = jnp.cos(angles)
    sine = jnp.sin(angles)
    steps = jnp.arange(blk).astype(F32)
    gap = steps[:, None] - steps[None, :]
    masks = jnp.where(
        gap[None] >= 0.0, jnp.exp(jnp.maximum(gap, 0.0)[None] * logs[:, None, None]), 0.0
    )
    q_decays = jnp.exp((steps + 1.0)[None, :] * logs[:, None])[..., None]
    k_decays = jnp.exp((blk - 1.0 - steps)[None, :] * logs[:, None])[..., None]
    block_decays = jnp.exp(blk * logs)

    xf = tokens.astype(F32)
    normed = gather_seq(rms_scale(xf, gain_attn).astype(BF16))
    d_ffn = gather_near(cotangent)
    slots = [gather_shard(offered(0))]
    slots[0], normed, d_ffn, cosine, sine, masks, q_decays, k_decays = tie(
        slots[0], normed, d_ffn, cosine, sine, masks, q_decays, k_decays
    )
    for h in range(1, local_heads):
        slots.append(gather_shard(offered(h)))
    mixer_out_cut = jnp.concatenate(
        [
            lax.dynamic_slice_in_dim(mixer_out, (h * group + s) * DV, DV, 1)
            for h in range(local_heads)
        ],
        axis=1,
    )
    mixer_out_cut, slots[0] = tie(mixer_out_cut, slots[0])
    w_out = gather_shard(mixer_out_cut)
    later = [
        lax.dynamic_slice_in_dim(ffn_in, s * sub, sub, 0),
        lax.dynamic_index_in_dim(ffn_out_cut, s, 2, keepdims=False).reshape(ffn_out.shape[0], -1),
    ]
    inner_cols = later[1].shape[1]

    ranks = segment_order
    piece = DK // segments

    def exchange_states(hs, totals, reverse, beside=()):
        cut = jnp.concatenate([t.reshape(segments, piece, DV) for t in totals], axis=1)
        got = lax.all_to_all(cut, "shard", split_axis=0, concat_axis=0, tiled=True)
        got, *beside = tie(got, *beside)
        apart = ranks[:, None] - ranks[None, :] - 1
        if reverse:
            apart = -apart - 2
        distance = apart.astype(F32)
        joined = []
        for n, h in enumerate(hs):
            coef = jnp.where(
                distance >= 0.0, jnp.exp(jnp.maximum(distance, 0.0) * seg_len * logs[h]), 0.0
            )
            part = got[:, n * piece : (n + 1) * piece].astype(F32)
            joined.append(jnp.sum(coef[..., None, None] * part[None], axis=1).astype(BF16))
        joined = jnp.concatenate(joined, axis=1)
        back_cut = lax.all_to_all(joined, "shard", split_axis=0, concat_axis=0, tiled=True)
        states = [
            back_cut[:, n * piece : (n + 1) * piece].reshape(DK, DV) for n in range(len(hs))
        ]
        return (states, *beside)

    def whole(n):
        return (0, 0)

    def ahead(n):
        return (n, 0)

    def behind(n):
        return (blocks - 1 - n, 0)

    def shaped(columns, kind, r=seg_len):
        return jax.ShapeDtypeStruct((r, columns), kind)

    state_scratch = [pltpu.VMEM((DK, DV), F32)]
    half_block = (blk, half)
    unit_block, v_block = (blk, DK), (blk, DV)
    ret_flops = 2 * seg_len * (DK + DV) * (blk + DK)
    low = s < group // 2
    if balanced:
        roles = [["q", "k", "va", "vb", "xv", "g", "g", "g"], ["q", "k", "vb", "g"]]
    else:
        roles = [["q", "k", "va", "vb", "g", "g"]] * local_heads
    params = [
        (jnp.stack([block_decays[h], low.astype(F32)]), None, None) for h in range(local_heads)
    ]
    heads_kept = []
    extra_v = None
    for h in range(local_heads):
        if balanced:
            weights = slots[h]
        else:
            cut = slots[h].reshape(-1, DK, width)
            weights = jnp.concatenate([pick(cut, place[h, s, c]) for c in range(6)], axis=0)
        carried = "va" not in roles[h]
        gate_count = roles[h].count("g")
        q, k, v, total, gates, *extra = head_call(
            functools.partial(project_kernel, blk, roles[h], carried),
            len(roles[h]) // 2,
            [
                params[h],
                (normed, (seg_len, width), whole),
                (weights, (2 * DK, width), ahead),
                (cosine, (seg_len, half), whole),
                (sine, (seg_len, half), whole),
                (k_decays[h], (blk, 1), whole),
            ]
            + ([(extra_v, (seg_len, DK), whole)] if carried else []),
            [
                (shaped(DK, BF16), (seg_len, DK), whole),
                (shaped(DK, BF16), (seg_len, DK), whole),
                (shaped(DV, BF16), (seg_len, DV), whole),
                (shaped(DV, BF16, DK), (DK, DV), whole),
                (shaped(gate_count * DK, BF16), (seg_len, gate_count * DK), whole),
            ]
            + ([(shaped(DK, BF16), (seg_len, DK), whole)] if "xv" in roles[h] else []),
            [pltpu.VMEM((seg_len, 2 * DK), F32)],
            2 * seg_len * width * len(roles[h]) * DK,
        )
        extra_v = extra[0] if extra else None
        (state_in,) = exchange_states([h], [total], False)[0]
        if h + 1 < local_heads:
            slots[h + 1], state_in, *later[:] = tie(slots[h + 1], state_in, *later)
        heads_kept.append((weights, q, k, v, gates, state_in))

    def columns(v, c, order):
        return (v, unit_block, lambda n, c=c: (order(n)[0], c))

    if balanced:
        gates0, gates1 = heads_kept[0][4], heads_kept[1][4]
        swapped = swap(jnp.where(low, gates1, gates0[:, :DK]), 2)

        def gate_operands(h, order):
            if h == 0:
                four = (gates0, 0), (gates0, 1), (swapped, 0), (gates0, 2)
            else:
                four = (gates0, 1), (gates1, 0), (gates0, 2), (swapped, 0)
            return [columns(v, c, order) for v, c in four]

    else:

        def gate_operands(h, order):
            return [columns(heads_kept[h][4], c, order) for c in (0, 0, 1, 1)]

    kept = []
    for h in range(local_heads):
        weights, q, k, v, gates, state_in = heads_kept[h]
        hidden, mixed, retained = head_call(
            retain_kernel,
            blocks,
            [
                params[h],
                (q, unit_block, ahead),
                (k, unit_block, ahead),
                (v, v_block, ahead),
                *gate_operands(h, ahead),
                (masks[h], (blk, blk), whole),
                (q_decays[h], (blk, 1), whole),
                (k_decays[h], (blk, 1), whole),
                (state_in, (DK, DV), whole),
            ],
            [
                (shaped(DV, BF16), v_block, ahead),
                (shaped(DV, BF16), v_block, ahead),
                (shaped(1, F32), (blk, 1), ahead),
            ],
            state_scratch,
            ret_flops,
        )
        kept.append((retained, mixed, hidden))
    hidden = jnp.concatenate([t[-1] for t in kept], axis=1)
    w_ffn_in, w_ffn_out = (gather_shard(t) for t in later)

    resid = xf + add_blocks(*send_blocks(seq_rows(dot_nt(hidden, w_out, BF16))))
    normed2 = gather_near(rms_scale(resid, gain_ffn).astype(BF16))
    proj2 = dot_nt(normed2, w_ffn_in)
    first, second = proj2[:, :inner_cols], proj2[:, inner_cols:]
    inner2 = gated_gelu(first, second).astype(BF16)

    g_ffn_out, d_ffn = tie(dot_tn(d_ffn, inner2, BF16), d_ffn)
    scattered = {"ffn_out": reduce_shard(g_ffn_out)}
    d_inner2 = dot_nn(d_ffn, w_ffn_out)
    ignored2, gelu_back = jax.vjp(gated_gelu, first, second)
    d_first, d_second = gelu_back(d_inner2)
    dproj2 = jnp.concatenate([d_first, d_second], axis=1).astype(BF16)
    d_normed2 = dot_nn(dproj2, w_ffn_in, BF16)
    g_ffn_in = dot_tn(dproj2, normed2, BF16)
    if group == 4:
        terms, ra, rb = first_step(near_rows(d_normed2))
        ra, rb, g_ffn_in = tie(ra, rb, g_ffn_in)
        d_normed2 = second_step(terms, ra, rb)
    else:
        d_normed2 = add_blocks(*send_blocks(near_rows(d_normed2)))
    scattered["ffn_in"] = reduce_shard(g_ffn_in)
    ignored3, norm2_back = jax.vjp(rms_scale, resid, gain_ffn)
    d_resid_part, d_gain_ffn = norm2_back(d_normed2)
    d_resid = cotangent.astype(F32) + d_resid_part
    (d_attn,) = tie(d_resid.astype(BF16))
    d_attn = gather_seq(d_attn)
    d_attn, scattered["ffn_out"] = tie(d_attn, scattered["ffn_out"])
    parts_ffn_out = spread(scattered["ffn_out"])

    def tie_parts(v, parts):
        flat = tie(v, *(piece for part in parts for piece in part))
        rest = list(flat[1:])
        return flat[0], [tuple(rest.pop(0) for _ in part) for part in parts]

    all_params = (
        jnp.concatenate([jnp.stack([jnp.float32(0.0), low.astype(F32)]), block_decays]),
        None,
        None,
    )
    outs = head_call(
        functools.partial(gate_back_kernel, local_heads),
        blocks,
        [
            all_params,
            (d_attn, (blk, width), behind),
            (w_out, (width, vcols), whole),
        ]
        + [
            t
            for h in range(local_heads)
            for t in (
                *gate_operands(h, behind),
                (kept[h][1], v_block, behind),
                (kept[h][0], (blk, 1), behind),
                (heads_kept[h][1], unit_block, behind),
                (q_decays[h], (blk, 1), whole),
            )
        ],
        [
            (shaped(DV, BF16), v_block, behind),
            (shaped(DV, BF16), v_block, behind),
            (shaped(DV, BF16, DK), (DK, DV), whole),
        ]
        * local_heads,
        state_scratch * local_heads,
        2 * seg_len * (DK * DV * local_heads + width * vcols),
    )
    d_gates, d_outs, totals = outs[0::3], outs[1::3], outs[2::3]
    if balanced:
        d_swapped = swap(jnp.where(low, d_gates[0][:, DK:], d_gates[1][:, DK:]), 2)
    else:
        d_swapped = totals[0]
    hidden, totals[0] = tie(hidden, totals[0])
    g_mixer_out = dot_tn(d_attn, hidden, BF16)
    inners = head_call(
        functools.partial(inner_back_kernel, local_heads),
        blocks,
        [all_params, (cosine, half_block, ahead), (sine, half_block, ahead)]
        + [
            t
            for h in range(local_heads)
            for t in (
                (heads_kept[h][1], unit_block, ahead),
                (heads_kept[h][2], unit_block, ahead),
                (heads_kept[h][3], v_block, ahead),
                (d_outs[h], v_block, ahead),
                (masks[h], (blk, blk), whole),
                (q_decays[h], (blk, 1), whole),
                (k_decays[h], (blk, 1), whole),
                (heads_kept[h][5], (DK, DV), whole),
            )
        ],
        [
            (shaped(DK, BF16), unit_block, ahead),
            (shaped(DK, F32), unit_block, ahead),
            (shaped(DV, F32), v_block, ahead),
        ]
        * local_heads,
        state_scratch * local_heads,
        2 * local_heads * ret_flops,
    )
    flat_ffn_out = [piece for part in parts_ffn_out for piece in part]
    grads_out, d_swapped, g_mixer_out, inner2, scattered["ffn_in"], *flat = exchange_states(
        range(local_heads),
        totals,
        True,
        (d_swapped, g_mixer_out, inner2, scattered["ffn_in"], *inners, *flat_ffn_out),
    )
    scattered["mixer_out"] = reduce_shard(g_mixer_out)
    inners = flat[: 3 * local_heads]
    rest = flat[3 * local_heads :]
    parts_ffn_out = [tuple(rest.pop(0) for _ in part) for part in parts_ffn_out]
    parts_ffn_in = spread(scattered["ffn_in"])
    near = jnp.arange(group)
    if sub % 128 == 0:
        g_ffn_out = place_blocks(
            parts_ffn_out,
            s ^ near,
            near,
            ffn_out.shape,
            (ffn_out.shape[0], sub),
            lambda o, n: (0, o * group + n),
            outer=segments // 2,
        )
    else:
        g_ffn_out = jnp.transpose(
            ordered(parts_ffn_out).reshape(group, ffn_out.shape[0], segments // 2, sub),
            (1, 2, 0, 3),
        ).reshape(ffn_out.shape).astype(F32)
    ffn_terms, g_ffn_out, *grads_out = tie(
        dot_nt(inner2, w_ffn_out, BF16), g_ffn_out, *grads_out
    )
    if balanced:
        d_gate_pairs = [
            [
                ((d_gates[0], 0), (d_swapped, 0)),
                ((d_gates[1], 0), (d_gates[0], 0)),
                ((d_gates[1], 1), (d_gates[0], 1)),
            ],
            [((d_swapped, 0), (d_gates[1], 0))],
        ]
    else:
        d_gate_pairs = [[((t, 0), (t, 0)), ((t, 1), (t, 1))] for t in d_gates]
    by_units = head_call(
        functools.partial(outer_back_kernel, roles),
        blocks,
        [all_params, (cosine, half_block, behind), (sine, half_block, behind)]
        + [
            t
            for h in range(local_heads)
            for t in (
                (heads_kept[h][1], unit_block, behind),
                (heads_kept[h][2], unit_block, behind),
                (heads_kept[h][3], v_block, behind),
                (d_outs[h], v_block, behind),
                (inners[3 * h], unit_block, behind),
                (inners[3 * h + 1], unit_block, behind),
                (inners[3 * h + 2], v_block, behind),
                (q_decays[h], (blk, 1), whole),
                (k_decays[h], (blk, 1), whole),
                (grads_out[h], (DK, DV), whole),
                *(columns(v, c, behind) for pair in d_gate_pairs[h] for v, c in pair),
            )
        ],
        [(shaped(len(t) * DK, BF16), (blk, len(t) * DK), behind) for t in roles],
        state_scratch * local_heads,
        seg_len * DK * DV,
    )

    if group == 4:
        late = first_step(near_rows(ffn_terms))
    else:
        late = send_blocks(near_rows(ffn_terms))
    by_units[0], parts_ffn_in[:3] = tie_parts(by_units[0], parts_ffn_in[:3])
    if group == 4:
        ffn_own, ra, rb = late
        by_units[0], ra, rb = tie(by_units[0], ra, rb)
        late = ffn_own, ra, rb
    g_units = [dot_tn(by_units[0], normed, BF16)]
    by_units[-1], g_units[0] = tie(by_units[-1], g_units[0])
    by_units[-1], scattered["mixer_out"] = tie(by_units[-1], scattered["mixer_out"])
    tile = 512
    rights = [t[0] for t in heads_kept]
    (d_normed,) = head_call(
        functools.partial(join_kernel, local_heads),
        width // tile,
        [(t, t.shape, whole) for t in by_units]
        + [(t, (t.shape[0], tile), lambda n: (0, n)) for t in rights],
        [(shaped(width, BF16), (seg_len, tile), lambda n: (0, n))],
        [],
        seg_len * width,
    )
    d_normed, parts_ffn_in = tie_parts(d_normed, parts_ffn_in)
    if group == 4:
        ffn_own, ra, rb = late
        first = first_step(seq_rows(d_normed))
        output = (resid + second_step(ffn_own, ra, rb)).astype(BF16)
    else:
        output = (resid + add_blocks(*late)).astype(BF16)
    parts_mixer_out = spread(scattered["mixer_out"])
    for h in range(1, local_heads):
        by_units[h], d_normed = tie(by_units[h], d_normed)
        g_units.append(dot_tn(by_units[h], normed, BF16))
    g_ffn_in = place_blocks(
        parts_ffn_in, s ^ near, near, ffn_in.shape, (sub, width), lambda o, n: (n, 0)
    )
    if group == 4:
        own, ra, rb = first
        ra, rb, g_units[-1], g_ffn_in = tie(ra, rb, g_units[-1], g_ffn_in)
        d_normed = second_step(own, ra, rb)
    else:
        d_normed = add_blocks(*send_blocks(seq_rows(d_normed)))
    g_slots = []
    for h in range(local_heads):
        if not balanced:
            cut = g_units[h].reshape(-1, DK, width)
            g_units[h] = jnp.concatenate(
                [pick(cut, jnp.maximum(held[h, c, s], 0)) for c in range(segments)], axis=0
            )
        g_slots.append(reduce_shard(g_units[h]))

    ignored8, norm1_back = jax.vjp(rms_scale, xf, gain_attn)
    d_x_part, d_gain_attn = norm1_back(d_normed)
    input_grad = (d_resid + d_x_part).astype(BF16)
    gains = lax.all_to_all(
        jnp.broadcast_to(jnp.concatenate([d_gain_attn, d_gain_ffn])[None], (segments, 2 * width)),
        "shard",
        split_axis=0,
        concat_axis=0,
        tiled=True,
    )
    gains = jnp.sum(gains, axis=0, keepdims=True)
    parts = []
    for h in range(local_heads):
        last = h == local_heads - 1
        beside = None
        if h == 0:
            g_slots[h], input_grad = tie(g_slots[h], input_grad)
            g_slots[h], parts_mixer_out = tie_parts(g_slots[h], parts_mixer_out)
            g_mixer_out = place_blocks(
                parts_mixer_out,
                s ^ near,
                near,
                mixer_out.shape,
                (mixer_out.shape[0], DV),
                lambda o, n: (0, o * group + n),
                outer=local_heads,
            )
            beside = [g_mixer_out, output, gains]
        if last and h > 0:
            g_slots[h], gains, g_mixer_out = tie(g_slots[h], gains, g_mixer_out)
            beside = []
            g_slots[h], parts = tie_parts(g_slots[h], parts)
        here = spread(g_slots[h], beside)
        if group == 4 and h == 0:
            g_mixer_out, output, gains = beside
        if last:
            if beside is not None and group == 4:
                here[1], gains = tie(here[1], gains)
                gains = gains + swap(gains, 1)
                here[3], gains = tie(here[3], gains)
                gains = gains + swap(gains, 2)
            else:
                step = 1
                while step < group:
                    gains = gains + swap(gains, step)
                    step *= 2
        if balanced and last:
            there = [tuple(cross(piece, 1) for piece in part) for part in here]
            parts += [a + b for a, b in zip(here, there)] + [b + a for a, b in zip(here, there)]
        else:
            lend_here = lend[j] if balanced else lend[h, j]
            stack = jnp.stack([jnp.concatenate(part, axis=0) for part in here])
            parts += here + [
                (cross(pick(stack, s ^ lend_here[n]), 1),) for n in range(lend_here.shape[0])
            ]
    gain_attn_grad, gain_ffn_grad = gains[0, :width], gains[0, width:]
    found = back[j]
    if balanced:
        spare = lend.shape[-1]
        source = jnp.where(
            found[:, 0] == 0,
            s ^ found[:, 1],
            jnp.where(
                found[:, 0] == 1,
                group + found[:, 1],
                group + spare + core * group + (s ^ found[:, 1]),
            ),
        )
    else:
        source = found[:, 0] * (group + lend.shape[-1]) + jnp.where(
            found[:, 2] < 0, s ^ found[:, 1], group + found[:, 2]
        )
    g_mixer_in = place_blocks(
        parts,
        jnp.arange(source.shape[0]),
        source,
        mixer_in.shape,
        (DK, width),
        lambda o, n: (n, 0),
    )
    return (
        output,
        input_grad,
        gain_attn_grad,
        gain_ffn_grad,
        g_mixer_in,
        g_mixer_out,
        g_ffn_in,
        g_ffn_out,
    )


def solution(mesh):
    return jax.shard_map(
        local,
        mesh=mesh,
        in_specs=(
            P(("shard", "seq"), None),
            P(("shard", "seq"), None),
            P(),
            P(),
            P("shard", None),
            P("shard", None),
            P("shard", None),
            P("shard", None),
            P(),
            P(),
        ),
        out_specs=(
            P(("shard", "seq"), None),
            P(("shard", "seq"), None),
            P(),
            P(),
            P("shard", None),
            P("shard", None),
            P("shard", None),
            P("shard", None),
        ),
        check_vma=False,
    )
```

```python
import functools

import jax
import jax.numpy as jnp
import numpy as np
from jax import lax
from jax.experimental import pallas as pl
from jax.experimental.pallas import tpu as pltpu
from jax.sharding import PartitionSpec as P

DK = 256
DV = 512
FF = 4096
QK = 2048
V = 4096


EPS_NORM = 1e-06
EPS_GROUP = 1e-05

F32 = jnp.float32
BF16 = jnp.bfloat16


def dot_nt(left, right, kind=F32):
    return lax.dot_general(
        left, right, (((1,), (1,)), ((), ())), preferred_element_type=F32
    ).astype(kind)


def dot_nn(left, right, kind=F32):
    return lax.dot_general(
        left, right, (((1,), (0,)), ((), ())), preferred_element_type=F32
    ).astype(kind)


def dot_tn(left, right, kind=F32):
    return lax.dot_general(
        left, right, (((0,), (0,)), ((), ())), preferred_element_type=F32
    ).astype(kind)


def rms_scale(v, gain):
    return v * lax.rsqrt(jnp.mean(v * v, axis=-1, keepdims=True) + EPS_NORM) * gain


def gated_gelu(first, second):
    return jax.nn.gelu(first) * second


def unit_owners(heads):
    owners = [(n, 0) for n in range(heads)] + [(n, 1) for n in range(heads)]
    for base in (2, 4):
        owners += [(n, base + half) for n in range(heads) for half in range(2)]
    return owners


def balanced_tables():
    group, segments, per_shard = 4, 8, 6
    number = {owner: u for u, owner in enumerate(unit_owners(8))}
    keep = np.full((2, segments, group), -1, np.int32)
    give = np.zeros((2, segments, group), np.int32)
    back = np.zeros((segments, per_shard, 2), np.int32)
    lend = [[] for _ in range(segments)]
    seen = set()
    for s in range(group):
        a, b = s, s + 4
        if s < 2:
            gates = [(a, 4), (b, 4), (b, 5)], (b + 2, 5)
        else:
            gates = [(a - 2, 5), (a, 4), (a, 5)], (b, 4)
        first = [(a, 0), (a, 1), (a, 2), (a, 3), (b, 2)] + gates[0]
        second = [(b, 0), (b, 1), (b, 3), gates[1]]
        for slot, owner in enumerate(first):
            home, index = divmod(number[owner], per_shard)
            seen.add(number[owner])
            assert home // 2 == slot // 2
            if home == slot:
                keep[0, slot, s] = index
                back[home, index] = (0, s)
            else:
                give[0, home, s] = index
                back[home, index] = (1, len(lend[slot]))
                lend[slot].append(s)
        for chip, owner in enumerate(second):
            home, index = divmod(number[owner], per_shard)
            seen.add(number[owner])
            assert home // 2 == chip
            keep[1, home, s] = index
            give[1, home, s] = index
            back[home, index] = (2, s)
    assert len(seen) == segments * per_shard
    most = max(len(t) for t in lend)
    return keep, give, back, np.asarray([(t + [0] * most)[:most] for t in lend], np.int32)


def unit_tables(group, local_heads, segments):
    heads = group * local_heads
    owners = unit_owners(heads)
    per_shard = len(owners) // segments
    keep = np.full((local_heads, segments, group), -1, np.int32)
    give = np.zeros((local_heads, segments, group), np.int32)
    place = np.zeros((local_heads, group, 6), np.int32)
    held = np.full((local_heads, segments, group), -1, np.int32)
    slot_of = {}
    for chip in range(segments // 2):
        for head in range(heads):
            h, s = divmod(head, group)
            span = range(2 * per_shard * chip, 2 * per_shard * (chip + 1))
            mine = [u for u in span if owners[u][0] == head]
            assert len(mine) <= 2
            for n, u in enumerate(mine):
                home = u // per_shard
                slot = home if len(mine) == 1 else 2 * chip + n
                if slot == home:
                    keep[h, slot, s] = u % per_shard
                else:
                    give[h, home, s] = u % per_shard
                place[h, s, owners[u][1]] = slot
                held[h, slot, s] = owners[u][1]
                slot_of[u] = slot
    lends = [[[] for _ in range(segments)] for _ in range(local_heads)]
    back = np.zeros((segments, per_shard, 3), np.int32)
    for u, (head, _) in enumerate(owners):
        home = u // per_shard
        h, s = divmod(head, group)
        back[home, u % per_shard] = (h, s, -1)
        if slot_of[u] != home:
            assert slot_of[u] == home ^ 1
            back[home, u % per_shard, 2] = len(lends[h][home ^ 1])
            lends[h][home ^ 1].append(s)
    most = max(1, max(len(t) for row in lends for t in row))
    lend = np.asarray(
        [[(t + [0] * most)[:most] for t in row] for row in lends], np.int32
    )
    return keep, give, place, held, back, lend


def tie(*values):
    return lax.optimization_barrier(values)


def mm(left, right, dims):
    return lax.dot_general(left, right, (dims, ((), ())), preferred_element_type=F32)


NN = ((1,), (0,))
NT = ((1,), (1,))
TN = ((0,), (0,))


def turn(v, cosine, sine):
    half = v.shape[-1] // 2
    first, second = v[:, :half], v[:, half:]
    return jnp.concatenate(
        [first * cosine - second * sine, second * cosine + first * sine], axis=-1
    )


def scaled(v, decay):
    return (v.astype(F32) * decay).astype(BF16)


def project_kernel(blk, roles, carried, params, x, w, cosine, sine, k_decay, *refs):
    if carried:
        v_a, *refs = refs
    q, k, v, total, gates, *rest = refs
    y = rest[-1]
    rows = y.shape[0]
    y[...] = mm(x[...], w[...], NT)

    def put(role, part, gate_at):
        value = y[:, part * DK : (part + 1) * DK]
        if role == "q":
            q[...] = turn(value, cosine[...], sine[...]).astype(BF16)
        elif role == "k":
            k[...] = turn(value, cosine[...], sine[...]).astype(BF16)
        elif role == "va":
            v[:, :DK] = value.astype(BF16)
        elif role == "vb":
            v[:, DK:] = value.astype(BF16)
        elif role == "xv":
            rest[0][...] = value.astype(BF16)
        else:
            gates[:, gate_at * DK : (gate_at + 1) * DK] = value.astype(BF16)

    for step in range(len(roles) // 2):

        @pl.when(pl.program_id(0) == step)
        def _(step=step):
            for part in range(2):
                at = 2 * step + part
                put(roles[at], part, roles[:at].count("g"))
            if step == 1:
                if carried:
                    v[:, :DK] = v_a[...]
                state = jnp.zeros(total.shape, F32)
                for r in range(0, rows, blk):
                    kd = scaled(k[r : r + blk, :], k_decay[...])
                    state = params[0] * state + mm(kd, v[r : r + blk, :], TN)
                total[...] = state.astype(BF16)


def join_kernel(count, *refs):
    out = refs[-1]
    total = None
    for n in range(count):
        early, late, weights = refs[3 * n : 3 * n + 3]
        middle = DK + late.shape[1]
        part = mm(early[:, :DK], weights[:DK, :], NN)
        part += mm(early[:, DK:], weights[middle:, :], NN)
        part += mm(late[...], weights[DK:middle, :], NN)
        total = part if total is None else total + part
    out[...] = total.astype(out.dtype)


def select(params, low, high):
    return jnp.where(params[1] > 0.5, low[...].astype(F32), high[...].astype(F32))


def retain_kernel(
    params, q, k, v, low_a, high_a, low_b, high_b, mask, q_decay, k_decay, start,
    hidden, mixed, kept, state,
):
    @pl.when(pl.program_id(0) == 0)
    def _():
        state[...] = start[...].astype(F32)

    weights = (mm(q[...], k[...], NT) * mask[...]).astype(BF16)
    o = mm(weights, v[...], NN)
    o += mm(scaled(q[...], q_decay[...]), state[...].astype(BF16), NN)
    state[...] = params[0] * state[...] + mm(scaled(k[...], k_decay[...]), v[...], TN)
    o = o - jnp.mean(o, axis=-1, keepdims=True)
    inverse = lax.rsqrt(jnp.mean(o * o, axis=-1, keepdims=True) + EPS_GROUP)
    kept[...] = inverse
    low = (o * inverse).astype(BF16)
    mixed[...] = low
    for n, (one, two) in enumerate(((low_a, high_a), (low_b, high_b))):
        columns = slice(n * DK, (n + 1) * DK)
        g = select(params, one, two)
        hidden[:, columns] = (g * jax.nn.sigmoid(g) * low[:, columns].astype(F32)).astype(BF16)


def take(refs, counts):
    pieces, at = [], 0
    for count in counts:
        pieces.append(refs[at : at + count])
        at += count
    return pieces


def gate_back_kernel(heads, params, d_attn, w_out, *refs):
    inputs = take(refs, [8] * heads)
    outputs = take(refs[8 * heads :], [3] * heads)
    states = refs[11 * heads :]

    @pl.when(pl.program_id(0) == 0)
    def _():
        for state in states:
            state[...] = jnp.zeros(state.shape, F32)

    d_hidden = mm(d_attn[...], w_out[...], NN)
    for h in range(heads):
        low_a, high_a, low_b, high_b, mixed, inverse, q, q_decay = inputs[h]
        d_gate, d_out, total = outputs[h]
        g = jnp.concatenate(
            [select(params, low_a, high_a), select(params, low_b, high_b)], axis=1
        )
        dh = d_hidden[:, h * DV : (h + 1) * DV]
        sig = jax.nn.sigmoid(g)
        o = mixed[...].astype(F32)
        d_gate[...] = (dh * o * (sig * (1.0 + g * (1.0 - sig)))).astype(BF16)
        dy = (dh * (g * sig)).astype(BF16).astype(F32)
        do = inverse[...] * (
            dy
            - jnp.mean(dy, axis=-1, keepdims=True)
            - o * jnp.mean(dy * o, axis=-1, keepdims=True)
        )
        do = do.astype(BF16)
        d_out[...] = do
        state = states[h]
        state[...] = params[2 + h] * state[...] + mm(scaled(q[...], q_decay[...]), do, TN)
        total[...] = state[...].astype(BF16)


def inner_back_kernel(roles, params, cosine, sine, *refs):
    heads = len(roles)
    counts = [8 + 2 * t.count("g") for t in roles]
    inputs = take(refs, counts)
    outputs = take(refs[sum(counts) :], [3] * heads)
    states = refs[sum(counts) + 3 * heads :]

    @pl.when(pl.program_id(0) == 0)
    def _():
        for h in range(heads):
            states[h][...] = inputs[h][7][...].astype(F32)

    for h in range(heads):
        q, k, v, d_out, mask, q_decay, k_decay, ignored, *gates = inputs[h]
        early, d_k, d_v = outputs[h]
        state = states[h]
        do = d_out[...]
        weights = (mm(q[...], k[...], NT) * mask[...]).astype(BF16)
        d_v[...] = mm(weights, do, TN)
        d_scores = mm(do, v[...], NT).astype(BF16).astype(F32)
        d_scores = (d_scores * mask[...]).astype(BF16)
        d_k[...] = mm(d_scores, q[...], TN)
        far = mm(do, state[...].astype(BF16), NT).astype(BF16).astype(F32)
        dq = mm(d_scores, k[...], NN) + far * q_decay[...]
        dq = dq.astype(BF16).astype(F32)
        early[:, :DK] = turn(dq, cosine[...], -sine[...]).astype(BF16)
        for n in range(len(gates) // 2):
            value = select(params, gates[2 * n], gates[2 * n + 1]).astype(BF16)
            early[:, (n + 1) * DK : (n + 2) * DK] = value
        state[...] = params[2 + h] * state[...] + mm(scaled(k[...], k_decay[...]), v[...], TN)


def outer_back_kernel(roles, params, cosine, sine, *refs):
    heads = len(roles)
    inputs = take(refs, [9] * heads)
    outputs = refs[9 * heads : 10 * heads]
    states = refs[10 * heads :]

    @pl.when(pl.program_id(0) == 0)
    def _():
        for h in range(heads):
            states[h][...] = inputs[h][8][...].astype(F32)

    other = None
    for h in reversed(range(heads)):
        q, k, v, d_out, d_k, d_v, q_decay, k_decay, ignored = inputs[h]
        state = states[h]
        low = state[...].astype(BF16)
        far = mm(v[...], low, NT).astype(BF16).astype(F32)
        dk = (d_k[...] + far * k_decay[...]).astype(BF16).astype(F32)
        dk = turn(dk, cosine[...], -sine[...]).astype(BF16)
        dv = (d_v[...] + mm(scaled(k[...], k_decay[...]), low, NN)).astype(BF16)
        values = {"k": dk, "va": dv[:, :DK], "vb": dv[:, DK:], "xv": other}
        for n, role in enumerate(t for t in roles[h] if t in values):
            outputs[h][:, n * DK : (n + 1) * DK] = values[role]
        other = dv[:, :DK]
        state[...] = params[2 + h] * state[...] + mm(scaled(q[...], q_decay[...]), d_out[...], TN)


def unit_kernel(x, normed, *refs):
    refs[-1][...] = mm(x[...], normed[...], TN).astype(BF16)


def unit_rows(x, normed, count, late, into=None):
    rows, width = normed.shape
    units = x.shape[1] // DK

    def where(n):
        return (n + 1, 0) if late else (jnp.where(n == 0, 0, n + count - units), 0)

    arrays = [x, normed] + ([] if into is None else [into])
    return pl.pallas_call(
        unit_kernel,
        grid=(units,),
        in_specs=[
            pl.BlockSpec((rows, DK), lambda n: (0, n)),
            pl.BlockSpec((rows, width), lambda n: (0, 0)),
        ]
        + ([] if into is None else [pl.BlockSpec(memory_space=pl.ANY)]),
        out_specs=pl.BlockSpec((DK, width), where),
        out_shape=jax.ShapeDtypeStruct((count * DK, width), BF16),
        input_output_aliases={} if into is None else {2: 0},
        compiler_params=pltpu.CompilerParams(vmem_limit_bytes=48 * 2**20),
        cost_estimate=pl.CostEstimate(
            flops=rows * width * DK, bytes_accessed=rows * width, transcendentals=0
        ),
    )(*arrays)


def head_call(kernel, grid, operands, outputs, scratch, flops):
    arrays = [t[0] for t in operands]
    size = sum(t.size * t.dtype.itemsize for t in arrays + [t[0] for t in outputs])
    call = pl.pallas_call(
        kernel,
        grid=(grid,),
        in_specs=[
            pl.BlockSpec(memory_space=pltpu.SMEM) if block is None else pl.BlockSpec(block, where)
            for _, block, where in operands
        ],
        out_specs=[pl.BlockSpec(block, where) for _, block, where in outputs],
        scratch_shapes=scratch,
        out_shape=[t[0] for t in outputs],
        compiler_params=pltpu.CompilerParams(vmem_limit_bytes=56 * 2**20),
        cost_estimate=pl.CostEstimate(flops=flops, bytes_accessed=size, transcendentals=0),
    )
    return list(call(*arrays))


def place_kernel(parts, target, source, *refs):
    out = refs[-1]
    code = source[pl.program_id(1)]
    for i, part in enumerate(parts):

        @pl.when(code == i)
        def _(part=part):
            row = 0
            for n in part:
                piece = refs[n]
                out[row : row + piece.shape[0], :] = piece[...].astype(F32)
                row += piece.shape[0]


def place_blocks(parts, target, source, shape, block, where, outer=1):
    flat, index = [], []
    for part in parts:
        for piece in part:
            if not any(piece is t for t in flat):
                flat.append(piece)
        index.append([next(n for n, t in enumerate(flat) if t is piece) for piece in part])
    return pl.pallas_call(
        functools.partial(place_kernel, index),
        grid_spec=pltpu.PrefetchScalarGridSpec(
            num_scalar_prefetch=2,
            grid=(outer, target.shape[0]),
            in_specs=[
                pl.BlockSpec((t.shape[0], t.shape[1] // outer), lambda o, n, target, source: (0, o))
                for t in flat
            ],
            out_specs=pl.BlockSpec(block, lambda o, n, target, source: where(o, target[n])),
        ),
        out_shape=jax.ShapeDtypeStruct(shape, F32),
        compiler_params=pltpu.CompilerParams(vmem_limit_bytes=48 * 2**20),
    )(target.astype(jnp.int32), source.astype(jnp.int32), *flat)


def local(
    tokens,
    cotangent,
    gain_attn,
    gain_ffn,
    mixer_in,
    mixer_out,
    ffn_in,
    ffn_out,
    segment_order,
    decay_index,
):
    rows, width = tokens.shape
    group = lax.axis_size("seq")
    segments = lax.axis_size("shard")
    heads = decay_index.shape[0]
    local_heads = heads // group
    seg_len = rows * group
    blk = min(512, seg_len)
    blocks = seg_len // blk
    vcols = local_heads * DV
    s = lax.axis_index("seq")
    j = lax.axis_index("shard")

    def swap(v, d):
        return lax.ppermute(v, "seq", [(i, i ^ d) for i in range(group)])

    def cross(v, d):
        return lax.ppermute(v, "shard", [(i, i ^ d) for i in range(segments)])

    def pick(v, i):
        return lax.dynamic_index_in_dim(v, i, 0, keepdims=False)

    def spread(v, beside=None):
        if group == 4:
            h = v.shape[0] // 2
            r1 = swap(v, 1)
            r2 = swap(v, 2)
            if beside:
                r1, r2, beside[:] = tie(r1, r2, list(beside))
            return [(v,), (r1,), (r2,), (swap(r1[:h], 2), swap(r2[h:], 1))]
        return [(v,)] + [(swap(v, d),) for d in range(1, group)]

    def ordered(parts):
        r = parts[0][0].shape[0]
        out = jnp.zeros((group * r,) + parts[0][0].shape[1:], parts[0][0].dtype)
        for d, part in enumerate(parts):
            row = (s ^ d) * r
            for piece in part:
                out = lax.dynamic_update_slice_in_dim(out, piece, row, 0)
                row = row + piece.shape[0]
        return out

    def gather_near(v):
        return jnp.concatenate([piece for part in spread(v) for piece in part], axis=0)

    def gather_seq(v):
        return ordered(spread(v))

    def first_step(blk_of):
        b = [blk_of(d) for d in range(4)]
        h = b[0].shape[0] // 2
        sa = jnp.concatenate([b[1][:h], b[3][:h]], axis=0)
        sb = jnp.concatenate([b[2][h:], b[3][h:]], axis=0)
        sa, sb = tie(sa, sb)
        return b, swap(sa, 1), swap(sb, 2)

    def second_step(b, ra, rb):
        h = b[0].shape[0] // 2
        ra, rb = ra.astype(F32), rb.astype(F32)
        qa = (b[2][:h].astype(F32) + ra[h:]).astype(BF16)
        qb = (b[1][h:].astype(F32) + rb[h:]).astype(BF16)
        qa, qb = tie(qa, qb)
        qa, qb = swap(qa, 2), swap(qb, 1)
        top = b[0][:h].astype(F32) + ra[:h] + qa.astype(F32)
        return jnp.concatenate([top, b[0][h:].astype(F32) + rb[:h] + qb.astype(F32)], axis=0)

    def send_blocks(blk_of):
        sent = tie(*(blk_of(d) for d in range(group)))
        return sent[0], [swap(sent[d], d) for d in range(group - 1, 0, -1)]

    def add_blocks(own, got):
        own = own.astype(F32)
        for t in got:
            own = own + t.astype(F32)
        return own

    def near_rows(v):
        return lambda d: v[d * rows : (d + 1) * rows]

    def seq_rows(v):
        return lambda d: lax.dynamic_slice_in_dim(v, (s ^ d) * rows, rows, 0)

    def gather_shard(v):
        return lax.all_gather(v, "shard", axis=0, tiled=True)

    def reduce_shard(v):
        return lax.psum_scatter(v, "shard", scatter_dimension=0, tiled=True)

    balanced = group == 4 and local_heads == 2 and segments == 8
    units = mixer_in.reshape(-1, DK, width)
    if balanced:
        keep, give, back, lend = (jnp.asarray(t) for t in balanced_tables())
        core = j % 2
    else:
        keep, give, place, held, back, lend = (
            jnp.asarray(t) for t in unit_tables(group, local_heads, segments)
        )

    def offered(h):
        kept, given = keep[h, j, s], give[h, j, s]
        if balanced and h == 1:
            cut = mixer_in.reshape(-1, DK // 2, width)
            own = pick(cut, 2 * jnp.maximum(kept, 0) + core)
            given = cross(pick(cut, 2 * given + 1 - core), 1)
        else:
            own = pick(units, jnp.maximum(kept, 0))
            given = cross(pick(units, given), 1)
        return jnp.where(kept >= 0, own, given)

    sub = ffn_in.shape[0] // group
    ffn_out_cut = ffn_out.reshape(ffn_out.shape[0], segments // 2, group, sub)

    my_rank = jnp.sum(jnp.where(jnp.arange(segments) == j, segment_order, 0))
    all_logs = jnp.log1p(-jnp.exp2(-(5.0 + decay_index.astype(F32))))
    logs = lax.dynamic_index_in_dim(all_logs.reshape(local_heads, group), s, 1, keepdims=False)
    half = DK // 2
    inv_freq = jnp.exp(-jnp.log(10000.0) * jnp.arange(half).astype(F32) / half)
    positions = my_rank * seg_len + jnp.arange(seg_len, dtype=jnp.int32)
    angles = positions.astype(F32)[:, None] * inv_freq[None, :]
    cosine = jnp.cos(angles)
    sine = jnp.sin(angles)
    steps = jnp.arange(blk).astype(F32)
    gap = steps[:, None] - steps[None, :]
    masks = jnp.where(
        gap[None] >= 0.0, jnp.exp(jnp.maximum(gap, 0.0)[None] * logs[:, None, None]), 0.0
    )
    q_decays = jnp.exp((steps + 1.0)[None, :] * logs[:, None])[..., None]
    k_decays = jnp.exp((blk - 1.0 - steps)[None, :] * logs[:, None])[..., None]
    block_decays = jnp.exp(blk * logs)

    xf = tokens.astype(F32)
    normed = gather_seq(rms_scale(xf, gain_attn).astype(BF16))
    d_ffn = gather_near(cotangent)
    slots = [gather_shard(offered(0))]
    slots[0], normed, d_ffn, cosine, sine, masks, q_decays, k_decays = tie(
        slots[0], normed, d_ffn, cosine, sine, masks, q_decays, k_decays
    )
    for h in range(1, local_heads):
        slots.append(gather_shard(offered(h)))
    mixer_out_cut = jnp.concatenate(
        [
            lax.dynamic_slice_in_dim(mixer_out, (h * group + s) * DV, DV, 1)
            for h in range(local_heads)
        ],
        axis=1,
    )
    mixer_out_cut, slots[0] = tie(mixer_out_cut, slots[0])
    w_out = gather_shard(mixer_out_cut)
    later = [
        lax.dynamic_slice_in_dim(ffn_in, s * sub, sub, 0),
        lax.dynamic_index_in_dim(ffn_out_cut, s, 2, keepdims=False).reshape(ffn_out.shape[0], -1),
    ]
    inner_cols = later[1].shape[1]

    ranks = segment_order
    piece = DK // segments

    def exchange_states(hs, totals, reverse, beside=()):
        cut = jnp.concatenate([t.reshape(segments, piece, DV) for t in totals], axis=1)
        got = lax.all_to_all(cut, "shard", split_axis=0, concat_axis=0, tiled=True)
        got, *beside = tie(got, *beside)
        apart = ranks[:, None] - ranks[None, :] - 1
        if reverse:
            apart = -apart - 2
        distance = apart.astype(F32)
        joined = []
        for n, h in enumerate(hs):
            coef = jnp.where(
                distance >= 0.0, jnp.exp(jnp.maximum(distance, 0.0) * seg_len * logs[h]), 0.0
            )
            part = got[:, n * piece : (n + 1) * piece].astype(F32)
            joined.append(jnp.sum(coef[..., None, None] * part[None], axis=1).astype(BF16))
        joined = jnp.concatenate(joined, axis=1)
        back_cut = lax.all_to_all(joined, "shard", split_axis=0, concat_axis=0, tiled=True)
        states = [
            back_cut[:, n * piece : (n + 1) * piece].reshape(DK, DV) for n in range(len(hs))
        ]
        return (states, *beside)

    def whole(n):
        return (0, 0)

    def ahead(n):
        return (n, 0)

    def behind(n):
        return (blocks - 1 - n, 0)

    def shaped(columns, kind, r=seg_len):
        return jax.ShapeDtypeStruct((r, columns), kind)

    state_scratch = [pltpu.VMEM((DK, DV), F32)]
    half_block = (blk, half)
    unit_block, v_block = (blk, DK), (blk, DV)
    ret_flops = 2 * seg_len * (DK + DV) * (blk + DK)
    low = s < group // 2
    if balanced:
        roles = [["q", "k", "va", "vb", "xv", "g", "g", "g"], ["q", "k", "vb", "g"]]
    else:
        roles = [["q", "k", "va", "vb", "g", "g"]] * local_heads
    params = [
        (jnp.stack([block_decays[h], low.astype(F32)]), None, None) for h in range(local_heads)
    ]
    heads_kept = []
    extra_v = None
    for h in range(local_heads):
        if balanced:
            weights = slots[h]
        else:
            cut = slots[h].reshape(-1, DK, width)
            weights = jnp.concatenate([pick(cut, place[h, s, c]) for c in range(6)], axis=0)
        carried = "va" not in roles[h]
        gate_count = roles[h].count("g")
        q, k, v, total, gates, *extra = head_call(
            functools.partial(project_kernel, blk, roles[h], carried),
            len(roles[h]) // 2,
            [
                params[h],
                (normed, (seg_len, width), whole),
                (weights, (2 * DK, width), ahead),
                (cosine, (seg_len, half), whole),
                (sine, (seg_len, half), whole),
                (k_decays[h], (blk, 1), whole),
            ]
            + ([(extra_v, (seg_len, DK), whole)] if carried else []),
            [
                (shaped(DK, BF16), (seg_len, DK), whole),
                (shaped(DK, BF16), (seg_len, DK), whole),
                (shaped(DV, BF16), (seg_len, DV), whole),
                (shaped(DV, BF16, DK), (DK, DV), whole),
                (shaped(gate_count * DK, BF16), (seg_len, gate_count * DK), whole),
            ]
            + ([(shaped(DK, BF16), (seg_len, DK), whole)] if "xv" in roles[h] else []),
            [pltpu.VMEM((seg_len, 2 * DK), F32)],
            2 * seg_len * width * len(roles[h]) * DK,
        )
        extra_v = extra[0] if extra else None
        (state_in,) = exchange_states([h], [total], False)[0]
        if h + 1 < local_heads:
            slots[h + 1], state_in, *later[:] = tie(slots[h + 1], state_in, *later)
        heads_kept.append((weights, q, k, v, gates, state_in))

    def columns(v, c, order):
        return (v, unit_block, lambda n, c=c: (order(n)[0], c))

    if balanced:
        gates0, gates1 = heads_kept[0][4], heads_kept[1][4]
        swapped = swap(jnp.where(low, gates1, gates0[:, :DK]), 2)

        def gate_operands(h, order):
            if h == 0:
                four = (gates0, 0), (gates0, 1), (swapped, 0), (gates0, 2)
            else:
                four = (gates0, 1), (gates1, 0), (gates0, 2), (swapped, 0)
            return [columns(v, c, order) for v, c in four]

    else:

        def gate_operands(h, order):
            return [columns(heads_kept[h][4], c, order) for c in (0, 0, 1, 1)]

    kept = []
    for h in range(local_heads):
        weights, q, k, v, gates, state_in = heads_kept[h]
        hidden, mixed, retained = head_call(
            retain_kernel,
            blocks,
            [
                params[h],
                (q, unit_block, ahead),
                (k, unit_block, ahead),
                (v, v_block, ahead),
                *gate_operands(h, ahead),
                (masks[h], (blk, blk), whole),
                (q_decays[h], (blk, 1), whole),
                (k_decays[h], (blk, 1), whole),
                (state_in, (DK, DV), whole),
            ],
            [
                (shaped(DV, BF16), v_block, ahead),
                (shaped(DV, BF16), v_block, ahead),
                (shaped(1, F32), (blk, 1), ahead),
            ],
            state_scratch,
            ret_flops,
        )
        kept.append((retained, mixed, hidden))
    hidden = jnp.concatenate([t[-1] for t in kept], axis=1)
    w_ffn_in, w_ffn_out = (gather_shard(t) for t in later)

    resid = xf + add_blocks(*send_blocks(seq_rows(dot_nt(hidden, w_out, BF16))))
    normed2 = gather_near(rms_scale(resid, gain_ffn).astype(BF16))
    proj2 = dot_nt(normed2, w_ffn_in)
    first, second = proj2[:, :inner_cols], proj2[:, inner_cols:]
    inner2 = gated_gelu(first, second).astype(BF16)

    g_ffn_out, d_ffn = tie(dot_tn(d_ffn, inner2, BF16), d_ffn)
    scattered = {"ffn_out": reduce_shard(g_ffn_out)}
    d_inner2 = dot_nn(d_ffn, w_ffn_out)
    ignored2, gelu_back = jax.vjp(gated_gelu, first, second)
    d_first, d_second = gelu_back(d_inner2)
    dproj2 = jnp.concatenate([d_first, d_second], axis=1).astype(BF16)
    d_normed2 = dot_nn(dproj2, w_ffn_in, BF16)
    g_ffn_in = dot_tn(dproj2, normed2, BF16)
    if group == 4:
        terms, ra, rb = first_step(near_rows(d_normed2))
        ra, rb, g_ffn_in = tie(ra, rb, g_ffn_in)
        d_normed2 = second_step(terms, ra, rb)
    else:
        d_normed2 = add_blocks(*send_blocks(near_rows(d_normed2)))
    scattered["ffn_in"] = reduce_shard(g_ffn_in)
    ignored3, norm2_back = jax.vjp(rms_scale, resid, gain_ffn)
    d_resid_part, d_gain_ffn = norm2_back(d_normed2)
    d_resid = cotangent.astype(F32) + d_resid_part
    (d_attn,) = tie(d_resid.astype(BF16))
    d_attn = gather_seq(d_attn)
    d_attn, scattered["ffn_out"] = tie(d_attn, scattered["ffn_out"])
    parts_ffn_out = spread(scattered["ffn_out"])

    def tie_parts(v, parts):
        flat = tie(v, *(piece for part in parts for piece in part))
        rest = list(flat[1:])
        return flat[0], [tuple(rest.pop(0) for _ in part) for part in parts]

    all_params = (
        jnp.concatenate([jnp.stack([jnp.float32(0.0), low.astype(F32)]), block_decays]),
        None,
        None,
    )
    outs = head_call(
        functools.partial(gate_back_kernel, local_heads),
        blocks,
        [
            all_params,
            (d_attn, (blk, width), behind),
            (w_out, (width, vcols), whole),
        ]
        + [
            t
            for h in range(local_heads)
            for t in (
                *gate_operands(h, behind),
                (kept[h][1], v_block, behind),
                (kept[h][0], (blk, 1), behind),
                (heads_kept[h][1], unit_block, behind),
                (q_decays[h], (blk, 1), whole),
            )
        ],
        [
            (shaped(DV, BF16), v_block, behind),
            (shaped(DV, BF16), v_block, behind),
            (shaped(DV, BF16, DK), (DK, DV), whole),
        ]
        * local_heads,
        state_scratch * local_heads,
        2 * seg_len * (DK * DV * local_heads + width * vcols),
    )
    d_gates, d_outs, totals = outs[0::3], outs[1::3], outs[2::3]
    if balanced:
        d_swapped = swap(jnp.where(low, d_gates[0][:, DK:], d_gates[1][:, DK:]), 2)
    else:
        d_swapped = totals[0]
    hidden, totals[0] = tie(hidden, totals[0])
    g_mixer_out = dot_tn(d_attn, hidden, BF16)
    d_outs[0], g_mixer_out = tie(d_outs[0], g_mixer_out)
    scattered["mixer_out"] = reduce_shard(g_mixer_out)
    if balanced:
        d_gate_pairs = [
            [
                ((d_gates[0], 0), (d_swapped, 0)),
                ((d_gates[1], 0), (d_gates[0], 0)),
                ((d_gates[1], 1), (d_gates[0], 1)),
            ],
            [((d_swapped, 0), (d_gates[1], 0))],
        ]
    else:
        d_gate_pairs = [[((t, 0), (t, 0)), ((t, 1), (t, 1))] for t in d_gates]
    inners = head_call(
        functools.partial(inner_back_kernel, roles),
        blocks,
        [all_params, (cosine, half_block, ahead), (sine, half_block, ahead)]
        + [
            t
            for h in range(local_heads)
            for t in (
                (heads_kept[h][1], unit_block, ahead),
                (heads_kept[h][2], unit_block, ahead),
                (heads_kept[h][3], v_block, ahead),
                (d_outs[h], v_block, ahead),
                (masks[h], (blk, blk), whole),
                (q_decays[h], (blk, 1), whole),
                (k_decays[h], (blk, 1), whole),
                (heads_kept[h][5], (DK, DV), whole),
                *(columns(v, c, ahead) for pair in d_gate_pairs[h] for v, c in pair),
            )
        ],
        [
            t
            for h in range(local_heads)
            for t in (
                (
                    shaped((1 + len(d_gate_pairs[h])) * DK, BF16),
                    (blk, (1 + len(d_gate_pairs[h])) * DK),
                    ahead,
                ),
                (shaped(DK, F32), unit_block, ahead),
                (shaped(DV, F32), v_block, ahead),
            )
        ],
        state_scratch * local_heads,
        ret_flops,
    )
    flat_ffn_out = [piece for part in parts_ffn_out for piece in part]
    grads_out, inner2, scattered["ffn_in"], *flat = exchange_states(
        range(local_heads),
        totals,
        True,
        (inner2, scattered["ffn_in"], *inners, *flat_ffn_out),
    )
    inners = flat[: 3 * local_heads]
    rest = flat[3 * local_heads :]
    parts_ffn_out = [tuple(rest.pop(0) for _ in part) for part in parts_ffn_out]
    parts_ffn_in = spread(scattered["ffn_in"])
    near = jnp.arange(group)
    if sub % 128 == 0:
        g_ffn_out = place_blocks(
            parts_ffn_out,
            s ^ near,
            near,
            ffn_out.shape,
            (ffn_out.shape[0], sub),
            lambda o, n: (0, o * group + n),
            outer=segments // 2,
        )
    else:
        g_ffn_out = jnp.transpose(
            ordered(parts_ffn_out).reshape(group, ffn_out.shape[0], segments // 2, sub),
            (1, 2, 0, 3),
        ).reshape(ffn_out.shape).astype(F32)
    earlies = inners[0::3]
    g_units = [
        unit_rows(earlies[h], normed, len(roles[h]), False) for h in range(local_heads)
    ]
    ffn_terms, g_ffn_out, *flat = tie(
        dot_nt(inner2, w_ffn_out, BF16), g_ffn_out, *grads_out, *g_units
    )
    grads_out, g_units = flat[:local_heads], flat[local_heads:]
    lates = head_call(
        functools.partial(outer_back_kernel, roles),
        blocks,
        [all_params, (cosine, half_block, behind), (sine, half_block, behind)]
        + [
            t
            for h in range(local_heads)
            for t in (
                (heads_kept[h][1], unit_block, behind),
                (heads_kept[h][2], unit_block, behind),
                (heads_kept[h][3], v_block, behind),
                (d_outs[h], v_block, behind),
                (inners[3 * h + 1], unit_block, behind),
                (inners[3 * h + 2], v_block, behind),
                (q_decays[h], (blk, 1), whole),
                (k_decays[h], (blk, 1), whole),
                (grads_out[h], (DK, DV), whole),
            )
        ],
        [
            (
                shaped(len(t) * DK - e.shape[1], BF16),
                (blk, len(t) * DK - e.shape[1]),
                behind,
            )
            for t, e in zip(roles, earlies)
        ],
        state_scratch * local_heads,
        seg_len * DK * DV,
    )

    if group == 4:
        late = first_step(near_rows(ffn_terms))
    else:
        late = send_blocks(near_rows(ffn_terms))
    lates[0], parts_ffn_in[:3] = tie_parts(lates[0], parts_ffn_in[:3])
    g_units[0] = unit_rows(lates[0], normed, len(roles[0]), True, g_units[0])
    joined = [t for pair in zip(earlies, lates) for t in pair]
    joined[0], g_units[0] = tie(joined[0], g_units[0])
    joined[0], scattered["mixer_out"] = tie(joined[0], scattered["mixer_out"])
    tile = 512
    operands = []
    for h in range(local_heads):
        weights = heads_kept[h][0]
        operands += [(t, t.shape, whole) for t in joined[2 * h : 2 * h + 2]]
        operands.append((weights, (weights.shape[0], tile), lambda n: (0, n)))
    (d_normed,) = head_call(
        functools.partial(join_kernel, local_heads),
        width // tile,
        operands,
        [(shaped(width, BF16), (seg_len, tile), lambda n: (0, n))],
        [],
        seg_len * width,
    )
    d_normed, parts_ffn_in = tie_parts(d_normed, parts_ffn_in)
    if group == 4:
        ffn_own, ra, rb = late
        d_normed, ra, rb = tie(d_normed, ra, rb)
        first = first_step(seq_rows(d_normed))
        output = (resid + second_step(ffn_own, ra, rb)).astype(BF16)
    else:
        output = (resid + add_blocks(*late)).astype(BF16)
    parts_mixer_out = spread(scattered["mixer_out"])
    for h in range(1, local_heads):
        lates[h], d_normed = tie(lates[h], d_normed)
        g_units[h] = unit_rows(lates[h], normed, len(roles[h]), True, g_units[h])
    g_ffn_in = place_blocks(
        parts_ffn_in, s ^ near, near, ffn_in.shape, (sub, width), lambda o, n: (n, 0)
    )
    if group == 4:
        own, ra, rb = first
        ra, rb, g_units[-1], g_ffn_in = tie(ra, rb, g_units[-1], g_ffn_in)
        d_normed = second_step(own, ra, rb)
    else:
        d_normed = add_blocks(*send_blocks(seq_rows(d_normed)))
    g_slots = []
    for h in range(local_heads):
        if not balanced:
            cut = g_units[h].reshape(-1, DK, width)
            g_units[h] = jnp.concatenate(
                [pick(cut, jnp.maximum(held[h, c, s], 0)) for c in range(segments)], axis=0
            )
        g_slots.append(reduce_shard(g_units[h]))

    ignored8, norm1_back = jax.vjp(rms_scale, xf, gain_attn)
    d_x_part, d_gain_attn = norm1_back(d_normed)
    input_grad = (d_resid + d_x_part).astype(BF16)
    gains = lax.all_to_all(
        jnp.broadcast_to(jnp.concatenate([d_gain_attn, d_gain_ffn])[None], (segments, 2 * width)),
        "shard",
        split_axis=0,
        concat_axis=0,
        tiled=True,
    )
    gains = jnp.sum(gains, axis=0, keepdims=True)
    parts = []
    for h in range(local_heads):
        last = h == local_heads - 1
        beside = None
        if h == 0:
            g_slots[h], input_grad = tie(g_slots[h], input_grad)
            g_slots[h], parts_mixer_out = tie_parts(g_slots[h], parts_mixer_out)
            g_mixer_out = place_blocks(
                parts_mixer_out,
                s ^ near,
                near,
                mixer_out.shape,
                (mixer_out.shape[0], DV),
                lambda o, n: (0, o * group + n),
                outer=local_heads,
            )
            beside = [g_mixer_out, output, gains]
        if last and h > 0:
            g_slots[h], gains, g_mixer_out = tie(g_slots[h], gains, g_mixer_out)
            beside = []
            g_slots[h], parts = tie_parts(g_slots[h], parts)
        here = spread(g_slots[h], beside)
        if group == 4 and h == 0:
            g_mixer_out, output, gains = beside
        if last:
            if beside is not None and group == 4:
                here[1], gains = tie(here[1], gains)
                gains = gains + swap(gains, 1)
                here[3], gains = tie(here[3], gains)
                gains = gains + swap(gains, 2)
            else:
                step = 1
                while step < group:
                    gains = gains + swap(gains, step)
                    step *= 2
        if balanced and last:
            there = [tuple(cross(piece, 1) for piece in part) for part in here]
            parts += [a + b for a, b in zip(here, there)] + [b + a for a, b in zip(here, there)]
        else:
            lend_here = lend[j] if balanced else lend[h, j]
            stack = jnp.stack([jnp.concatenate(part, axis=0) for part in here])
            parts += here + [
                (cross(pick(stack, s ^ lend_here[n]), 1),) for n in range(lend_here.shape[0])
            ]
    gain_attn_grad, gain_ffn_grad = gains[0, :width], gains[0, width:]
    found = back[j]
    if balanced:
        spare = lend.shape[-1]
        source = jnp.where(
            found[:, 0] == 0,
            s ^ found[:, 1],
            jnp.where(
                found[:, 0] == 1,
                group + found[:, 1],
                group + spare + core * group + (s ^ found[:, 1]),
            ),
        )
    else:
        source = found[:, 0] * (group + lend.shape[-1]) + jnp.where(
            found[:, 2] < 0, s ^ found[:, 1], group + found[:, 2]
        )
    g_mixer_in = place_blocks(
        parts,
        jnp.arange(source.shape[0]),
        source,
        mixer_in.shape,
        (DK, width),
        lambda o, n: (n, 0),
    )
    return (
        output,
        input_grad,
        gain_attn_grad,
        gain_ffn_grad,
        g_mixer_in,
        g_mixer_out,
        g_ffn_in,
        g_ffn_out,
    )


def solution(mesh):
    return jax.shard_map(
        local,
        mesh=mesh,
        in_specs=(
            P(("shard", "seq"), None),
            P(("shard", "seq"), None),
            P(),
            P(),
            P("shard", None),
            P("shard", None),
            P("shard", None),
            P("shard", None),
            P(),
            P(),
        ),
        out_specs=(
            P(("shard", "seq"), None),
            P(("shard", "seq"), None),
            P(),
            P(),
            P("shard", None),
            P("shard", None),
            P("shard", None),
            P("shard", None),
        ),
        check_vma=False,
    )
```

```python
import functools

import jax
import jax.numpy as jnp
import numpy as np
from jax import lax
from jax.experimental import pallas as pl
from jax.experimental.pallas import tpu as pltpu
from jax.sharding import PartitionSpec as P

DK = 256
DV = 512
FF = 4096
QK = 2048
V = 4096


EPS_NORM = 1e-06
EPS_GROUP = 1e-05

F32 = jnp.float32
BF16 = jnp.bfloat16


def dot_nt(left, right, kind=F32):
    return lax.dot_general(
        left, right, (((1,), (1,)), ((), ())), preferred_element_type=F32
    ).astype(kind)


def dot_nn(left, right, kind=F32):
    return lax.dot_general(
        left, right, (((1,), (0,)), ((), ())), preferred_element_type=F32
    ).astype(kind)


def dot_tn(left, right, kind=F32):
    return lax.dot_general(
        left, right, (((0,), (0,)), ((), ())), preferred_element_type=F32
    ).astype(kind)


def rms_scale(v, gain):
    return v * lax.rsqrt(jnp.mean(v * v, axis=-1, keepdims=True) + EPS_NORM) * gain


def gated_gelu(first, second):
    return jax.nn.gelu(first) * second


def unit_owners(heads):
    owners = [(n, 0) for n in range(heads)] + [(n, 1) for n in range(heads)]
    for base in (2, 4):
        owners += [(n, base + half) for n in range(heads) for half in range(2)]
    return owners


def balanced_tables():
    group, segments, per_shard = 4, 8, 6
    number = {owner: u for u, owner in enumerate(unit_owners(8))}
    keep = np.full((2, segments, group), -1, np.int32)
    give = np.zeros((2, segments, group), np.int32)
    back = np.zeros((segments, per_shard, 2), np.int32)
    lend = [[] for _ in range(segments)]
    seen = set()
    for s in range(group):
        a, b = s, s + 4
        if s < 2:
            gates = [(a, 4), (b, 4), (b, 5)], (b + 2, 5)
        else:
            gates = [(a - 2, 5), (a, 4), (a, 5)], (b, 4)
        first = [(a, 0), (a, 1), (a, 2), (a, 3), (b, 2)] + gates[0]
        second = [(b, 0), (b, 1), (b, 3), gates[1]]
        for slot, owner in enumerate(first):
            home, index = divmod(number[owner], per_shard)
            seen.add(number[owner])
            assert home // 2 == slot // 2
            if home == slot:
                keep[0, slot, s] = index
                back[home, index] = (0, s)
            else:
                give[0, home, s] = index
                back[home, index] = (1, len(lend[slot]))
                lend[slot].append(s)
        for chip, owner in enumerate(second):
            home, index = divmod(number[owner], per_shard)
            seen.add(number[owner])
            assert home // 2 == chip
            keep[1, home, s] = index
            give[1, home, s] = index
            back[home, index] = (2, s)
    assert len(seen) == segments * per_shard
    most = max(len(t) for t in lend)
    return keep, give, back, np.asarray([(t + [0] * most)[:most] for t in lend], np.int32)


def unit_tables(group, local_heads, segments):
    heads = group * local_heads
    owners = unit_owners(heads)
    per_shard = len(owners) // segments
    keep = np.full((local_heads, segments, group), -1, np.int32)
    give = np.zeros((local_heads, segments, group), np.int32)
    place = np.zeros((local_heads, group, 6), np.int32)
    held = np.full((local_heads, segments, group), -1, np.int32)
    slot_of = {}
    for chip in range(segments // 2):
        for head in range(heads):
            h, s = divmod(head, group)
            span = range(2 * per_shard * chip, 2 * per_shard * (chip + 1))
            mine = [u for u in span if owners[u][0] == head]
            assert len(mine) <= 2
            for n, u in enumerate(mine):
                home = u // per_shard
                slot = home if len(mine) == 1 else 2 * chip + n
                if slot == home:
                    keep[h, slot, s] = u % per_shard
                else:
                    give[h, home, s] = u % per_shard
                place[h, s, owners[u][1]] = slot
                held[h, slot, s] = owners[u][1]
                slot_of[u] = slot
    lends = [[[] for _ in range(segments)] for _ in range(local_heads)]
    back = np.zeros((segments, per_shard, 3), np.int32)
    for u, (head, _) in enumerate(owners):
        home = u // per_shard
        h, s = divmod(head, group)
        back[home, u % per_shard] = (h, s, -1)
        if slot_of[u] != home:
            assert slot_of[u] == home ^ 1
            back[home, u % per_shard, 2] = len(lends[h][home ^ 1])
            lends[h][home ^ 1].append(s)
    most = max(1, max(len(t) for row in lends for t in row))
    lend = np.asarray(
        [[(t + [0] * most)[:most] for t in row] for row in lends], np.int32
    )
    return keep, give, place, held, back, lend


def tie(*values):
    return lax.optimization_barrier(values)


def mm(left, right, dims):
    return lax.dot_general(left, right, (dims, ((), ())), preferred_element_type=F32)


NN = ((1,), (0,))
NT = ((1,), (1,))
TN = ((0,), (0,))


def turn(v, cosine, sine):
    half = v.shape[-1] // 2
    first, second = v[:, :half], v[:, half:]
    return jnp.concatenate(
        [first * cosine - second * sine, second * cosine + first * sine], axis=-1
    )


def scaled(v, decay):
    return (v.astype(F32) * decay).astype(BF16)


def project_kernel(blk, roles, carried, params, x, w, cosine, sine, k_decay, *refs):
    if carried:
        v_a, *refs = refs
    q, k, v, total, gates, *rest = refs
    y = rest[-1]
    rows = y.shape[0]
    y[...] = mm(x[...], w[...], NT)

    def put(role, part, gate_at):
        value = y[:, part * DK : (part + 1) * DK]
        if role == "q":
            q[...] = turn(value, cosine[...], sine[...]).astype(BF16)
        elif role == "k":
            k[...] = turn(value, cosine[...], sine[...]).astype(BF16)
        elif role == "va":
            v[:, :DK] = value.astype(BF16)
        elif role == "vb":
            v[:, DK:] = value.astype(BF16)
        elif role == "xv":
            rest[0][...] = value.astype(BF16)
        else:
            gates[:, gate_at * DK : (gate_at + 1) * DK] = value.astype(BF16)

    for step in range(len(roles) // 2):

        @pl.when(pl.program_id(0) == step)
        def _(step=step):
            for part in range(2):
                at = 2 * step + part
                put(roles[at], part, roles[:at].count("g"))
            if step == 1:
                if carried:
                    v[:, :DK] = v_a[...]
                state = jnp.zeros(total.shape, F32)
                for r in range(0, rows, blk):
                    kd = scaled(k[r : r + blk, :], k_decay[...])
                    state = params[0] * state + mm(kd, v[r : r + blk, :], TN)
                total[...] = state.astype(BF16)


def join_kernel(count, *refs):
    out = refs[-1]
    total = None
    for n in range(count):
        early, late, weights = refs[3 * n : 3 * n + 3]
        middle = DK + late.shape[1]
        part = mm(early[:, :DK], weights[:DK, :], NN)
        part += mm(early[:, DK:], weights[middle:, :], NN)
        part += mm(late[...], weights[DK:middle, :], NN)
        total = part if total is None else total + part
    out[...] = total.astype(out.dtype)


def select(params, low, high):
    return jnp.where(params[1] > 0.5, low[...].astype(F32), high[...].astype(F32))


def retain_kernel(
    params, q, k, v, low_a, high_a, low_b, high_b, mask, q_decay, k_decay, start,
    hidden, mixed, kept, state,
):
    @pl.when(pl.program_id(0) == 0)
    def _():
        state[...] = start[...].astype(F32)

    weights = (mm(q[...], k[...], NT) * mask[...]).astype(BF16)
    o = mm(weights, v[...], NN)
    o += mm(scaled(q[...], q_decay[...]), state[...].astype(BF16), NN)
    state[...] = params[0] * state[...] + mm(scaled(k[...], k_decay[...]), v[...], TN)
    o = o - jnp.mean(o, axis=-1, keepdims=True)
    inverse = lax.rsqrt(jnp.mean(o * o, axis=-1, keepdims=True) + EPS_GROUP)
    kept[...] = inverse
    low = (o * inverse).astype(BF16)
    mixed[...] = low
    for n, (one, two) in enumerate(((low_a, high_a), (low_b, high_b))):
        columns = slice(n * DK, (n + 1) * DK)
        g = select(params, one, two)
        hidden[:, columns] = (g * jax.nn.sigmoid(g) * low[:, columns].astype(F32)).astype(BF16)


def take(refs, counts):
    pieces, at = [], 0
    for count in counts:
        pieces.append(refs[at : at + count])
        at += count
    return pieces


def gate_back_kernel(heads, params, d_attn, w_out, *refs):
    inputs = take(refs, [8] * heads)
    outputs = take(refs[8 * heads :], [3] * heads)
    states = refs[11 * heads :]

    @pl.when(pl.program_id(0) == 0)
    def _():
        for state in states:
            state[...] = jnp.zeros(state.shape, F32)

    d_hidden = mm(d_attn[...], w_out[...], NN)
    for h in range(heads):
        low_a, high_a, low_b, high_b, mixed, inverse, q, q_decay = inputs[h]
        d_gate, d_out, total = outputs[h]
        g = jnp.concatenate(
            [select(params, low_a, high_a), select(params, low_b, high_b)], axis=1
        )
        dh = d_hidden[:, h * DV : (h + 1) * DV]
        sig = jax.nn.sigmoid(g)
        o = mixed[...].astype(F32)
        d_gate[...] = (dh * o * (sig * (1.0 + g * (1.0 - sig)))).astype(BF16)
        dy = (dh * (g * sig)).astype(BF16).astype(F32)
        do = inverse[...] * (
            dy
            - jnp.mean(dy, axis=-1, keepdims=True)
            - o * jnp.mean(dy * o, axis=-1, keepdims=True)
        )
        do = do.astype(BF16)
        d_out[...] = do
        state = states[h]
        state[...] = params[2 + h] * state[...] + mm(scaled(q[...], q_decay[...]), do, TN)
        total[...] = state[...].astype(BF16)


def inner_back_kernel(roles, params, cosine, sine, *refs):
    heads = len(roles)
    counts = [8 + 2 * t.count("g") for t in roles]
    inputs = take(refs, counts)
    outputs = take(refs[sum(counts) :], [3] * heads)
    states = refs[sum(counts) + 3 * heads :]

    @pl.when(pl.program_id(0) == 0)
    def _():
        for h in range(heads):
            states[h][...] = inputs[h][7][...].astype(F32)

    for h in range(heads):
        q, k, v, d_out, mask, q_decay, k_decay, ignored, *gates = inputs[h]
        early, d_k, d_v = outputs[h]
        state = states[h]
        do = d_out[...]
        weights = (mm(q[...], k[...], NT) * mask[...]).astype(BF16)
        d_v[...] = mm(weights, do, TN)
        d_scores = mm(do, v[...], NT).astype(BF16).astype(F32)
        d_scores = (d_scores * mask[...]).astype(BF16)
        d_k[...] = mm(d_scores, q[...], TN)
        far = mm(do, state[...].astype(BF16), NT).astype(BF16).astype(F32)
        dq = mm(d_scores, k[...], NN) + far * q_decay[...]
        dq = dq.astype(BF16).astype(F32)
        early[:, :DK] = turn(dq, cosine[...], -sine[...]).astype(BF16)
        for n in range(len(gates) // 2):
            value = select(params, gates[2 * n], gates[2 * n + 1]).astype(BF16)
            early[:, (n + 1) * DK : (n + 2) * DK] = value
        state[...] = params[2 + h] * state[...] + mm(scaled(k[...], k_decay[...]), v[...], TN)


def outer_back_kernel(roles, params, cosine, sine, *refs):
    heads = len(roles)
    inputs = take(refs, [9] * heads)
    outputs = refs[9 * heads : 10 * heads]
    states = refs[10 * heads :]

    @pl.when(pl.program_id(0) == 0)
    def _():
        for h in range(heads):
            states[h][...] = inputs[h][8][...].astype(F32)

    other = None
    for h in reversed(range(heads)):
        q, k, v, d_out, d_k, d_v, q_decay, k_decay, ignored = inputs[h]
        state = states[h]
        low = state[...].astype(BF16)
        far = mm(v[...], low, NT).astype(BF16).astype(F32)
        dk = (d_k[...] + far * k_decay[...]).astype(BF16).astype(F32)
        dk = turn(dk, cosine[...], -sine[...]).astype(BF16)
        dv = (d_v[...] + mm(scaled(k[...], k_decay[...]), low, NN)).astype(BF16)
        values = {"k": dk, "va": dv[:, :DK], "vb": dv[:, DK:], "xv": other}
        for n, role in enumerate(t for t in roles[h] if t in values):
            outputs[h][:, n * DK : (n + 1) * DK] = values[role]
        other = dv[:, :DK]
        state[...] = params[2 + h] * state[...] + mm(scaled(q[...], q_decay[...]), d_out[...], TN)


def unit_kernel(x, normed, *refs):
    refs[-1][...] = mm(x[...], normed[...], TN).astype(BF16)


def unit_rows(x, normed, count, late, into=None):
    rows, width = normed.shape
    units = x.shape[1] // DK

    def where(n):
        return (n + 1, 0) if late else (jnp.where(n == 0, 0, n + count - units), 0)

    arrays = [x, normed] + ([] if into is None else [into])
    return pl.pallas_call(
        unit_kernel,
        grid=(units,),
        in_specs=[
            pl.BlockSpec((rows, DK), lambda n: (0, n)),
            pl.BlockSpec((rows, width), lambda n: (0, 0)),
        ]
        + ([] if into is None else [pl.BlockSpec(memory_space=pl.ANY)]),
        out_specs=pl.BlockSpec((DK, width), where),
        out_shape=jax.ShapeDtypeStruct((count * DK, width), BF16),
        input_output_aliases={} if into is None else {2: 0},
        compiler_params=pltpu.CompilerParams(vmem_limit_bytes=48 * 2**20),
        cost_estimate=pl.CostEstimate(
            flops=rows * width * DK, bytes_accessed=rows * width, transcendentals=0
        ),
    )(*arrays)


def head_call(kernel, grid, operands, outputs, scratch, flops, size=None):
    arrays = [t[0] for t in operands]
    if size is None:
        size = sum(t.size * t.dtype.itemsize for t in arrays + [t[0] for t in outputs])
    call = pl.pallas_call(
        kernel,
        grid=(grid,),
        in_specs=[
            pl.BlockSpec(memory_space=pltpu.SMEM) if block is None else pl.BlockSpec(block, where)
            for _, block, where in operands
        ],
        out_specs=[pl.BlockSpec(block, where) for _, block, where in outputs],
        scratch_shapes=scratch,
        out_shape=[t[0] for t in outputs],
        compiler_params=pltpu.CompilerParams(vmem_limit_bytes=56 * 2**20),
        cost_estimate=pl.CostEstimate(flops=flops, bytes_accessed=size, transcendentals=0),
    )
    return list(call(*arrays))


def place_kernel(parts, target, source, *refs):
    out = refs[-1]
    code = source[pl.program_id(1)]
    for i, part in enumerate(parts):

        @pl.when(code == i)
        def _(part=part):
            row = 0
            for n in part:
                piece = refs[n]
                out[row : row + piece.shape[0], :] = piece[...].astype(F32)
                row += piece.shape[0]


def place_blocks(parts, target, source, shape, block, where, outer=1):
    flat, index = [], []
    for part in parts:
        for piece in part:
            if not any(piece is t for t in flat):
                flat.append(piece)
        index.append([next(n for n, t in enumerate(flat) if t is piece) for piece in part])
    return pl.pallas_call(
        functools.partial(place_kernel, index),
        grid_spec=pltpu.PrefetchScalarGridSpec(
            num_scalar_prefetch=2,
            grid=(outer, target.shape[0]),
            in_specs=[
                pl.BlockSpec((t.shape[0], t.shape[1] // outer), lambda o, n, target, source: (0, o))
                for t in flat
            ],
            out_specs=pl.BlockSpec(block, lambda o, n, target, source: where(o, target[n])),
        ),
        out_shape=jax.ShapeDtypeStruct(shape, F32),
        compiler_params=pltpu.CompilerParams(vmem_limit_bytes=48 * 2**20),
    )(target.astype(jnp.int32), source.astype(jnp.int32), *flat)


def local(
    tokens,
    cotangent,
    gain_attn,
    gain_ffn,
    mixer_in,
    mixer_out,
    ffn_in,
    ffn_out,
    segment_order,
    decay_index,
):
    rows, width = tokens.shape
    group = lax.axis_size("seq")
    segments = lax.axis_size("shard")
    heads = decay_index.shape[0]
    local_heads = heads // group
    seg_len = rows * group
    blk = min(512, seg_len)
    blocks = seg_len // blk
    vcols = local_heads * DV
    s = lax.axis_index("seq")
    j = lax.axis_index("shard")

    def swap(v, d):
        return lax.ppermute(v, "seq", [(i, i ^ d) for i in range(group)])

    def cross(v, d):
        return lax.ppermute(v, "shard", [(i, i ^ d) for i in range(segments)])

    def pick(v, i):
        return lax.dynamic_index_in_dim(v, i, 0, keepdims=False)

    def spread(v, beside=None):
        if group == 4:
            h = v.shape[0] // 2
            r1 = swap(v, 1)
            r2 = swap(v, 2)
            if beside:
                r1, r2, beside[:] = tie(r1, r2, list(beside))
            return [(v,), (r1,), (r2,), (swap(r1[:h], 2), swap(r2[h:], 1))]
        return [(v,)] + [(swap(v, d),) for d in range(1, group)]

    def ordered(parts):
        r = parts[0][0].shape[0]
        out = jnp.zeros((group * r,) + parts[0][0].shape[1:], parts[0][0].dtype)
        for d, part in enumerate(parts):
            row = (s ^ d) * r
            for piece in part:
                out = lax.dynamic_update_slice_in_dim(out, piece, row, 0)
                row = row + piece.shape[0]
        return out

    def gather_near(v):
        return jnp.concatenate([piece for part in spread(v) for piece in part], axis=0)

    def gather_seq(v):
        return ordered(spread(v))

    def first_step(blk_of):
        b = [blk_of(d) for d in range(4)]
        h = b[0].shape[0] // 2
        sa = jnp.concatenate([b[1][:h], b[3][:h]], axis=0)
        sb = jnp.concatenate([b[2][h:], b[3][h:]], axis=0)
        sa, sb = tie(sa, sb)
        return b, swap(sa, 1), swap(sb, 2)

    def second_step(b, ra, rb):
        h = b[0].shape[0] // 2
        ra, rb = ra.astype(F32), rb.astype(F32)
        qa = (b[2][:h].astype(F32) + ra[h:]).astype(BF16)
        qb = (b[1][h:].astype(F32) + rb[h:]).astype(BF16)
        qa, qb = tie(qa, qb)
        qa, qb = swap(qa, 2), swap(qb, 1)
        top = b[0][:h].astype(F32) + ra[:h] + qa.astype(F32)
        return jnp.concatenate([top, b[0][h:].astype(F32) + rb[:h] + qb.astype(F32)], axis=0)

    def send_blocks(blk_of):
        sent = tie(*(blk_of(d) for d in range(group)))
        return sent[0], [swap(sent[d], d) for d in range(group - 1, 0, -1)]

    def add_blocks(own, got):
        own = own.astype(F32)
        for t in got:
            own = own + t.astype(F32)
        return own

    def near_rows(v):
        return lambda d: v[d * rows : (d + 1) * rows]

    def seq_rows(v):
        return lambda d: lax.dynamic_slice_in_dim(v, (s ^ d) * rows, rows, 0)

    def gather_shard(v):
        return lax.all_gather(v, "shard", axis=0, tiled=True)

    def reduce_shard(v):
        return lax.psum_scatter(v, "shard", scatter_dimension=0, tiled=True)

    balanced = group == 4 and local_heads == 2 and segments == 8
    units = mixer_in.reshape(-1, DK, width)
    if balanced:
        keep, give, back, lend = (jnp.asarray(t) for t in balanced_tables())
        core = j % 2
    else:
        keep, give, place, held, back, lend = (
            jnp.asarray(t) for t in unit_tables(group, local_heads, segments)
        )

    def offered(h):
        kept, given = keep[h, j, s], give[h, j, s]
        if balanced and h == 1:
            cut = mixer_in.reshape(-1, DK // 2, width)
            own = pick(cut, 2 * jnp.maximum(kept, 0) + core)
            given = cross(pick(cut, 2 * given + 1 - core), 1)
        else:
            own = pick(units, jnp.maximum(kept, 0))
            given = cross(pick(units, given), 1)
        return jnp.where(kept >= 0, own, given)

    sub = ffn_in.shape[0] // group
    ffn_out_cut = ffn_out.reshape(ffn_out.shape[0], segments // 2, group, sub)

    my_rank = jnp.sum(jnp.where(jnp.arange(segments) == j, segment_order, 0))
    all_logs = jnp.log1p(-jnp.exp2(-(5.0 + decay_index.astype(F32))))
    logs = lax.dynamic_index_in_dim(all_logs.reshape(local_heads, group), s, 1, keepdims=False)
    half = DK // 2
    inv_freq = jnp.exp(-jnp.log(10000.0) * jnp.arange(half).astype(F32) / half)
    positions = my_rank * seg_len + jnp.arange(seg_len, dtype=jnp.int32)
    angles = positions.astype(F32)[:, None] * inv_freq[None, :]
    cosine = jnp.cos(angles)
    sine = jnp.sin(angles)
    steps = jnp.arange(blk).astype(F32)
    gap = steps[:, None] - steps[None, :]
    masks = jnp.where(
        gap[None] >= 0.0, jnp.exp(jnp.maximum(gap, 0.0)[None] * logs[:, None, None]), 0.0
    )
    q_decays = jnp.exp((steps + 1.0)[None, :] * logs[:, None])[..., None]
    k_decays = jnp.exp((blk - 1.0 - steps)[None, :] * logs[:, None])[..., None]
    block_decays = jnp.exp(blk * logs)

    xf = tokens.astype(F32)
    normed = gather_seq(rms_scale(xf, gain_attn).astype(BF16))
    d_ffn = gather_near(cotangent)
    slots = [gather_shard(offered(0))]
    slots[0], normed, d_ffn, cosine, sine, masks, q_decays, k_decays = tie(
        slots[0], normed, d_ffn, cosine, sine, masks, q_decays, k_decays
    )
    for h in range(1, local_heads):
        slots.append(gather_shard(offered(h)))
    mixer_out_cut = jnp.concatenate(
        [
            lax.dynamic_slice_in_dim(mixer_out, (h * group + s) * DV, DV, 1)
            for h in range(local_heads)
        ],
        axis=1,
    )
    mixer_out_cut, slots[0] = tie(mixer_out_cut, slots[0])
    w_out = gather_shard(mixer_out_cut)
    later = [
        lax.dynamic_slice_in_dim(ffn_in, s * sub, sub, 0),
        lax.dynamic_index_in_dim(ffn_out_cut, s, 2, keepdims=False).reshape(ffn_out.shape[0], -1),
    ]
    inner_cols = later[1].shape[1]

    ranks = segment_order
    piece = DK // segments

    def exchange_states(hs, totals, reverse, beside=()):
        cut = jnp.concatenate([t.reshape(segments, piece, DV) for t in totals], axis=1)
        got = lax.all_to_all(cut, "shard", split_axis=0, concat_axis=0, tiled=True)
        got, *beside = tie(got, *beside)
        apart = ranks[:, None] - ranks[None, :] - 1
        if reverse:
            apart = -apart - 2
        distance = apart.astype(F32)
        joined = []
        for n, h in enumerate(hs):
            coef = jnp.where(
                distance >= 0.0, jnp.exp(jnp.maximum(distance, 0.0) * seg_len * logs[h]), 0.0
            )
            part = got[:, n * piece : (n + 1) * piece].astype(F32)
            joined.append(jnp.sum(coef[..., None, None] * part[None], axis=1).astype(BF16))
        joined = jnp.concatenate(joined, axis=1)
        back_cut = lax.all_to_all(joined, "shard", split_axis=0, concat_axis=0, tiled=True)
        states = [
            back_cut[:, n * piece : (n + 1) * piece].reshape(DK, DV) for n in range(len(hs))
        ]
        return (states, *beside)

    def whole(n):
        return (0, 0)

    def ahead(n):
        return (n, 0)

    def behind(n):
        return (blocks - 1 - n, 0)

    def shaped(columns, kind, r=seg_len):
        return jax.ShapeDtypeStruct((r, columns), kind)

    state_scratch = [pltpu.VMEM((DK, DV), F32)]
    half_block = (blk, half)
    unit_block, v_block = (blk, DK), (blk, DV)
    ret_flops = 2 * seg_len * (DK + DV) * (blk + DK)
    low = s < group // 2
    if balanced:
        roles = [["q", "k", "va", "vb", "xv", "g", "g", "g"], ["q", "k", "vb", "g"]]
    else:
        roles = [["q", "k", "va", "vb", "g", "g"]] * local_heads
    params = [
        (jnp.stack([block_decays[h], low.astype(F32)]), None, None) for h in range(local_heads)
    ]
    heads_kept = []
    extra_v = None
    for h in range(local_heads):
        if balanced:
            weights = slots[h]
        else:
            cut = slots[h].reshape(-1, DK, width)
            weights = jnp.concatenate([pick(cut, place[h, s, c]) for c in range(6)], axis=0)
        carried = "va" not in roles[h]
        gate_count = roles[h].count("g")
        q, k, v, total, gates, *extra = head_call(
            functools.partial(project_kernel, blk, roles[h], carried),
            len(roles[h]) // 2,
            [
                params[h],
                (normed, (seg_len, width), whole),
                (weights, (2 * DK, width), ahead),
                (cosine, (seg_len, half), whole),
                (sine, (seg_len, half), whole),
                (k_decays[h], (blk, 1), whole),
            ]
            + ([(extra_v, (seg_len, DK), whole)] if carried else []),
            [
                (shaped(DK, BF16), (seg_len, DK), whole),
                (shaped(DK, BF16), (seg_len, DK), whole),
                (shaped(DV, BF16), (seg_len, DV), whole),
                (shaped(DV, BF16, DK), (DK, DV), whole),
                (shaped(gate_count * DK, BF16), (seg_len, gate_count * DK), whole),
            ]
            + ([(shaped(DK, BF16), (seg_len, DK), whole)] if "xv" in roles[h] else []),
            [pltpu.VMEM((seg_len, 2 * DK), F32)],
            2 * seg_len * width * len(roles[h]) * DK,
        )
        extra_v = extra[0] if extra else None
        (state_in,) = exchange_states([h], [total], False)[0]
        if h + 1 < local_heads:
            slots[h + 1], state_in, *later[:] = tie(slots[h + 1], state_in, *later)
        heads_kept.append((weights, q, k, v, gates, state_in))

    def columns(v, c, order):
        return (v, unit_block, lambda n, c=c: (order(n)[0], c))

    if balanced:
        gates0, gates1 = heads_kept[0][4], heads_kept[1][4]
        swapped = swap(jnp.where(low, gates1, gates0[:, :DK]), 2)

        def gate_operands(h, order):
            if h == 0:
                four = (gates0, 0), (gates0, 1), (swapped, 0), (gates0, 2)
            else:
                four = (gates0, 1), (gates1, 0), (gates0, 2), (swapped, 0)
            return [columns(v, c, order) for v, c in four]

    else:

        def gate_operands(h, order):
            return [columns(heads_kept[h][4], c, order) for c in (0, 0, 1, 1)]

    kept = []
    for h in range(local_heads):
        weights, q, k, v, gates, state_in = heads_kept[h]
        hidden, mixed, retained = head_call(
            retain_kernel,
            blocks,
            [
                params[h],
                (q, unit_block, ahead),
                (k, unit_block, ahead),
                (v, v_block, ahead),
                *gate_operands(h, ahead),
                (masks[h], (blk, blk), whole),
                (q_decays[h], (blk, 1), whole),
                (k_decays[h], (blk, 1), whole),
                (state_in, (DK, DV), whole),
            ],
            [
                (shaped(DV, BF16), v_block, ahead),
                (shaped(DV, BF16), v_block, ahead),
                (shaped(1, F32), (blk, 1), ahead),
            ],
            state_scratch,
            ret_flops,
        )
        kept.append((retained, mixed, hidden))
    hidden = jnp.concatenate([t[-1] for t in kept], axis=1)
    w_ffn_in, w_ffn_out = (gather_shard(t) for t in later)

    resid = xf + add_blocks(*send_blocks(seq_rows(dot_nt(hidden, w_out, BF16))))
    normed2 = gather_near(rms_scale(resid, gain_ffn).astype(BF16))
    proj2 = dot_nt(normed2, w_ffn_in)
    first, second = proj2[:, :inner_cols], proj2[:, inner_cols:]
    inner2 = gated_gelu(first, second).astype(BF16)

    g_ffn_out, d_ffn = tie(dot_tn(d_ffn, inner2, BF16), d_ffn)
    scattered = {"ffn_out": reduce_shard(g_ffn_out)}
    d_inner2 = dot_nn(d_ffn, w_ffn_out)
    ignored2, gelu_back = jax.vjp(gated_gelu, first, second)
    d_first, d_second = gelu_back(d_inner2)
    dproj2 = jnp.concatenate([d_first, d_second], axis=1).astype(BF16)
    d_normed2 = dot_nn(dproj2, w_ffn_in, BF16)
    g_ffn_in = dot_tn(dproj2, normed2, BF16)
    if group == 4:
        terms, ra, rb = first_step(near_rows(d_normed2))
        ra, rb, g_ffn_in = tie(ra, rb, g_ffn_in)
        d_normed2 = second_step(terms, ra, rb)
    else:
        d_normed2 = add_blocks(*send_blocks(near_rows(d_normed2)))
    scattered["ffn_in"] = reduce_shard(g_ffn_in)
    ignored3, norm2_back = jax.vjp(rms_scale, resid, gain_ffn)
    d_resid_part, d_gain_ffn = norm2_back(d_normed2)
    d_resid = cotangent.astype(F32) + d_resid_part
    (d_attn,) = tie(d_resid.astype(BF16))
    d_attn = gather_seq(d_attn)
    d_attn, scattered["ffn_out"] = tie(d_attn, scattered["ffn_out"])
    parts_ffn_out = spread(scattered["ffn_out"])

    def tie_parts(v, parts):
        flat = tie(v, *(piece for part in parts for piece in part))
        rest = list(flat[1:])
        return flat[0], [tuple(rest.pop(0) for _ in part) for part in parts]

    all_params = (
        jnp.concatenate([jnp.stack([jnp.float32(0.0), low.astype(F32)]), block_decays]),
        None,
        None,
    )
    outs = head_call(
        functools.partial(gate_back_kernel, local_heads),
        blocks,
        [
            all_params,
            (d_attn, (blk, width), behind),
            (w_out, (width, vcols), whole),
        ]
        + [
            t
            for h in range(local_heads)
            for t in (
                *gate_operands(h, behind),
                (kept[h][1], v_block, behind),
                (kept[h][0], (blk, 1), behind),
                (heads_kept[h][1], unit_block, behind),
                (q_decays[h], (blk, 1), whole),
            )
        ],
        [
            (shaped(DV, BF16), v_block, behind),
            (shaped(DV, BF16), v_block, behind),
            (shaped(DV, BF16, DK), (DK, DV), whole),
        ]
        * local_heads,
        state_scratch * local_heads,
        2 * seg_len * (DK * DV * local_heads + width * vcols),
    )
    d_gates, d_outs, totals = outs[0::3], outs[1::3], outs[2::3]
    if balanced:
        d_swapped = swap(jnp.where(low, d_gates[0][:, DK:], d_gates[1][:, DK:]), 2)
    else:
        d_swapped = totals[0]
    hidden, totals[0] = tie(hidden, totals[0])
    g_mixer_out = dot_tn(d_attn, hidden, BF16)
    totals[0], d_swapped, g_mixer_out = tie(totals[0], d_swapped, g_mixer_out)
    if group == 4:
        totals[0], parts_ffn_out[:3] = tie_parts(totals[0], parts_ffn_out[:3])
    d_outs[0], g_mixer_out = tie(d_outs[0], g_mixer_out)
    scattered["mixer_out"] = reduce_shard(g_mixer_out)
    if balanced:
        d_gate_pairs = [
            [
                ((d_gates[0], 0), (d_swapped, 0)),
                ((d_gates[1], 0), (d_gates[0], 0)),
                ((d_gates[1], 1), (d_gates[0], 1)),
            ],
            [((d_swapped, 0), (d_gates[1], 0))],
        ]
    else:
        d_gate_pairs = [[((t, 0), (t, 0)), ((t, 1), (t, 1))] for t in d_gates]
    inners = head_call(
        functools.partial(inner_back_kernel, roles),
        blocks,
        [all_params, (cosine, half_block, ahead), (sine, half_block, ahead)]
        + [
            t
            for h in range(local_heads)
            for t in (
                (heads_kept[h][1], unit_block, ahead),
                (heads_kept[h][2], unit_block, ahead),
                (heads_kept[h][3], v_block, ahead),
                (d_outs[h], v_block, ahead),
                (masks[h], (blk, blk), whole),
                (q_decays[h], (blk, 1), whole),
                (k_decays[h], (blk, 1), whole),
                (heads_kept[h][5], (DK, DV), whole),
                *(columns(v, c, ahead) for pair in d_gate_pairs[h] for v, c in pair),
            )
        ],
        [
            t
            for h in range(local_heads)
            for t in (
                (
                    shaped((1 + len(d_gate_pairs[h])) * DK, BF16),
                    (blk, (1 + len(d_gate_pairs[h])) * DK),
                    ahead,
                ),
                (shaped(DK, F32), unit_block, ahead),
                (shaped(DV, F32), v_block, ahead),
            )
        ],
        state_scratch * local_heads,
        ret_flops,
    )
    flat_ffn_out = [piece for part in parts_ffn_out for piece in part]
    grads_out, inner2, scattered["ffn_in"], *flat = exchange_states(
        range(local_heads),
        totals,
        True,
        (inner2, scattered["ffn_in"], *inners, *flat_ffn_out),
    )
    inners = flat[: 3 * local_heads]
    rest = flat[3 * local_heads :]
    parts_ffn_out = [tuple(rest.pop(0) for _ in part) for part in parts_ffn_out]
    parts_ffn_in = spread(scattered["ffn_in"])
    near = jnp.arange(group)
    if sub % 128 == 0:
        g_ffn_out = place_blocks(
            parts_ffn_out,
            s ^ near,
            near,
            ffn_out.shape,
            (ffn_out.shape[0], sub),
            lambda o, n: (0, o * group + n),
            outer=segments // 2,
        )
    else:
        g_ffn_out = jnp.transpose(
            ordered(parts_ffn_out).reshape(group, ffn_out.shape[0], segments // 2, sub),
            (1, 2, 0, 3),
        ).reshape(ffn_out.shape).astype(F32)
    earlies = inners[0::3]
    g_units = [
        unit_rows(earlies[h], normed, len(roles[h]), False) for h in range(local_heads)
    ]
    ffn_terms, g_ffn_out, *flat = tie(
        dot_nt(inner2, w_ffn_out, BF16), g_ffn_out, *grads_out, *g_units
    )
    grads_out, g_units = flat[:local_heads], flat[local_heads:]
    lates = head_call(
        functools.partial(outer_back_kernel, roles),
        blocks,
        [all_params, (cosine, half_block, behind), (sine, half_block, behind)]
        + [
            t
            for h in range(local_heads)
            for t in (
                (heads_kept[h][1], unit_block, behind),
                (heads_kept[h][2], unit_block, behind),
                (heads_kept[h][3], v_block, behind),
                (d_outs[h], v_block, behind),
                (inners[3 * h + 1], unit_block, behind),
                (inners[3 * h + 2], v_block, behind),
                (q_decays[h], (blk, 1), whole),
                (k_decays[h], (blk, 1), whole),
                (grads_out[h], (DK, DV), whole),
            )
        ],
        [
            (
                shaped(len(t) * DK - e.shape[1], BF16),
                (blk, len(t) * DK - e.shape[1]),
                behind,
            )
            for t, e in zip(roles, earlies)
        ],
        state_scratch * local_heads,
        seg_len * DK * DV,
    )

    if group == 4:
        late = first_step(near_rows(ffn_terms))
    else:
        late = send_blocks(near_rows(ffn_terms))
    lates[0], parts_ffn_in[:3] = tie_parts(lates[0], parts_ffn_in[:3])
    g_units[0] = unit_rows(lates[0], normed, len(roles[0]), True, g_units[0])
    joined = [t for pair in zip(earlies, lates) for t in pair]
    joined[0], g_units[0] = tie(joined[0], g_units[0])
    joined[0], scattered["mixer_out"] = tie(joined[0], scattered["mixer_out"])
    tile = 512
    operands = []
    for h in range(local_heads):
        weights = heads_kept[h][0]
        operands += [(t, t.shape, whole) for t in joined[2 * h : 2 * h + 2]]
        operands.append((weights, (weights.shape[0], tile), lambda n: (0, n)))
    (d_normed,) = head_call(
        functools.partial(join_kernel, local_heads),
        width // tile,
        operands,
        [(shaped(width, BF16), (seg_len, tile), lambda n: (0, n))],
        [],
        seg_len * width,
        seg_len * width,
    )
    d_normed, parts_ffn_in = tie_parts(d_normed, parts_ffn_in)
    if group == 4:
        ffn_own, ra, rb = late
        d_normed, ra, rb = tie(d_normed, ra, rb)
        first = first_step(seq_rows(d_normed))
        output = (resid + second_step(ffn_own, ra, rb)).astype(BF16)
    else:
        output = (resid + add_blocks(*late)).astype(BF16)
    parts_mixer_out = spread(scattered["mixer_out"])
    for h in range(1, local_heads):
        lates[h], d_normed = tie(lates[h], d_normed)
        g_units[h] = unit_rows(lates[h], normed, len(roles[h]), True, g_units[h])
    g_ffn_in = place_blocks(
        parts_ffn_in, s ^ near, near, ffn_in.shape, (sub, width), lambda o, n: (n, 0)
    )
    if group == 4:
        own, ra, rb = first
        ra, rb, g_units[-1], g_ffn_in, output = tie(ra, rb, g_units[-1], g_ffn_in, output)
        d_normed = second_step(own, ra, rb)
    else:
        d_normed = add_blocks(*send_blocks(seq_rows(d_normed)))
    g_slots = []
    for h in range(local_heads):
        if not balanced:
            cut = g_units[h].reshape(-1, DK, width)
            g_units[h] = jnp.concatenate(
                [pick(cut, jnp.maximum(held[h, c, s], 0)) for c in range(segments)], axis=0
            )
        g_slots.append(reduce_shard(g_units[h]))

    ignored8, norm1_back = jax.vjp(rms_scale, xf, gain_attn)
    d_x_part, d_gain_attn = norm1_back(d_normed)
    input_grad = (d_resid + d_x_part).astype(BF16)
    gains = lax.all_to_all(
        jnp.broadcast_to(jnp.concatenate([d_gain_attn, d_gain_ffn])[None], (segments, 2 * width)),
        "shard",
        split_axis=0,
        concat_axis=0,
        tiled=True,
    )
    gains = jnp.sum(gains, axis=0, keepdims=True)
    parts = []
    for h in range(local_heads):
        last = h == local_heads - 1
        beside = None
        if h == 0:
            g_slots[h], input_grad = tie(g_slots[h], input_grad)
            g_slots[h], parts_mixer_out = tie_parts(g_slots[h], parts_mixer_out)
            g_mixer_out = place_blocks(
                parts_mixer_out,
                s ^ near,
                near,
                mixer_out.shape,
                (mixer_out.shape[0], DV),
                lambda o, n: (0, o * group + n),
                outer=local_heads,
            )
            beside = [g_mixer_out, output, gains]
        if last and h > 0:
            g_slots[h], gains, g_mixer_out = tie(g_slots[h], gains, g_mixer_out)
            beside = []
            g_slots[h], parts = tie_parts(g_slots[h], parts)
        here = spread(g_slots[h], beside)
        if group == 4 and h == 0:
            g_mixer_out, output, gains = beside
        if last:
            if beside is not None and group == 4:
                here[1], gains = tie(here[1], gains)
                gains = gains + swap(gains, 1)
                here[3], gains = tie(here[3], gains)
                gains = gains + swap(gains, 2)
            else:
                step = 1
                while step < group:
                    gains = gains + swap(gains, step)
                    step *= 2
        if balanced and last:
            there = [tuple(cross(piece, 1) for piece in part) for part in here]
            parts += [a + b for a, b in zip(here, there)] + [b + a for a, b in zip(here, there)]
        else:
            lend_here = lend[j] if balanced else lend[h, j]
            stack = jnp.stack([jnp.concatenate(part, axis=0) for part in here])
            parts += here + [
                (cross(pick(stack, s ^ lend_here[n]), 1),) for n in range(lend_here.shape[0])
            ]
    gain_attn_grad, gain_ffn_grad = gains[0, :width], gains[0, width:]
    found = back[j]
    if balanced:
        spare = lend.shape[-1]
        source = jnp.where(
            found[:, 0] == 0,
            s ^ found[:, 1],
            jnp.where(
                found[:, 0] == 1,
                group + found[:, 1],
                group + spare + core * group + (s ^ found[:, 1]),
            ),
        )
    else:
        source = found[:, 0] * (group + lend.shape[-1]) + jnp.where(
            found[:, 2] < 0, s ^ found[:, 1], group + found[:, 2]
        )
    g_mixer_in = place_blocks(
        parts,
        jnp.arange(source.shape[0]),
        source,
        mixer_in.shape,
        (DK, width),
        lambda o, n: (n, 0),
    )
    return (
        output,
        input_grad,
        gain_attn_grad,
        gain_ffn_grad,
        g_mixer_in,
        g_mixer_out,
        g_ffn_in,
        g_ffn_out,
    )


def solution(mesh):
    return jax.shard_map(
        local,
        mesh=mesh,
        in_specs=(
            P(("shard", "seq"), None),
            P(("shard", "seq"), None),
            P(),
            P(),
            P("shard", None),
            P("shard", None),
            P("shard", None),
            P("shard", None),
            P(),
            P(),
        ),
        out_specs=(
            P(("shard", "seq"), None),
            P(("shard", "seq"), None),
            P(),
            P(),
            P("shard", None),
            P("shard", None),
            P("shard", None),
            P("shard", None),
        ),
        check_vma=False,
    )
```

```python
import functools

import jax
import jax.numpy as jnp
import numpy as np
from jax import lax
from jax.experimental import pallas as pl
from jax.experimental.pallas import tpu as pltpu
from jax.sharding import PartitionSpec as P

DK = 256
DV = 512
FF = 4096
QK = 2048
V = 4096


EPS_NORM = 1e-06
EPS_GROUP = 1e-05

F32 = jnp.float32
BF16 = jnp.bfloat16


def dot_nt(left, right, kind=F32):
    return lax.dot_general(
        left, right, (((1,), (1,)), ((), ())), preferred_element_type=F32
    ).astype(kind)


def dot_nn(left, right, kind=F32):
    return lax.dot_general(
        left, right, (((1,), (0,)), ((), ())), preferred_element_type=F32
    ).astype(kind)


def dot_tn(left, right, kind=F32):
    return lax.dot_general(
        left, right, (((0,), (0,)), ((), ())), preferred_element_type=F32
    ).astype(kind)


def rms_scale(v, gain):
    return v * lax.rsqrt(jnp.mean(v * v, axis=-1, keepdims=True) + EPS_NORM) * gain


def gated_gelu(first, second):
    return jax.nn.gelu(first) * second


def unit_owners(heads):
    owners = [(n, 0) for n in range(heads)] + [(n, 1) for n in range(heads)]
    for base in (2, 4):
        owners += [(n, base + half) for n in range(heads) for half in range(2)]
    return owners


def balanced_tables():
    group, segments, per_shard = 4, 8, 6
    number = {owner: u for u, owner in enumerate(unit_owners(8))}
    keep = np.full((2, segments, group), -1, np.int32)
    give = np.zeros((2, segments, group), np.int32)
    back = np.zeros((segments, per_shard, 2), np.int32)
    lend = [[] for _ in range(segments)]
    seen = set()
    for s in range(group):
        a, b = s, s + 4
        if s < 2:
            gates = [(a, 4), (b, 4), (b, 5)], (b + 2, 5)
        else:
            gates = [(a - 2, 5), (a, 4), (a, 5)], (b, 4)
        first = [(a, 0), (a, 1), (a, 2), (a, 3), (b, 2)] + gates[0]
        second = [(b, 0), (b, 1), (b, 3), gates[1]]
        for slot, owner in enumerate(first):
            home, index = divmod(number[owner], per_shard)
            seen.add(number[owner])
            assert home // 2 == slot // 2
            if home == slot:
                keep[0, slot, s] = index
                back[home, index] = (0, s)
            else:
                give[0, home, s] = index
                back[home, index] = (1, len(lend[slot]))
                lend[slot].append(s)
        for chip, owner in enumerate(second):
            home, index = divmod(number[owner], per_shard)
            seen.add(number[owner])
            assert home // 2 == chip
            keep[1, home, s] = index
            give[1, home, s] = index
            back[home, index] = (2, s)
    assert len(seen) == segments * per_shard
    most = max(len(t) for t in lend)
    return keep, give, back, np.asarray([(t + [0] * most)[:most] for t in lend], np.int32)


def unit_tables(group, local_heads, segments):
    heads = group * local_heads
    owners = unit_owners(heads)
    per_shard = len(owners) // segments
    keep = np.full((local_heads, segments, group), -1, np.int32)
    give = np.zeros((local_heads, segments, group), np.int32)
    place = np.zeros((local_heads, group, 6), np.int32)
    held = np.full((local_heads, segments, group), -1, np.int32)
    slot_of = {}
    for chip in range(segments // 2):
        for head in range(heads):
            h, s = divmod(head, group)
            span = range(2 * per_shard * chip, 2 * per_shard * (chip + 1))
            mine = [u for u in span if owners[u][0] == head]
            assert len(mine) <= 2
            for n, u in enumerate(mine):
                home = u // per_shard
                slot = home if len(mine) == 1 else 2 * chip + n
                if slot == home:
                    keep[h, slot, s] = u % per_shard
                else:
                    give[h, home, s] = u % per_shard
                place[h, s, owners[u][1]] = slot
                held[h, slot, s] = owners[u][1]
                slot_of[u] = slot
    lends = [[[] for _ in range(segments)] for _ in range(local_heads)]
    back = np.zeros((segments, per_shard, 3), np.int32)
    for u, (head, _) in enumerate(owners):
        home = u // per_shard
        h, s = divmod(head, group)
        back[home, u % per_shard] = (h, s, -1)
        if slot_of[u] != home:
            assert slot_of[u] == home ^ 1
            back[home, u % per_shard, 2] = len(lends[h][home ^ 1])
            lends[h][home ^ 1].append(s)
    most = max(1, max(len(t) for row in lends for t in row))
    lend = np.asarray(
        [[(t + [0] * most)[:most] for t in row] for row in lends], np.int32
    )
    return keep, give, place, held, back, lend


def tie(*values):
    return lax.optimization_barrier(values)


def mm(left, right, dims):
    return lax.dot_general(left, right, (dims, ((), ())), preferred_element_type=F32)


NN = ((1,), (0,))
NT = ((1,), (1,))
TN = ((0,), (0,))


def turn(v, cosine, sine):
    half = v.shape[-1] // 2
    first, second = v[:, :half], v[:, half:]
    return jnp.concatenate(
        [first * cosine - second * sine, second * cosine + first * sine], axis=-1
    )


def scaled(v, decay):
    return (v.astype(F32) * decay).astype(BF16)


def project_kernel(blk, roles, carried, params, x, w, cosine, sine, k_decay, *refs):
    if carried:
        v_a, *refs = refs
    q, k, v, total, gates, *rest = refs
    y = rest[-1]
    rows = y.shape[0]
    y[...] = mm(x[...], w[...], NT)

    def put(role, part, gate_at):
        value = y[:, part * DK : (part + 1) * DK]
        if role == "q":
            q[...] = turn(value, cosine[...], sine[...]).astype(BF16)
        elif role == "k":
            k[...] = turn(value, cosine[...], sine[...]).astype(BF16)
        elif role == "va":
            v[:, :DK] = value.astype(BF16)
        elif role == "vb":
            v[:, DK:] = value.astype(BF16)
        elif role == "xv":
            rest[0][...] = value.astype(BF16)
        else:
            gates[:, gate_at * DK : (gate_at + 1) * DK] = value.astype(BF16)

    for step in range(len(roles) // 2):

        @pl.when(pl.program_id(0) == step)
        def _(step=step):
            for part in range(2):
                at = 2 * step + part
                put(roles[at], part, roles[:at].count("g"))
            if step == 1:
                if carried:
                    v[:, :DK] = v_a[...]
                state = jnp.zeros(total.shape, F32)
                for r in range(0, rows, blk):
                    kd = scaled(k[r : r + blk, :], k_decay[...])
                    state = params[0] * state + mm(kd, v[r : r + blk, :], TN)
                total[...] = state.astype(BF16)


def join_kernel(count, *refs):
    out = refs[-1]
    total = None
    for n in range(count):
        early, late, weights = refs[3 * n : 3 * n + 3]
        middle = DK + late.shape[1]
        part = mm(early[:, :DK], weights[:DK, :], NN)
        part += mm(early[:, DK:], weights[middle:, :], NN)
        part += mm(late[...], weights[DK:middle, :], NN)
        total = part if total is None else total + part
    out[...] = total.astype(out.dtype)


def select(params, low, high):
    return jnp.where(params[1] > 0.5, low[...].astype(F32), high[...].astype(F32))


def retain_kernel(
    params, q, k, v, low_a, high_a, low_b, high_b, mask, q_decay, k_decay, start,
    hidden, mixed, kept, state,
):
    @pl.when(pl.program_id(0) == 0)
    def _():
        state[...] = start[...].astype(F32)

    weights = (mm(q[...], k[...], NT) * mask[...]).astype(BF16)
    o = mm(weights, v[...], NN)
    o += mm(scaled(q[...], q_decay[...]), state[...].astype(BF16), NN)
    state[...] = params[0] * state[...] + mm(scaled(k[...], k_decay[...]), v[...], TN)
    o = o - jnp.mean(o, axis=-1, keepdims=True)
    inverse = lax.rsqrt(jnp.mean(o * o, axis=-1, keepdims=True) + EPS_GROUP)
    kept[...] = inverse
    low = (o * inverse).astype(BF16)
    mixed[...] = low
    for n, (one, two) in enumerate(((low_a, high_a), (low_b, high_b))):
        columns = slice(n * DK, (n + 1) * DK)
        g = select(params, one, two)
        hidden[:, columns] = (g * jax.nn.sigmoid(g) * low[:, columns].astype(F32)).astype(BF16)


def take(refs, counts):
    pieces, at = [], 0
    for count in counts:
        pieces.append(refs[at : at + count])
        at += count
    return pieces


def gate_back_kernel(heads, params, d_attn, w_out, *refs):
    inputs = take(refs, [8] * heads)
    outputs = take(refs[8 * heads :], [3] * heads)
    states = refs[11 * heads :]

    @pl.when(pl.program_id(0) == 0)
    def _():
        for state in states:
            state[...] = jnp.zeros(state.shape, F32)

    d_hidden = mm(d_attn[...], w_out[...], NN)
    for h in range(heads):
        low_a, high_a, low_b, high_b, mixed, inverse, q, q_decay = inputs[h]
        d_gate, d_out, total = outputs[h]
        g = jnp.concatenate(
            [select(params, low_a, high_a), select(params, low_b, high_b)], axis=1
        )
        dh = d_hidden[:, h * DV : (h + 1) * DV]
        sig = jax.nn.sigmoid(g)
        o = mixed[...].astype(F32)
        d_gate[...] = (dh * o * (sig * (1.0 + g * (1.0 - sig)))).astype(BF16)
        dy = (dh * (g * sig)).astype(BF16).astype(F32)
        do = inverse[...] * (
            dy
            - jnp.mean(dy, axis=-1, keepdims=True)
            - o * jnp.mean(dy * o, axis=-1, keepdims=True)
        )
        do = do.astype(BF16)
        d_out[...] = do
        state = states[h]
        state[...] = params[2 + h] * state[...] + mm(scaled(q[...], q_decay[...]), do, TN)
        total[...] = state[...].astype(BF16)


def inner_back_kernel(roles, params, cosine, sine, *refs):
    heads = len(roles)
    counts = [8 + 2 * t.count("g") for t in roles]
    inputs = take(refs, counts)
    outputs = take(refs[sum(counts) :], [3] * heads)
    states = refs[sum(counts) + 3 * heads :]

    @pl.when(pl.program_id(0) == 0)
    def _():
        for h in range(heads):
            states[h][...] = inputs[h][7][...].astype(F32)

    for h in range(heads):
        q, k, v, d_out, mask, q_decay, k_decay, ignored, *gates = inputs[h]
        early, d_k, d_v = outputs[h]
        state = states[h]
        do = d_out[...]
        weights = (mm(q[...], k[...], NT) * mask[...]).astype(BF16)
        d_v[...] = mm(weights, do, TN)
        d_scores = mm(do, v[...], NT).astype(BF16).astype(F32)
        d_scores = (d_scores * mask[...]).astype(BF16)
        d_k[...] = mm(d_scores, q[...], TN)
        far = mm(do, state[...].astype(BF16), NT).astype(BF16).astype(F32)
        dq = mm(d_scores, k[...], NN) + far * q_decay[...]
        dq = dq.astype(BF16).astype(F32)
        early[:, :DK] = turn(dq, cosine[...], -sine[...]).astype(BF16)
        for n in range(len(gates) // 2):
            value = select(params, gates[2 * n], gates[2 * n + 1]).astype(BF16)
            early[:, (n + 1) * DK : (n + 2) * DK] = value
        state[...] = params[2 + h] * state[...] + mm(scaled(k[...], k_decay[...]), v[...], TN)


def outer_back_kernel(roles, params, cosine, sine, *refs):
    heads = len(roles)
    inputs = take(refs, [9] * heads)
    outputs = refs[9 * heads : 10 * heads]
    states = refs[10 * heads :]

    @pl.when(pl.program_id(0) == 0)
    def _():
        for h in range(heads):
            states[h][...] = inputs[h][8][...].astype(F32)

    other = None
    for h in reversed(range(heads)):
        q, k, v, d_out, d_k, d_v, q_decay, k_decay, ignored = inputs[h]
        state = states[h]
        low = state[...].astype(BF16)
        far = mm(v[...], low, NT).astype(BF16).astype(F32)
        dk = (d_k[...] + far * k_decay[...]).astype(BF16).astype(F32)
        dk = turn(dk, cosine[...], -sine[...]).astype(BF16)
        dv = (d_v[...] + mm(scaled(k[...], k_decay[...]), low, NN)).astype(BF16)
        values = {"k": dk, "va": dv[:, :DK], "vb": dv[:, DK:], "xv": other}
        for n, role in enumerate(t for t in roles[h] if t in values):
            outputs[h][:, n * DK : (n + 1) * DK] = values[role]
        other = dv[:, :DK]
        state[...] = params[2 + h] * state[...] + mm(scaled(q[...], q_decay[...]), d_out[...], TN)


def unit_kernel(x, normed, *refs):
    refs[-1][...] = mm(x[...], normed[...], TN).astype(BF16)


def unit_rows(x, normed, count, late, into=None):
    rows, width = normed.shape
    units = x.shape[1] // DK

    def where(n):
        return (n + 1, 0) if late else (jnp.where(n == 0, 0, n + count - units), 0)

    arrays = [x, normed] + ([] if into is None else [into])
    return pl.pallas_call(
        unit_kernel,
        grid=(units,),
        in_specs=[
            pl.BlockSpec((rows, DK), lambda n: (0, n)),
            pl.BlockSpec((rows, width), lambda n: (0, 0)),
        ]
        + ([] if into is None else [pl.BlockSpec(memory_space=pl.ANY)]),
        out_specs=pl.BlockSpec((DK, width), where),
        out_shape=jax.ShapeDtypeStruct((count * DK, width), BF16),
        input_output_aliases={} if into is None else {2: 0},
        compiler_params=pltpu.CompilerParams(vmem_limit_bytes=48 * 2**20),
        cost_estimate=pl.CostEstimate(
            flops=rows * width * DK, bytes_accessed=rows * width, transcendentals=0
        ),
    )(*arrays)


def head_call(kernel, grid, operands, outputs, scratch, flops, size=None):
    arrays = [t[0] for t in operands]
    if size is None:
        size = sum(t.size * t.dtype.itemsize for t in arrays + [t[0] for t in outputs])
    call = pl.pallas_call(
        kernel,
        grid=(grid,),
        in_specs=[
            pl.BlockSpec(memory_space=pltpu.SMEM) if block is None else pl.BlockSpec(block, where)
            for _, block, where in operands
        ],
        out_specs=[pl.BlockSpec(block, where) for _, block, where in outputs],
        scratch_shapes=scratch,
        out_shape=[t[0] for t in outputs],
        compiler_params=pltpu.CompilerParams(vmem_limit_bytes=56 * 2**20),
        cost_estimate=pl.CostEstimate(flops=flops, bytes_accessed=size, transcendentals=0),
    )
    return list(call(*arrays))


def place_kernel(parts, target, source, *refs):
    out = refs[-1]
    code = source[pl.program_id(1)]
    for i, part in enumerate(parts):

        @pl.when(code == i)
        def _(part=part):
            row = 0
            for n in part:
                piece = refs[n]
                out[row : row + piece.shape[0], :] = piece[...].astype(F32)
                row += piece.shape[0]


def place_blocks(parts, target, source, shape, block, where, outer=1):
    flat, index = [], []
    for part in parts:
        for piece in part:
            if not any(piece is t for t in flat):
                flat.append(piece)
        index.append([next(n for n, t in enumerate(flat) if t is piece) for piece in part])
    return pl.pallas_call(
        functools.partial(place_kernel, index),
        grid_spec=pltpu.PrefetchScalarGridSpec(
            num_scalar_prefetch=2,
            grid=(outer, target.shape[0]),
            in_specs=[
                pl.BlockSpec((t.shape[0], t.shape[1] // outer), lambda o, n, target, source: (0, o))
                for t in flat
            ],
            out_specs=pl.BlockSpec(block, lambda o, n, target, source: where(o, target[n])),
        ),
        out_shape=jax.ShapeDtypeStruct(shape, F32),
        compiler_params=pltpu.CompilerParams(vmem_limit_bytes=48 * 2**20),
    )(target.astype(jnp.int32), source.astype(jnp.int32), *flat)


def local(
    tokens,
    cotangent,
    gain_attn,
    gain_ffn,
    mixer_in,
    mixer_out,
    ffn_in,
    ffn_out,
    segment_order,
    decay_index,
):
    rows, width = tokens.shape
    group = lax.axis_size("seq")
    segments = lax.axis_size("shard")
    heads = decay_index.shape[0]
    local_heads = heads // group
    seg_len = rows * group
    blk = min(512, seg_len)
    blocks = seg_len // blk
    vcols = local_heads * DV
    s = lax.axis_index("seq")
    j = lax.axis_index("shard")

    def swap(v, d):
        return lax.ppermute(v, "seq", [(i, i ^ d) for i in range(group)])

    def cross(v, d):
        return lax.ppermute(v, "shard", [(i, i ^ d) for i in range(segments)])

    def pick(v, i):
        return lax.dynamic_index_in_dim(v, i, 0, keepdims=False)

    def spread(v, beside=None):
        if group == 4:
            h = v.shape[0] // 2
            r1 = swap(v, 1)
            r2 = swap(v, 2)
            if beside:
                r1, r2, beside[:] = tie(r1, r2, list(beside))
            return [(v,), (r1,), (r2,), (swap(r1[:h], 2), swap(r2[h:], 1))]
        return [(v,)] + [(swap(v, d),) for d in range(1, group)]

    def ordered(parts):
        r = parts[0][0].shape[0]
        out = jnp.zeros((group * r,) + parts[0][0].shape[1:], parts[0][0].dtype)
        for d, part in enumerate(parts):
            row = (s ^ d) * r
            for piece in part:
                out = lax.dynamic_update_slice_in_dim(out, piece, row, 0)
                row = row + piece.shape[0]
        return out

    def gather_near(v):
        return jnp.concatenate([piece for part in spread(v) for piece in part], axis=0)

    def gather_seq(v):
        return ordered(spread(v))

    def first_step(blk_of):
        b = [blk_of(d) for d in range(4)]
        h = b[0].shape[0] // 2
        sa = jnp.concatenate([b[1][:h], b[3][:h]], axis=0)
        sb = jnp.concatenate([b[2][h:], b[3][h:]], axis=0)
        sa, sb = tie(sa, sb)
        return b, swap(sa, 1), swap(sb, 2)

    def second_step(b, ra, rb):
        h = b[0].shape[0] // 2
        ra, rb = ra.astype(F32), rb.astype(F32)
        qa = (b[2][:h].astype(F32) + ra[h:]).astype(BF16)
        qb = (b[1][h:].astype(F32) + rb[h:]).astype(BF16)
        qa, qb = tie(qa, qb)
        qa, qb = swap(qa, 2), swap(qb, 1)
        top = b[0][:h].astype(F32) + ra[:h] + qa.astype(F32)
        return jnp.concatenate([top, b[0][h:].astype(F32) + rb[:h] + qb.astype(F32)], axis=0)

    def send_blocks(blk_of):
        sent = tie(*(blk_of(d) for d in range(group)))
        return sent[0], [swap(sent[d], d) for d in range(group - 1, 0, -1)]

    def add_blocks(own, got):
        own = own.astype(F32)
        for t in got:
            own = own + t.astype(F32)
        return own

    def near_rows(v):
        return lambda d: v[d * rows : (d + 1) * rows]

    def seq_rows(v):
        return lambda d: lax.dynamic_slice_in_dim(v, (s ^ d) * rows, rows, 0)

    def gather_shard(v):
        return lax.all_gather(v, "shard", axis=0, tiled=True)

    def reduce_shard(v):
        return lax.psum_scatter(v, "shard", scatter_dimension=0, tiled=True)

    balanced = group == 4 and local_heads == 2 and segments == 8
    units = mixer_in.reshape(-1, DK, width)
    if balanced:
        keep, give, back, lend = (jnp.asarray(t) for t in balanced_tables())
        core = j % 2
    else:
        keep, give, place, held, back, lend = (
            jnp.asarray(t) for t in unit_tables(group, local_heads, segments)
        )

    def offered(h):
        kept, given = keep[h, j, s], give[h, j, s]
        if balanced and h == 1:
            cut = mixer_in.reshape(-1, DK // 2, width)
            own = pick(cut, 2 * jnp.maximum(kept, 0) + core)
            given = cross(pick(cut, 2 * given + 1 - core), 1)
        else:
            own = pick(units, jnp.maximum(kept, 0))
            given = cross(pick(units, given), 1)
        return jnp.where(kept >= 0, own, given)

    sub = ffn_in.shape[0] // group
    ffn_out_cut = ffn_out.reshape(ffn_out.shape[0], segments // 2, group, sub)

    my_rank = jnp.sum(jnp.where(jnp.arange(segments) == j, segment_order, 0))
    all_logs = jnp.log1p(-jnp.exp2(-(5.0 + decay_index.astype(F32))))
    logs = lax.dynamic_index_in_dim(all_logs.reshape(local_heads, group), s, 1, keepdims=False)
    half = DK // 2
    inv_freq = jnp.exp(-jnp.log(10000.0) * jnp.arange(half).astype(F32) / half)
    positions = my_rank * seg_len + jnp.arange(seg_len, dtype=jnp.int32)
    angles = positions.astype(F32)[:, None] * inv_freq[None, :]
    cosine = jnp.cos(angles)
    sine = jnp.sin(angles)
    steps = jnp.arange(blk).astype(F32)
    gap = steps[:, None] - steps[None, :]
    masks = jnp.where(
        gap[None] >= 0.0, jnp.exp(jnp.maximum(gap, 0.0)[None] * logs[:, None, None]), 0.0
    )
    q_decays = jnp.exp((steps + 1.0)[None, :] * logs[:, None])[..., None]
    k_decays = jnp.exp((blk - 1.0 - steps)[None, :] * logs[:, None])[..., None]
    block_decays = jnp.exp(blk * logs)

    xf = tokens.astype(F32)
    normed = gather_seq(rms_scale(xf, gain_attn).astype(BF16))
    d_ffn = gather_near(cotangent)
    slots = [gather_shard(offered(0))]
    slots[0], normed, d_ffn, cosine, sine, masks, q_decays, k_decays = tie(
        slots[0], normed, d_ffn, cosine, sine, masks, q_decays, k_decays
    )
    for h in range(1, local_heads):
        slots.append(gather_shard(offered(h)))
    mixer_out_cut = jnp.concatenate(
        [
            lax.dynamic_slice_in_dim(mixer_out, (h * group + s) * DV, DV, 1)
            for h in range(local_heads)
        ],
        axis=1,
    )
    mixer_out_cut, slots[0] = tie(mixer_out_cut, slots[0])
    w_out = gather_shard(mixer_out_cut)
    later = [
        lax.dynamic_slice_in_dim(ffn_in, s * sub, sub, 0),
        lax.dynamic_index_in_dim(ffn_out_cut, s, 2, keepdims=False).reshape(ffn_out.shape[0], -1),
    ]
    inner_cols = later[1].shape[1]

    ranks = segment_order
    piece = DK // segments

    def exchange_states(hs, totals, reverse, beside=()):
        cut = jnp.concatenate([t.reshape(segments, piece, DV) for t in totals], axis=1)
        got = lax.all_to_all(cut, "shard", split_axis=0, concat_axis=0, tiled=True)
        got, *beside = tie(got, *beside)
        apart = ranks[:, None] - ranks[None, :] - 1
        if reverse:
            apart = -apart - 2
        distance = apart.astype(F32)
        joined = []
        for n, h in enumerate(hs):
            coef = jnp.where(
                distance >= 0.0, jnp.exp(jnp.maximum(distance, 0.0) * seg_len * logs[h]), 0.0
            )
            part = got[:, n * piece : (n + 1) * piece].astype(F32)
            joined.append(jnp.sum(coef[..., None, None] * part[None], axis=1).astype(BF16))
        joined = jnp.concatenate(joined, axis=1)
        back_cut = lax.all_to_all(joined, "shard", split_axis=0, concat_axis=0, tiled=True)
        states = [
            back_cut[:, n * piece : (n + 1) * piece].reshape(DK, DV) for n in range(len(hs))
        ]
        return (states, *beside)

    def whole(n):
        return (0, 0)

    def ahead(n):
        return (n, 0)

    def behind(n):
        return (blocks - 1 - n, 0)

    def shaped(columns, kind, r=seg_len):
        return jax.ShapeDtypeStruct((r, columns), kind)

    state_scratch = [pltpu.VMEM((DK, DV), F32)]
    half_block = (blk, half)
    unit_block, v_block = (blk, DK), (blk, DV)
    ret_flops = 2 * seg_len * (DK + DV) * (blk + DK)
    low = s < group // 2
    if balanced:
        roles = [["q", "k", "va", "vb", "xv", "g", "g", "g"], ["q", "k", "vb", "g"]]
    else:
        roles = [["q", "k", "va", "vb", "g", "g"]] * local_heads
    params = [
        (jnp.stack([block_decays[h], low.astype(F32)]), None, None) for h in range(local_heads)
    ]
    heads_kept = []
    extra_v = None
    for h in range(local_heads):
        if balanced:
            weights = slots[h]
        else:
            cut = slots[h].reshape(-1, DK, width)
            weights = jnp.concatenate([pick(cut, place[h, s, c]) for c in range(6)], axis=0)
        carried = "va" not in roles[h]
        gate_count = roles[h].count("g")
        q, k, v, total, gates, *extra = head_call(
            functools.partial(project_kernel, blk, roles[h], carried),
            len(roles[h]) // 2,
            [
                params[h],
                (normed, (seg_len, width), whole),
                (weights, (2 * DK, width), ahead),
                (cosine, (seg_len, half), whole),
                (sine, (seg_len, half), whole),
                (k_decays[h], (blk, 1), whole),
            ]
            + ([(extra_v, (seg_len, DK), whole)] if carried else []),
            [
                (shaped(DK, BF16), (seg_len, DK), whole),
                (shaped(DK, BF16), (seg_len, DK), whole),
                (shaped(DV, BF16), (seg_len, DV), whole),
                (shaped(DV, BF16, DK), (DK, DV), whole),
                (shaped(gate_count * DK, BF16), (seg_len, gate_count * DK), whole),
            ]
            + ([(shaped(DK, BF16), (seg_len, DK), whole)] if "xv" in roles[h] else []),
            [pltpu.VMEM((seg_len, 2 * DK), F32)],
            2 * seg_len * width * len(roles[h]) * DK,
        )
        extra_v = extra[0] if extra else None
        (state_in,) = exchange_states([h], [total], False)[0]
        if h + 1 < local_heads:
            slots[h + 1], state_in, *later[:] = tie(slots[h + 1], state_in, *later)
        heads_kept.append((weights, q, k, v, gates, state_in))

    def columns(v, c, order):
        return (v, unit_block, lambda n, c=c: (order(n)[0], c))

    if balanced:
        gates0, gates1 = heads_kept[0][4], heads_kept[1][4]
        swapped = swap(jnp.where(low, gates1, gates0[:, :DK]), 2)

        def gate_operands(h, order):
            if h == 0:
                four = (gates0, 0), (gates0, 1), (swapped, 0), (gates0, 2)
            else:
                four = (gates0, 1), (gates1, 0), (gates0, 2), (swapped, 0)
            return [columns(v, c, order) for v, c in four]

    else:

        def gate_operands(h, order):
            return [columns(heads_kept[h][4], c, order) for c in (0, 0, 1, 1)]

    kept = []
    for h in range(local_heads):
        weights, q, k, v, gates, state_in = heads_kept[h]
        hidden, mixed, retained = head_call(
            retain_kernel,
            blocks,
            [
                params[h],
                (q, unit_block, ahead),
                (k, unit_block, ahead),
                (v, v_block, ahead),
                *gate_operands(h, ahead),
                (masks[h], (blk, blk), whole),
                (q_decays[h], (blk, 1), whole),
                (k_decays[h], (blk, 1), whole),
                (state_in, (DK, DV), whole),
            ],
            [
                (shaped(DV, BF16), v_block, ahead),
                (shaped(DV, BF16), v_block, ahead),
                (shaped(1, F32), (blk, 1), ahead),
            ],
            state_scratch,
            ret_flops,
        )
        kept.append((retained, mixed, hidden))
    hidden = jnp.concatenate([t[-1] for t in kept], axis=1)
    w_ffn_in, w_ffn_out = (gather_shard(t) for t in later)

    resid = xf + add_blocks(*send_blocks(seq_rows(dot_nt(hidden, w_out, BF16))))
    normed2 = gather_near(rms_scale(resid, gain_ffn).astype(BF16))
    proj2 = dot_nt(normed2, w_ffn_in)
    first, second = proj2[:, :inner_cols], proj2[:, inner_cols:]
    inner2 = gated_gelu(first, second).astype(BF16)

    g_ffn_out, d_ffn = tie(dot_tn(d_ffn, inner2, BF16), d_ffn)
    scattered = {"ffn_out": reduce_shard(g_ffn_out)}
    d_inner2 = dot_nn(d_ffn, w_ffn_out)
    ignored2, gelu_back = jax.vjp(gated_gelu, first, second)
    d_first, d_second = gelu_back(d_inner2)
    dproj2 = jnp.concatenate([d_first, d_second], axis=1).astype(BF16)
    d_normed2 = dot_nn(dproj2, w_ffn_in, BF16)
    g_ffn_in = dot_tn(dproj2, normed2, BF16)
    if group == 4:
        terms, ra, rb = first_step(near_rows(d_normed2))
        ra, rb, g_ffn_in = tie(ra, rb, g_ffn_in)
        d_normed2 = second_step(terms, ra, rb)
    else:
        d_normed2 = add_blocks(*send_blocks(near_rows(d_normed2)))
    scattered["ffn_in"] = reduce_shard(g_ffn_in)
    ignored3, norm2_back = jax.vjp(rms_scale, resid, gain_ffn)
    d_resid_part, d_gain_ffn = norm2_back(d_normed2)
    d_resid = cotangent.astype(F32) + d_resid_part
    (d_attn,) = tie(d_resid.astype(BF16))
    d_attn = gather_seq(d_attn)
    d_attn, scattered["ffn_out"] = tie(d_attn, scattered["ffn_out"])
    parts_ffn_out = spread(scattered["ffn_out"])

    def tie_parts(v, parts):
        flat = tie(v, *(piece for part in parts for piece in part))
        rest = list(flat[1:])
        return flat[0], [tuple(rest.pop(0) for _ in part) for part in parts]

    all_params = (
        jnp.concatenate([jnp.stack([jnp.float32(0.0), low.astype(F32)]), block_decays]),
        None,
        None,
    )
    outs = head_call(
        functools.partial(gate_back_kernel, local_heads),
        blocks,
        [
            all_params,
            (d_attn, (blk, width), behind),
            (w_out, (width, vcols), whole),
        ]
        + [
            t
            for h in range(local_heads)
            for t in (
                *gate_operands(h, behind),
                (kept[h][1], v_block, behind),
                (kept[h][0], (blk, 1), behind),
                (heads_kept[h][1], unit_block, behind),
                (q_decays[h], (blk, 1), whole),
            )
        ],
        [
            (shaped(DV, BF16), v_block, behind),
            (shaped(DV, BF16), v_block, behind),
            (shaped(DV, BF16, DK), (DK, DV), whole),
        ]
        * local_heads,
        state_scratch * local_heads,
        2 * seg_len * (DK * DV * local_heads + width * vcols),
    )
    d_gates, d_outs, totals = outs[0::3], outs[1::3], outs[2::3]
    if balanced:
        d_swapped = swap(jnp.where(low, d_gates[0][:, DK:], d_gates[1][:, DK:]), 2)
    else:
        d_swapped = totals[0]
    hidden, totals[0] = tie(hidden, totals[0])
    g_mixer_out = dot_tn(d_attn, hidden, BF16)
    totals[0], d_swapped, g_mixer_out = tie(totals[0], d_swapped, g_mixer_out)
    d_outs[0], g_mixer_out = tie(d_outs[0], g_mixer_out)
    scattered["mixer_out"] = reduce_shard(g_mixer_out)
    if balanced:
        d_gate_pairs = [
            [
                ((d_gates[0], 0), (d_swapped, 0)),
                ((d_gates[1], 0), (d_gates[0], 0)),
                ((d_gates[1], 1), (d_gates[0], 1)),
            ],
            [((d_swapped, 0), (d_gates[1], 0))],
        ]
    else:
        d_gate_pairs = [[((t, 0), (t, 0)), ((t, 1), (t, 1))] for t in d_gates]
    inners = head_call(
        functools.partial(inner_back_kernel, roles),
        blocks,
        [all_params, (cosine, half_block, ahead), (sine, half_block, ahead)]
        + [
            t
            for h in range(local_heads)
            for t in (
                (heads_kept[h][1], unit_block, ahead),
                (heads_kept[h][2], unit_block, ahead),
                (heads_kept[h][3], v_block, ahead),
                (d_outs[h], v_block, ahead),
                (masks[h], (blk, blk), whole),
                (q_decays[h], (blk, 1), whole),
                (k_decays[h], (blk, 1), whole),
                (heads_kept[h][5], (DK, DV), whole),
                *(columns(v, c, ahead) for pair in d_gate_pairs[h] for v, c in pair),
            )
        ],
        [
            t
            for h in range(local_heads)
            for t in (
                (
                    shaped((1 + len(d_gate_pairs[h])) * DK, BF16),
                    (blk, (1 + len(d_gate_pairs[h])) * DK),
                    ahead,
                ),
                (shaped(DK, F32), unit_block, ahead),
                (shaped(DV, F32), v_block, ahead),
            )
        ],
        state_scratch * local_heads,
        ret_flops,
    )
    grads_out, inner2, scattered["ffn_in"], *inners = exchange_states(
        range(local_heads), totals, True, (inner2, scattered["ffn_in"], *inners)
    )
    parts_ffn_in = spread(scattered["ffn_in"])
    near = jnp.arange(group)
    earlies = inners[0::3]
    g_units = [
        unit_rows(earlies[h], normed, len(roles[h]), False) for h in range(local_heads)
    ]
    ffn_terms, *flat = tie(dot_nt(inner2, w_ffn_out, BF16), *grads_out, *g_units)
    grads_out, g_units = flat[:local_heads], flat[local_heads:]
    lates = head_call(
        functools.partial(outer_back_kernel, roles),
        blocks,
        [all_params, (cosine, half_block, behind), (sine, half_block, behind)]
        + [
            t
            for h in range(local_heads)
            for t in (
                (heads_kept[h][1], unit_block, behind),
                (heads_kept[h][2], unit_block, behind),
                (heads_kept[h][3], v_block, behind),
                (d_outs[h], v_block, behind),
                (inners[3 * h + 1], unit_block, behind),
                (inners[3 * h + 2], v_block, behind),
                (q_decays[h], (blk, 1), whole),
                (k_decays[h], (blk, 1), whole),
                (grads_out[h], (DK, DV), whole),
            )
        ],
        [
            (
                shaped(len(t) * DK - e.shape[1], BF16),
                (blk, len(t) * DK - e.shape[1]),
                behind,
            )
            for t, e in zip(roles, earlies)
        ],
        state_scratch * local_heads,
        seg_len * DK * DV,
    )

    if group == 4:
        late = first_step(near_rows(ffn_terms))
    else:
        late = send_blocks(near_rows(ffn_terms))
    lates[0], parts_ffn_in[:3] = tie_parts(lates[0], parts_ffn_in[:3])
    lates[0], parts_ffn_out = tie_parts(lates[0], parts_ffn_out)
    g_units[0] = unit_rows(lates[0], normed, len(roles[0]), True, g_units[0])
    joined = [t for pair in zip(earlies, lates) for t in pair]
    joined[0], g_units[0] = tie(joined[0], g_units[0])
    joined[0], scattered["mixer_out"] = tie(joined[0], scattered["mixer_out"])
    tile = 512
    operands = []
    for h in range(local_heads):
        weights = heads_kept[h][0]
        operands += [(t, t.shape, whole) for t in joined[2 * h : 2 * h + 2]]
        operands.append((weights, (weights.shape[0], tile), lambda n: (0, n)))
    (d_normed,) = head_call(
        functools.partial(join_kernel, local_heads),
        width // tile,
        operands,
        [(shaped(width, BF16), (seg_len, tile), lambda n: (0, n))],
        [],
        seg_len * width,
    )
    d_normed, parts_ffn_in = tie_parts(d_normed, parts_ffn_in)
    if group == 4:
        ffn_own, ra, rb = late
        d_normed, ra, rb = tie(d_normed, ra, rb)
        first = first_step(seq_rows(d_normed))
        output = (resid + second_step(ffn_own, ra, rb)).astype(BF16)
    else:
        output = (resid + add_blocks(*late)).astype(BF16)
    parts_mixer_out = spread(scattered["mixer_out"])
    for h in range(1, local_heads):
        lates[h], d_normed = tie(lates[h], d_normed)
        g_units[h] = unit_rows(lates[h], normed, len(roles[h]), True, g_units[h])
    g_ffn_in = place_blocks(
        parts_ffn_in, s ^ near, near, ffn_in.shape, (sub, width), lambda o, n: (n, 0)
    )
    if group == 4:
        own, ra, rb = first
        ra, rb, g_units[-1], g_ffn_in = tie(ra, rb, g_units[-1], g_ffn_in)
        d_normed = second_step(own, ra, rb)
    else:
        d_normed = add_blocks(*send_blocks(seq_rows(d_normed)))
    g_slots = []
    for h in range(local_heads):
        if not balanced:
            cut = g_units[h].reshape(-1, DK, width)
            g_units[h] = jnp.concatenate(
                [pick(cut, jnp.maximum(held[h, c, s], 0)) for c in range(segments)], axis=0
            )
        g_slots.append(reduce_shard(g_units[h]))

    ignored8, norm1_back = jax.vjp(rms_scale, xf, gain_attn)
    d_x_part, d_gain_attn = norm1_back(d_normed)
    input_grad = (d_resid + d_x_part).astype(BF16)
    gains = lax.all_to_all(
        jnp.broadcast_to(jnp.concatenate([d_gain_attn, d_gain_ffn])[None], (segments, 2 * width)),
        "shard",
        split_axis=0,
        concat_axis=0,
        tiled=True,
    )
    gains = jnp.sum(gains, axis=0, keepdims=True)
    parts = []
    for h in range(local_heads):
        last = h == local_heads - 1
        beside = None
        if h == 0:
            g_slots[h], input_grad = tie(g_slots[h], input_grad)
            g_slots[h], parts_mixer_out = tie_parts(g_slots[h], parts_mixer_out)
            g_mixer_out = place_blocks(
                parts_mixer_out,
                s ^ near,
                near,
                mixer_out.shape,
                (mixer_out.shape[0], DV),
                lambda o, n: (0, o * group + n),
                outer=local_heads,
            )
            if sub % 128 == 0:
                g_ffn_out = place_blocks(
                    parts_ffn_out,
                    s ^ near,
                    near,
                    ffn_out.shape,
                    (ffn_out.shape[0], sub),
                    lambda o, n: (0, o * group + n),
                    outer=segments // 2,
                )
            else:
                g_ffn_out = jnp.transpose(
                    ordered(parts_ffn_out).reshape(group, ffn_out.shape[0], segments // 2, sub),
                    (1, 2, 0, 3),
                ).reshape(ffn_out.shape).astype(F32)
            beside = [g_mixer_out, output, gains, g_ffn_out]
        if last and h > 0:
            g_slots[h], gains, g_mixer_out = tie(g_slots[h], gains, g_mixer_out)
            beside = []
            g_slots[h], parts = tie_parts(g_slots[h], parts)
        here = spread(g_slots[h], beside)
        if group == 4 and h == 0:
            g_mixer_out, output, gains, g_ffn_out = beside
        if last:
            if beside is not None and group == 4:
                here[1], gains = tie(here[1], gains)
                gains = gains + swap(gains, 1)
                here[3], gains = tie(here[3], gains)
                gains = gains + swap(gains, 2)
            else:
                step = 1
                while step < group:
                    gains = gains + swap(gains, step)
                    step *= 2
        if balanced and last:
            there = [tuple(cross(piece, 1) for piece in part) for part in here]
            parts += [a + b for a, b in zip(here, there)] + [b + a for a, b in zip(here, there)]
        else:
            lend_here = lend[j] if balanced else lend[h, j]
            stack = jnp.stack([jnp.concatenate(part, axis=0) for part in here])
            parts += here + [
                (cross(pick(stack, s ^ lend_here[n]), 1),) for n in range(lend_here.shape[0])
            ]
    gain_attn_grad, gain_ffn_grad = gains[0, :width], gains[0, width:]
    found = back[j]
    if balanced:
        spare = lend.shape[-1]
        source = jnp.where(
            found[:, 0] == 0,
            s ^ found[:, 1],
            jnp.where(
                found[:, 0] == 1,
                group + found[:, 1],
                group + spare + core * group + (s ^ found[:, 1]),
            ),
        )
    else:
        source = found[:, 0] * (group + lend.shape[-1]) + jnp.where(
            found[:, 2] < 0, s ^ found[:, 1], group + found[:, 2]
        )
    g_mixer_in = place_blocks(
        parts,
        jnp.arange(source.shape[0]),
        source,
        mixer_in.shape,
        (DK, width),
        lambda o, n: (n, 0),
    )
    return (
        output,
        input_grad,
        gain_attn_grad,
        gain_ffn_grad,
        g_mixer_in,
        g_mixer_out,
        g_ffn_in,
        g_ffn_out,
    )


def solution(mesh):
    return jax.shard_map(
        local,
        mesh=mesh,
        in_specs=(
            P(("shard", "seq"), None),
            P(("shard", "seq"), None),
            P(),
            P(),
            P("shard", None),
            P("shard", None),
            P("shard", None),
            P("shard", None),
            P(),
            P(),
        ),
        out_specs=(
            P(("shard", "seq"), None),
            P(("shard", "seq"), None),
            P(),
            P(),
            P("shard", None),
            P("shard", None),
            P("shard", None),
            P("shard", None),
        ),
        check_vma=False,
    )
```

```python
import functools

import jax
import jax.numpy as jnp
import numpy as np
from jax import lax
from jax.experimental import pallas as pl
from jax.experimental.pallas import tpu as pltpu
from jax.sharding import PartitionSpec as P

DK = 256
DV = 512
FF = 4096
QK = 2048
V = 4096


EPS_NORM = 1e-06
EPS_GROUP = 1e-05

F32 = jnp.float32
BF16 = jnp.bfloat16


def dot_nt(left, right, kind=F32):
    return lax.dot_general(
        left, right, (((1,), (1,)), ((), ())), preferred_element_type=F32
    ).astype(kind)


def dot_nn(left, right, kind=F32):
    return lax.dot_general(
        left, right, (((1,), (0,)), ((), ())), preferred_element_type=F32
    ).astype(kind)


def dot_tn(left, right, kind=F32):
    return lax.dot_general(
        left, right, (((0,), (0,)), ((), ())), preferred_element_type=F32
    ).astype(kind)


def rms_scale(v, gain):
    return v * lax.rsqrt(jnp.mean(v * v, axis=-1, keepdims=True) + EPS_NORM) * gain


def gated_gelu(first, second):
    return jax.nn.gelu(first) * second


def unit_owners(heads):
    owners = [(n, 0) for n in range(heads)] + [(n, 1) for n in range(heads)]
    for base in (2, 4):
        owners += [(n, base + half) for n in range(heads) for half in range(2)]
    return owners


def balanced_tables():
    group, segments, per_shard = 4, 8, 6
    number = {owner: u for u, owner in enumerate(unit_owners(8))}
    keep = np.full((2, segments, group), -1, np.int32)
    give = np.zeros((2, segments, group), np.int32)
    back = np.zeros((segments, per_shard, 2), np.int32)
    lend = [[] for _ in range(segments)]
    seen = set()
    for s in range(group):
        a, b = s, s + 4
        if s < 2:
            gates = [(a, 4), (b, 4), (b, 5)], (b + 2, 5)
        else:
            gates = [(a - 2, 5), (a, 4), (a, 5)], (b, 4)
        first = [(a, 0), (a, 1), (a, 2), (a, 3), (b, 2)] + gates[0]
        second = [(b, 0), (b, 1), (b, 3), gates[1]]
        for slot, owner in enumerate(first):
            home, index = divmod(number[owner], per_shard)
            seen.add(number[owner])
            assert home // 2 == slot // 2
            if home == slot:
                keep[0, slot, s] = index
                back[home, index] = (0, s)
            else:
                give[0, home, s] = index
                back[home, index] = (1, len(lend[slot]))
                lend[slot].append(s)
        for chip, owner in enumerate(second):
            home, index = divmod(number[owner], per_shard)
            seen.add(number[owner])
            assert home // 2 == chip
            keep[1, home, s] = index
            give[1, home, s] = index
            back[home, index] = (2, s)
    assert len(seen) == segments * per_shard
    most = max(len(t) for t in lend)
    return keep, give, back, np.asarray([(t + [0] * most)[:most] for t in lend], np.int32)


def unit_tables(group, local_heads, segments):
    heads = group * local_heads
    owners = unit_owners(heads)
    per_shard = len(owners) // segments
    keep = np.full((local_heads, segments, group), -1, np.int32)
    give = np.zeros((local_heads, segments, group), np.int32)
    place = np.zeros((local_heads, group, 6), np.int32)
    held = np.full((local_heads, segments, group), -1, np.int32)
    slot_of = {}
    for chip in range(segments // 2):
        for head in range(heads):
            h, s = divmod(head, group)
            span = range(2 * per_shard * chip, 2 * per_shard * (chip + 1))
            mine = [u for u in span if owners[u][0] == head]
            assert len(mine) <= 2
            for n, u in enumerate(mine):
                home = u // per_shard
                slot = home if len(mine) == 1 else 2 * chip + n
                if slot == home:
                    keep[h, slot, s] = u % per_shard
                else:
                    give[h, home, s] = u % per_shard
                place[h, s, owners[u][1]] = slot
                held[h, slot, s] = owners[u][1]
                slot_of[u] = slot
    lends = [[[] for _ in range(segments)] for _ in range(local_heads)]
    back = np.zeros((segments, per_shard, 3), np.int32)
    for u, (head, _) in enumerate(owners):
        home = u // per_shard
        h, s = divmod(head, group)
        back[home, u % per_shard] = (h, s, -1)
        if slot_of[u] != home:
            assert slot_of[u] == home ^ 1
            back[home, u % per_shard, 2] = len(lends[h][home ^ 1])
            lends[h][home ^ 1].append(s)
    most = max(1, max(len(t) for row in lends for t in row))
    lend = np.asarray(
        [[(t + [0] * most)[:most] for t in row] for row in lends], np.int32
    )
    return keep, give, place, held, back, lend


def tie(*values):
    return lax.optimization_barrier(values)


def mm(left, right, dims):
    return lax.dot_general(left, right, (dims, ((), ())), preferred_element_type=F32)


NN = ((1,), (0,))
NT = ((1,), (1,))
TN = ((0,), (0,))


def turn(v, cosine, sine):
    half = v.shape[-1] // 2
    first, second = v[:, :half], v[:, half:]
    return jnp.concatenate(
        [first * cosine - second * sine, second * cosine + first * sine], axis=-1
    )


def scaled(v, decay):
    return (v.astype(F32) * decay).astype(BF16)


def project_kernel(blk, roles, carried, params, x, w, cosine, sine, k_decay, *refs):
    if carried:
        v_a, *refs = refs
    q, k, v, total, gates, *rest = refs
    y = rest[-1]
    rows = y.shape[0]
    y[...] = mm(x[...], w[...], NT)

    def put(role, part, gate_at):
        value = y[:, part * DK : (part + 1) * DK]
        if role == "q":
            q[...] = turn(value, cosine[...], sine[...]).astype(BF16)
        elif role == "k":
            k[...] = turn(value, cosine[...], sine[...]).astype(BF16)
        elif role == "va":
            v[:, :DK] = value.astype(BF16)
        elif role == "vb":
            v[:, DK:] = value.astype(BF16)
        elif role == "xv":
            rest[0][...] = value.astype(BF16)
        else:
            gates[:, gate_at * DK : (gate_at + 1) * DK] = value.astype(BF16)

    for step in range(len(roles) // 2):

        @pl.when(pl.program_id(0) == step)
        def _(step=step):
            for part in range(2):
                at = 2 * step + part
                put(roles[at], part, roles[:at].count("g"))
            if step == 1:
                if carried:
                    v[:, :DK] = v_a[...]
                state = jnp.zeros(total.shape, F32)
                for r in range(0, rows, blk):
                    kd = scaled(k[r : r + blk, :], k_decay[...])
                    state = params[0] * state + mm(kd, v[r : r + blk, :], TN)
                total[...] = state.astype(BF16)


def join_kernel(count, *refs):
    out = refs[-1]
    total = None
    for n in range(count):
        early, late, weights = refs[3 * n : 3 * n + 3]
        middle = DK + late.shape[1]
        part = mm(early[:, :DK], weights[:DK, :], NN)
        part += mm(early[:, DK:], weights[middle:, :], NN)
        part += mm(late[...], weights[DK:middle, :], NN)
        total = part if total is None else total + part
    out[...] = total.astype(out.dtype)


def select(params, low, high):
    return jnp.where(params[1] > 0.5, low[...].astype(F32), high[...].astype(F32))


def retain_kernel(
    params, q, k, v, low_a, high_a, low_b, high_b, mask, q_decay, k_decay, start,
    hidden, mixed, kept, state,
):
    @pl.when(pl.program_id(0) == 0)
    def _():
        state[...] = start[...].astype(F32)

    weights = (mm(q[...], k[...], NT) * mask[...]).astype(BF16)
    o = mm(weights, v[...], NN)
    o += mm(scaled(q[...], q_decay[...]), state[...].astype(BF16), NN)
    state[...] = params[0] * state[...] + mm(scaled(k[...], k_decay[...]), v[...], TN)
    o = o - jnp.mean(o, axis=-1, keepdims=True)
    inverse = lax.rsqrt(jnp.mean(o * o, axis=-1, keepdims=True) + EPS_GROUP)
    kept[...] = inverse
    low = (o * inverse).astype(BF16)
    mixed[...] = low
    for n, (one, two) in enumerate(((low_a, high_a), (low_b, high_b))):
        columns = slice(n * DK, (n + 1) * DK)
        g = select(params, one, two)
        hidden[:, columns] = (g * jax.nn.sigmoid(g) * low[:, columns].astype(F32)).astype(BF16)


def take(refs, counts):
    pieces, at = [], 0
    for count in counts:
        pieces.append(refs[at : at + count])
        at += count
    return pieces


def gate_back_kernel(heads, params, d_attn, w_out, *refs):
    inputs = take(refs, [8] * heads)
    outputs = take(refs[8 * heads :], [3] * heads)
    states = refs[11 * heads :]

    @pl.when(pl.program_id(0) == 0)
    def _():
        for state in states:
            state[...] = jnp.zeros(state.shape, F32)

    d_hidden = mm(d_attn[...], w_out[...], NN)
    for h in range(heads):
        low_a, high_a, low_b, high_b, mixed, inverse, q, q_decay = inputs[h]
        d_gate, d_out, total = outputs[h]
        g = jnp.concatenate(
            [select(params, low_a, high_a), select(params, low_b, high_b)], axis=1
        )
        dh = d_hidden[:, h * DV : (h + 1) * DV]
        sig = jax.nn.sigmoid(g)
        o = mixed[...].astype(F32)
        d_gate[...] = (dh * o * (sig * (1.0 + g * (1.0 - sig)))).astype(BF16)
        dy = (dh * (g * sig)).astype(BF16).astype(F32)
        do = inverse[...] * (
            dy
            - jnp.mean(dy, axis=-1, keepdims=True)
            - o * jnp.mean(dy * o, axis=-1, keepdims=True)
        )
        do = do.astype(BF16)
        d_out[...] = do
        state = states[h]
        state[...] = params[2 + h] * state[...] + mm(scaled(q[...], q_decay[...]), do, TN)
        total[...] = state[...].astype(BF16)


def inner_back_kernel(roles, params, cosine, sine, *refs):
    heads = len(roles)
    counts = [8 + 2 * t.count("g") for t in roles]
    inputs = take(refs, counts)
    outputs = take(refs[sum(counts) :], [3] * heads)
    states = refs[sum(counts) + 3 * heads :]

    @pl.when(pl.program_id(0) == 0)
    def _():
        for h in range(heads):
            states[h][...] = inputs[h][7][...].astype(F32)

    for h in range(heads):
        q, k, v, d_out, mask, q_decay, k_decay, ignored, *gates = inputs[h]
        early, d_k, d_v = outputs[h]
        state = states[h]
        do = d_out[...]
        weights = (mm(q[...], k[...], NT) * mask[...]).astype(BF16)
        d_v[...] = mm(weights, do, TN)
        d_scores = mm(do, v[...], NT).astype(BF16).astype(F32)
        d_scores = (d_scores * mask[...]).astype(BF16)
        d_k[...] = mm(d_scores, q[...], TN)
        far = mm(do, state[...].astype(BF16), NT).astype(BF16).astype(F32)
        dq = mm(d_scores, k[...], NN) + far * q_decay[...]
        dq = dq.astype(BF16).astype(F32)
        early[:, :DK] = turn(dq, cosine[...], -sine[...]).astype(BF16)
        for n in range(len(gates) // 2):
            value = select(params, gates[2 * n], gates[2 * n + 1]).astype(BF16)
            early[:, (n + 1) * DK : (n + 2) * DK] = value
        state[...] = params[2 + h] * state[...] + mm(scaled(k[...], k_decay[...]), v[...], TN)


def outer_back_kernel(roles, params, cosine, sine, *refs):
    heads = len(roles)
    inputs = take(refs, [9] * heads)
    outputs = refs[9 * heads : 10 * heads]
    states = refs[10 * heads :]

    @pl.when(pl.program_id(0) == 0)
    def _():
        for h in range(heads):
            states[h][...] = inputs[h][8][...].astype(F32)

    other = None
    for h in reversed(range(heads)):
        q, k, v, d_out, d_k, d_v, q_decay, k_decay, ignored = inputs[h]
        state = states[h]
        low = state[...].astype(BF16)
        far = mm(v[...], low, NT).astype(BF16).astype(F32)
        dk = (d_k[...] + far * k_decay[...]).astype(BF16).astype(F32)
        dk = turn(dk, cosine[...], -sine[...]).astype(BF16)
        dv = (d_v[...] + mm(scaled(k[...], k_decay[...]), low, NN)).astype(BF16)
        values = {"k": dk, "va": dv[:, :DK], "vb": dv[:, DK:], "xv": other}
        for n, role in enumerate(t for t in roles[h] if t in values):
            outputs[h][:, n * DK : (n + 1) * DK] = values[role]
        other = dv[:, :DK]
        state[...] = params[2 + h] * state[...] + mm(scaled(q[...], q_decay[...]), d_out[...], TN)


def unit_kernel(x, normed, *refs):
    refs[-1][...] = mm(x[...], normed[...], TN).astype(BF16)


def unit_rows(x, normed, count, late, into=None):
    rows, width = normed.shape
    units = x.shape[1] // DK

    def where(n):
        return (n + 1, 0) if late else (jnp.where(n == 0, 0, n + count - units), 0)

    arrays = [x, normed] + ([] if into is None else [into])
    return pl.pallas_call(
        unit_kernel,
        grid=(units,),
        in_specs=[
            pl.BlockSpec((rows, DK), lambda n: (0, n)),
            pl.BlockSpec((rows, width), lambda n: (0, 0)),
        ]
        + ([] if into is None else [pl.BlockSpec(memory_space=pl.ANY)]),
        out_specs=pl.BlockSpec((DK, width), where),
        out_shape=jax.ShapeDtypeStruct((count * DK, width), BF16),
        input_output_aliases={} if into is None else {2: 0},
        compiler_params=pltpu.CompilerParams(vmem_limit_bytes=48 * 2**20),
        cost_estimate=pl.CostEstimate(
            flops=rows * width * DK, bytes_accessed=rows * width, transcendentals=0
        ),
    )(*arrays)


def head_call(kernel, grid, operands, outputs, scratch, flops, size=None):
    arrays = [t[0] for t in operands]
    if size is None:
        size = sum(t.size * t.dtype.itemsize for t in arrays + [t[0] for t in outputs])
    call = pl.pallas_call(
        kernel,
        grid=(grid,),
        in_specs=[
            pl.BlockSpec(memory_space=pltpu.SMEM) if block is None else pl.BlockSpec(block, where)
            for _, block, where in operands
        ],
        out_specs=[pl.BlockSpec(block, where) for _, block, where in outputs],
        scratch_shapes=scratch,
        out_shape=[t[0] for t in outputs],
        compiler_params=pltpu.CompilerParams(vmem_limit_bytes=56 * 2**20),
        cost_estimate=pl.CostEstimate(flops=flops, bytes_accessed=size, transcendentals=0),
    )
    return list(call(*arrays))


def place_kernel(parts, target, source, *refs):
    out = refs[-1]
    code = source[pl.program_id(1)]
    for i, part in enumerate(parts):

        @pl.when(code == i)
        def _(part=part):
            row = 0
            for n in part:
                piece = refs[n]
                out[row : row + piece.shape[0], :] = piece[...].astype(F32)
                row += piece.shape[0]


def place_blocks(parts, target, source, shape, block, where, outer=1):
    flat, index = [], []
    for part in parts:
        for piece in part:
            if not any(piece is t for t in flat):
                flat.append(piece)
        index.append([next(n for n, t in enumerate(flat) if t is piece) for piece in part])
    return pl.pallas_call(
        functools.partial(place_kernel, index),
        grid_spec=pltpu.PrefetchScalarGridSpec(
            num_scalar_prefetch=2,
            grid=(outer, target.shape[0]),
            in_specs=[
                pl.BlockSpec((t.shape[0], t.shape[1] // outer), lambda o, n, target, source: (0, o))
                for t in flat
            ],
            out_specs=pl.BlockSpec(block, lambda o, n, target, source: where(o, target[n])),
        ),
        out_shape=jax.ShapeDtypeStruct(shape, F32),
        compiler_params=pltpu.CompilerParams(vmem_limit_bytes=48 * 2**20),
    )(target.astype(jnp.int32), source.astype(jnp.int32), *flat)


def local(
    tokens,
    cotangent,
    gain_attn,
    gain_ffn,
    mixer_in,
    mixer_out,
    ffn_in,
    ffn_out,
    segment_order,
    decay_index,
):
    rows, width = tokens.shape
    group = lax.axis_size("seq")
    segments = lax.axis_size("shard")
    heads = decay_index.shape[0]
    local_heads = heads // group
    seg_len = rows * group
    blk = min(512, seg_len)
    blocks = seg_len // blk
    vcols = local_heads * DV
    s = lax.axis_index("seq")
    j = lax.axis_index("shard")

    def swap(v, d):
        return lax.ppermute(v, "seq", [(i, i ^ d) for i in range(group)])

    def cross(v, d):
        return lax.ppermute(v, "shard", [(i, i ^ d) for i in range(segments)])

    def pick(v, i):
        return lax.dynamic_index_in_dim(v, i, 0, keepdims=False)

    def spread(v, beside=None):
        if group == 4:
            h = v.shape[0] // 2
            r1 = swap(v, 1)
            r2 = swap(v, 2)
            if beside:
                r1, r2, beside[:] = tie(r1, r2, list(beside))
            return [(v,), (r1,), (r2,), (swap(r1[:h], 2), swap(r2[h:], 1))]
        return [(v,)] + [(swap(v, d),) for d in range(1, group)]

    def ordered(parts):
        r = parts[0][0].shape[0]
        out = jnp.zeros((group * r,) + parts[0][0].shape[1:], parts[0][0].dtype)
        for d, part in enumerate(parts):
            row = (s ^ d) * r
            for piece in part:
                out = lax.dynamic_update_slice_in_dim(out, piece, row, 0)
                row = row + piece.shape[0]
        return out

    def gather_seq(v):
        return ordered(spread(v))

    def first_step(blk_of):
        b = [blk_of(d) for d in range(4)]
        h = b[0].shape[0] // 2
        sa = jnp.concatenate([b[1][:h], b[3][:h]], axis=0)
        sb = jnp.concatenate([b[2][h:], b[3][h:]], axis=0)
        sa, sb = tie(sa, sb)
        return b, swap(sa, 1), swap(sb, 2)

    def second_step(b, ra, rb):
        h = b[0].shape[0] // 2
        ra, rb = ra.astype(F32), rb.astype(F32)
        qa = (b[2][:h].astype(F32) + ra[h:]).astype(BF16)
        qb = (b[1][h:].astype(F32) + rb[h:]).astype(BF16)
        qa, qb = tie(qa, qb)
        qa, qb = swap(qa, 2), swap(qb, 1)
        top = b[0][:h].astype(F32) + ra[:h] + qa.astype(F32)
        return jnp.concatenate([top, b[0][h:].astype(F32) + rb[:h] + qb.astype(F32)], axis=0)

    def send_blocks(blk_of):
        sent = tie(*(blk_of(d) for d in range(group)))
        return sent[0], [swap(sent[d], d) for d in range(group - 1, 0, -1)]

    def exchange_rows(v):
        got = lax.all_to_all(
            v.reshape(group, rows, width), "seq", split_axis=0, concat_axis=0, tiled=True
        )
        return got

    def add_rows(got):
        return jnp.sum(got.astype(F32), axis=0)

    def add_blocks(own, got):
        own = own.astype(F32)
        for t in got:
            own = own + t.astype(F32)
        return own

    def seq_rows(v):
        return lambda d: lax.dynamic_slice_in_dim(v, (s ^ d) * rows, rows, 0)

    def gather_shard(v):
        return lax.all_gather(v, "shard", axis=0, tiled=True)

    def reduce_shard(v):
        return lax.psum_scatter(v, "shard", scatter_dimension=0, tiled=True)

    balanced = group == 4 and local_heads == 2 and segments == 8
    units = mixer_in.reshape(-1, DK, width)
    if balanced:
        keep, give, back, lend = (jnp.asarray(t) for t in balanced_tables())
        core = j % 2
    else:
        keep, give, place, held, back, lend = (
            jnp.asarray(t) for t in unit_tables(group, local_heads, segments)
        )

    def offered(h):
        kept, given = keep[h, j, s], give[h, j, s]
        if balanced and h == 1:
            cut = mixer_in.reshape(-1, DK // 2, width)
            own = pick(cut, 2 * jnp.maximum(kept, 0) + core)
            given = cross(pick(cut, 2 * given + 1 - core), 1)
        else:
            own = pick(units, jnp.maximum(kept, 0))
            given = cross(pick(units, given), 1)
        return jnp.where(kept >= 0, own, given)

    sub = ffn_in.shape[0] // group
    ffn_out_cut = ffn_out.reshape(ffn_out.shape[0], segments // 2, group, sub)

    my_rank = jnp.sum(jnp.where(jnp.arange(segments) == j, segment_order, 0))
    all_logs = jnp.log1p(-jnp.exp2(-(5.0 + decay_index.astype(F32))))
    logs = lax.dynamic_index_in_dim(all_logs.reshape(local_heads, group), s, 1, keepdims=False)
    half = DK // 2
    inv_freq = jnp.exp(-jnp.log(10000.0) * jnp.arange(half).astype(F32) / half)
    positions = my_rank * seg_len + jnp.arange(seg_len, dtype=jnp.int32)
    angles = positions.astype(F32)[:, None] * inv_freq[None, :]
    cosine = jnp.cos(angles)
    sine = jnp.sin(angles)
    steps = jnp.arange(blk).astype(F32)
    gap = steps[:, None] - steps[None, :]
    masks = jnp.where(
        gap[None] >= 0.0, jnp.exp(jnp.maximum(gap, 0.0)[None] * logs[:, None, None]), 0.0
    )
    q_decays = jnp.exp((steps + 1.0)[None, :] * logs[:, None])[..., None]
    k_decays = jnp.exp((blk - 1.0 - steps)[None, :] * logs[:, None])[..., None]
    block_decays = jnp.exp(blk * logs)

    xf = tokens.astype(F32)
    normed = gather_seq(rms_scale(xf, gain_attn).astype(BF16))
    d_ffn = gather_seq(cotangent)
    slots = [gather_shard(offered(0))]
    slots[0], normed, d_ffn, cosine, sine, masks, q_decays, k_decays = tie(
        slots[0], normed, d_ffn, cosine, sine, masks, q_decays, k_decays
    )
    for h in range(1, local_heads):
        slots.append(gather_shard(offered(h)))
    mixer_out_cut = jnp.concatenate(
        [
            lax.dynamic_slice_in_dim(mixer_out, (h * group + s) * DV, DV, 1)
            for h in range(local_heads)
        ],
        axis=1,
    )
    mixer_out_cut, slots[0] = tie(mixer_out_cut, slots[0])
    w_out = gather_shard(mixer_out_cut)
    later = [
        lax.dynamic_slice_in_dim(ffn_in, s * sub, sub, 0),
        lax.dynamic_index_in_dim(ffn_out_cut, s, 2, keepdims=False).reshape(ffn_out.shape[0], -1),
    ]
    inner_cols = later[1].shape[1]

    ranks = segment_order
    piece = DK // segments

    def exchange_states(hs, totals, reverse, beside=()):
        cut = jnp.concatenate([t.reshape(segments, piece, DV) for t in totals], axis=1)
        got = lax.all_to_all(cut, "shard", split_axis=0, concat_axis=0, tiled=True)
        got, *beside = tie(got, *beside)
        apart = ranks[:, None] - ranks[None, :] - 1
        if reverse:
            apart = -apart - 2
        distance = apart.astype(F32)
        joined = []
        for n, h in enumerate(hs):
            coef = jnp.where(
                distance >= 0.0, jnp.exp(jnp.maximum(distance, 0.0) * seg_len * logs[h]), 0.0
            )
            part = got[:, n * piece : (n + 1) * piece].astype(F32)
            joined.append(jnp.sum(coef[..., None, None] * part[None], axis=1).astype(BF16))
        joined = jnp.concatenate(joined, axis=1)
        back_cut = lax.all_to_all(joined, "shard", split_axis=0, concat_axis=0, tiled=True)
        states = [
            back_cut[:, n * piece : (n + 1) * piece].reshape(DK, DV) for n in range(len(hs))
        ]
        return (states, *beside)

    def whole(n):
        return (0, 0)

    def ahead(n):
        return (n, 0)

    def behind(n):
        return (blocks - 1 - n, 0)

    def shaped(columns, kind, r=seg_len):
        return jax.ShapeDtypeStruct((r, columns), kind)

    state_scratch = [pltpu.VMEM((DK, DV), F32)]
    half_block = (blk, half)
    unit_block, v_block = (blk, DK), (blk, DV)
    ret_flops = 2 * seg_len * (DK + DV) * (blk + DK)
    low = s < group // 2
    if balanced:
        roles = [["q", "k", "va", "vb", "xv", "g", "g", "g"], ["q", "k", "vb", "g"]]
    else:
        roles = [["q", "k", "va", "vb", "g", "g"]] * local_heads
    params = [
        (jnp.stack([block_decays[h], low.astype(F32)]), None, None) for h in range(local_heads)
    ]
    heads_kept = []
    extra_v = None
    for h in range(local_heads):
        if balanced:
            weights = slots[h]
        else:
            cut = slots[h].reshape(-1, DK, width)
            weights = jnp.concatenate([pick(cut, place[h, s, c]) for c in range(6)], axis=0)
        carried = "va" not in roles[h]
        gate_count = roles[h].count("g")
        q, k, v, total, gates, *extra = head_call(
            functools.partial(project_kernel, blk, roles[h], carried),
            len(roles[h]) // 2,
            [
                params[h],
                (normed, (seg_len, width), whole),
                (weights, (2 * DK, width), ahead),
                (cosine, (seg_len, half), whole),
                (sine, (seg_len, half), whole),
                (k_decays[h], (blk, 1), whole),
            ]
            + ([(extra_v, (seg_len, DK), whole)] if carried else []),
            [
                (shaped(DK, BF16), (seg_len, DK), whole),
                (shaped(DK, BF16), (seg_len, DK), whole),
                (shaped(DV, BF16), (seg_len, DV), whole),
                (shaped(DV, BF16, DK), (DK, DV), whole),
                (shaped(gate_count * DK, BF16), (seg_len, gate_count * DK), whole),
            ]
            + ([(shaped(DK, BF16), (seg_len, DK), whole)] if "xv" in roles[h] else []),
            [pltpu.VMEM((seg_len, 2 * DK), F32)],
            2 * seg_len * width * len(roles[h]) * DK,
        )
        extra_v = extra[0] if extra else None
        (state_in,) = exchange_states([h], [total], False)[0]
        if h + 1 < local_heads:
            slots[h + 1], state_in, *later[:] = tie(slots[h + 1], state_in, *later)
        heads_kept.append((weights, q, k, v, gates, state_in))

    def columns(v, c, order):
        return (v, unit_block, lambda n, c=c: (order(n)[0], c))

    if balanced:
        gates0, gates1 = heads_kept[0][4], heads_kept[1][4]
        swapped = swap(jnp.where(low, gates1, gates0[:, :DK]), 2)

        def gate_operands(h, order):
            if h == 0:
                four = (gates0, 0), (gates0, 1), (swapped, 0), (gates0, 2)
            else:
                four = (gates0, 1), (gates1, 0), (gates0, 2), (swapped, 0)
            return [columns(v, c, order) for v, c in four]

    else:

        def gate_operands(h, order):
            return [columns(heads_kept[h][4], c, order) for c in (0, 0, 1, 1)]

    kept = []
    for h in range(local_heads):
        weights, q, k, v, gates, state_in = heads_kept[h]
        hidden, mixed, retained = head_call(
            retain_kernel,
            blocks,
            [
                params[h],
                (q, unit_block, ahead),
                (k, unit_block, ahead),
                (v, v_block, ahead),
                *gate_operands(h, ahead),
                (masks[h], (blk, blk), whole),
                (q_decays[h], (blk, 1), whole),
                (k_decays[h], (blk, 1), whole),
                (state_in, (DK, DV), whole),
            ],
            [
                (shaped(DV, BF16), v_block, ahead),
                (shaped(DV, BF16), v_block, ahead),
                (shaped(1, F32), (blk, 1), ahead),
            ],
            state_scratch,
            ret_flops,
        )
        kept.append((retained, mixed, hidden))
    hidden = jnp.concatenate([t[-1] for t in kept], axis=1)
    w_ffn_in, w_ffn_out = (gather_shard(t) for t in later)

    resid = xf + add_blocks(*send_blocks(seq_rows(dot_nt(hidden, w_out, BF16))))
    normed2 = gather_seq(rms_scale(resid, gain_ffn).astype(BF16))
    proj2 = dot_nt(normed2, w_ffn_in)
    first, second = proj2[:, :inner_cols], proj2[:, inner_cols:]
    inner2 = gated_gelu(first, second).astype(BF16)

    g_ffn_out, d_ffn = tie(dot_tn(d_ffn, inner2, BF16), d_ffn)
    scattered = {"ffn_out": reduce_shard(g_ffn_out)}
    d_inner2 = dot_nn(d_ffn, w_ffn_out)
    ignored2, gelu_back = jax.vjp(gated_gelu, first, second)
    d_first, d_second = gelu_back(d_inner2)
    dproj2 = jnp.concatenate([d_first, d_second], axis=1).astype(BF16)
    d_normed2 = dot_nn(dproj2, w_ffn_in, BF16)
    g_ffn_in = dot_tn(dproj2, normed2, BF16)
    if group == 4:
        terms, ra, rb = first_step(seq_rows(d_normed2))
        ra, rb, g_ffn_in = tie(ra, rb, g_ffn_in)
        d_normed2 = second_step(terms, ra, rb)
    else:
        d_normed2 = add_blocks(*send_blocks(seq_rows(d_normed2)))
    scattered["ffn_in"] = reduce_shard(g_ffn_in)
    ignored3, norm2_back = jax.vjp(rms_scale, resid, gain_ffn)
    d_resid_part, d_gain_ffn = norm2_back(d_normed2)
    d_resid = cotangent.astype(F32) + d_resid_part
    (d_attn,) = tie(d_resid.astype(BF16))
    d_attn = gather_seq(d_attn)
    d_attn, scattered["ffn_out"] = tie(d_attn, scattered["ffn_out"])
    parts_ffn_out = spread(scattered["ffn_out"])

    def tie_parts(v, parts):
        flat = tie(v, *(piece for part in parts for piece in part))
        rest = list(flat[1:])
        return flat[0], [tuple(rest.pop(0) for _ in part) for part in parts]

    all_params = (
        jnp.concatenate([jnp.stack([jnp.float32(0.0), low.astype(F32)]), block_decays]),
        None,
        None,
    )
    outs = head_call(
        functools.partial(gate_back_kernel, local_heads),
        blocks,
        [
            all_params,
            (d_attn, (blk, width), behind),
            (w_out, (width, vcols), whole),
        ]
        + [
            t
            for h in range(local_heads)
            for t in (
                *gate_operands(h, behind),
                (kept[h][1], v_block, behind),
                (kept[h][0], (blk, 1), behind),
                (heads_kept[h][1], unit_block, behind),
                (q_decays[h], (blk, 1), whole),
            )
        ],
        [
            (shaped(DV, BF16), v_block, behind),
            (shaped(DV, BF16), v_block, behind),
            (shaped(DV, BF16, DK), (DK, DV), whole),
        ]
        * local_heads,
        state_scratch * local_heads,
        2 * seg_len * (DK * DV * local_heads + width * vcols),
    )
    d_gates, d_outs, totals = outs[0::3], outs[1::3], outs[2::3]
    if balanced:
        d_swapped = jnp.where(low, d_gates[0][:, DK:], d_gates[1][:, DK:])
        d_swapped, parts_ffn_out[:3] = tie_parts(d_swapped, parts_ffn_out[:3])
        d_swapped = swap(d_swapped, 2)
    else:
        d_swapped = totals[0]
    hidden, totals[0] = tie(hidden, totals[0])
    g_mixer_out = dot_tn(d_attn, hidden, BF16)
    totals[0], d_swapped, g_mixer_out = tie(totals[0], d_swapped, g_mixer_out)
    d_outs[0], g_mixer_out = tie(d_outs[0], g_mixer_out)
    scattered["mixer_out"] = reduce_shard(g_mixer_out)
    if balanced:
        d_gate_pairs = [
            [
                ((d_gates[0], 0), (d_swapped, 0)),
                ((d_gates[1], 0), (d_gates[0], 0)),
                ((d_gates[1], 1), (d_gates[0], 1)),
            ],
            [((d_swapped, 0), (d_gates[1], 0))],
        ]
    else:
        d_gate_pairs = [[((t, 0), (t, 0)), ((t, 1), (t, 1))] for t in d_gates]
    inners = head_call(
        functools.partial(inner_back_kernel, roles),
        blocks,
        [all_params, (cosine, half_block, ahead), (sine, half_block, ahead)]
        + [
            t
            for h in range(local_heads)
            for t in (
                (heads_kept[h][1], unit_block, ahead),
                (heads_kept[h][2], unit_block, ahead),
                (heads_kept[h][3], v_block, ahead),
                (d_outs[h], v_block, ahead),
                (masks[h], (blk, blk), whole),
                (q_decays[h], (blk, 1), whole),
                (k_decays[h], (blk, 1), whole),
                (heads_kept[h][5], (DK, DV), whole),
                *(columns(v, c, ahead) for pair in d_gate_pairs[h] for v, c in pair),
            )
        ],
        [
            t
            for h in range(local_heads)
            for t in (
                (
                    shaped((1 + len(d_gate_pairs[h])) * DK, BF16),
                    (blk, (1 + len(d_gate_pairs[h])) * DK),
                    ahead,
                ),
                (shaped(DK, F32), unit_block, ahead),
                (shaped(DV, F32), v_block, ahead),
            )
        ],
        state_scratch * local_heads,
        ret_flops,
    )
    flat_ffn_out = [piece for part in parts_ffn_out for piece in part]
    grads_out, inner2, scattered["ffn_in"], *flat = exchange_states(
        range(local_heads), totals, True, (inner2, scattered["ffn_in"], *inners, *flat_ffn_out)
    )
    inners = flat[: 3 * local_heads]
    rest = flat[3 * local_heads :]
    parts_ffn_out = [tuple(rest.pop(0) for _ in part) for part in parts_ffn_out]
    parts_ffn_in = spread(scattered["ffn_in"])
    near = jnp.arange(group)
    earlies = inners[0::3]
    g_units = [
        unit_rows(earlies[h], normed, len(roles[h]), False) for h in range(local_heads)
    ]
    ffn_terms, *flat = tie(dot_nt(inner2, w_ffn_out, BF16), *grads_out, *g_units)
    grads_out, g_units = flat[:local_heads], flat[local_heads:]
    lates = head_call(
        functools.partial(outer_back_kernel, roles),
        blocks,
        [all_params, (cosine, half_block, behind), (sine, half_block, behind)]
        + [
            t
            for h in range(local_heads)
            for t in (
                (heads_kept[h][1], unit_block, behind),
                (heads_kept[h][2], unit_block, behind),
                (heads_kept[h][3], v_block, behind),
                (d_outs[h], v_block, behind),
                (inners[3 * h + 1], unit_block, behind),
                (inners[3 * h + 2], v_block, behind),
                (q_decays[h], (blk, 1), whole),
                (k_decays[h], (blk, 1), whole),
                (grads_out[h], (DK, DV), whole),
            )
        ],
        [
            (
                shaped(len(t) * DK - e.shape[1], BF16),
                (blk, len(t) * DK - e.shape[1]),
                behind,
            )
            for t, e in zip(roles, earlies)
        ],
        state_scratch * local_heads,
        seg_len * DK * DV,
    )

    ffn_terms = exchange_rows(ffn_terms)
    lates[0], parts_ffn_in[:3] = tie_parts(lates[0], parts_ffn_in[:3])
    g_units[0] = unit_rows(lates[0], normed, len(roles[0]), True, g_units[0])
    joined = [t for pair in zip(earlies, lates) for t in pair]
    joined[0], g_units[0] = tie(joined[0], g_units[0])
    joined[0], scattered["mixer_out"] = tie(joined[0], scattered["mixer_out"])
    tile = 512
    operands = []
    for h in range(local_heads):
        weights = heads_kept[h][0]
        operands += [(t, t.shape, whole) for t in joined[2 * h : 2 * h + 2]]
        operands.append((weights, (weights.shape[0], tile), lambda n: (0, n)))
    (d_normed,) = head_call(
        functools.partial(join_kernel, local_heads),
        width // tile,
        operands,
        [(shaped(width, BF16), (seg_len, tile), lambda n: (0, n))],
        [],
        seg_len * width,
    )
    d_normed, parts_ffn_in = tie_parts(d_normed, parts_ffn_in)
    d_normed, ffn_terms = tie(d_normed, ffn_terms)
    output = (resid + add_rows(ffn_terms)).astype(BF16)
    d_normed = exchange_rows(d_normed)
    parts_mixer_out = spread(scattered["mixer_out"])
    for h in range(1, local_heads):
        g_units[h] = unit_rows(lates[h], normed, len(roles[h]), True, g_units[h])
    g_ffn_in = place_blocks(
        parts_ffn_in, s ^ near, near, ffn_in.shape, (sub, width), lambda o, n: (n, 0)
    )
    d_normed, g_units[-1], g_ffn_in = tie(d_normed, g_units[-1], g_ffn_in)
    d_normed = add_rows(d_normed)
    g_slots = []
    for h in range(local_heads):
        if not balanced:
            cut = g_units[h].reshape(-1, DK, width)
            g_units[h] = jnp.concatenate(
                [pick(cut, jnp.maximum(held[h, c, s], 0)) for c in range(segments)], axis=0
            )
        g_slots.append(reduce_shard(g_units[h]))

    ignored8, norm1_back = jax.vjp(rms_scale, xf, gain_attn)
    d_x_part, d_gain_attn = norm1_back(d_normed)
    input_grad = (d_resid + d_x_part).astype(BF16)
    gains = lax.all_to_all(
        jnp.broadcast_to(jnp.concatenate([d_gain_attn, d_gain_ffn])[None], (segments, 2 * width)),
        "shard",
        split_axis=0,
        concat_axis=0,
        tiled=True,
    )
    gains = jnp.sum(gains, axis=0, keepdims=True)
    parts = []
    for h in range(local_heads):
        last = h == local_heads - 1
        beside = None
        if h == 0:
            g_slots[h], input_grad = tie(g_slots[h], input_grad)
            g_slots[h], parts_mixer_out = tie_parts(g_slots[h], parts_mixer_out)
            g_mixer_out = place_blocks(
                parts_mixer_out,
                s ^ near,
                near,
                mixer_out.shape,
                (mixer_out.shape[0], DV),
                lambda o, n: (0, o * group + n),
                outer=local_heads,
            )
            if sub % 128 == 0:
                g_ffn_out = place_blocks(
                    parts_ffn_out,
                    s ^ near,
                    near,
                    ffn_out.shape,
                    (ffn_out.shape[0], sub),
                    lambda o, n: (0, o * group + n),
                    outer=segments // 2,
                )
            else:
                g_ffn_out = jnp.transpose(
                    ordered(parts_ffn_out).reshape(group, ffn_out.shape[0], segments // 2, sub),
                    (1, 2, 0, 3),
                ).reshape(ffn_out.shape).astype(F32)
            beside = [g_mixer_out, output, gains, g_ffn_out]
        if last and h > 0:
            g_slots[h], gains, g_mixer_out = tie(g_slots[h], gains, g_mixer_out)
            beside = []
            g_slots[h], parts = tie_parts(g_slots[h], parts)
        here = spread(g_slots[h], beside)
        if group == 4 and h == 0:
            g_mixer_out, output, gains, g_ffn_out = beside
        if last:
            if beside is not None and group == 4:
                here[1], gains = tie(here[1], gains)
                gains = gains + swap(gains, 1)
                here[3], gains = tie(here[3], gains)
                gains = gains + swap(gains, 2)
            else:
                step = 1
                while step < group:
                    gains = gains + swap(gains, step)
                    step *= 2
        if balanced and last:
            there = [tuple(cross(piece, 1) for piece in part) for part in here]
            parts += [a + b for a, b in zip(here, there)] + [b + a for a, b in zip(here, there)]
        else:
            lend_here = lend[j] if balanced else lend[h, j]
            stack = jnp.stack([jnp.concatenate(part, axis=0) for part in here])
            parts += here + [
                (cross(pick(stack, s ^ lend_here[n]), 1),) for n in range(lend_here.shape[0])
            ]
    gain_attn_grad, gain_ffn_grad = gains[0, :width], gains[0, width:]
    found = back[j]
    if balanced:
        spare = lend.shape[-1]
        source = jnp.where(
            found[:, 0] == 0,
            s ^ found[:, 1],
            jnp.where(
                found[:, 0] == 1,
                group + found[:, 1],
                group + spare + core * group + (s ^ found[:, 1]),
            ),
        )
    else:
        source = found[:, 0] * (group + lend.shape[-1]) + jnp.where(
            found[:, 2] < 0, s ^ found[:, 1], group + found[:, 2]
        )
    g_mixer_in = place_blocks(
        parts,
        jnp.arange(source.shape[0]),
        source,
        mixer_in.shape,
        (DK, width),
        lambda o, n: (n, 0),
    )
    return (
        output,
        input_grad,
        gain_attn_grad,
        gain_ffn_grad,
        g_mixer_in,
        g_mixer_out,
        g_ffn_in,
        g_ffn_out,
    )


def solution(mesh):
    return jax.shard_map(
        local,
        mesh=mesh,
        in_specs=(
            P(("shard", "seq"), None),
            P(("shard", "seq"), None),
            P(),
            P(),
            P("shard", None),
            P("shard", None),
            P("shard", None),
            P("shard", None),
            P(),
            P(),
        ),
        out_specs=(
            P(("shard", "seq"), None),
            P(("shard", "seq"), None),
            P(),
            P(),
            P("shard", None),
            P("shard", None),
            P("shard", None),
            P("shard", None),
        ),
        check_vma=False,
    )
```

```python
import functools

import jax
import jax.numpy as jnp
import numpy as np
from jax import lax
from jax.experimental import pallas as pl
from jax.experimental.pallas import tpu as pltpu
from jax.sharding import PartitionSpec as P

DK = 256
DV = 512
FF = 4096
QK = 2048
V = 4096


EPS_NORM = 1e-06
EPS_GROUP = 1e-05

F32 = jnp.float32
BF16 = jnp.bfloat16


def dot_nt(left, right, kind=F32):
    return lax.dot_general(
        left, right, (((1,), (1,)), ((), ())), preferred_element_type=F32
    ).astype(kind)


def dot_nn(left, right, kind=F32):
    return lax.dot_general(
        left, right, (((1,), (0,)), ((), ())), preferred_element_type=F32
    ).astype(kind)


def dot_tn(left, right, kind=F32):
    return lax.dot_general(
        left, right, (((0,), (0,)), ((), ())), preferred_element_type=F32
    ).astype(kind)


def rms_scale(v, gain):
    return v * lax.rsqrt(jnp.mean(v * v, axis=-1, keepdims=True) + EPS_NORM) * gain


def gated_gelu(first, second):
    return jax.nn.gelu(first) * second


def unit_owners(heads):
    owners = [(n, 0) for n in range(heads)] + [(n, 1) for n in range(heads)]
    for base in (2, 4):
        owners += [(n, base + half) for n in range(heads) for half in range(2)]
    return owners


def balanced_tables():
    group, segments, per_shard = 4, 8, 6
    number = {owner: u for u, owner in enumerate(unit_owners(8))}
    keep = np.full((2, segments, group), -1, np.int32)
    give = np.zeros((2, segments, group), np.int32)
    back = np.zeros((segments, per_shard, 2), np.int32)
    lend = [[] for _ in range(segments)]
    seen = set()
    for s in range(group):
        a, b = s, s + 4
        if s < 2:
            gates = [(a, 4), (b, 4), (b, 5)], (b + 2, 5)
        else:
            gates = [(a - 2, 5), (a, 4), (a, 5)], (b, 4)
        first = [(a, 0), (a, 1), (a, 2), (a, 3), (b, 2)] + gates[0]
        second = [(b, 0), (b, 1), (b, 3), gates[1]]
        for slot, owner in enumerate(first):
            home, index = divmod(number[owner], per_shard)
            seen.add(number[owner])
            assert home // 2 == slot // 2
            if home == slot:
                keep[0, slot, s] = index
                back[home, index] = (0, s)
            else:
                give[0, home, s] = index
                back[home, index] = (1, len(lend[slot]))
                lend[slot].append(s)
        for chip, owner in enumerate(second):
            home, index = divmod(number[owner], per_shard)
            seen.add(number[owner])
            assert home // 2 == chip
            keep[1, home, s] = index
            give[1, home, s] = index
            back[home, index] = (2, s)
    assert len(seen) == segments * per_shard
    most = max(len(t) for t in lend)
    return keep, give, back, np.asarray([(t + [0] * most)[:most] for t in lend], np.int32)


def unit_tables(group, local_heads, segments):
    heads = group * local_heads
    owners = unit_owners(heads)
    per_shard = len(owners) // segments
    keep = np.full((local_heads, segments, group), -1, np.int32)
    give = np.zeros((local_heads, segments, group), np.int32)
    place = np.zeros((local_heads, group, 6), np.int32)
    held = np.full((local_heads, segments, group), -1, np.int32)
    slot_of = {}
    for chip in range(segments // 2):
        for head in range(heads):
            h, s = divmod(head, group)
            span = range(2 * per_shard * chip, 2 * per_shard * (chip + 1))
            mine = [u for u in span if owners[u][0] == head]
            assert len(mine) <= 2
            for n, u in enumerate(mine):
                home = u // per_shard
                slot = home if len(mine) == 1 else 2 * chip + n
                if slot == home:
                    keep[h, slot, s] = u % per_shard
                else:
                    give[h, home, s] = u % per_shard
                place[h, s, owners[u][1]] = slot
                held[h, slot, s] = owners[u][1]
                slot_of[u] = slot
    lends = [[[] for _ in range(segments)] for _ in range(local_heads)]
    back = np.zeros((segments, per_shard, 3), np.int32)
    for u, (head, _) in enumerate(owners):
        home = u // per_shard
        h, s = divmod(head, group)
        back[home, u % per_shard] = (h, s, -1)
        if slot_of[u] != home:
            assert slot_of[u] == home ^ 1
            back[home, u % per_shard, 2] = len(lends[h][home ^ 1])
            lends[h][home ^ 1].append(s)
    most = max(1, max(len(t) for row in lends for t in row))
    lend = np.asarray(
        [[(t + [0] * most)[:most] for t in row] for row in lends], np.int32
    )
    return keep, give, place, held, back, lend


def tie(*values):
    return lax.optimization_barrier(values)


def mm(left, right, dims):
    return lax.dot_general(left, right, (dims, ((), ())), preferred_element_type=F32)


NN = ((1,), (0,))
NT = ((1,), (1,))
TN = ((0,), (0,))


def turn(v, cosine, sine):
    half = v.shape[-1] // 2
    first, second = v[:, :half], v[:, half:]
    return jnp.concatenate(
        [first * cosine - second * sine, second * cosine + first * sine], axis=-1
    )


def scaled(v, decay):
    return (v.astype(F32) * decay).astype(BF16)


def project_kernel(blk, roles, carried, params, x, w, cosine, sine, k_decay, *refs):
    if carried:
        v_a, *refs = refs
    q, k, v, total, gates, *rest = refs
    y = rest[-1]
    rows = y.shape[0]
    y[...] = mm(x[...], w[...], NT)

    def put(role, part, gate_at):
        value = y[:, part * DK : (part + 1) * DK]
        if role == "q":
            q[...] = turn(value, cosine[...], sine[...]).astype(BF16)
        elif role == "k":
            k[...] = turn(value, cosine[...], sine[...]).astype(BF16)
        elif role == "va":
            v[:, :DK] = value.astype(BF16)
        elif role == "vb":
            v[:, DK:] = value.astype(BF16)
        elif role == "xv":
            rest[0][...] = value.astype(BF16)
        else:
            gates[:, gate_at * DK : (gate_at + 1) * DK] = value.astype(BF16)

    for step in range(len(roles) // 2):

        @pl.when(pl.program_id(0) == step)
        def _(step=step):
            for part in range(2):
                at = 2 * step + part
                put(roles[at], part, roles[:at].count("g"))
            if step == 1:
                if carried:
                    v[:, :DK] = v_a[...]
                state = jnp.zeros(total.shape, F32)
                for r in range(0, rows, blk):
                    kd = scaled(k[r : r + blk, :], k_decay[...])
                    state = params[0] * state + mm(kd, v[r : r + blk, :], TN)
                total[...] = state.astype(BF16)


def join_kernel(count, *refs):
    out = refs[-1]
    total = None
    for n in range(count):
        early, late, weights = refs[3 * n : 3 * n + 3]
        middle = DK + late.shape[1]
        part = mm(early[:, :DK], weights[:DK, :], NN)
        part += mm(early[:, DK:], weights[middle:, :], NN)
        part += mm(late[...], weights[DK:middle, :], NN)
        total = part if total is None else total + part
    out[...] = total.astype(out.dtype)


def select(params, low, high):
    return jnp.where(params[1] > 0.5, low[...].astype(F32), high[...].astype(F32))


def retain_kernel(
    params, q, k, v, low_a, high_a, low_b, high_b, mask, q_decay, k_decay, start,
    hidden, mixed, kept, state,
):
    @pl.when(pl.program_id(0) == 0)
    def _():
        state[...] = start[...].astype(F32)

    weights = (mm(q[...], k[...], NT) * mask[...]).astype(BF16)
    o = mm(weights, v[...], NN)
    o += mm(scaled(q[...], q_decay[...]), state[...].astype(BF16), NN)
    state[...] = params[0] * state[...] + mm(scaled(k[...], k_decay[...]), v[...], TN)
    o = o - jnp.mean(o, axis=-1, keepdims=True)
    inverse = lax.rsqrt(jnp.mean(o * o, axis=-1, keepdims=True) + EPS_GROUP)
    kept[...] = inverse
    low = (o * inverse).astype(BF16)
    mixed[...] = low
    for n, (one, two) in enumerate(((low_a, high_a), (low_b, high_b))):
        columns = slice(n * DK, (n + 1) * DK)
        g = select(params, one, two)
        hidden[:, columns] = (g * jax.nn.sigmoid(g) * low[:, columns].astype(F32)).astype(BF16)


def take(refs, counts):
    pieces, at = [], 0
    for count in counts:
        pieces.append(refs[at : at + count])
        at += count
    return pieces


def gate_back_kernel(heads, params, d_attn, w_out, *refs):
    inputs = take(refs, [8] * heads)
    outputs = take(refs[8 * heads :], [3] * heads)
    states = refs[11 * heads :]

    @pl.when(pl.program_id(0) == 0)
    def _():
        for state in states:
            state[...] = jnp.zeros(state.shape, F32)

    d_hidden = mm(d_attn[...], w_out[...], NN)
    for h in range(heads):
        low_a, high_a, low_b, high_b, mixed, inverse, q, q_decay = inputs[h]
        d_gate, d_out, total = outputs[h]
        g = jnp.concatenate(
            [select(params, low_a, high_a), select(params, low_b, high_b)], axis=1
        )
        dh = d_hidden[:, h * DV : (h + 1) * DV]
        sig = jax.nn.sigmoid(g)
        o = mixed[...].astype(F32)
        d_gate[...] = (dh * o * (sig * (1.0 + g * (1.0 - sig)))).astype(BF16)
        dy = (dh * (g * sig)).astype(BF16).astype(F32)
        do = inverse[...] * (
            dy
            - jnp.mean(dy, axis=-1, keepdims=True)
            - o * jnp.mean(dy * o, axis=-1, keepdims=True)
        )
        do = do.astype(BF16)
        d_out[...] = do
        state = states[h]
        state[...] = params[2 + h] * state[...] + mm(scaled(q[...], q_decay[...]), do, TN)
        total[...] = state[...].astype(BF16)


def inner_back_kernel(roles, params, cosine, sine, *refs):
    heads = len(roles)
    counts = [8 + 2 * t.count("g") for t in roles]
    inputs = take(refs, counts)
    outputs = take(refs[sum(counts) :], [3] * heads)
    states = refs[sum(counts) + 3 * heads :]

    @pl.when(pl.program_id(0) == 0)
    def _():
        for h in range(heads):
            states[h][...] = inputs[h][7][...].astype(F32)

    for h in range(heads):
        q, k, v, d_out, mask, q_decay, k_decay, ignored, *gates = inputs[h]
        early, d_k, d_v = outputs[h]
        state = states[h]
        do = d_out[...]
        weights = (mm(q[...], k[...], NT) * mask[...]).astype(BF16)
        d_v[...] = mm(weights, do, TN)
        d_scores = mm(do, v[...], NT).astype(BF16).astype(F32)
        d_scores = (d_scores * mask[...]).astype(BF16)
        d_k[...] = mm(d_scores, q[...], TN)
        far = mm(do, state[...].astype(BF16), NT).astype(BF16).astype(F32)
        dq = mm(d_scores, k[...], NN) + far * q_decay[...]
        dq = dq.astype(BF16).astype(F32)
        early[:, :DK] = turn(dq, cosine[...], -sine[...]).astype(BF16)
        for n in range(len(gates) // 2):
            value = select(params, gates[2 * n], gates[2 * n + 1]).astype(BF16)
            early[:, (n + 1) * DK : (n + 2) * DK] = value
        state[...] = params[2 + h] * state[...] + mm(scaled(k[...], k_decay[...]), v[...], TN)


def outer_back_kernel(roles, params, cosine, sine, *refs):
    heads = len(roles)
    inputs = take(refs, [9] * heads)
    outputs = refs[9 * heads : 10 * heads]
    states = refs[10 * heads :]

    @pl.when(pl.program_id(0) == 0)
    def _():
        for h in range(heads):
            states[h][...] = inputs[h][8][...].astype(F32)

    other = None
    for h in reversed(range(heads)):
        q, k, v, d_out, d_k, d_v, q_decay, k_decay, ignored = inputs[h]
        state = states[h]
        low = state[...].astype(BF16)
        far = mm(v[...], low, NT).astype(BF16).astype(F32)
        dk = (d_k[...] + far * k_decay[...]).astype(BF16).astype(F32)
        dk = turn(dk, cosine[...], -sine[...]).astype(BF16)
        dv = (d_v[...] + mm(scaled(k[...], k_decay[...]), low, NN)).astype(BF16)
        values = {"k": dk, "va": dv[:, :DK], "vb": dv[:, DK:], "xv": other}
        for n, role in enumerate(t for t in roles[h] if t in values):
            outputs[h][:, n * DK : (n + 1) * DK] = values[role]
        other = dv[:, :DK]
        state[...] = params[2 + h] * state[...] + mm(scaled(q[...], q_decay[...]), d_out[...], TN)


def unit_kernel(x, normed, *refs):
    refs[-1][...] = mm(x[...], normed[...], TN).astype(BF16)


def unit_rows(x, normed, count, late, into=None):
    rows, width = normed.shape
    units = x.shape[1] // DK

    def where(n):
        return (n + 1, 0) if late else (jnp.where(n == 0, 0, n + count - units), 0)

    arrays = [x, normed] + ([] if into is None else [into])
    return pl.pallas_call(
        unit_kernel,
        grid=(units,),
        in_specs=[
            pl.BlockSpec((rows, DK), lambda n: (0, n)),
            pl.BlockSpec((rows, width), lambda n: (0, 0)),
        ]
        + ([] if into is None else [pl.BlockSpec(memory_space=pl.ANY)]),
        out_specs=pl.BlockSpec((DK, width), where),
        out_shape=jax.ShapeDtypeStruct((count * DK, width), BF16),
        input_output_aliases={} if into is None else {2: 0},
        compiler_params=pltpu.CompilerParams(vmem_limit_bytes=48 * 2**20),
        cost_estimate=pl.CostEstimate(
            flops=rows * width * DK, bytes_accessed=rows * width, transcendentals=0
        ),
    )(*arrays)


def head_call(kernel, grid, operands, outputs, scratch, flops, size=None):
    arrays = [t[0] for t in operands]
    if size is None:
        size = sum(t.size * t.dtype.itemsize for t in arrays + [t[0] for t in outputs])
    call = pl.pallas_call(
        kernel,
        grid=(grid,),
        in_specs=[
            pl.BlockSpec(memory_space=pltpu.SMEM) if block is None else pl.BlockSpec(block, where)
            for _, block, where in operands
        ],
        out_specs=[pl.BlockSpec(block, where) for _, block, where in outputs],
        scratch_shapes=scratch,
        out_shape=[t[0] for t in outputs],
        compiler_params=pltpu.CompilerParams(vmem_limit_bytes=56 * 2**20),
        cost_estimate=pl.CostEstimate(flops=flops, bytes_accessed=size, transcendentals=0),
    )
    return list(call(*arrays))


def place_kernel(parts, target, source, *refs):
    out = refs[-1]
    code = source[pl.program_id(1)]
    for i, part in enumerate(parts):

        @pl.when(code == i)
        def _(part=part):
            row = 0
            for n in part:
                piece = refs[n]
                out[row : row + piece.shape[0], :] = piece[...].astype(F32)
                row += piece.shape[0]


def place_blocks(parts, target, source, shape, block, where, outer=1):
    flat, index = [], []
    for part in parts:
        for piece in part:
            if not any(piece is t for t in flat):
                flat.append(piece)
        index.append([next(n for n, t in enumerate(flat) if t is piece) for piece in part])
    return pl.pallas_call(
        functools.partial(place_kernel, index),
        grid_spec=pltpu.PrefetchScalarGridSpec(
            num_scalar_prefetch=2,
            grid=(outer, target.shape[0]),
            in_specs=[
                pl.BlockSpec((t.shape[0], t.shape[1] // outer), lambda o, n, target, source: (0, o))
                for t in flat
            ],
            out_specs=pl.BlockSpec(block, lambda o, n, target, source: where(o, target[n])),
        ),
        out_shape=jax.ShapeDtypeStruct(shape, F32),
        compiler_params=pltpu.CompilerParams(vmem_limit_bytes=48 * 2**20),
    )(target.astype(jnp.int32), source.astype(jnp.int32), *flat)


def local(
    tokens,
    cotangent,
    gain_attn,
    gain_ffn,
    mixer_in,
    mixer_out,
    ffn_in,
    ffn_out,
    segment_order,
    decay_index,
):
    rows, width = tokens.shape
    group = lax.axis_size("seq")
    segments = lax.axis_size("shard")
    heads = decay_index.shape[0]
    local_heads = heads // group
    seg_len = rows * group
    blk = min(512, seg_len)
    blocks = seg_len // blk
    vcols = local_heads * DV
    s = lax.axis_index("seq")
    j = lax.axis_index("shard")

    def swap(v, d):
        return lax.ppermute(v, "seq", [(i, i ^ d) for i in range(group)])

    def cross(v, d):
        return lax.ppermute(v, "shard", [(i, i ^ d) for i in range(segments)])

    def pick(v, i):
        return lax.dynamic_index_in_dim(v, i, 0, keepdims=False)

    def spread(v, beside=None):
        if group == 4:
            h = v.shape[0] // 2
            r1 = swap(v, 1)
            r2 = swap(v, 2)
            if beside:
                r1, r2, beside[:] = tie(r1, r2, list(beside))
            return [(v,), (r1,), (r2,), (swap(r1[:h], 2), swap(r2[h:], 1))]
        return [(v,)] + [(swap(v, d),) for d in range(1, group)]

    def ordered(parts):
        r = parts[0][0].shape[0]
        out = jnp.zeros((group * r,) + parts[0][0].shape[1:], parts[0][0].dtype)
        for d, part in enumerate(parts):
            row = (s ^ d) * r
            for piece in part:
                out = lax.dynamic_update_slice_in_dim(out, piece, row, 0)
                row = row + piece.shape[0]
        return out

    def gather_near(v):
        return jnp.concatenate([piece for part in spread(v) for piece in part], axis=0)

    def gather_seq(v):
        return ordered(spread(v))

    def first_step(blk_of):
        b = [blk_of(d) for d in range(4)]
        h = b[0].shape[0] // 2
        sa = jnp.concatenate([b[1][:h], b[3][:h]], axis=0)
        sb = jnp.concatenate([b[2][h:], b[3][h:]], axis=0)
        return b, *tie(sa, sb)

    def send_step(b, sa, sb):
        return b, swap(sa, 1), swap(sb, 2)

    def second_step(b, ra, rb, held=()):
        h = b[0].shape[0] // 2
        ra, rb = ra.astype(F32), rb.astype(F32)
        qa = (b[2][:h].astype(F32) + ra[h:]).astype(BF16)
        qb = (b[1][h:].astype(F32) + rb[h:]).astype(BF16)
        qa, qb, *held = tie(qa, qb, *held)
        qa, qb = swap(qa, 2), swap(qb, 1)
        top = b[0][:h].astype(F32) + ra[:h] + qa.astype(F32)
        low_half = b[0][h:].astype(F32) + rb[:h] + qb.astype(F32)
        total = jnp.concatenate([top, low_half], axis=0)
        return (total, *held) if held else total

    def send_blocks(blk_of):
        sent = tie(*(blk_of(d) for d in range(group)))
        return sent[0], [swap(sent[d], d) for d in range(group - 1, 0, -1)]

    def add_blocks(own, got):
        own = own.astype(F32)
        for t in got:
            own = own + t.astype(F32)
        return own

    def near_rows(v):
        return lambda d: v[d * rows : (d + 1) * rows]

    def seq_rows(v):
        return lambda d: lax.dynamic_slice_in_dim(v, (s ^ d) * rows, rows, 0)

    def gather_shard(v):
        return lax.all_gather(v, "shard", axis=0, tiled=True)

    def reduce_shard(v):
        return lax.psum_scatter(v, "shard", scatter_dimension=0, tiled=True)

    balanced = group == 4 and local_heads == 2 and segments == 8
    units = mixer_in.reshape(-1, DK, width)
    if balanced:
        keep, give, back, lend = (jnp.asarray(t) for t in balanced_tables())
        core = j % 2
    else:
        keep, give, place, held, back, lend = (
            jnp.asarray(t) for t in unit_tables(group, local_heads, segments)
        )

    def offered(h):
        kept, given = keep[h, j, s], give[h, j, s]
        if balanced and h == 1:
            cut = mixer_in.reshape(-1, DK // 2, width)
            own = pick(cut, 2 * jnp.maximum(kept, 0) + core)
            given = cross(pick(cut, 2 * given + 1 - core), 1)
        else:
            own = pick(units, jnp.maximum(kept, 0))
            given = cross(pick(units, given), 1)
        return jnp.where(kept >= 0, own, given)

    sub = ffn_in.shape[0] // group
    ffn_out_cut = ffn_out.reshape(ffn_out.shape[0], segments // 2, group, sub)

    my_rank = jnp.sum(jnp.where(jnp.arange(segments) == j, segment_order, 0))
    all_logs = jnp.log1p(-jnp.exp2(-(5.0 + decay_index.astype(F32))))
    logs = lax.dynamic_index_in_dim(all_logs.reshape(local_heads, group), s, 1, keepdims=False)
    half = DK // 2
    inv_freq = jnp.exp(-jnp.log(10000.0) * jnp.arange(half).astype(F32) / half)
    positions = my_rank * seg_len + jnp.arange(seg_len, dtype=jnp.int32)
    angles = positions.astype(F32)[:, None] * inv_freq[None, :]
    cosine = jnp.cos(angles)
    sine = jnp.sin(angles)
    steps = jnp.arange(blk).astype(F32)
    gap = steps[:, None] - steps[None, :]
    masks = jnp.where(
        gap[None] >= 0.0, jnp.exp(jnp.maximum(gap, 0.0)[None] * logs[:, None, None]), 0.0
    )
    q_decays = jnp.exp((steps + 1.0)[None, :] * logs[:, None])[..., None]
    k_decays = jnp.exp((blk - 1.0 - steps)[None, :] * logs[:, None])[..., None]
    block_decays = jnp.exp(blk * logs)

    xf = tokens.astype(F32)
    normed = gather_seq(rms_scale(xf, gain_attn).astype(BF16))
    d_ffn = gather_near(cotangent)
    slots = [gather_shard(offered(0))]
    slots[0], normed, d_ffn, cosine, sine, masks, q_decays, k_decays = tie(
        slots[0], normed, d_ffn, cosine, sine, masks, q_decays, k_decays
    )
    for h in range(1, local_heads):
        slots.append(gather_shard(offered(h)))
    mixer_out_cut = jnp.concatenate(
        [
            lax.dynamic_slice_in_dim(mixer_out, (h * group + s) * DV, DV, 1)
            for h in range(local_heads)
        ],
        axis=1,
    )
    mixer_out_cut, slots[0] = tie(mixer_out_cut, slots[0])
    w_out = gather_shard(mixer_out_cut)
    later = [
        lax.dynamic_slice_in_dim(ffn_in, s * sub, sub, 0),
        lax.dynamic_index_in_dim(ffn_out_cut, s, 2, keepdims=False).reshape(ffn_out.shape[0], -1),
    ]
    inner_cols = later[1].shape[1]

    ranks = segment_order
    piece = DK // segments

    def exchange_states(hs, totals, reverse, beside=()):
        cut = jnp.concatenate([t.reshape(segments, piece, DV) for t in totals], axis=1)
        got = lax.all_to_all(cut, "shard", split_axis=0, concat_axis=0, tiled=True)
        got, *beside = tie(got, *beside)
        apart = ranks[:, None] - ranks[None, :] - 1
        if reverse:
            apart = -apart - 2
        distance = apart.astype(F32)
        joined = []
        for n, h in enumerate(hs):
            coef = jnp.where(
                distance >= 0.0, jnp.exp(jnp.maximum(distance, 0.0) * seg_len * logs[h]), 0.0
            )
            part = got[:, n * piece : (n + 1) * piece].astype(F32)
            joined.append(jnp.sum(coef[..., None, None] * part[None], axis=1).astype(BF16))
        joined = jnp.concatenate(joined, axis=1)
        back_cut = lax.all_to_all(joined, "shard", split_axis=0, concat_axis=0, tiled=True)
        states = [
            back_cut[:, n * piece : (n + 1) * piece].reshape(DK, DV) for n in range(len(hs))
        ]
        return (states, *beside)

    def whole(n):
        return (0, 0)

    def ahead(n):
        return (n, 0)

    def behind(n):
        return (blocks - 1 - n, 0)

    def shaped(columns, kind, r=seg_len):
        return jax.ShapeDtypeStruct((r, columns), kind)

    state_scratch = [pltpu.VMEM((DK, DV), F32)]
    half_block = (blk, half)
    unit_block, v_block = (blk, DK), (blk, DV)
    ret_flops = 2 * seg_len * (DK + DV) * (blk + DK)
    low = s < group // 2
    if balanced:
        roles = [["q", "k", "va", "vb", "xv", "g", "g", "g"], ["q", "k", "vb", "g"]]
    else:
        roles = [["q", "k", "va", "vb", "g", "g"]] * local_heads
    params = [
        (jnp.stack([block_decays[h], low.astype(F32)]), None, None) for h in range(local_heads)
    ]
    heads_kept = []
    extra_v = None
    for h in range(local_heads):
        if balanced:
            weights = slots[h]
        else:
            cut = slots[h].reshape(-1, DK, width)
            weights = jnp.concatenate([pick(cut, place[h, s, c]) for c in range(6)], axis=0)
        carried = "va" not in roles[h]
        gate_count = roles[h].count("g")
        q, k, v, total, gates, *extra = head_call(
            functools.partial(project_kernel, blk, roles[h], carried),
            len(roles[h]) // 2,
            [
                params[h],
                (normed, (seg_len, width), whole),
                (weights, (2 * DK, width), ahead),
                (cosine, (seg_len, half), whole),
                (sine, (seg_len, half), whole),
                (k_decays[h], (blk, 1), whole),
            ]
            + ([(extra_v, (seg_len, DK), whole)] if carried else []),
            [
                (shaped(DK, BF16), (seg_len, DK), whole),
                (shaped(DK, BF16), (seg_len, DK), whole),
                (shaped(DV, BF16), (seg_len, DV), whole),
                (shaped(DV, BF16, DK), (DK, DV), whole),
                (shaped(gate_count * DK, BF16), (seg_len, gate_count * DK), whole),
            ]
            + ([(shaped(DK, BF16), (seg_len, DK), whole)] if "xv" in roles[h] else []),
            [pltpu.VMEM((seg_len, 2 * DK), F32)],
            2 * seg_len * width * len(roles[h]) * DK,
        )
        extra_v = extra[0] if extra else None
        (state_in,) = exchange_states([h], [total], False)[0]
        if h + 1 < local_heads:
            slots[h + 1], state_in, *later[:] = tie(slots[h + 1], state_in, *later)
        heads_kept.append((weights, q, k, v, gates, state_in))

    def columns(v, c, order):
        return (v, unit_block, lambda n, c=c: (order(n)[0], c))

    if balanced:
        gates0, gates1 = heads_kept[0][4], heads_kept[1][4]
        swapped = swap(jnp.where(low, gates1, gates0[:, :DK]), 2)

        def gate_operands(h, order):
            if h == 0:
                four = (gates0, 0), (gates0, 1), (swapped, 0), (gates0, 2)
            else:
                four = (gates0, 1), (gates1, 0), (gates0, 2), (swapped, 0)
            return [columns(v, c, order) for v, c in four]

    else:

        def gate_operands(h, order):
            return [columns(heads_kept[h][4], c, order) for c in (0, 0, 1, 1)]

    kept = []
    for h in range(local_heads):
        weights, q, k, v, gates, state_in = heads_kept[h]
        hidden, mixed, retained = head_call(
            retain_kernel,
            blocks,
            [
                params[h],
                (q, unit_block, ahead),
                (k, unit_block, ahead),
                (v, v_block, ahead),
                *gate_operands(h, ahead),
                (masks[h], (blk, blk), whole),
                (q_decays[h], (blk, 1), whole),
                (k_decays[h], (blk, 1), whole),
                (state_in, (DK, DV), whole),
            ],
            [
                (shaped(DV, BF16), v_block, ahead),
                (shaped(DV, BF16), v_block, ahead),
                (shaped(1, F32), (blk, 1), ahead),
            ],
            state_scratch,
            ret_flops,
        )
        kept.append((retained, mixed, hidden))
    hidden = jnp.concatenate([t[-1] for t in kept], axis=1)
    w_ffn_in, w_ffn_out = (gather_shard(t) for t in later)

    resid = xf + add_blocks(*send_blocks(seq_rows(dot_nt(hidden, w_out, BF16))))
    normed2 = gather_near(rms_scale(resid, gain_ffn).astype(BF16))
    proj2 = dot_nt(normed2, w_ffn_in)
    first, second = proj2[:, :inner_cols], proj2[:, inner_cols:]
    inner2 = gated_gelu(first, second).astype(BF16)

    g_ffn_out, d_ffn = tie(dot_tn(d_ffn, inner2, BF16), d_ffn)
    scattered = {"ffn_out": reduce_shard(g_ffn_out)}
    d_inner2 = dot_nn(d_ffn, w_ffn_out)
    ignored2, gelu_back = jax.vjp(gated_gelu, first, second)
    d_first, d_second = gelu_back(d_inner2)
    dproj2 = jnp.concatenate([d_first, d_second], axis=1).astype(BF16)
    d_normed2 = dot_nn(dproj2, w_ffn_in, BF16)
    g_ffn_in = dot_tn(dproj2, normed2, BF16)
    if group == 4:
        terms, ra, rb = send_step(*first_step(near_rows(d_normed2)))
        ra, rb, g_ffn_in = tie(ra, rb, g_ffn_in)
        d_normed2 = second_step(terms, ra, rb)
    else:
        d_normed2 = add_blocks(*send_blocks(near_rows(d_normed2)))
    scattered["ffn_in"] = reduce_shard(g_ffn_in)
    ignored3, norm2_back = jax.vjp(rms_scale, resid, gain_ffn)
    d_resid_part, d_gain_ffn = norm2_back(d_normed2)
    d_resid = cotangent.astype(F32) + d_resid_part
    (d_attn,) = tie(d_resid.astype(BF16))
    d_attn = gather_seq(d_attn)
    d_attn, scattered["ffn_out"] = tie(d_attn, scattered["ffn_out"])
    parts_ffn_out = spread(scattered["ffn_out"])

    def tie_parts(v, parts):
        flat = tie(v, *(piece for part in parts for piece in part))
        rest = list(flat[1:])
        return flat[0], [tuple(rest.pop(0) for _ in part) for part in parts]

    all_params = (
        jnp.concatenate([jnp.stack([jnp.float32(0.0), low.astype(F32)]), block_decays]),
        None,
        None,
    )
    outs = head_call(
        functools.partial(gate_back_kernel, local_heads),
        blocks,
        [
            all_params,
            (d_attn, (blk, width), behind),
            (w_out, (width, vcols), whole),
        ]
        + [
            t
            for h in range(local_heads)
            for t in (
                *gate_operands(h, behind),
                (kept[h][1], v_block, behind),
                (kept[h][0], (blk, 1), behind),
                (heads_kept[h][1], unit_block, behind),
                (q_decays[h], (blk, 1), whole),
            )
        ],
        [
            (shaped(DV, BF16), v_block, behind),
            (shaped(DV, BF16), v_block, behind),
            (shaped(DV, BF16, DK), (DK, DV), whole),
        ]
        * local_heads,
        state_scratch * local_heads,
        2 * seg_len * (DK * DV * local_heads + width * vcols),
    )
    d_gates, d_outs, totals = outs[0::3], outs[1::3], outs[2::3]
    if balanced:
        d_swapped = jnp.where(low, d_gates[0][:, DK:], d_gates[1][:, DK:])
        d_swapped, parts_ffn_out[:3] = tie_parts(d_swapped, parts_ffn_out[:3])
        d_swapped = swap(d_swapped, 2)
    else:
        d_swapped = totals[0]
    hidden, totals[0] = tie(hidden, totals[0])
    g_mixer_out = dot_tn(d_attn, hidden, BF16)
    totals[0], d_swapped, g_mixer_out = tie(totals[0], d_swapped, g_mixer_out)
    d_outs[0], g_mixer_out = tie(d_outs[0], g_mixer_out)
    scattered["mixer_out"] = reduce_shard(g_mixer_out)
    if balanced:
        d_gate_pairs = [
            [
                ((d_gates[0], 0), (d_swapped, 0)),
                ((d_gates[1], 0), (d_gates[0], 0)),
                ((d_gates[1], 1), (d_gates[0], 1)),
            ],
            [((d_swapped, 0), (d_gates[1], 0))],
        ]
    else:
        d_gate_pairs = [[((t, 0), (t, 0)), ((t, 1), (t, 1))] for t in d_gates]
    inners = head_call(
        functools.partial(inner_back_kernel, roles),
        blocks,
        [all_params, (cosine, half_block, ahead), (sine, half_block, ahead)]
        + [
            t
            for h in range(local_heads)
            for t in (
                (heads_kept[h][1], unit_block, ahead),
                (heads_kept[h][2], unit_block, ahead),
                (heads_kept[h][3], v_block, ahead),
                (d_outs[h], v_block, ahead),
                (masks[h], (blk, blk), whole),
                (q_decays[h], (blk, 1), whole),
                (k_decays[h], (blk, 1), whole),
                (heads_kept[h][5], (DK, DV), whole),
                *(columns(v, c, ahead) for pair in d_gate_pairs[h] for v, c in pair),
            )
        ],
        [
            t
            for h in range(local_heads)
            for t in (
                (
                    shaped((1 + len(d_gate_pairs[h])) * DK, BF16),
                    (blk, (1 + len(d_gate_pairs[h])) * DK),
                    ahead,
                ),
                (shaped(DK, F32), unit_block, ahead),
                (shaped(DV, F32), v_block, ahead),
            )
        ],
        state_scratch * local_heads,
        ret_flops,
    )
    inner2, totals[0] = tie(inner2, totals[0])
    ffn_terms = near_rows(dot_nt(inner2, w_ffn_out, BF16))
    if group == 4:
        ffn_own, *prepared = first_step(ffn_terms)
    else:
        prepared = [ffn_terms(d) for d in range(group)]
    flat_ffn_out = [piece for part in parts_ffn_out for piece in part]
    beside = [scattered["ffn_in"], *inners, *flat_ffn_out, *prepared]
    grads_out, scattered["ffn_in"], *flat = exchange_states(
        range(local_heads), totals, True, beside
    )
    inners = flat[: 3 * local_heads]
    rest = flat[3 * local_heads :]
    parts_ffn_out = [tuple(rest.pop(0) for _ in part) for part in parts_ffn_out]
    if group == 4:
        late = send_step(ffn_own, *rest)
    else:
        late = send_blocks(lambda d: rest[d])
    parts_ffn_in = spread(scattered["ffn_in"])
    near = jnp.arange(group)
    earlies = inners[0::3]
    g_units = [
        unit_rows(earlies[h], normed, len(roles[h]), False) for h in range(local_heads)
    ]
    flat = list(tie(*grads_out, *g_units))
    grads_out, g_units = flat[:local_heads], flat[local_heads:]
    lates = head_call(
        functools.partial(outer_back_kernel, roles),
        blocks,
        [all_params, (cosine, half_block, behind), (sine, half_block, behind)]
        + [
            t
            for h in range(local_heads)
            for t in (
                (heads_kept[h][1], unit_block, behind),
                (heads_kept[h][2], unit_block, behind),
                (heads_kept[h][3], v_block, behind),
                (d_outs[h], v_block, behind),
                (inners[3 * h + 1], unit_block, behind),
                (inners[3 * h + 2], v_block, behind),
                (q_decays[h], (blk, 1), whole),
                (k_decays[h], (blk, 1), whole),
                (grads_out[h], (DK, DV), whole),
            )
        ],
        [
            (
                shaped(len(t) * DK - e.shape[1], BF16),
                (blk, len(t) * DK - e.shape[1]),
                behind,
            )
            for t, e in zip(roles, earlies)
        ],
        state_scratch * local_heads,
        seg_len * DK * DV,
    )

    lates[0], parts_ffn_in[:3] = tie_parts(lates[0], parts_ffn_in[:3])
    if group == 4:
        ffn_own, ra, rb = late
        lates[0], ra, rb = tie(lates[0], ra, rb)
        late = ffn_own, ra, rb
    g_units[0] = unit_rows(lates[0], normed, len(roles[0]), True, g_units[0])
    joined = [t for pair in zip(earlies, lates) for t in pair]
    if group == 4:
        ffn_own, ra, rb = late
        joined[0], g_units[0], ra, rb = tie(joined[0], g_units[0], ra, rb)
        ffn_sum, joined[0] = second_step(ffn_own, ra, rb, (joined[0],))
    else:
        ffn_sum = add_blocks(*late)
    joined[0], scattered["mixer_out"] = tie(joined[0], scattered["mixer_out"])
    tile = 512
    operands = []
    for h in range(local_heads):
        weights = heads_kept[h][0]
        operands += [(t, t.shape, whole) for t in joined[2 * h : 2 * h + 2]]
        operands.append((weights, (weights.shape[0], tile), lambda n: (0, n)))
    (d_normed,) = head_call(
        functools.partial(join_kernel, local_heads),
        width // tile,
        operands,
        [(shaped(width, BF16), (seg_len, tile), lambda n: (0, n))],
        [],
        seg_len * width,
    )
    d_normed, parts_ffn_in = tie_parts(d_normed, parts_ffn_in)
    output = (resid + ffn_sum).astype(BF16)
    d_normed, output = tie(d_normed, output)
    if group == 4:
        first = send_step(*first_step(seq_rows(d_normed)))
    parts_mixer_out = spread(scattered["mixer_out"])
    for h in range(1, local_heads):
        lates[h], d_normed = tie(lates[h], d_normed)
        g_units[h] = unit_rows(lates[h], normed, len(roles[h]), True, g_units[h])
    g_ffn_in = place_blocks(
        parts_ffn_in, s ^ near, near, ffn_in.shape, (sub, width), lambda o, n: (n, 0)
    )
    if group == 4:
        own, ra, rb = first
        ra, rb, g_units[-1], g_ffn_in = tie(ra, rb, g_units[-1], g_ffn_in)
        d_normed = second_step(own, ra, rb)
    else:
        d_normed = add_blocks(*send_blocks(seq_rows(d_normed)))
    g_slots = []
    for h in range(local_heads):
        if not balanced:
            cut = g_units[h].reshape(-1, DK, width)
            g_units[h] = jnp.concatenate(
                [pick(cut, jnp.maximum(held[h, c, s], 0)) for c in range(segments)], axis=0
            )
        g_slots.append(reduce_shard(g_units[h]))

    ignored8, norm1_back = jax.vjp(rms_scale, xf, gain_attn)
    d_x_part, d_gain_attn = norm1_back(d_normed)
    input_grad = (d_resid + d_x_part).astype(BF16)
    gains = lax.all_to_all(
        jnp.broadcast_to(jnp.concatenate([d_gain_attn, d_gain_ffn])[None], (segments, 2 * width)),
        "shard",
        split_axis=0,
        concat_axis=0,
        tiled=True,
    )
    gains = jnp.sum(gains, axis=0, keepdims=True)
    parts = []
    for h in range(local_heads):
        last = h == local_heads - 1
        beside = None
        if h == 0:
            g_slots[h], input_grad = tie(g_slots[h], input_grad)
            g_slots[h], parts_mixer_out = tie_parts(g_slots[h], parts_mixer_out)
            g_mixer_out = place_blocks(
                parts_mixer_out,
                s ^ near,
                near,
                mixer_out.shape,
                (mixer_out.shape[0], DV),
                lambda o, n: (0, o * group + n),
                outer=local_heads,
            )
            if sub % 128 == 0:
                g_ffn_out = place_blocks(
                    parts_ffn_out,
                    s ^ near,
                    near,
                    ffn_out.shape,
                    (ffn_out.shape[0], sub),
                    lambda o, n: (0, o * group + n),
                    outer=segments // 2,
                )
            else:
                g_ffn_out = jnp.transpose(
                    ordered(parts_ffn_out).reshape(group, ffn_out.shape[0], segments // 2, sub),
                    (1, 2, 0, 3),
                ).reshape(ffn_out.shape).astype(F32)
            beside = [g_mixer_out, output, gains, g_ffn_out]
        if last and h > 0:
            g_slots[h], gains, g_mixer_out = tie(g_slots[h], gains, g_mixer_out)
            beside = []
            g_slots[h], parts = tie_parts(g_slots[h], parts)
        here = spread(g_slots[h], beside)
        if group == 4 and h == 0:
            g_mixer_out, output, gains, g_ffn_out = beside
        if last:
            if beside is not None and group == 4:
                here[1], gains = tie(here[1], gains)
                gains = gains + swap(gains, 1)
                here[3], gains = tie(here[3], gains)
                gains = gains + swap(gains, 2)
            else:
                step = 1
                while step < group:
                    gains = gains + swap(gains, step)
                    step *= 2
        if balanced and last:
            there = [tuple(cross(piece, 1) for piece in part) for part in here]
            parts += [a + b for a, b in zip(here, there)] + [b + a for a, b in zip(here, there)]
        else:
            lend_here = lend[j] if balanced else lend[h, j]
            stack = jnp.stack([jnp.concatenate(part, axis=0) for part in here])
            parts += here + [
                (cross(pick(stack, s ^ lend_here[n]), 1),) for n in range(lend_here.shape[0])
            ]
    gain_attn_grad, gain_ffn_grad = gains[0, :width], gains[0, width:]
    found = back[j]
    if balanced:
        spare = lend.shape[-1]
        source = jnp.where(
            found[:, 0] == 0,
            s ^ found[:, 1],
            jnp.where(
                found[:, 0] == 1,
                group + found[:, 1],
                group + spare + core * group + (s ^ found[:, 1]),
            ),
        )
    else:
        source = found[:, 0] * (group + lend.shape[-1]) + jnp.where(
            found[:, 2] < 0, s ^ found[:, 1], group + found[:, 2]
        )
    g_mixer_in = place_blocks(
        parts,
        jnp.arange(source.shape[0]),
        source,
        mixer_in.shape,
        (DK, width),
        lambda o, n: (n, 0),
    )
    return (
        output,
        input_grad,
        gain_attn_grad,
        gain_ffn_grad,
        g_mixer_in,
        g_mixer_out,
        g_ffn_in,
        g_ffn_out,
    )


def solution(mesh):
    return jax.shard_map(
        local,
        mesh=mesh,
        in_specs=(
            P(("shard", "seq"), None),
            P(("shard", "seq"), None),
            P(),
            P(),
            P("shard", None),
            P("shard", None),
            P("shard", None),
            P("shard", None),
            P(),
            P(),
        ),
        out_specs=(
            P(("shard", "seq"), None),
            P(("shard", "seq"), None),
            P(),
            P(),
            P("shard", None),
            P("shard", None),
            P("shard", None),
            P("shard", None),
        ),
        check_vma=False,
    )
```

```python
import functools

import jax
import jax.numpy as jnp
import numpy as np
from jax import lax
from jax.experimental import pallas as pl
from jax.experimental.pallas import tpu as pltpu
from jax.sharding import PartitionSpec as P

DK = 256
DV = 512
FF = 4096
QK = 2048
V = 4096


EPS_NORM = 1e-06
EPS_GROUP = 1e-05

F32 = jnp.float32
BF16 = jnp.bfloat16


def dot_nt(left, right, kind=F32):
    return lax.dot_general(
        left, right, (((1,), (1,)), ((), ())), preferred_element_type=F32
    ).astype(kind)


def dot_nn(left, right, kind=F32):
    return lax.dot_general(
        left, right, (((1,), (0,)), ((), ())), preferred_element_type=F32
    ).astype(kind)


def dot_tn(left, right, kind=F32):
    return lax.dot_general(
        left, right, (((0,), (0,)), ((), ())), preferred_element_type=F32
    ).astype(kind)


def rms_scale(v, gain):
    return v * lax.rsqrt(jnp.mean(v * v, axis=-1, keepdims=True) + EPS_NORM) * gain


def gated_gelu(first, second):
    return jax.nn.gelu(first) * second


def unit_owners(heads):
    owners = [(n, 0) for n in range(heads)] + [(n, 1) for n in range(heads)]
    for base in (2, 4):
        owners += [(n, base + half) for n in range(heads) for half in range(2)]
    return owners


def balanced_tables():
    group, segments, per_shard = 4, 8, 6
    number = {owner: u for u, owner in enumerate(unit_owners(8))}
    keep = np.full((2, segments, group), -1, np.int32)
    give = np.zeros((2, segments, group), np.int32)
    back = np.zeros((segments, per_shard, 2), np.int32)
    lend = [[] for _ in range(segments)]
    seen = set()
    for s in range(group):
        a, b = s, s + 4
        if s < 2:
            gates = [(a, 4), (b, 4), (b, 5)], (b + 2, 5)
        else:
            gates = [(a - 2, 5), (a, 4), (a, 5)], (b, 4)
        first = [(a, 0), (a, 1), (a, 2), (a, 3), (b, 2)] + gates[0]
        second = [(b, 0), (b, 1), (b, 3), gates[1]]
        for slot, owner in enumerate(first):
            home, index = divmod(number[owner], per_shard)
            seen.add(number[owner])
            assert home // 2 == slot // 2
            if home == slot:
                keep[0, slot, s] = index
                back[home, index] = (0, s)
            else:
                give[0, home, s] = index
                back[home, index] = (1, len(lend[slot]))
                lend[slot].append(s)
        for chip, owner in enumerate(second):
            home, index = divmod(number[owner], per_shard)
            seen.add(number[owner])
            assert home // 2 == chip
            keep[1, home, s] = index
            give[1, home, s] = index
            back[home, index] = (2, s)
    assert len(seen) == segments * per_shard
    most = max(len(t) for t in lend)
    return keep, give, back, np.asarray([(t + [0] * most)[:most] for t in lend], np.int32)


def unit_tables(group, local_heads, segments):
    heads = group * local_heads
    owners = unit_owners(heads)
    per_shard = len(owners) // segments
    keep = np.full((local_heads, segments, group), -1, np.int32)
    give = np.zeros((local_heads, segments, group), np.int32)
    place = np.zeros((local_heads, group, 6), np.int32)
    held = np.full((local_heads, segments, group), -1, np.int32)
    slot_of = {}
    for chip in range(segments // 2):
        for head in range(heads):
            h, s = divmod(head, group)
            span = range(2 * per_shard * chip, 2 * per_shard * (chip + 1))
            mine = [u for u in span if owners[u][0] == head]
            assert len(mine) <= 2
            for n, u in enumerate(mine):
                home = u // per_shard
                slot = home if len(mine) == 1 else 2 * chip + n
                if slot == home:
                    keep[h, slot, s] = u % per_shard
                else:
                    give[h, home, s] = u % per_shard
                place[h, s, owners[u][1]] = slot
                held[h, slot, s] = owners[u][1]
                slot_of[u] = slot
    lends = [[[] for _ in range(segments)] for _ in range(local_heads)]
    back = np.zeros((segments, per_shard, 3), np.int32)
    for u, (head, _) in enumerate(owners):
        home = u // per_shard
        h, s = divmod(head, group)
        back[home, u % per_shard] = (h, s, -1)
        if slot_of[u] != home:
            assert slot_of[u] == home ^ 1
            back[home, u % per_shard, 2] = len(lends[h][home ^ 1])
            lends[h][home ^ 1].append(s)
    most = max(1, max(len(t) for row in lends for t in row))
    lend = np.asarray(
        [[(t + [0] * most)[:most] for t in row] for row in lends], np.int32
    )
    return keep, give, place, held, back, lend


def tie(*values):
    return lax.optimization_barrier(values)


def mm(left, right, dims):
    return lax.dot_general(left, right, (dims, ((), ())), preferred_element_type=F32)


NN = ((1,), (0,))
NT = ((1,), (1,))
TN = ((0,), (0,))


def turn(v, cosine, sine):
    half = v.shape[-1] // 2
    first, second = v[:, :half], v[:, half:]
    return jnp.concatenate(
        [first * cosine - second * sine, second * cosine + first * sine], axis=-1
    )


def scaled(v, decay):
    return (v.astype(F32) * decay).astype(BF16)


def project_kernel(blk, roles, carried, params, x, w, cosine, sine, k_decay, *refs):
    if carried:
        v_a, *refs = refs
    q, k, v, total, gates, *rest = refs
    y = rest[-1]
    rows = y.shape[0]
    y[...] = mm(x[...], w[...], NT)

    def put(role, part, gate_at):
        value = y[:, part * DK : (part + 1) * DK]
        if role == "q":
            q[...] = turn(value, cosine[...], sine[...]).astype(BF16)
        elif role == "k":
            k[...] = turn(value, cosine[...], sine[...]).astype(BF16)
        elif role == "va":
            v[:, :DK] = value.astype(BF16)
        elif role == "vb":
            v[:, DK:] = value.astype(BF16)
        elif role == "xv":
            rest[0][...] = value.astype(BF16)
        else:
            gates[:, gate_at * DK : (gate_at + 1) * DK] = value.astype(BF16)

    for step in range(len(roles) // 2):

        @pl.when(pl.program_id(0) == step)
        def _(step=step):
            for part in range(2):
                at = 2 * step + part
                put(roles[at], part, roles[:at].count("g"))
            if step == 1:
                if carried:
                    v[:, :DK] = v_a[...]
                state = jnp.zeros(total.shape, F32)
                for r in range(0, rows, blk):
                    kd = scaled(k[r : r + blk, :], k_decay[...])
                    state = params[0] * state + mm(kd, v[r : r + blk, :], TN)
                total[...] = state.astype(BF16)


def join_kernel(count, *refs):
    out = refs[-1]
    total = None
    for n in range(count):
        early, late, weights = refs[3 * n : 3 * n + 3]
        middle = DK + late.shape[1]
        part = mm(early[:, :DK], weights[:DK, :], NN)
        part += mm(early[:, DK:], weights[middle:, :], NN)
        part += mm(late[...], weights[DK:middle, :], NN)
        total = part if total is None else total + part
    out[...] = total.astype(out.dtype)


def select(params, low, high):
    return jnp.where(params[1] > 0.5, low[...].astype(F32), high[...].astype(F32))


def retain_kernel(
    params, q, k, v, low_a, high_a, low_b, high_b, mask, q_decay, k_decay, start,
    hidden, mixed, kept, state,
):
    @pl.when(pl.program_id(0) == 0)
    def _():
        state[...] = start[...].astype(F32)

    weights = (mm(q[...], k[...], NT) * mask[...]).astype(BF16)
    o = mm(weights, v[...], NN)
    o += mm(scaled(q[...], q_decay[...]), state[...].astype(BF16), NN)
    state[...] = params[0] * state[...] + mm(scaled(k[...], k_decay[...]), v[...], TN)
    o = o - jnp.mean(o, axis=-1, keepdims=True)
    inverse = lax.rsqrt(jnp.mean(o * o, axis=-1, keepdims=True) + EPS_GROUP)
    kept[...] = inverse
    low = (o * inverse).astype(BF16)
    mixed[...] = low
    for n, (one, two) in enumerate(((low_a, high_a), (low_b, high_b))):
        columns = slice(n * DK, (n + 1) * DK)
        g = select(params, one, two)
        hidden[:, columns] = (g * jax.nn.sigmoid(g) * low[:, columns].astype(F32)).astype(BF16)


def take(refs, counts):
    pieces, at = [], 0
    for count in counts:
        pieces.append(refs[at : at + count])
        at += count
    return pieces


def gate_back_kernel(heads, params, d_attn, w_out, *refs):
    inputs = take(refs, [8] * heads)
    outputs = take(refs[8 * heads :], [3] * heads)
    states = refs[11 * heads :]

    @pl.when(pl.program_id(0) == 0)
    def _():
        for state in states:
            state[...] = jnp.zeros(state.shape, F32)

    d_hidden = mm(d_attn[...], w_out[...], NN)
    for h in range(heads):
        low_a, high_a, low_b, high_b, mixed, inverse, q, q_decay = inputs[h]
        d_gate, d_out, total = outputs[h]
        g = jnp.concatenate(
            [select(params, low_a, high_a), select(params, low_b, high_b)], axis=1
        )
        dh = d_hidden[:, h * DV : (h + 1) * DV]
        sig = jax.nn.sigmoid(g)
        o = mixed[...].astype(F32)
        d_gate[...] = (dh * o * (sig * (1.0 + g * (1.0 - sig)))).astype(BF16)
        dy = (dh * (g * sig)).astype(BF16).astype(F32)
        do = inverse[...] * (
            dy
            - jnp.mean(dy, axis=-1, keepdims=True)
            - o * jnp.mean(dy * o, axis=-1, keepdims=True)
        )
        do = do.astype(BF16)
        d_out[...] = do
        state = states[h]
        state[...] = params[2 + h] * state[...] + mm(scaled(q[...], q_decay[...]), do, TN)
        total[...] = state[...].astype(BF16)


def inner_back_kernel(roles, params, cosine, sine, *refs):
    heads = len(roles)
    counts = [8 + 2 * t.count("g") for t in roles]
    inputs = take(refs, counts)
    outputs = take(refs[sum(counts) :], [3] * heads)
    states = refs[sum(counts) + 3 * heads :]

    @pl.when(pl.program_id(0) == 0)
    def _():
        for h in range(heads):
            states[h][...] = inputs[h][7][...].astype(F32)

    for h in range(heads):
        q, k, v, d_out, mask, q_decay, k_decay, ignored, *gates = inputs[h]
        early, d_k, d_v = outputs[h]
        state = states[h]
        do = d_out[...]
        weights = (mm(q[...], k[...], NT) * mask[...]).astype(BF16)
        d_v[...] = mm(weights, do, TN)
        d_scores = mm(do, v[...], NT).astype(BF16).astype(F32)
        d_scores = (d_scores * mask[...]).astype(BF16)
        d_k[...] = mm(d_scores, q[...], TN)
        far = mm(do, state[...].astype(BF16), NT).astype(BF16).astype(F32)
        dq = mm(d_scores, k[...], NN) + far * q_decay[...]
        dq = dq.astype(BF16).astype(F32)
        early[:, :DK] = turn(dq, cosine[...], -sine[...]).astype(BF16)
        for n in range(len(gates) // 2):
            value = select(params, gates[2 * n], gates[2 * n + 1]).astype(BF16)
            early[:, (n + 1) * DK : (n + 2) * DK] = value
        state[...] = params[2 + h] * state[...] + mm(scaled(k[...], k_decay[...]), v[...], TN)


def outer_back_kernel(roles, params, cosine, sine, *refs):
    heads = len(roles)
    inputs = take(refs, [9] * heads)
    outputs = refs[9 * heads : 10 * heads]
    states = refs[10 * heads :]

    @pl.when(pl.program_id(0) == 0)
    def _():
        for h in range(heads):
            states[h][...] = inputs[h][8][...].astype(F32)

    other = None
    for h in reversed(range(heads)):
        q, k, v, d_out, d_k, d_v, q_decay, k_decay, ignored = inputs[h]
        state = states[h]
        low = state[...].astype(BF16)
        far = mm(v[...], low, NT).astype(BF16).astype(F32)
        dk = (d_k[...] + far * k_decay[...]).astype(BF16).astype(F32)
        dk = turn(dk, cosine[...], -sine[...]).astype(BF16)
        dv = (d_v[...] + mm(scaled(k[...], k_decay[...]), low, NN)).astype(BF16)
        values = {"k": dk, "va": dv[:, :DK], "vb": dv[:, DK:], "xv": other}
        for n, role in enumerate(t for t in roles[h] if t in values):
            outputs[h][:, n * DK : (n + 1) * DK] = values[role]
        other = dv[:, :DK]
        state[...] = params[2 + h] * state[...] + mm(scaled(q[...], q_decay[...]), d_out[...], TN)


def unit_kernel(x, normed, *refs):
    refs[-1][...] = mm(x[...], normed[...], TN).astype(BF16)


def unit_rows(x, normed, count, late, into=None):
    rows, width = normed.shape
    units = x.shape[1] // DK

    def where(n):
        return (n + 1, 0) if late else (jnp.where(n == 0, 0, n + count - units), 0)

    arrays = [x, normed] + ([] if into is None else [into])
    return pl.pallas_call(
        unit_kernel,
        grid=(units,),
        in_specs=[
            pl.BlockSpec((rows, DK), lambda n: (0, n)),
            pl.BlockSpec((rows, width), lambda n: (0, 0)),
        ]
        + ([] if into is None else [pl.BlockSpec(memory_space=pl.ANY)]),
        out_specs=pl.BlockSpec((DK, width), where),
        out_shape=jax.ShapeDtypeStruct((count * DK, width), BF16),
        input_output_aliases={} if into is None else {2: 0},
        compiler_params=pltpu.CompilerParams(vmem_limit_bytes=48 * 2**20),
        cost_estimate=pl.CostEstimate(
            flops=rows * width * DK, bytes_accessed=rows * width, transcendentals=0
        ),
    )(*arrays)


def head_call(kernel, grid, operands, outputs, scratch, flops, size=None):
    arrays = [t[0] for t in operands]
    if size is None:
        size = sum(t.size * t.dtype.itemsize for t in arrays + [t[0] for t in outputs])
    call = pl.pallas_call(
        kernel,
        grid=(grid,),
        in_specs=[
            pl.BlockSpec(memory_space=pltpu.SMEM) if block is None else pl.BlockSpec(block, where)
            for _, block, where in operands
        ],
        out_specs=[pl.BlockSpec(block, where) for _, block, where in outputs],
        scratch_shapes=scratch,
        out_shape=[t[0] for t in outputs],
        compiler_params=pltpu.CompilerParams(vmem_limit_bytes=56 * 2**20),
        cost_estimate=pl.CostEstimate(flops=flops, bytes_accessed=size, transcendentals=0),
    )
    return list(call(*arrays))


def place_kernel(parts, target, source, *refs):
    out = refs[-1]
    code = source[pl.program_id(1)]
    for i, part in enumerate(parts):

        @pl.when(code == i)
        def _(part=part):
            row = 0
            for n in part:
                piece = refs[n]
                out[row : row + piece.shape[0], :] = piece[...].astype(F32)
                row += piece.shape[0]


def place_blocks(parts, target, source, shape, block, where, outer=1):
    flat, index = [], []
    for part in parts:
        for piece in part:
            if not any(piece is t for t in flat):
                flat.append(piece)
        index.append([next(n for n, t in enumerate(flat) if t is piece) for piece in part])
    return pl.pallas_call(
        functools.partial(place_kernel, index),
        grid_spec=pltpu.PrefetchScalarGridSpec(
            num_scalar_prefetch=2,
            grid=(outer, target.shape[0]),
            in_specs=[
                pl.BlockSpec((t.shape[0], t.shape[1] // outer), lambda o, n, target, source: (0, o))
                for t in flat
            ],
            out_specs=pl.BlockSpec(block, lambda o, n, target, source: where(o, target[n])),
        ),
        out_shape=jax.ShapeDtypeStruct(shape, F32),
        compiler_params=pltpu.CompilerParams(vmem_limit_bytes=48 * 2**20),
    )(target.astype(jnp.int32), source.astype(jnp.int32), *flat)


def local(
    tokens,
    cotangent,
    gain_attn,
    gain_ffn,
    mixer_in,
    mixer_out,
    ffn_in,
    ffn_out,
    segment_order,
    decay_index,
):
    rows, width = tokens.shape
    group = lax.axis_size("seq")
    segments = lax.axis_size("shard")
    heads = decay_index.shape[0]
    local_heads = heads // group
    seg_len = rows * group
    blk = min(512, seg_len)
    blocks = seg_len // blk
    vcols = local_heads * DV
    s = lax.axis_index("seq")
    j = lax.axis_index("shard")

    def swap(v, d):
        return lax.ppermute(v, "seq", [(i, i ^ d) for i in range(group)])

    def cross(v, d):
        return lax.ppermute(v, "shard", [(i, i ^ d) for i in range(segments)])

    def pick(v, i):
        return lax.dynamic_index_in_dim(v, i, 0, keepdims=False)

    def spread(v, beside=None):
        if group == 4:
            h = v.shape[0] // 2
            r1 = swap(v, 1)
            r2 = swap(v, 2)
            if beside:
                r1, r2, beside[:] = tie(r1, r2, list(beside))
            return [(v,), (r1,), (r2,), (swap(r1[:h], 2), swap(r2[h:], 1))]
        return [(v,)] + [(swap(v, d),) for d in range(1, group)]

    def ordered(parts):
        r = parts[0][0].shape[0]
        out = jnp.zeros((group * r,) + parts[0][0].shape[1:], parts[0][0].dtype)
        for d, part in enumerate(parts):
            row = (s ^ d) * r
            for piece in part:
                out = lax.dynamic_update_slice_in_dim(out, piece, row, 0)
                row = row + piece.shape[0]
        return out

    def gather_near(v):
        return jnp.concatenate([piece for part in spread(v) for piece in part], axis=0)

    def gather_seq(v):
        return ordered(spread(v))

    def first_step(blk_of):
        b = [blk_of(d) for d in range(4)]
        h = b[0].shape[0] // 2
        sa = jnp.concatenate([b[1][:h], b[3][:h]], axis=0)
        sb = jnp.concatenate([b[2][h:], b[3][h:]], axis=0)
        return b, *tie(sa, sb)

    def send_step(b, sa, sb):
        return b, swap(sa, 1), swap(sb, 2)

    def second_step(b, ra, rb, held=()):
        h = b[0].shape[0] // 2
        ra, rb = ra.astype(F32), rb.astype(F32)
        qa = (b[2][:h].astype(F32) + ra[h:]).astype(BF16)
        qb = (b[1][h:].astype(F32) + rb[h:]).astype(BF16)
        qa, qb, *held = tie(qa, qb, *held)
        qa, qb = swap(qa, 2), swap(qb, 1)
        top = b[0][:h].astype(F32) + ra[:h] + qa.astype(F32)
        low_half = b[0][h:].astype(F32) + rb[:h] + qb.astype(F32)
        total = jnp.concatenate([top, low_half], axis=0)
        return (total, *held) if held else total

    def send_blocks(blk_of):
        sent = tie(*(blk_of(d) for d in range(group)))
        return sent[0], [swap(sent[d], d) for d in range(group - 1, 0, -1)]

    def add_blocks(own, got):
        own = own.astype(F32)
        for t in got:
            own = own + t.astype(F32)
        return own

    def near_rows(v):
        return lambda d: v[d * rows : (d + 1) * rows]

    def seq_rows(v):
        return lambda d: lax.dynamic_slice_in_dim(v, (s ^ d) * rows, rows, 0)

    def gather_shard(v):
        return lax.all_gather(v, "shard", axis=0, tiled=True)

    def reduce_shard(v):
        return lax.psum_scatter(v, "shard", scatter_dimension=0, tiled=True)

    balanced = group == 4 and local_heads == 2 and segments == 8
    units = mixer_in.reshape(-1, DK, width)
    if balanced:
        keep, give, back, lend = (jnp.asarray(t) for t in balanced_tables())
        core = j % 2
    else:
        keep, give, place, held, back, lend = (
            jnp.asarray(t) for t in unit_tables(group, local_heads, segments)
        )

    def offered(h):
        kept, given = keep[h, j, s], give[h, j, s]
        if balanced and h == 1:
            cut = mixer_in.reshape(-1, DK // 2, width)
            own = pick(cut, 2 * jnp.maximum(kept, 0) + core)
            given = cross(pick(cut, 2 * given + 1 - core), 1)
        else:
            own = pick(units, jnp.maximum(kept, 0))
            given = cross(pick(units, given), 1)
        return jnp.where(kept >= 0, own, given)

    sub = ffn_in.shape[0] // group
    ffn_out_cut = ffn_out.reshape(ffn_out.shape[0], segments // 2, group, sub)

    my_rank = jnp.sum(jnp.where(jnp.arange(segments) == j, segment_order, 0))
    all_logs = jnp.log1p(-jnp.exp2(-(5.0 + decay_index.astype(F32))))
    logs = lax.dynamic_index_in_dim(all_logs.reshape(local_heads, group), s, 1, keepdims=False)
    half = DK // 2
    inv_freq = jnp.exp(-jnp.log(10000.0) * jnp.arange(half).astype(F32) / half)
    positions = my_rank * seg_len + jnp.arange(seg_len, dtype=jnp.int32)
    angles = positions.astype(F32)[:, None] * inv_freq[None, :]
    cosine = jnp.cos(angles)
    sine = jnp.sin(angles)
    steps = jnp.arange(blk).astype(F32)
    gap = steps[:, None] - steps[None, :]
    masks = jnp.where(
        gap[None] >= 0.0, jnp.exp(jnp.maximum(gap, 0.0)[None] * logs[:, None, None]), 0.0
    )
    q_decays = jnp.exp((steps + 1.0)[None, :] * logs[:, None])[..., None]
    k_decays = jnp.exp((blk - 1.0 - steps)[None, :] * logs[:, None])[..., None]
    block_decays = jnp.exp(blk * logs)

    xf = tokens.astype(F32)
    normed = gather_seq(rms_scale(xf, gain_attn).astype(BF16))
    d_ffn = gather_near(cotangent)
    slots = [gather_shard(offered(0))]
    slots[0], normed, d_ffn, cosine, sine, masks, q_decays, k_decays = tie(
        slots[0], normed, d_ffn, cosine, sine, masks, q_decays, k_decays
    )
    for h in range(1, local_heads):
        slots.append(gather_shard(offered(h)))
    mixer_out_cut = jnp.concatenate(
        [
            lax.dynamic_slice_in_dim(mixer_out, (h * group + s) * DV, DV, 1)
            for h in range(local_heads)
        ],
        axis=1,
    )
    mixer_out_cut, slots[0] = tie(mixer_out_cut, slots[0])
    w_out = gather_shard(mixer_out_cut)
    later = [
        lax.dynamic_slice_in_dim(ffn_in, s * sub, sub, 0),
        lax.dynamic_index_in_dim(ffn_out_cut, s, 2, keepdims=False).reshape(ffn_out.shape[0], -1),
    ]
    inner_cols = later[1].shape[1]

    ranks = segment_order
    piece = DK // segments

    def exchange_states(hs, totals, reverse, beside=()):
        cut = jnp.concatenate([t.reshape(segments, piece, DV) for t in totals], axis=1)
        got = lax.all_to_all(cut, "shard", split_axis=0, concat_axis=0, tiled=True)
        got, *beside = tie(got, *beside)
        apart = ranks[:, None] - ranks[None, :] - 1
        if reverse:
            apart = -apart - 2
        distance = apart.astype(F32)
        joined = []
        for n, h in enumerate(hs):
            coef = jnp.where(
                distance >= 0.0, jnp.exp(jnp.maximum(distance, 0.0) * seg_len * logs[h]), 0.0
            )
            part = got[:, n * piece : (n + 1) * piece].astype(F32)
            joined.append(jnp.sum(coef[..., None, None] * part[None], axis=1).astype(BF16))
        joined = jnp.concatenate(joined, axis=1)
        back_cut = lax.all_to_all(joined, "shard", split_axis=0, concat_axis=0, tiled=True)
        states = [
            back_cut[:, n * piece : (n + 1) * piece].reshape(DK, DV) for n in range(len(hs))
        ]
        return (states, *beside)

    def whole(n):
        return (0, 0)

    def ahead(n):
        return (n, 0)

    def behind(n):
        return (blocks - 1 - n, 0)

    def shaped(columns, kind, r=seg_len):
        return jax.ShapeDtypeStruct((r, columns), kind)

    state_scratch = [pltpu.VMEM((DK, DV), F32)]
    half_block = (blk, half)
    unit_block, v_block = (blk, DK), (blk, DV)
    ret_flops = 2 * seg_len * (DK + DV) * (blk + DK)
    low = s < group // 2
    if balanced:
        roles = [["q", "k", "va", "vb", "xv", "g", "g", "g"], ["q", "k", "vb", "g"]]
    else:
        roles = [["q", "k", "va", "vb", "g", "g"]] * local_heads
    params = [
        (jnp.stack([block_decays[h], low.astype(F32)]), None, None) for h in range(local_heads)
    ]
    heads_kept = []
    extra_v = None
    for h in range(local_heads):
        if balanced:
            weights = slots[h]
        else:
            cut = slots[h].reshape(-1, DK, width)
            weights = jnp.concatenate([pick(cut, place[h, s, c]) for c in range(6)], axis=0)
        carried = "va" not in roles[h]
        gate_count = roles[h].count("g")
        q, k, v, total, gates, *extra = head_call(
            functools.partial(project_kernel, blk, roles[h], carried),
            len(roles[h]) // 2,
            [
                params[h],
                (normed, (seg_len, width), whole),
                (weights, (2 * DK, width), ahead),
                (cosine, (seg_len, half), whole),
                (sine, (seg_len, half), whole),
                (k_decays[h], (blk, 1), whole),
            ]
            + ([(extra_v, (seg_len, DK), whole)] if carried else []),
            [
                (shaped(DK, BF16), (seg_len, DK), whole),
                (shaped(DK, BF16), (seg_len, DK), whole),
                (shaped(DV, BF16), (seg_len, DV), whole),
                (shaped(DV, BF16, DK), (DK, DV), whole),
                (shaped(gate_count * DK, BF16), (seg_len, gate_count * DK), whole),
            ]
            + ([(shaped(DK, BF16), (seg_len, DK), whole)] if "xv" in roles[h] else []),
            [pltpu.VMEM((seg_len, 2 * DK), F32)],
            2 * seg_len * width * len(roles[h]) * DK,
        )
        extra_v = extra[0] if extra else None
        (state_in,) = exchange_states([h], [total], False)[0]
        if h + 1 < local_heads:
            slots[h + 1], state_in, *later[:] = tie(slots[h + 1], state_in, *later)
        heads_kept.append((weights, q, k, v, gates, state_in))

    def columns(v, c, order):
        return (v, unit_block, lambda n, c=c: (order(n)[0], c))

    if balanced:
        gates0, gates1 = heads_kept[0][4], heads_kept[1][4]
        swapped = swap(jnp.where(low, gates1, gates0[:, :DK]), 2)

        def gate_operands(h, order):
            if h == 0:
                four = (gates0, 0), (gates0, 1), (swapped, 0), (gates0, 2)
            else:
                four = (gates0, 1), (gates1, 0), (gates0, 2), (swapped, 0)
            return [columns(v, c, order) for v, c in four]

    else:

        def gate_operands(h, order):
            return [columns(heads_kept[h][4], c, order) for c in (0, 0, 1, 1)]

    kept = []
    for h in range(local_heads):
        weights, q, k, v, gates, state_in = heads_kept[h]
        hidden, mixed, retained = head_call(
            retain_kernel,
            blocks,
            [
                params[h],
                (q, unit_block, ahead),
                (k, unit_block, ahead),
                (v, v_block, ahead),
                *gate_operands(h, ahead),
                (masks[h], (blk, blk), whole),
                (q_decays[h], (blk, 1), whole),
                (k_decays[h], (blk, 1), whole),
                (state_in, (DK, DV), whole),
            ],
            [
                (shaped(DV, BF16), v_block, ahead),
                (shaped(DV, BF16), v_block, ahead),
                (shaped(1, F32), (blk, 1), ahead),
            ],
            state_scratch,
            ret_flops,
        )
        kept.append((retained, mixed, hidden))
    hidden = jnp.concatenate([t[-1] for t in kept], axis=1)
    w_ffn_in, w_ffn_out = (gather_shard(t) for t in later)

    resid = xf + add_blocks(*send_blocks(seq_rows(dot_nt(hidden, w_out, BF16))))
    normed2 = gather_near(rms_scale(resid, gain_ffn).astype(BF16))
    proj2 = dot_nt(normed2, w_ffn_in)
    first, second = proj2[:, :inner_cols], proj2[:, inner_cols:]
    inner2 = gated_gelu(first, second).astype(BF16)

    g_ffn_out, d_ffn = tie(dot_tn(d_ffn, inner2, BF16), d_ffn)
    scattered = {"ffn_out": reduce_shard(g_ffn_out)}
    d_inner2 = dot_nn(d_ffn, w_ffn_out)
    ignored2, gelu_back = jax.vjp(gated_gelu, first, second)
    d_first, d_second = gelu_back(d_inner2)
    dproj2 = jnp.concatenate([d_first, d_second], axis=1).astype(BF16)
    d_normed2 = dot_nn(dproj2, w_ffn_in, BF16)
    g_ffn_in = dot_tn(dproj2, normed2, BF16)
    if group == 4:
        terms, ra, rb = send_step(*first_step(near_rows(d_normed2)))
        ra, rb, g_ffn_in = tie(ra, rb, g_ffn_in)
        d_normed2 = second_step(terms, ra, rb)
    else:
        d_normed2 = add_blocks(*send_blocks(near_rows(d_normed2)))
    scattered["ffn_in"] = reduce_shard(g_ffn_in)
    ignored3, norm2_back = jax.vjp(rms_scale, resid, gain_ffn)
    d_resid_part, d_gain_ffn = norm2_back(d_normed2)
    d_resid = cotangent.astype(F32) + d_resid_part
    (d_attn,) = tie(d_resid.astype(BF16))
    d_attn = gather_seq(d_attn)
    d_attn, scattered["ffn_out"] = tie(d_attn, scattered["ffn_out"])
    parts_ffn_out = spread(scattered["ffn_out"])

    def tie_parts(v, parts):
        flat = tie(v, *(piece for part in parts for piece in part))
        rest = list(flat[1:])
        return flat[0], [tuple(rest.pop(0) for _ in part) for part in parts]

    all_params = (
        jnp.concatenate([jnp.stack([jnp.float32(0.0), low.astype(F32)]), block_decays]),
        None,
        None,
    )
    outs = head_call(
        functools.partial(gate_back_kernel, local_heads),
        blocks,
        [
            all_params,
            (d_attn, (blk, width), behind),
            (w_out, (width, vcols), whole),
        ]
        + [
            t
            for h in range(local_heads)
            for t in (
                *gate_operands(h, behind),
                (kept[h][1], v_block, behind),
                (kept[h][0], (blk, 1), behind),
                (heads_kept[h][1], unit_block, behind),
                (q_decays[h], (blk, 1), whole),
            )
        ],
        [
            (shaped(DV, BF16), v_block, behind),
            (shaped(DV, BF16), v_block, behind),
            (shaped(DV, BF16, DK), (DK, DV), whole),
        ]
        * local_heads,
        state_scratch * local_heads,
        2 * seg_len * (DK * DV * local_heads + width * vcols),
    )
    d_gates, d_outs, totals = outs[0::3], outs[1::3], outs[2::3]
    if balanced:
        d_swapped = jnp.where(low, d_gates[0][:, DK:], d_gates[1][:, DK:])
        d_swapped, parts_ffn_out[:3] = tie_parts(d_swapped, parts_ffn_out[:3])
        d_swapped = swap(d_swapped, 2)
    else:
        d_swapped = totals[0]
    hidden, totals[0] = tie(hidden, totals[0])
    g_mixer_out = dot_tn(d_attn, hidden, BF16)
    totals[0], d_swapped, g_mixer_out = tie(totals[0], d_swapped, g_mixer_out)
    d_outs[0], g_mixer_out = tie(d_outs[0], g_mixer_out)
    scattered["mixer_out"] = reduce_shard(g_mixer_out)
    if balanced:
        d_gate_pairs = [
            [
                ((d_gates[0], 0), (d_swapped, 0)),
                ((d_gates[1], 0), (d_gates[0], 0)),
                ((d_gates[1], 1), (d_gates[0], 1)),
            ],
            [((d_swapped, 0), (d_gates[1], 0))],
        ]
    else:
        d_gate_pairs = [[((t, 0), (t, 0)), ((t, 1), (t, 1))] for t in d_gates]
    inners = head_call(
        functools.partial(inner_back_kernel, roles),
        blocks,
        [all_params, (cosine, half_block, ahead), (sine, half_block, ahead)]
        + [
            t
            for h in range(local_heads)
            for t in (
                (heads_kept[h][1], unit_block, ahead),
                (heads_kept[h][2], unit_block, ahead),
                (heads_kept[h][3], v_block, ahead),
                (d_outs[h], v_block, ahead),
                (masks[h], (blk, blk), whole),
                (q_decays[h], (blk, 1), whole),
                (k_decays[h], (blk, 1), whole),
                (heads_kept[h][5], (DK, DV), whole),
                *(columns(v, c, ahead) for pair in d_gate_pairs[h] for v, c in pair),
            )
        ],
        [
            t
            for h in range(local_heads)
            for t in (
                (
                    shaped((1 + len(d_gate_pairs[h])) * DK, BF16),
                    (blk, (1 + len(d_gate_pairs[h])) * DK),
                    ahead,
                ),
                (shaped(DK, F32), unit_block, ahead),
                (shaped(DV, F32), v_block, ahead),
            )
        ],
        state_scratch * local_heads,
        ret_flops,
    )
    inner2, totals[0] = tie(inner2, totals[0])
    ffn_terms = near_rows(dot_nt(inner2, w_ffn_out, BF16))
    if group == 4:
        ffn_own, *prepared = first_step(ffn_terms)
    else:
        prepared = [ffn_terms(d) for d in range(group)]
    flat_ffn_out = [piece for part in parts_ffn_out for piece in part]
    beside = [scattered["ffn_in"], *inners, *flat_ffn_out, *prepared]
    grads_out, scattered["ffn_in"], *flat = exchange_states(
        range(local_heads), totals, True, beside
    )
    inners = flat[: 3 * local_heads]
    rest = flat[3 * local_heads :]
    parts_ffn_out = [tuple(rest.pop(0) for _ in part) for part in parts_ffn_out]
    if group == 4:
        late = send_step(ffn_own, *rest)
    else:
        late = send_blocks(lambda d: rest[d])
    parts_ffn_in = spread(scattered["ffn_in"])
    near = jnp.arange(group)
    earlies = inners[0::3]
    g_units = [
        unit_rows(earlies[h], normed, len(roles[h]), False) for h in range(local_heads)
    ]
    flat = list(tie(*grads_out, *g_units))
    grads_out, g_units = flat[:local_heads], flat[local_heads:]
    lates = head_call(
        functools.partial(outer_back_kernel, roles),
        blocks,
        [all_params, (cosine, half_block, behind), (sine, half_block, behind)]
        + [
            t
            for h in range(local_heads)
            for t in (
                (heads_kept[h][1], unit_block, behind),
                (heads_kept[h][2], unit_block, behind),
                (heads_kept[h][3], v_block, behind),
                (d_outs[h], v_block, behind),
                (inners[3 * h + 1], unit_block, behind),
                (inners[3 * h + 2], v_block, behind),
                (q_decays[h], (blk, 1), whole),
                (k_decays[h], (blk, 1), whole),
                (grads_out[h], (DK, DV), whole),
            )
        ],
        [
            (
                shaped(len(t) * DK - e.shape[1], BF16),
                (blk, len(t) * DK - e.shape[1]),
                behind,
            )
            for t, e in zip(roles, earlies)
        ],
        state_scratch * local_heads,
        seg_len * DK * DV,
    )

    if group == 4:
        ffn_own, ra, rb = late
        lates[0], ra, rb = tie(lates[0], ra, rb)
        late = ffn_own, ra, rb
    g_units[0] = unit_rows(lates[0], normed, len(roles[0]), True, g_units[0])
    joined = [t for pair in zip(earlies, lates) for t in pair]
    if group == 4:
        ffn_own, ra, rb = late
        joined[0], g_units[0], ra, rb = tie(joined[0], g_units[0], ra, rb)
        ffn_sum, joined[0] = second_step(ffn_own, ra, rb, (joined[0],))
    else:
        ffn_sum = add_blocks(*late)
    joined[0], scattered["mixer_out"] = tie(joined[0], scattered["mixer_out"])
    joined[0], parts_ffn_in[:3] = tie_parts(joined[0], parts_ffn_in[:3])
    tile = 512
    operands = []
    for h in range(local_heads):
        weights = heads_kept[h][0]
        operands += [(t, t.shape, whole) for t in joined[2 * h : 2 * h + 2]]
        operands.append((weights, (weights.shape[0], tile), lambda n: (0, n)))
    (d_normed,) = head_call(
        functools.partial(join_kernel, local_heads),
        width // tile,
        operands,
        [(shaped(width, BF16), (seg_len, tile), lambda n: (0, n))],
        [],
        seg_len * width,
    )
    d_normed, parts_ffn_in = tie_parts(d_normed, parts_ffn_in)
    output = (resid + ffn_sum).astype(BF16)
    d_normed, output = tie(d_normed, output)
    if group == 4:
        first = send_step(*first_step(seq_rows(d_normed)))
    parts_mixer_out = spread(scattered["mixer_out"])
    for h in range(1, local_heads):
        lates[h], d_normed = tie(lates[h], d_normed)
        g_units[h] = unit_rows(lates[h], normed, len(roles[h]), True, g_units[h])
    g_ffn_in = place_blocks(
        parts_ffn_in, s ^ near, near, ffn_in.shape, (sub, width), lambda o, n: (n, 0)
    )
    if group == 4:
        own, ra, rb = first
        ra, rb, g_units[-1], g_ffn_in = tie(ra, rb, g_units[-1], g_ffn_in)
        d_normed = second_step(own, ra, rb)
    else:
        d_normed = add_blocks(*send_blocks(seq_rows(d_normed)))
    g_slots = []
    for h in range(local_heads):
        if not balanced:
            cut = g_units[h].reshape(-1, DK, width)
            g_units[h] = jnp.concatenate(
                [pick(cut, jnp.maximum(held[h, c, s], 0)) for c in range(segments)], axis=0
            )
        g_slots.append(reduce_shard(g_units[h]))

    ignored8, norm1_back = jax.vjp(rms_scale, xf, gain_attn)
    d_x_part, d_gain_attn = norm1_back(d_normed)
    input_grad = (d_resid + d_x_part).astype(BF16)
    gains = lax.all_to_all(
        jnp.broadcast_to(jnp.concatenate([d_gain_attn, d_gain_ffn])[None], (segments, 2 * width)),
        "shard",
        split_axis=0,
        concat_axis=0,
        tiled=True,
    )
    gains = jnp.sum(gains, axis=0, keepdims=True)
    parts = []
    for h in range(local_heads):
        last = h == local_heads - 1
        beside = None
        if h == 0:
            g_slots[h], input_grad = tie(g_slots[h], input_grad)
            g_slots[h], parts_mixer_out = tie_parts(g_slots[h], parts_mixer_out)
            g_mixer_out = place_blocks(
                parts_mixer_out,
                s ^ near,
                near,
                mixer_out.shape,
                (mixer_out.shape[0], DV),
                lambda o, n: (0, o * group + n),
                outer=local_heads,
            )
            if sub % 128 == 0:
                g_ffn_out = place_blocks(
                    parts_ffn_out,
                    s ^ near,
                    near,
                    ffn_out.shape,
                    (ffn_out.shape[0], sub),
                    lambda o, n: (0, o * group + n),
                    outer=segments // 2,
                )
            else:
                g_ffn_out = jnp.transpose(
                    ordered(parts_ffn_out).reshape(group, ffn_out.shape[0], segments // 2, sub),
                    (1, 2, 0, 3),
                ).reshape(ffn_out.shape).astype(F32)
            beside = [g_mixer_out, output, gains, g_ffn_out]
        if last and h > 0:
            g_slots[h], gains, g_mixer_out = tie(g_slots[h], gains, g_mixer_out)
            beside = []
            g_slots[h], parts = tie_parts(g_slots[h], parts)
        here = spread(g_slots[h], beside)
        if group == 4 and h == 0:
            g_mixer_out, output, gains, g_ffn_out = beside
        if last:
            if beside is not None and group == 4:
                here[1], gains = tie(here[1], gains)
                gains = gains + swap(gains, 1)
                here[3], gains = tie(here[3], gains)
                gains = gains + swap(gains, 2)
            else:
                step = 1
                while step < group:
                    gains = gains + swap(gains, step)
                    step *= 2
        if balanced and last:
            there = [tuple(cross(piece, 1) for piece in part) for part in here]
            parts += [a + b for a, b in zip(here, there)] + [b + a for a, b in zip(here, there)]
        else:
            lend_here = lend[j] if balanced else lend[h, j]
            stack = jnp.stack([jnp.concatenate(part, axis=0) for part in here])
            parts += here + [
                (cross(pick(stack, s ^ lend_here[n]), 1),) for n in range(lend_here.shape[0])
            ]
    gain_attn_grad, gain_ffn_grad = gains[0, :width], gains[0, width:]
    found = back[j]
    if balanced:
        spare = lend.shape[-1]
        source = jnp.where(
            found[:, 0] == 0,
            s ^ found[:, 1],
            jnp.where(
                found[:, 0] == 1,
                group + found[:, 1],
                group + spare + core * group + (s ^ found[:, 1]),
            ),
        )
    else:
        source = found[:, 0] * (group + lend.shape[-1]) + jnp.where(
            found[:, 2] < 0, s ^ found[:, 1], group + found[:, 2]
        )
    g_mixer_in = place_blocks(
        parts,
        jnp.arange(source.shape[0]),
        source,
        mixer_in.shape,
        (DK, width),
        lambda o, n: (n, 0),
    )
    return (
        output,
        input_grad,
        gain_attn_grad,
        gain_ffn_grad,
        g_mixer_in,
        g_mixer_out,
        g_ffn_in,
        g_ffn_out,
    )


def solution(mesh):
    return jax.shard_map(
        local,
        mesh=mesh,
        in_specs=(
            P(("shard", "seq"), None),
            P(("shard", "seq"), None),
            P(),
            P(),
            P("shard", None),
            P("shard", None),
            P("shard", None),
            P("shard", None),
            P(),
            P(),
        ),
        out_specs=(
            P(("shard", "seq"), None),
            P(("shard", "seq"), None),
            P(),
            P(),
            P("shard", None),
            P("shard", None),
            P("shard", None),
            P("shard", None),
        ),
        check_vma=False,
    )
```
